32 devices in a mesh: dp: 8 (over y, x, core), tensor: 4 (over z).
Axes of the slice: x: 2, y: 2, z: 4, core: 2. Of those that a mesh axis runs over, the one named last changes fastest.
Arguments:
- h_in: bfloat16 [32, 256, 768], P(('dp', 'tensor')), may hold values from -6 to 6
- g_in: bfloat16 [32, 256, 768], P(('dp', 'tensor')), may hold values from -6 to 6
- seg_ids: int32 [32, 256], P(('dp', 'tensor')), may hold values from 0 to 15, as said below
- target_flags: int32 [32, 256], P(('dp', 'tensor')), may hold values from 0 to 1, as said below
- perm_order: int32 [32, 256], P(('dp', 'tensor')), may hold values from 0 to 255, each once within a row
- w_query: bfloat16 [1, 768, 768], replicated, may hold values from -0.21875 to 0.21875
- w_key: bfloat16 [1, 768, 768], replicated, may hold values from -0.21875 to 0.21875
- w_value: bfloat16 [1, 768, 768], replicated, may hold values from -0.21875 to 0.21875
- w_out: bfloat16 [1, 768, 768], replicated, may hold values from -0.875 to 0.875
- w_rel: bfloat16 [1, 768, 768], replicated, may hold values from -0.21875 to 0.21875
- attn_bias: float32 [1, 3, 768], replicated, may hold values from -3 to 3
- seg_embed: float32 [1, 2, 768], replicated, may hold values from -3 to 3
- norm_gain: float32 [1, 2, 768], replicated, may hold values from 0.5 to 1.5
- norm_bias: float32 [1, 2, 768], replicated, may hold values from -2 to 2
- w_up: bfloat16 [1, 768, 3072], P(None, None, 'tensor'), may hold values from -0.21875 to 0.21875
- b_up: bfloat16 [1, 3072], P(None, 'tensor'), may hold values from -3 to 3
- w_down: bfloat16 [1, 3072, 768], P(None, 'tensor'), may hold values from -0.109375 to 0.109375
- b_down: float32 [1, 768], replicated, may hold values from -2 to 2
- d_h_out: bfloat16 [32, 256, 768], P(('dp', 'tensor')), may hold values from -6 to 6
- d_g_out: bfloat16 [32, 256, 768], P(('dp', 'tensor')), may hold values from -6 to 6
Outputs:
- h_out: bfloat16 [32, 256, 768], P(('dp', 'tensor'))
- g_out: bfloat16 [32, 256, 768], P(('dp', 'tensor'))
- d_h_in: float32 [32, 256, 768], P(('dp', 'tensor'))
- d_g_in: float32 [32, 256, 768], P(('dp', 'tensor'))
- d_w_query: float32 [1, 768, 768], P(None, 'dp', 'tensor')
- d_w_key: float32 [1, 768, 768], P(None, 'dp', 'tensor')
- d_w_value: float32 [1, 768, 768], P(None, 'dp', 'tensor')
- d_w_out: float32 [1, 768, 768], P(None, 'dp', 'tensor')
- d_w_rel: float32 [1, 768, 768], P(None, 'dp', 'tensor')
- d_w_up: float32 [1, 768, 3072], P(None, 'dp', 'tensor')
- d_w_down: float32 [1, 3072, 768], P(None, 'tensor', 'dp')
- d_vectors: float32 [1, 10752], P(None, ('dp', 'tensor'))
The draws below stay inside these ranges and needn't reach their ends.
Inputs may be any that keep to these rules, and one draw needn't show every extreme that they name: `seg_ids`: within each sequence the ids start at 0, never fall and rise by one at each new document; every sequence holds exactly 16 documents, each of an even number of tokens, 2 or more. `target_flags`: the first two tokens of every document are 0. `perm_order`: each sequence holds every number of 0 to 255 once.
All inputs are finite; a program needn't handle non-finite values.
Results may differ from the reference program's by a relative error of at most 0.024.
Values may be sent and summed in bfloat16 or wider, within the bound.
No kernel may reach another device: no remote copies, remote signals or barrier semaphores. Data moves between devices by JAX's collectives and lax.ppermute only.
A program may use at most 192 MiB of HBM per device.

```python
import math
import jax
import jax.numpy as jnp
from jax import lax

D = 768
HEADS = 12
HEAD_DIM = 64
FF = 3072
SEQ_LEN = 256
LAYERS = 1
SEQS = 32


def doc_starts(key):
    slot_count = SEQ_LEN // 2 - 1
    picks = SEQ_LEN // 16 - 1
    scores = jax.random.randint(key, (SEQS, slot_count), 0, 1 << 20) * slot_count + jnp.arange(slot_count)[None, :]
    ranks = jnp.argsort(jnp.argsort(scores, axis=1), axis=1)
    chosen = (ranks < picks).astype(jnp.int32)
    starts = jnp.zeros((SEQS, SEQ_LEN), jnp.int32)
    places = 2 * jnp.arange(slot_count) + 2
    starts = starts.at[:, places].set(chosen)
    return starts > 0


def draw_seg_ids(key, part):
    starts = doc_starts(key)
    return jnp.cumsum(starts.astype(jnp.int32), axis=1).astype(jnp.int32)


def draw_target_flags(key, part):
    starts = doc_starts(key)
    key = jax.random.fold_in(key, 7)
    position = jnp.arange(SEQ_LEN)[None, :]
    first_place = starts | (position == 0)
    second_place = jnp.pad(starts[:, :-1], ((0, 0), (1, 0))) | (position == 1)
    picked = jax.random.randint(key, (SEQS, SEQ_LEN), 0, 6) == 0
    return (picked & ~first_place & ~second_place).astype(jnp.int32)


def levels(own_key, shape, split, low, top_value):
    loudness = 1.0
    for dim, shards_of in split:
        steps = jax.random.uniform(jax.random.fold_in(jax.random.fold_in(own_key, 6), dim), (shards_of,), jnp.float32, low / len(split), top_value / len(split))
        loudness = loudness * jnp.repeat(jnp.exp(steps), shape[dim] // shards_of).reshape((-1,) + (1,) * (len(shape) - 1 - dim))
    return loudness


def scatter_about(rng, dims, scale, bound, shards=(), held_as=jnp.bfloat16):
    drawn = scale * jax.random.normal(rng, dims, jnp.float32)
    if shards:
        drawn = drawn * levels(rng, dims, shards, -0.22, 0.18)
    return jnp.clip(drawn, -bound, bound).astype(held_as)


def setup_inputs(seed: int = 0) -> dict:
    seeds = jax.random.split(jax.random.key(seed), 21)
    h_in = scatter_about(seeds[0], (SEQS, SEQ_LEN, D), 1.0, 6.0, ((0, 32),))
    g_in = scatter_about(seeds[1], (SEQS, SEQ_LEN, D), 1.0, 6.0, ((0, 32),))
    seg_ids = draw_seg_ids(jax.random.fold_in(seeds[20], 71), 0)
    target_flags = draw_target_flags(jax.random.fold_in(seeds[20], 71), 0)
    perm_order = jax.vmap(lambda own: jax.random.permutation(own, SEQ_LEN))(jax.random.split(seeds[4], SEQS)).reshape((SEQS, SEQ_LEN)).astype(jnp.int32)
    w_query = scatter_about(seeds[5], (LAYERS, D, D), D ** -0.5, 0.21875)
    w_key = scatter_about(seeds[6], (LAYERS, D, D), D ** -0.5, 0.21875)
    w_value = scatter_about(seeds[7], (LAYERS, D, D), D ** -0.5, 0.21875)
    w_out = scatter_about(seeds[8], (LAYERS, D, D), (D // 16) ** -0.5, 0.875)
    w_rel = scatter_about(seeds[9], (LAYERS, D, D), D ** -0.5, 0.21875)
    attn_bias = scatter_about(seeds[10], (LAYERS, 3, D), 0.5, 3.0, (), jnp.float32)
    seg_embed = scatter_about(seeds[11], (LAYERS, 2, D), 0.5, 3.0, (), jnp.float32)
    norm_gain = jnp.clip(1.0 + 0.1 * jax.random.normal(seeds[12], (LAYERS, 2, D), jnp.float32), 0.5, 1.5)
    norm_bias = scatter_about(seeds[13], (LAYERS, 2, D), 0.3, 2.0, (), jnp.float32)
    w_up = scatter_about(seeds[14], (LAYERS, D, FF), D ** -0.5, 0.21875, ((2, 4),))
    b_up = scatter_about(seeds[15], (LAYERS, FF), 0.5, 3.0, ((1, 4),))
    w_down = scatter_about(seeds[16], (LAYERS, FF, D), FF ** -0.5, 0.109375, ((1, 4),))
    b_down = scatter_about(seeds[17], (LAYERS, D), 0.3, 2.0, (), jnp.float32)
    d_h_out = scatter_about(seeds[18], (SEQS, SEQ_LEN, D), 1.0, 6.0, ((0, 32),))
    d_g_out = scatter_about(seeds[19], (SEQS, SEQ_LEN, D), 1.0, 6.0, ((0, 32),))
    return dict(h_in=h_in, g_in=g_in, seg_ids=seg_ids, target_flags=target_flags, perm_order=perm_order, w_query=w_query, w_key=w_key, w_value=w_value, w_out=w_out, w_rel=w_rel, attn_bias=attn_bias, seg_embed=seg_embed, norm_gain=norm_gain, norm_bias=norm_bias, w_up=w_up, b_up=b_up, w_down=w_down, b_down=b_down, d_h_out=d_h_out, d_g_out=d_g_out)


@jax.custom_vjp
def low(v):
    return lax.optimization_barrier(v.astype(jnp.bfloat16)).astype(jnp.float32)

@jax.custom_vjp
def low_back(v):
    return v

def low_keep(v):
    return (low(v), None)

def low_pass(kept, grad):
    return (grad,)

def back_keep(v):
    return (v, None)

def back_low(kept, grad):
    return (low(grad),)
low.defvjp(low_keep, low_pass)
low_back.defvjp(back_keep, back_low)
HIGHEST_PRECISION = lax.Precision.HIGHEST
NEGATIVE = -1e+30
EPSILON = 1e-06

def matmul(left_side, right_side):
    return jnp.dot(left_side, right_side, precision=HIGHEST_PRECISION)

def both_round(operand):
    return low_back(low(operand))

def norm_rows(source, norm_scale, norm_shift):
    row_mean = lax.optimization_barrier(jnp.mean(source, axis=-1, keepdims=True))
    centered = source - row_mean
    variance = lax.optimization_barrier(jnp.mean(centered * centered, axis=-1, keepdims=True))
    return centered * lax.rsqrt(variance + EPSILON) * norm_scale + norm_shift

def rel_table(length, model_width):
    position = (length - jnp.arange(2 * length)).astype(jnp.float32)
    frequency = 1.0 / 10000.0 ** (jnp.arange(0, model_width, 2).astype(jnp.float32) / model_width)
    angles = position[:, None] * frequency[None, :]
    return jnp.concatenate([jnp.sin(angles), jnp.cos(angles)], axis=1)

def shift_rel(raw_rel, length):
    head_count = raw_rel.shape[0]
    flattened = raw_rel.reshape(head_count, -1)[:, length:]
    return flattened.reshape(head_count, length, 2 * length - 1)[:, :, :length]

def build_masks(seg_row, flag_row, order_row):
    length = seg_row.shape[0]
    position = jnp.arange(length, dtype=jnp.int32)
    same_doc = seg_row[:, None] == seg_row[None, :]
    doc_start = lax.optimization_barrier(jnp.min(jnp.where(same_doc, position[None, :], length), axis=1))
    doc_count = lax.optimization_barrier(jnp.sum(same_doc.astype(jnp.int32), axis=1))
    second = 2 * (position - doc_start) >= doc_count
    differ = second[:, None] != second[None, :]
    open_key = (flag_row[None, :] == 0) | (order_row[None, :] <= order_row[:, None])
    content = same_doc & open_key
    query_mask = content & (position[:, None] != position[None, :])
    return (differ, content, query_mask)

def attend_ref(query_f, table_bias, seg_table, key_vals, value_vals, rel_key, differ, visible):
    length = query_f.shape[0]
    word_query = low(query_f + table_bias[0])
    rel_query = low(query_f + table_bias[1])
    seg_query = query_f + table_bias[2]
    plain_score = jnp.einsum('ihe,jhe->hij', word_query, key_vals, precision=HIGHEST_PRECISION)
    raw_rel = jnp.einsum('ihe,mhe->him', rel_query, rel_key, precision=HIGHEST_PRECISION)
    segment = jnp.einsum('ihe,she->hsi', seg_query, seg_table, precision=HIGHEST_PRECISION)
    picked = jnp.where(differ[None], segment[:, 1, :, None], segment[:, 0, :, None])
    score_total = low_back(plain_score + shift_rel(raw_rel, length) + picked)
    logits = jnp.where(visible[None], score_total * (1.0 / math.sqrt(HEAD_DIM)), NEGATIVE)
    prob_low = low(jax.nn.softmax(logits, axis=-1))
    return jnp.einsum('hij,jhe->ihe', prob_low, value_vals, precision=HIGHEST_PRECISION)

def feed_forward(middle, weight_up, bias_up, weight_down, bias_down, norm_scale, norm_shift):
    pre_act = low_back(matmul(low(middle), weight_up) + bias_up)
    activation = low(jax.nn.gelu(pre_act, approximate=True))
    branch = low_back(matmul(activation, weight_down) + bias_down)
    return norm_rows(middle + branch, norm_scale[1], norm_shift[1])

def layer_seq(layer_params, inputs):
    weight_query, weight_key, weight_value, weight_out, weight_rel, bias_rows, seg_rows, norm_scale, norm_shift, weight_up, bias_up, weight_down, bias_down = layer_params
    hidden, stream, seg_row, flag_row, order_row = inputs
    length = hidden.shape[0]
    differ, content, query_mask = build_masks(seg_row, flag_row, order_row)
    heads_shape = (length, HEADS, HEAD_DIM)
    hidden_low = low(hidden)
    stream_low = low(stream)
    query_h = low_back(matmul(hidden_low, weight_query)).reshape(heads_shape)
    query_g = low_back(matmul(stream_low, weight_query)).reshape(heads_shape)
    key_vals = both_round(matmul(hidden_low, weight_key)).reshape(heads_shape)
    value_vals = both_round(matmul(hidden_low, weight_value)).reshape(heads_shape)
    rel_key = both_round(matmul(low(rel_table(length, D)), weight_rel)).reshape(2 * length, HEADS, HEAD_DIM)
    table_bias = bias_rows.reshape(3, HEADS, HEAD_DIM)
    seg_table = seg_rows.reshape(2, HEADS, HEAD_DIM)
    attended_h = both_round(attend_ref(query_h, table_bias, seg_table, key_vals, value_vals, rel_key, differ, content).reshape(length, D))
    attended_g = both_round(attend_ref(query_g, table_bias, seg_table, key_vals, value_vals, rel_key, differ, query_mask).reshape(length, D))
    middle_h = norm_rows(hidden + low_back(matmul(attended_h, weight_out)), norm_scale[0], norm_shift[0])
    middle_g = norm_rows(stream + low_back(matmul(attended_g, weight_out)), norm_scale[0], norm_shift[0])
    result_h = feed_forward(middle_h, weight_up, bias_up, weight_down, bias_down, norm_scale, norm_shift)
    result_g = feed_forward(middle_g, weight_up, bias_up, weight_down, bias_down, norm_scale, norm_shift)
    return (result_h, result_g)

def forward(primals, seg_ids, target_flags, perm_order):
    hidden, stream = (primals[0], primals[1])
    layer_weights = primals[2:]
    layer_step = jax.checkpoint(layer_seq)
    for layer_index in range(LAYERS):
        layer_params = tuple((item[layer_index] for item in layer_weights))

        def per_sequence(inputs):
            return layer_step(layer_params, inputs)
        hidden, stream = lax.map(per_sequence, (hidden, stream, seg_ids, target_flags, perm_order))
    return (hidden, stream)

def reference(h_in, g_in, seg_ids, target_flags, perm_order, w_query, w_key, w_value, w_out, w_rel, attn_bias, seg_embed, norm_gain, norm_bias, w_up, b_up, w_down, b_down, d_h_out, d_g_out):
    floats = tuple((item.astype(jnp.float32) for item in (h_in, g_in, w_query, w_key, w_value, w_out, w_rel, attn_bias, seg_embed, norm_gain, norm_bias, w_up, b_up, w_down, b_down)))

    def run_layers(*primals):
        return forward(primals, seg_ids, target_flags, perm_order)
    results, pullback = jax.vjp(run_layers, *floats)
    gradients = pullback((d_h_out.astype(jnp.float32), d_g_out.astype(jnp.float32)))
    grad_h, grad_g, grad_query, grad_key, grad_value, grad_out, grad_rel, grad_bias_rows, grad_seg_rows, grad_gain, grad_shift, grad_up, grad_bias_up, grad_down, grad_bias_down = gradients
    d_vectors = jnp.concatenate([grad_bias_rows.reshape(LAYERS, -1), grad_seg_rows.reshape(LAYERS, -1), grad_gain.reshape(LAYERS, -1), grad_shift.reshape(LAYERS, -1), grad_bias_down, grad_bias_up], axis=1)
    return (results[0].astype(jnp.bfloat16), results[1].astype(jnp.bfloat16), grad_h, grad_g, grad_query, grad_key, grad_value, grad_out, grad_rel, grad_up, grad_down, d_vectors)
```

```python
import math

import jax
import jax.numpy as jnp
from jax import lax
from jax.experimental import pallas as pl
from jax.experimental.pallas import tpu as pltpu
from jax.sharding import PartitionSpec as P

HEADS = 12
HEAD_DIM = 64
LANES = 128
PAIRS = HEADS // 2
NEGATIVE = -1e30
EPSILON = 1e-06
AXES = ("dp", "tensor")
BF = jnp.bfloat16
F32 = jnp.float32
VMEM_LIMIT = 60 * 1024 * 1024


def rel_table(length, model_width):
    position = (length - jnp.arange(2 * length)).astype(jnp.float32)
    frequency = 1.0 / 10000.0 ** (jnp.arange(0, model_width, 2).astype(jnp.float32) / model_width)
    angles = position[:, None] * frequency[None, :]
    return jnp.concatenate([jnp.sin(angles), jnp.cos(angles)], axis=1)


def nn(left, right):
    return lax.dot_general(left, right, (((1,), (0,)), ((), ())), preferred_element_type=F32)


def nt(left, right):
    return lax.dot_general(left, right, (((1,), (1,)), ((), ())), preferred_element_type=F32)


def tn(left, right):
    return lax.dot_general(left, right, (((0,), (0,)), ((), ())), preferred_element_type=F32)


def lane_index(rows):
    return lax.broadcasted_iota(jnp.int32, (rows, LANES), 1)


def pair_lanes(pair):
    return pl.ds(pl.multiple_of(pair * LANES, LANES), LANES)


def norm_stats(source):
    mean = jnp.mean(source, axis=-1, keepdims=True)
    centered = source - mean
    variance = jnp.mean(centered * centered, axis=-1, keepdims=True)
    rstd = lax.rsqrt(variance + EPSILON)
    return centered * rstd, rstd


def norm_back(grad, xhat, rstd, gain):
    dxhat = grad * gain
    mean_one = jnp.mean(dxhat, axis=-1, keepdims=True)
    mean_two = jnp.mean(dxhat * xhat, axis=-1, keepdims=True)
    return rstd * (dxhat - mean_one - xhat * mean_two)


def seg_coefficients(half_wide, lane):
    return jnp.where(lane % HEAD_DIM == 0, half_wide, 1.0 - 2.0 * half_wide)


def seg_keys(half_wide, lane):
    place = lane % HEAD_DIM
    return jnp.where(place == 0, 1.0, jnp.where(place == 1, half_wide, 0.0))


def attention_forward_kernel(
    h_ref, g_ref, seg_row, flag_row, order_row, seg_col, order_col,
    wq_ref, wk_ref, wv_ref, wo_ref, wr_ref, rel_ref, rev_ref, bias_ref, table_ref, gain_ref, shift_ref,
    q_ref, key_ref, value_ref, prob_ref, att_ref, resid_ref, mid_ref, relrev_ref, half_ref,
    x_ref, relkey_ref, mask_ref,
):
    length, width = h_ref.shape
    block = length // 2
    x_ref[:length] = h_ref[...]
    x_ref[length:] = g_ref[...]
    for col in range(0, width, 256):
        cols = slice(col, col + 256)
        q_ref[:, cols] = nn(x_ref[...], wq_ref[:, cols])
        key_ref[:, cols] = nn(h_ref[...], wk_ref[:, cols]).astype(BF)
        value_ref[:, cols] = nn(h_ref[...], wv_ref[:, cols]).astype(BF)
        relkey_ref[:, cols] = nn(rel_ref[...], wr_ref[:, cols]).astype(BF)
        relrev_ref[:, cols] = nn(rev_ref[...], wr_ref[:, cols]).astype(BF)

    row_at = lax.broadcasted_iota(jnp.int32, (length, length), 0)
    col_at = lax.broadcasted_iota(jnp.int32, (length, length), 1)
    same_doc = seg_col[...] == seg_row[...]
    start = jnp.min(jnp.where(same_doc, col_at.astype(F32), float(length)), axis=1, keepdims=True)
    count = jnp.sum(jnp.where(same_doc, 1.0, 0.0), axis=1, keepdims=True)
    place = lax.broadcasted_iota(jnp.int32, (length, 1), 0).astype(F32)
    half = jnp.where(2.0 * (place - start) >= count, 1.0, 0.0)
    half_wide = jnp.broadcast_to(half, (length, LANES))
    half_ref[...] = half_wide
    content = same_doc & ((flag_row[...] == 0) | (order_row[...] <= order_col[...]))
    mask_ref[:length] = jnp.where(content, 0.0, NEGATIVE)
    mask_ref[length:] = jnp.where(content & (row_at != col_at), 0.0, NEGATIVE)

    def pair_step(pair, carry):
        lanes = pair_lanes(pair)
        lane_q = lane_index(2 * length)
        lane_k = lane_index(length)
        low_q = lane_q < HEAD_DIM
        low_k = lane_k < HEAD_DIM
        half_w = half_ref[...]
        scale = 1.0 / math.sqrt(HEAD_DIM)
        query = q_ref[:, lanes]
        word = ((query + bias_ref[0:1, lanes]) * scale).astype(BF)
        relq = ((query + bias_ref[1:2, lanes]) * scale).astype(BF)
        segq = ((query + bias_ref[2:3, lanes]) * scale).astype(BF)
        terms = nn(segq, table_ref[pair])
        coef = seg_coefficients(jnp.concatenate([half_w, half_w], axis=0), lane_q)
        extra = (terms[:, :LANES] + terms[:, LANES:] * coef).astype(BF)
        key_extra = seg_keys(half_w, lane_k).astype(BF)
        key = key_ref[:, lanes]
        value = value_ref[:, lanes]
        zero = jnp.zeros_like(relq)
        attended = []
        for head in (0, 1):
            if head == 0:
                word_one = jnp.where(low_q, word, extra)
                key_one = jnp.where(low_k, key, key_extra)
                rel_one = jnp.where(low_q, relq, zero)
            else:
                word_one = jnp.where(low_q, extra, word)
                key_one = jnp.where(low_k, key_extra, key)
                rel_one = jnp.where(low_q, zero, relq)
            score = nt(word_one, key_one)
            for part in (0, 1):
                base = block - block * part
                rows_h = slice(block * part, block * part + block)
                rows_g = slice(length + block * part, length + block * part + block)
                rel_rows = jnp.concatenate([rel_one[rows_h], rel_one[rows_g]], axis=0)
                raw = nt(rel_rows, relkey_ref[base : base + 3 * block, lanes])
                for place_at, rows in ((0, rows_h), (1, rows_g)):
                    shifted = pltpu.roll(
                        raw[place_at * block : (place_at + 1) * block], 2 * block, 1, stride=1, stride_axis=0
                    )[:, :length]
                    logits = score[rows] + shifted + mask_ref[rows]
                    top = jnp.max(logits, axis=1, keepdims=True)
                    power = jnp.exp(logits - top)
                    total = jnp.sum(power, axis=1, keepdims=True)
                    prob_ref[2 * pair + head, rows, :] = (power * (1.0 / total)).astype(BF)
            attended.append(nn(prob_ref[2 * pair + head], value))
        att_ref[:, lanes] = jnp.where(low_q, attended[0], attended[1]).astype(BF)
        return carry

    lax.fori_loop(0, PAIRS, pair_step, 0)
    for col in range(0, width, 256):
        cols = slice(col, col + 256)
        resid_ref[:, cols] = x_ref[:, cols].astype(F32) + nn(att_ref[...], wo_ref[:, cols])

    def norm_step(step, carry):
        rows = pl.ds(pl.multiple_of(step * 64, 64), 64)
        xhat, _ = norm_stats(resid_ref[rows, :])
        mid_ref[rows, :] = (xhat * gain_ref[...] + shift_ref[...]).astype(BF)
        return carry

    lax.fori_loop(0, 2 * length // 64, norm_step, 0)


def attention_forward(h, g, seg, flag, order, wq, wk, wv, wo, wr, rel, rev, bias, table, gain, shift):
    length, width = h.shape
    out_shape = (
        jax.ShapeDtypeStruct((2 * length, width), F32),
        jax.ShapeDtypeStruct((length, width), BF),
        jax.ShapeDtypeStruct((length, width), BF),
        jax.ShapeDtypeStruct((HEADS, 2 * length, length), BF),
        jax.ShapeDtypeStruct((2 * length, width), BF),
        jax.ShapeDtypeStruct((2 * length, width), F32),
        jax.ShapeDtypeStruct((2 * length, width), BF),
        jax.ShapeDtypeStruct((2 * length, width), BF),
        jax.ShapeDtypeStruct((length, LANES), F32),
    )
    return pl.pallas_call(
        attention_forward_kernel,
        out_shape=out_shape,
        scratch_shapes=[
            pltpu.VMEM((2 * length, width), BF),
            pltpu.VMEM((2 * length, width), BF),
            pltpu.VMEM((2 * length, length), F32),
        ],
        compiler_params=pltpu.CompilerParams(vmem_limit_bytes=VMEM_LIMIT),
        cost_estimate=pl.CostEstimate(flops=8 * 10**9, bytes_accessed=20 * 10**6, transcendentals=2 * 10**6),
        name="attention_forward",
    )(
        h, g, seg.reshape(1, length), flag.reshape(1, length), order.reshape(1, length),
        seg.reshape(length, 1), order.reshape(length, 1), wq, wk, wv, wo, wr, rel, rev, bias, table, gain, shift,
    )


def attention_backward_kernel(
    dproj_ref, wo_ref, q_ref, att_ref, key_ref, value_ref, prob_ref, relrev_ref, half_ref, bias_ref, table_ref,
    dq_ref, dkey_ref, dvalue_ref, drel_ref, vec_ref,
    datt_ref,
):
    length, width = key_ref.shape
    block = length // 2
    for col in range(0, width, 256):
        cols = slice(col, col + 256)
        datt_ref[:, cols] = nt(dproj_ref[...], wo_ref[cols, :]).astype(BF)
    vec_ref[...] = jnp.zeros_like(vec_ref)

    def pair_step(pair, carry):
        lanes = pair_lanes(pair)
        lane_q = lane_index(2 * length)
        lane_k = lane_index(length)
        low_q = lane_q < HEAD_DIM
        low_k = lane_k < HEAD_DIM
        half_w = half_ref[...]
        flip_row = lax.broadcasted_iota(jnp.int32, (length, length), 0)
        flip_col = lax.broadcasted_iota(jnp.int32, (length, length), 1)
        flip = jnp.where(flip_row + flip_col == length - 1, 1.0, 0.0).astype(BF)
        sel_row = lax.broadcasted_iota(jnp.int32, (2 * LANES, LANES), 0) % LANES
        sel_col = lax.broadcasted_iota(jnp.int32, (2 * LANES, LANES), 1)
        select = jnp.where(
            ((sel_row < HEAD_DIM) & ((sel_col == HEAD_DIM) | (sel_col == HEAD_DIM + 1)))
            | ((sel_row >= HEAD_DIM) & (sel_col < 2)),
            1.0,
            0.0,
        ).astype(BF)
        query = q_ref[:, lanes]
        word = query + bias_ref[0:1, lanes]
        relq = query + bias_ref[1:2, lanes]
        segq = (query + bias_ref[2:3, lanes]).astype(BF)
        word_t = word.T.astype(BF)
        relq_t = relq.T.astype(BF)
        datt = datt_ref[:, lanes]
        datt_wide = datt.astype(F32)
        datt_t = datt_wide.T.astype(BF)
        datt_scaled = datt_wide * (1.0 / math.sqrt(HEAD_DIM))
        product = datt_scaled * att_ref[:, lanes].astype(F32)
        product_high = product.astype(BF)
        product_low = (product - product_high.astype(F32)).astype(BF)
        delta = nn(jnp.concatenate([product_high, product_low], axis=1), select)
        delta_high = delta.astype(BF).astype(F32)
        minus = jnp.where(lane_q % HEAD_DIM == 0, -delta_high, delta_high - delta).astype(BF)
        datt_low = datt_scaled.astype(BF)
        key_extra = seg_keys(half_w, lane_k).astype(BF)
        ones_extra = jnp.where(lane_k % HEAD_DIM < 2, 1.0, 0.0).astype(BF)
        key = key_ref[:, lanes]
        value = value_ref[:, lanes]
        dword, drel = [], []
        for head in (0, 1):
            rows_t = slice(HEAD_DIM * head, HEAD_DIM * head + HEAD_DIM)
            if head == 0:
                datt_one = jnp.where(low_q, datt_low, minus)
                value_one = jnp.where(low_k, value, ones_extra)
                key_one = jnp.where(low_k, key, key_extra)
            else:
                datt_one = jnp.where(low_q, minus, datt_low)
                value_one = jnp.where(low_k, ones_extra, value)
                key_one = jnp.where(low_k, key_extra, key)
            prob = prob_ref[2 * pair + head]
            dprob = nt(datt_one, value_one)
            dscore = (prob.astype(F32) * dprob).astype(BF)
            dword.append(nn(dscore, key_one))
            rows_out = pl.ds(pl.multiple_of(pair * LANES + HEAD_DIM * head, HEAD_DIM), HEAD_DIM)
            dkey_ref[rows_out, :] = nn(word_t[rows_t], dscore).astype(BF)
            dvalue_ref[rows_out, :] = nn(datt_t[rows_t], prob).astype(BF)
            flipped = nn(dscore, flip).astype(BF)
            pad = jnp.zeros((block, block), BF)
            rel_parts, drel_t = [], []
            for part in (0, 1):
                rows_h = slice(block * part, block * part + block)
                rows_g = slice(length + block * part, length + block * part + block)
                draw = jnp.concatenate(
                    [
                        pltpu.roll(jnp.concatenate([flipped[rows], pad], axis=1), 0, 1, stride=1, stride_axis=0)
                        for rows in (rows_h, rows_g)
                    ],
                    axis=0,
                )
                rel_parts.append(nn(draw, relrev_ref[block * part : block * part + 3 * block, lanes]))
                rel_cols = jnp.concatenate([relq_t[rows_t, rows_h], relq_t[rows_t, rows_g]], axis=1)
                drel_t.append(nn(rel_cols, draw))
            drel.append(
                jnp.concatenate(
                    [rel_parts[0][:block], rel_parts[1][:block], rel_parts[0][block:], rel_parts[1][block:]], axis=0
                )
            )
            drel_ref[rows_out, :] = jnp.concatenate(
                [
                    drel_t[0][:, :block],
                    drel_t[0][:, block:] + drel_t[1][:, : 2 * block],
                    drel_t[1][:, 2 * block :],
                ],
                axis=1,
            ).astype(BF)
        extra = jnp.where(low_q, dword[1], dword[0])
        dword_all = jnp.where(low_q, dword[0], dword[1])
        drel_all = jnp.where(low_q, drel[0], drel[1])
        coef = seg_coefficients(jnp.concatenate([half_w, half_w], axis=0), lane_q)
        dterms = jnp.concatenate([extra, extra * coef], axis=1).astype(BF)
        dsegq = nt(dterms, table_ref[pair])
        dtable = tn(dterms, segq)
        dq_ref[:, lanes] = (dword_all + drel_all + dsegq).astype(BF)
        low_one = lane_index(1) < HEAD_DIM
        first = jnp.where(low_one, dtable[HEAD_DIM : HEAD_DIM + 1], dtable[0:1])
        at = LANES + HEAD_DIM
        second = jnp.where(
            low_one, dtable[at : at + 1] + dtable[at + 1 : at + 2], dtable[LANES : LANES + 1] + dtable[LANES + 1 : LANES + 2]
        )
        vec_ref[0:1, lanes] = jnp.sum(dword_all, axis=0, keepdims=True)
        vec_ref[1:2, lanes] = jnp.sum(drel_all, axis=0, keepdims=True)
        vec_ref[2:3, lanes] = jnp.sum(dsegq, axis=0, keepdims=True)
        vec_ref[3:4, lanes] = first - second
        vec_ref[4:5, lanes] = second
        return carry

    lax.fori_loop(0, PAIRS, pair_step, 0)


def attention_backward(dproj, wo, q, att, key, value, prob, relrev, half, bias, table):
    length, width = key.shape
    out_shape = (
        jax.ShapeDtypeStruct((2 * length, width), BF),
        jax.ShapeDtypeStruct((width, length), BF),
        jax.ShapeDtypeStruct((width, length), BF),
        jax.ShapeDtypeStruct((width, 2 * length), BF),
        jax.ShapeDtypeStruct((8, width), F32),
    )
    return pl.pallas_call(
        attention_backward_kernel,
        out_shape=out_shape,
        scratch_shapes=[pltpu.VMEM((2 * length, width), BF)],
        compiler_params=pltpu.CompilerParams(vmem_limit_bytes=VMEM_LIMIT),
        cost_estimate=pl.CostEstimate(flops=8 * 10**9, bytes_accessed=20 * 10**6, transcendentals=0),
        name="attention_backward",
    )(dproj, wo, q, att, key, value, prob, relrev, half, bias, table)


def place_rows(raw_ref, out_ref, parts, index_ref):
    rows = raw_ref.shape[0] // parts
    for block in range(parts):
        source = pl.multiple_of(index_ref[block] * rows, rows)
        out_ref[block * rows : (block + 1) * rows, :] = raw_ref[pl.ds(source, rows), :]


def weight_grads_kernel(
    index_ref, h_ref, g_ref, att_ref, rev_ref, dproj_ref, dq_ref, dkey_ref, dvalue_ref, drel_ref,
    keep_ref, send_ref,
    raw_all, left_all,
):
    length, width = h_ref.shape
    parts = index_ref.shape[0]
    split = width // 2

    def put(slot, left, right, dot):
        for col in range(0, width, 256):
            piece = dot(left, right(col)).astype(BF)
            keep_ref[slot, :, col : col + 256] = piece[:split]
            send_ref[slot, :, col : col + 256] = piece[split:]

    def turn(source):
        for col in range(0, width, 256):
            raw_ref[col : col + 256, :] = source(col).astype(F32).T.astype(BF)
        place_rows(raw_ref, left_ref, parts, index_ref)

    left_ref = left_all.at[0]
    raw_ref = raw_all.at[0]
    turn(lambda col: att_ref[:, col : col + 256])
    put(4, left_ref[...], lambda col: dproj_ref[:, col : col + 256], nn)
    left_ref = left_all.at[1]
    raw_ref = raw_all.at[1]
    turn(lambda col: rev_ref[:, col : col + 256])
    put(3, left_ref[...], lambda col: drel_ref[col : col + 256, :], nt)
    left_ref = left_all.at[2]
    raw_ref = raw_all.at[2]
    turn(lambda col: jnp.concatenate([h_ref[:, col : col + 256], g_ref[:, col : col + 256]], axis=0))
    put(0, left_ref[...], lambda col: dq_ref[:, col : col + 256], nn)
    put(1, left_ref[:, :length], lambda col: dkey_ref[col : col + 256, :], nt)
    put(2, left_ref[:, :length], lambda col: dvalue_ref[col : col + 256, :], nt)


def weight_grads(index, h, g, att, rev, dproj, dq, dkey, dvalue, drel):
    length, width = h.shape
    shape = jax.ShapeDtypeStruct((5, width // 2, width), BF)
    vm = pl.BlockSpec(memory_space=pltpu.VMEM)
    return pl.pallas_call(
        weight_grads_kernel,
        out_shape=(shape, shape),
        in_specs=[pl.BlockSpec(memory_space=pltpu.SMEM)] + [vm] * 9,
        scratch_shapes=[pltpu.VMEM((3, width, 2 * length), BF), pltpu.VMEM((3, width, 2 * length), BF)],
        compiler_params=pltpu.CompilerParams(vmem_limit_bytes=VMEM_LIMIT),
        cost_estimate=pl.CostEstimate(flops=24 * 10**8, bytes_accessed=12 * 10**6, transcendentals=0),
        name="weight_grads",
    )(index, h, g, att, rev, dproj, dq, dkey, dvalue, drel)


def feed_forward_kernel(parts, shards, pieces, *refs):
    (
        place_ref, index_ref, own_up, own_down, resid_one_ref, mid_ref, up_bias, down_bias,
        gain_one, shift_one, gain_two, shift_two, dh_ref, dg_ref,
    ) = refs[:14]
    piece_refs = refs[14 : 14 + len(pieces)]
    (
        out_ref, dresid_ref, dbranch_ref, slope_ref, keep_ref, send_ref, vec_ref, up_out, down_out,
        up_ref, down_ref, act_ref, raw_ref, left_ref, in_sem, out_sem,
    ) = refs[14 + len(pieces) :]
    rows_all, width = mid_ref.shape
    length = rows_all // 2
    split = width // 2
    copies_up = [[] for _ in range(shards)]
    copies_down = [[] for _ in range(shards)]
    count = 0

    def start(source, target, group):
        nonlocal count
        copy = pltpu.make_async_copy(source, target, in_sem.at[count])
        count += 1
        copy.start()
        group.append(copy)

    start(own_up, up_ref.at[0], copies_up[0])
    start(own_down, down_ref.at[0], copies_down[0])
    for (kind, shard, block, offset, rows), source in zip(pieces, piece_refs, strict=True):
        where = pl.multiple_of(place_ref[block] * rows, rows)
        if "u" in kind:
            at = 0
            start(source.at[pl.ds(at, rows)], up_ref.at[shard, pl.ds(where, rows)], copies_up[shard])
        if "d" in kind:
            at = rows if "u" in kind else 0
            start(source.at[pl.ds(at, rows)], down_ref.at[shard, pl.ds(where, rows)], copies_down[shard])
    outs = []
    root = math.sqrt(2.0 / math.pi)
    for shard in range(shards):
        for copy in copies_up[shard]:
            copy.wait()
        back = pltpu.make_async_copy(up_ref.at[shard], up_out.at[shard], out_sem.at[shard])
        back.start()
        outs.append(back)
        for col in range(0, width, 256):
            cols = slice(shard * width + col, shard * width + col + 256)
            pre = nn(mid_ref[...], up_ref[shard, :, col : col + 256]) + up_bias[shard : shard + 1, col : col + 256]
            square = pre * pre
            bend = jnp.tanh(root * pre * (1.0 + 0.044715 * square))
            upper = 0.5 + 0.5 * bend
            act_ref[:, cols] = (pre * upper).astype(BF)
            slope = upper + (0.5 * root) * pre * (1.0 - bend * bend) * (1.0 + (3 * 0.044715) * square)
            slope_ref[:, cols] = slope.astype(BF)
    for shard in range(shards):
        for copy in copies_down[shard]:
            copy.wait()
        back = pltpu.make_async_copy(down_ref.at[shard], down_out.at[shard], out_sem.at[shards + shard])
        back.start()
        outs.append(back)
    down_all = down_ref.reshape(shards * width, width)
    for col in range(0, width, 256):
        cols = slice(col, col + 256)
        dresid_ref[:, cols] = nn(act_ref[...], down_all[:, cols])
    vec_ref[...] = jnp.zeros_like(vec_ref)
    step_rows = 64

    def norm_rows_of(grad_ref):
        def step(at, offset):
            rows = pl.ds(pl.multiple_of(at * step_rows + offset, step_rows), step_rows)
            near = pl.ds(pl.multiple_of(at * step_rows, step_rows), step_rows)
            xhat_one, _ = norm_stats(resid_one_ref[rows, :])
            middle = xhat_one * gain_one[...] + shift_one[...]
            xhat, rstd = norm_stats(middle + dresid_ref[rows, :] + down_bias[...])
            out_ref[rows, :] = (xhat * gain_two[...] + shift_two[...]).astype(BF)
            grad = grad_ref[near, :].astype(F32)
            dresid = norm_back(grad, xhat, rstd, gain_two[...])
            dresid_ref[rows, :] = dresid
            dbranch = dresid.astype(BF)
            dbranch_ref[rows, :] = dbranch
            vec_ref[0:1, :] += jnp.sum(grad * xhat, axis=0, keepdims=True)
            vec_ref[1:2, :] += jnp.sum(grad, axis=0, keepdims=True)
            vec_ref[2:3, :] += jnp.sum(dbranch.astype(F32), axis=0, keepdims=True)
            return offset

        return step

    lax.fori_loop(0, length // step_rows, norm_rows_of(dh_ref), 0)
    lax.fori_loop(0, length // step_rows, norm_rows_of(dg_ref), length)
    for col in range(0, width, 256):
        raw_ref[col : col + 256, :] = dbranch_ref[:, col : col + 256].astype(F32).T.astype(BF)
    place_rows(raw_ref, left_ref, parts, index_ref)

    def weight_step(step, carry):
        cols = pl.ds(pl.multiple_of(step * 256, 256), 256)
        piece = nn(left_ref[...], act_ref[:, cols]).astype(BF)
        keep_ref[:, cols] = piece[:split]
        send_ref[:, cols] = piece[split:]
        return carry

    lax.fori_loop(0, shards * width // 256, weight_step, 0)
    for back in outs:
        back.wait()


def feed_forward(parts, shards, place, index, own_up, own_down, resid_one, mid, up_bias, down_bias, gains, shifts, dh, dg, pieces):
    rows_all, width = mid.shape
    hidden = shards * width
    names = [entry[:5] for entry in pieces]
    arrays = [entry[5] for entry in pieces]
    vm = pl.BlockSpec(memory_space=pltpu.VMEM)
    sm = pl.BlockSpec(memory_space=pltpu.SMEM)
    hbm = pl.BlockSpec(memory_space=pl.ANY)
    copies = 2 + sum(len(kind) for kind, *_ in names)

    def kernel(*refs):
        feed_forward_kernel(parts, shards, names, *refs)

    return pl.pallas_call(
        kernel,
        out_shape=(
            jax.ShapeDtypeStruct((rows_all, width), BF),
            jax.ShapeDtypeStruct((rows_all, width), F32),
            jax.ShapeDtypeStruct((rows_all, width), BF),
            jax.ShapeDtypeStruct((rows_all, hidden), BF),
            jax.ShapeDtypeStruct((width // 2, hidden), BF),
            jax.ShapeDtypeStruct((width // 2, hidden), BF),
            jax.ShapeDtypeStruct((8, width), F32),
            jax.ShapeDtypeStruct((shards, width, width), BF),
            jax.ShapeDtypeStruct((shards, width, width), BF),
        ),
        in_specs=[sm, sm, hbm, hbm] + [vm] * 10 + [hbm] * len(arrays),
        out_specs=[vm] * 7 + [hbm] * 2,
        scratch_shapes=[
            pltpu.VMEM((shards, width, width), BF),
            pltpu.VMEM((shards, width, width), BF),
            pltpu.VMEM((rows_all, hidden), BF),
            pltpu.VMEM((width, rows_all), BF),
            pltpu.VMEM((width, rows_all), BF),
            pltpu.SemaphoreType.DMA((copies,)),
            pltpu.SemaphoreType.DMA((2 * shards,)),
        ],
        compiler_params=pltpu.CompilerParams(vmem_limit_bytes=VMEM_LIMIT),
        cost_estimate=pl.CostEstimate(flops=8 * 10**9, bytes_accessed=40 * 10**6, transcendentals=2 * 10**6),
        name="feed_forward",
    )(
        place, index, own_up, own_down, resid_one, mid, up_bias, down_bias,
        gains[0:1], shifts[0:1], gains[1:2], shifts[1:2], dh, dg, *arrays,
    )


def feed_backward_kernel(
    parts, shards, index_ref, up_hbm, down_hbm, dbranch_ref, dresid_ref, resid_one_ref, mid_ref, slope_ref, gain_one,
    dproj_ref, dresid_one_ref, keep_ref, send_ref, vec_ref, dbias_ref,
    up_ref, down_ref, dpre_ref, raw_ref, left_ref, sem,
):
    rows_all, width = mid_ref.shape
    split = width // 2
    downs = [pltpu.make_async_copy(down_hbm.at[shard], down_ref.at[shard], sem.at[shard]) for shard in range(shards)]
    ups = [pltpu.make_async_copy(up_hbm.at[shard], up_ref.at[shard], sem.at[shards + shard]) for shard in range(shards)]
    for copy in downs + ups:
        copy.start()
    for col in range(0, width, 256):
        raw_ref[col : col + 256, :] = mid_ref[:, col : col + 256].astype(F32).T.astype(BF)
    place_rows(raw_ref, left_ref, parts, index_ref)
    for shard in range(shards):
        downs[shard].wait()
        for col in range(0, width, 256):
            cols = slice(shard * width + col, shard * width + col + 256)
            dact = nt(dbranch_ref[...], down_ref[shard, col : col + 256, :])
            dpre = (dact * slope_ref[:, cols].astype(F32)).astype(BF)
            dpre_ref[:, cols] = dpre
            dbias_ref[:, cols] = jnp.sum(dpre.astype(F32), axis=0, keepdims=True)
            piece = nn(left_ref[...], dpre).astype(BF)
            keep_ref[:, cols] = piece[:split]
            send_ref[:, cols] = piece[split:]
    for copy in ups:
        copy.wait()
    for col in range(0, width, 256):
        cols = slice(col, col + 256)
        total = nt(dpre_ref[:, :width], up_ref[0, cols, :])
        for shard in range(1, shards):
            total += nt(dpre_ref[:, shard * width : (shard + 1) * width], up_ref[shard, cols, :])
        dresid_one_ref[:, cols] = total
    vec_ref[...] = jnp.zeros_like(vec_ref)
    step_rows = 64

    def norm_step(at, carry):
        rows = pl.ds(pl.multiple_of(at * step_rows, step_rows), step_rows)
        xhat, rstd = norm_stats(resid_one_ref[rows, :])
        grad = dresid_ref[rows, :] + dresid_one_ref[rows, :]
        dresid = norm_back(grad, xhat, rstd, gain_one[...])
        dresid_one_ref[rows, :] = dresid
        dproj_ref[rows, :] = dresid.astype(BF)
        vec_ref[0:1, :] += jnp.sum(grad * xhat, axis=0, keepdims=True)
        vec_ref[1:2, :] += jnp.sum(grad, axis=0, keepdims=True)
        return carry

    lax.fori_loop(0, rows_all // step_rows, norm_step, 0)


def feed_backward(parts, shards, index, up_all, down_all, dbranch, dresid, resid_one, mid, slope, gain_one):
    rows_all, width = mid.shape
    hidden = shards * width
    vm = pl.BlockSpec(memory_space=pltpu.VMEM)
    sm = pl.BlockSpec(memory_space=pltpu.SMEM)
    hbm = pl.BlockSpec(memory_space=pl.ANY)

    def kernel(*refs):
        feed_backward_kernel(parts, shards, *refs)

    return pl.pallas_call(
        kernel,
        out_shape=(
            jax.ShapeDtypeStruct((rows_all, width), BF),
            jax.ShapeDtypeStruct((rows_all, width), F32),
            jax.ShapeDtypeStruct((width // 2, hidden), BF),
            jax.ShapeDtypeStruct((width // 2, hidden), BF),
            jax.ShapeDtypeStruct((8, width), F32),
            jax.ShapeDtypeStruct((1, hidden), F32),
        ),
        in_specs=[sm, hbm, hbm] + [vm] * 6,
        out_specs=[vm] * 6,
        scratch_shapes=[
            pltpu.VMEM((shards, width, width), BF),
            pltpu.VMEM((shards, width, width), BF),
            pltpu.VMEM((rows_all, hidden), BF),
            pltpu.VMEM((width, rows_all), BF),
            pltpu.VMEM((width, rows_all), BF),
            pltpu.SemaphoreType.DMA((2 * shards,)),
        ],
        compiler_params=pltpu.CompilerParams(vmem_limit_bytes=VMEM_LIMIT),
        cost_estimate=pl.CostEstimate(flops=8 * 10**9, bytes_accessed=40 * 10**6, transcendentals=0),
        name="feed_backward",
    )(index, up_all, down_all, dbranch, dresid, resid_one, mid, slope, gain_one)


class Exchange:
    def __init__(self, width):
        self.data = lax.axis_size("dp")
        self.tensor = lax.axis_size("tensor")
        self.by_hand = width % (32 * self.data) == 0 and self.data & (self.data - 1) == 0
        self.blocks = self.data if self.by_hand else 1

    def data_swap(self, value, bit):
        pairs = [(at, at ^ bit) for at in range(self.data)]
        return lax.ppermute(value, "dp", pairs)

    def tensor_swap(self, value, bits):
        pairs = [(at, at ^ bits) for at in range(self.tensor)]
        return lax.ppermute(value, "tensor", pairs)


def add_low(left, right):
    return (left.astype(F32) + right.astype(F32)).astype(BF)


def gather_feed(swap, up, down, dp_at):
    parts = swap.blocks
    rows = up.shape[0] // parts
    at = dp_at * rows if parts > 1 else 0
    mine = jnp.concatenate(
        [lax.dynamic_slice_in_dim(up, at, rows, 0), lax.dynamic_slice_in_dim(down, at, rows, 0)], axis=0
    )
    pieces = []
    for shard in range(1, swap.tensor):
        own = swap.tensor_swap(mine, shard)
        if parts == 8:
            across = swap.data_swap(own, 2)
            along = swap.data_swap(own, 4)
            far_up = swap.data_swap(along[:rows], 2)
            far_down = swap.data_swap(across[rows:], 4)
            found = [("ud", 0, own), ("ud", 2, across), ("ud", 4, along), ("u", 6, far_up), ("d", 6, far_down)]
            found += [(kind, block | 1, swap.data_swap(value, 1)) for kind, block, value in found]
        else:
            found = [("ud", 0, own)]
            bit = 1
            while bit < parts:
                found += [(kind, block | bit, swap.data_swap(value, bit)) for kind, block, value in found]
                bit *= 2
        pieces += [(kind, shard, block, 0, rows, value) for kind, block, value in found]
    return pieces


def data_scatter(swap, keep, send, order):
    if not swap.by_hand:
        whole = jnp.concatenate([keep, send], axis=-2)
        return lax.psum_scatter(whole, "dp", scatter_dimension=whole.ndim - 2, tiled=True)
    total = add_low(keep, swap.data_swap(send, 1))
    bits = [1 << at for at in range(1, swap.data.bit_length() - 1)]
    lead = total.shape[:-2]
    rows = total.shape[-2] // (swap.data // 2)
    total = total.reshape(lead + (2,) * len(bits) + (rows, total.shape[-1]))
    left = sorted(bits, reverse=True)
    for bit in order:
        axis = len(lead) + left.index(bit)
        left.remove(bit)
        near = lax.index_in_dim(total, 0, axis, keepdims=False)
        far = lax.index_in_dim(total, 1, axis, keepdims=False)
        total = add_low(near, swap.data_swap(far, bit))
    return total


def per_device(
    h_in, g_in, seg_ids, target_flags, perm_order, w_query, w_key, w_value, w_out, w_rel, attn_bias, seg_embed,
    norm_gain, norm_bias, w_up, b_up, w_down, b_down, d_h_out, d_g_out,
):
    seq_count, length, width = h_in.shape
    assert seq_count == 1
    swap = Exchange(width)
    parts, shards = swap.blocks, swap.tensor
    dp_at, tensor_at = lax.axis_index("dp"), lax.axis_index("tensor")
    own_part = width // shards
    hidden = shards * width

    up, down = w_up[0], w_down[0]
    pieces = gather_feed(swap, up, down, dp_at)
    bias_own = b_up.astype(F32)
    up_bias = jnp.concatenate([bias_own] + [swap.tensor_swap(bias_own, bits) for bits in range(1, shards)], axis=0)

    def block_order():
        return [(low | (rest << 1)) for low in (0, 1) for rest in range(parts // 2)] if parts > 1 else [0]

    here = dp_at if parts > 1 else 0
    index = jnp.stack([jnp.int32(here ^ block) for block in block_order()])
    place = jnp.stack([jnp.int32(here ^ block) for block in range(parts)])

    rel = rel_table(length, width).astype(BF)
    rev = rel[::-1]
    heads = seg_embed[0].reshape(2, PAIRS, LANES)
    row = jnp.arange(LANES)[:, None]
    lane = jnp.arange(LANES)[None, :]
    at_one = jnp.where(row < HEAD_DIM, lane == HEAD_DIM, lane == 0)
    at_two = jnp.where(row < HEAD_DIM, (lane == HEAD_DIM) | (lane == HEAD_DIM + 1), lane < 2)
    table = jnp.concatenate(
        [
            jnp.where(at_one[None], heads[0][:, :, None], 0.0),
            jnp.where(at_two[None], (heads[1] - heads[0])[:, :, None], 0.0),
        ],
        axis=2,
    ).astype(BF)

    h, g = h_in[0], g_in[0]
    gains, shifts = norm_gain[0], norm_bias[0]
    q, key, value, prob, att, resid_one, mid, relrev, half = attention_forward(
        h, g, seg_ids[0], target_flags[0], perm_order[0], w_query[0], w_key[0], w_value[0], w_out[0], w_rel[0],
        rel, rev, attn_bias[0], table, gains[0:1], shifts[0:1],
    )
    out, dresid_two, dbranch, slope, keep_down, send_down, vec_two, up_all, down_all = feed_forward(
        parts, shards, place, index, up, down, resid_one, mid, up_bias, b_down, gains, shifts, d_h_out[0], d_g_out[0], pieces
    )
    dproj, dresid_one, keep_up, send_up, vec_one, dbias_up = feed_backward(
        parts, shards, index, up_all, down_all, dbranch, dresid_two, resid_one, mid, slope, gains[0:1]
    )
    dq, dkey, dvalue, drel, vec_att = attention_backward(
        dproj, w_out[0], q, att, key, value, prob, relrev, half, attn_bias[0], table
    )
    keep_att, send_att = weight_grads(index, h, g, att, rev, dproj, dq, dkey, dvalue, drel)

    upward = [1 << at for at in range(1, swap.data.bit_length() - 1)]
    downward = upward[::-1]
    sum_down = data_scatter(swap, keep_down, send_down, upward)
    sum_up = data_scatter(swap, keep_up, send_up, downward)
    sum_first = data_scatter(swap, keep_att[:2], send_att[:2], upward)
    sum_last = data_scatter(swap, keep_att[2:], send_att[2:], downward)

    def feed_total(value):
        total = value[:, :width].astype(F32)
        for shard in range(1, shards):
            total += swap.tensor_swap(value[:, shard * width : (shard + 1) * width], shard).astype(F32)
        return total

    d_up = feed_total(sum_up)
    d_down = feed_total(sum_down).T
    both = jnp.concatenate([sum_first, sum_last], axis=0)
    stacked = jnp.stack([both[:, :, shard * own_part : (shard + 1) * own_part] for shard in range(shards)])

    def stack_part(bits):
        return lax.dynamic_index_in_dim(stacked, tensor_at ^ bits, 0, keepdims=False)

    d_att = stack_part(0).astype(F32)
    for bits in range(1, shards):
        d_att += swap.tensor_swap(stack_part(bits), bits).astype(F32)

    low_q = lax.dot_general(dq, w_query[0], (((1,), (1,)), ((), ())), preferred_element_type=F32)
    grad_h = (
        dresid_one[:length]
        + low_q[:length]
        + lax.dot_general(dkey, w_key[0], (((0,), (1,)), ((), ())), preferred_element_type=F32)
        + lax.dot_general(dvalue, w_value[0], (((0,), (1,)), ((), ())), preferred_element_type=F32)
    )
    grad_g = dresid_one[length:] + low_q[length:]

    bias_blocks = dbias_up.reshape(shards, width)
    bias_true = jnp.concatenate(
        [lax.dynamic_index_in_dim(bias_blocks, tensor_at ^ shard, 0, keepdims=False) for shard in range(shards)]
    )
    vector = jnp.concatenate(
        [
            vec_att[:5].reshape(-1), vec_one[0], vec_two[0], vec_one[1], vec_two[1], vec_two[2], bias_true,
        ]
    )
    size = vector.shape[0]
    block = vector.reshape(size // LANES, LANES)
    bit = 1
    while bit < swap.data:
        block = block + swap.data_swap(block, bit)
        bit *= 2
    bit = 1
    while bit < shards:
        block = block + swap.tensor_swap(block, bit)
        bit *= 2
    own = size // (swap.data * shards)
    d_vectors = lax.dynamic_slice_in_dim(block.reshape(-1), (dp_at * shards + tensor_at) * own, own, 0)

    return (
        out[:length][None], out[length:][None], grad_h[None], grad_g[None],
        d_att[0][None], d_att[1][None], d_att[2][None], d_att[4][None], d_att[3][None],
        d_up[None], d_down[None], d_vectors[None],
    )


def solution(mesh):
    every = P(AXES, None, None)
    rows = P(AXES, None)
    in_specs = (
        every, every, rows, rows, rows, P(), P(), P(), P(), P(), P(), P(), P(), P(),
        P(None, None, "tensor"), P(None, "tensor"), P(None, "tensor", None), P(), every, every,
    )
    grads = P(None, "dp", "tensor")
    out_specs = (
        every, every, every, every, grads, grads, grads, grads, grads, grads,
        P(None, "tensor", "dp"), P(None, AXES),
    )
    return jax.shard_map(per_device, mesh=mesh, in_specs=in_specs, out_specs=out_specs, check_vma=False)
```

```python
import functools
import math

import jax
import jax.numpy as jnp
import numpy as np
from jax import lax
from jax.experimental import pallas as pl
from jax.experimental.pallas import tpu as pltpu
from jax.sharding import PartitionSpec as P

HEADS = 12
HEAD_DIM = 64
LANES = 128
PAIRS = HEADS // 2
NEGATIVE = -1e30
EPSILON = 1e-06
AXES = ("dp", "tensor")
BF = jnp.bfloat16
F32 = jnp.float32
FIRST_PAIRS = 2
EARLY_PAIRS, LAST_PAIRS = (0, 2, 3, 5), (1, 4)
VMEM_MIB = {
    "share_slices": 4, "attention_first": 20, "attention_second": 14, "feed_up_own": 6, "feed_up": 14, "feed_down": 22,
    "feed_back_up": 16, "feed_back_mid": 10, "attention_back_early": 20, "attention_back_last": 18, "pack_vectors": 2,
    "pack_rows": 2,
}


def rel_table(length, model_width):
    position = (length - np.arange(2 * length)).astype(np.float32)
    frequency = np.float32(1.0) / np.float32(10000.0) ** (
        np.arange(0, model_width, 2).astype(np.float32) / np.float32(model_width)
    )
    angles = position[:, None] * frequency[None, :]
    return np.concatenate([np.sin(angles), np.cos(angles)], axis=1).astype(BF)


class Late:
    def __init__(self, source, target, sem):
        self.target, self.waiting = target, True
        self.copy = pltpu.make_async_copy(source, target, sem)
        self.copy.start()

    def get(self):
        if self.waiting:
            self.copy.wait()
            self.waiting = False
        return self.target


class Early:
    def __init__(self, ref, target, sems):
        self.ref, self.target, self.sems, self.copies = ref, target, sems, []

    def send(self, *where):
        source, target = (self.ref.at[where], self.target.at[where]) if where else (self.ref, self.target)
        copy = pltpu.make_async_copy(source, target, self.sems.at[len(self.copies)])
        copy.start()
        self.copies.append(copy)


SENDS = 16


def call(kernel, outs, ins, deps, scratch, name, flops):
    deps = tuple(deps)
    spaces = {"s": pltpu.SMEM, "v": pltpu.VMEM, "h": pl.ANY, "l": pltpu.HBM, "e": pltpu.HBM, "b": pltpu.HBM}
    late = [value for kind, value in ins if kind == "l"]
    early = [(shape, dtype) for kind, shape, dtype in outs if kind == "e"]
    more = [pltpu.VMEM(value.shape, value.dtype) for value in late] + [pltpu.VMEM(*spec) for spec in early]
    if late:
        more.append(pltpu.SemaphoreType.DMA((len(late),)))
    if early:
        more.append(pltpu.SemaphoreType.DMA((len(early), SENDS)))
    first_out = len(ins) + len(deps)
    first_scratch = first_out + len(outs)

    def wrapped(*refs):
        own = refs[first_scratch + len(scratch) :]
        late_refs, early_refs = own[: len(late)], own[len(late) : len(late) + len(early)]
        sems = list(own[len(late) + len(early) :])
        late_sem = sems.pop(0) if late else None
        early_sem = sems.pop(0) if early else None
        given, at = [], 0
        for (kind, _), ref in zip(ins, refs[: len(ins)], strict=True):
            if kind == "l":
                ref = Late(ref, late_refs[at], late_sem.at[at])
                at += 1
            given.append(ref)
        made, at = [], 0
        for (kind, _, _), ref in zip(outs, refs[first_out:first_scratch], strict=True):
            if kind == "e":
                ref = Early(early_refs[at], ref, early_sem.at[at])
                at += 1
            made.append(ref)
        kernel(*given, *made, *refs[first_scratch : first_scratch + len(scratch)])
        for item in given:
            if isinstance(item, Late):
                item.get()
        for item in made:
            if isinstance(item, Early):
                for copy in item.copies:
                    copy.wait()

    return pl.pallas_call(
        wrapped,
        out_shape=[jax.ShapeDtypeStruct(shape, dtype) for _, shape, dtype in outs],
        in_specs=[pl.BlockSpec(memory_space=spaces[kind]) for kind, _ in ins]
        + [pl.BlockSpec(memory_space=pl.ANY)] * len(deps),
        out_specs=[pl.BlockSpec(memory_space=spaces[kind]) for kind, _, _ in outs],
        scratch_shapes=list(scratch) + more,
        compiler_params=pltpu.CompilerParams(vmem_limit_bytes=VMEM_MIB[name] * 1024 * 1024),
        cost_estimate=pl.CostEstimate(flops=flops * 100, bytes_accessed=10 * 10**6, transcendentals=0),
        name=name,
    )(*[value for _, value in ins], *deps)


def nn(left, right):
    return lax.dot_general(left, right, (((1,), (0,)), ((), ())), preferred_element_type=F32)


def nt(left, right):
    return lax.dot_general(left, right, (((1,), (1,)), ((), ())), preferred_element_type=F32)


def tn(left, right):
    return lax.dot_general(left, right, (((0,), (0,)), ((), ())), preferred_element_type=F32)


def lane_index(rows):
    return lax.broadcasted_iota(jnp.int32, (rows, LANES), 1)


def pair_lanes(pair):
    return pl.ds(pl.multiple_of(pair * LANES, LANES), LANES)


def row_lanes(row, pair, width):
    return pl.ds(pl.multiple_of(row * width + pair * LANES, LANES), LANES)


def norm_stats(source):
    mean = jnp.mean(source, axis=-1, keepdims=True)
    centered = source - mean
    variance = jnp.mean(centered * centered, axis=-1, keepdims=True)
    rstd = lax.rsqrt(variance + EPSILON)
    return centered * rstd, rstd


def norm_back(grad, xhat, rstd, gain):
    dxhat = grad * gain
    mean_one = jnp.mean(dxhat, axis=-1, keepdims=True)
    mean_two = jnp.mean(dxhat * xhat, axis=-1, keepdims=True)
    return rstd * (dxhat - mean_one - xhat * mean_two)


def seg_coefficients(half_wide, lane):
    return jnp.where(lane % HEAD_DIM == 0, half_wide, 1.0 - 2.0 * half_wide)


def seg_keys(half_wide, lane):
    place = lane % HEAD_DIM
    return jnp.where(place == 0, 1.0, jnp.where(place == 1, half_wide, 0.0))


def seg_table(seg_ref, pair, width):
    row = lax.broadcasted_iota(jnp.int32, (LANES, LANES), 0)
    lane = lax.broadcasted_iota(jnp.int32, (LANES, LANES), 1)
    one = jnp.broadcast_to(seg_ref[0:1, pair_lanes(pair)], (LANES, LANES)).T
    two = jnp.broadcast_to(seg_ref[0:1, row_lanes(1, pair, width)], (LANES, LANES)).T
    base = jnp.where(row < HEAD_DIM, HEAD_DIM, 0)
    at_one = lane == base
    at_two = at_one | (lane == base + 1)
    return jnp.concatenate([jnp.where(at_one, one, 0.0), jnp.where(at_two, two - one, 0.0)], axis=1).astype(BF)


def attend_pair(pair, first, q_ref, key_ref, value_ref, relkey_ref, mask_ref, half_ref, bias_ref, seg_ref, prob_ref, att_ref):
    length, width = key_ref.shape
    block = length // 2
    lanes = pair_lanes(pair)
    lane_q = lane_index(2 * length)
    lane_k = lane_index(length)
    low_q = lane_q < HEAD_DIM
    low_k = lane_k < HEAD_DIM
    half_w = half_ref[...]
    scale = 1.0 / math.sqrt(HEAD_DIM)
    query = q_ref[:, lanes]
    word = ((query + bias_ref[0:1, lanes]) * scale).astype(BF)
    relq = ((query + bias_ref[0:1, row_lanes(1, pair, width)]) * scale).astype(BF)
    segq = ((query + bias_ref[0:1, row_lanes(2, pair, width)]) * scale).astype(BF)
    terms = nn(segq, seg_table(seg_ref, pair, width))
    coef = seg_coefficients(jnp.concatenate([half_w, half_w], axis=0), lane_q)
    extra = (terms[:, :LANES] + terms[:, LANES:] * coef).astype(BF)
    key_extra = seg_keys(half_w, lane_k).astype(BF)
    key = key_ref[:, lanes]
    value = value_ref[:, lanes]
    zero = jnp.zeros_like(relq)
    attended = []
    for head in (0, 1):
        if head == 0:
            word_one = jnp.where(low_q, word, extra)
            key_one = jnp.where(low_k, key, key_extra)
            rel_one = jnp.where(low_q, relq, zero)
        else:
            word_one = jnp.where(low_q, extra, word)
            key_one = jnp.where(low_k, key_extra, key)
            rel_one = jnp.where(low_q, zero, relq)
        score = nt(word_one, key_one)
        for part in (0, 1):
            base = block - block * part
            rows_h = slice(block * part, block * part + block)
            rows_g = slice(length + block * part, length + block * part + block)
            rel_rows = jnp.concatenate([rel_one[rows_h], rel_one[rows_g]], axis=0)
            raw = nt(rel_rows, relkey_ref[base : base + 3 * block, lanes])
            for place_at, rows in ((0, rows_h), (1, rows_g)):
                shifted = pltpu.roll(
                    raw[place_at * block : (place_at + 1) * block], 2 * block, 1, stride=1, stride_axis=0
                )[:, :length]
                logits = score[rows] + shifted + mask_ref[rows]
                top = jnp.max(logits, axis=1, keepdims=True)
                power = jnp.exp(logits - top)
                total = jnp.sum(power, axis=1, keepdims=True)
                prob_ref[2 * (pair - first) + head, rows, :] = (power * (1.0 / total)).astype(BF)
        attended.append(nn(prob_ref[2 * (pair - first) + head], value))
    att_ref[:, lanes] = jnp.where(low_q, attended[0], attended[1]).astype(BF)


def attention_first_kernel(
    parts, h_late, g_late, wq_late, wk_late, wv_late, rel_late, wr_late, rev_late,
    seg_row, flag_row, order_row, bias_ref, seg_ref,
    q_ref, key_ref, value_ref, relkey_ref, mask_ref, half_ref, att_ref, relrev_out, prob_out, left_x_out, left_rev_out,
    x_ref, raw_ref,
):
    h_ref, g_ref = h_late.get(), g_late.get()
    length, width = h_ref.shape
    x_ref[:length] = h_ref[...]
    x_ref[length:] = g_ref[...]

    def project(left, right_late, target):
        right = right_late.get()
        for col in range(0, width, 256):
            cols = slice(col, col + 256)
            target[:, cols] = nn(left[...], right[:, cols]).astype(target.dtype)

    project(x_ref, wq_late, q_ref)
    project(h_ref, wk_late, key_ref)
    project(h_ref, wv_late, value_ref)
    project(rel_late.get(), wr_late, relkey_ref)

    def wide(row_ref):
        return jnp.broadcast_to(row_ref[...].astype(F32), (length, length))

    row_at = lax.broadcasted_iota(jnp.int32, (length, length), 0)
    col_at = lax.broadcasted_iota(jnp.int32, (length, length), 1)
    seg, order = wide(seg_row), wide(order_row)
    same_doc = seg.T == seg
    start = jnp.min(jnp.where(same_doc, col_at.astype(F32), float(length)), axis=1, keepdims=True)
    in_doc = jnp.sum(jnp.where(same_doc, 1.0, 0.0), axis=1, keepdims=True)
    place = lax.broadcasted_iota(jnp.int32, (length, 1), 0).astype(F32)
    half = jnp.where(2.0 * (place - start) >= in_doc, 1.0, 0.0)
    half_ref[...] = jnp.broadcast_to(half, (length, LANES))
    content = same_doc & ((wide(flag_row) == 0.0) | (order <= order.T))
    mask_ref[:length] = jnp.where(content, 0.0, NEGATIVE)
    mask_ref[length:] = jnp.where(content & (row_at != col_at), 0.0, NEGATIVE)

    def pair_step(pair, carry):
        attend_pair(
            pair, 0, q_ref, key_ref, value_ref, relkey_ref, mask_ref, half_ref, bias_ref, seg_ref, prob_out.ref, att_ref
        )
        return carry

    lax.fori_loop(0, FIRST_PAIRS, pair_step, 0)
    prob_out.send()
    project(rev_late.get(), wr_late, relrev_out.ref)
    relrev_out.send()
    turn_rows(lambda col: x_ref[:, col : col + 256], raw_ref.at[0], left_x_out.ref, parts)
    left_x_out.send()
    rev_ref = rev_late.get()
    turn_rows(lambda col: rev_ref[:, col : col + 256], raw_ref.at[1], left_rev_out.ref, parts)
    left_rev_out.send()


def attention_first(parts, h, g, seg, flag, order, wq, wk, wv, wr, rel, rev, bias, table, deps):
    length, width = h.shape
    two = 2 * length
    outs = [
        ("v", (two, width), F32), ("v", (length, width), BF), ("v", (length, width), BF), ("v", (two, width), BF),
        ("v", (two, length), F32), ("v", (length, LANES), F32), ("v", (two, FIRST_PAIRS * LANES), BF), ("e", (two, width), BF),
        ("e", (2 * FIRST_PAIRS, two, length), BF), ("e", (width, two), BF), ("e", (width, two), BF),
    ]
    ins = [("l", value) for value in (h, g, wq, wk, wv, rel, wr, rev)]
    ins += [("v", value) for value in (seg, flag, order, bias, table)]
    scratch = [pltpu.VMEM((two, width), BF), pltpu.VMEM((2, width, two), BF)]
    return call(functools.partial(attention_first_kernel, parts), outs, ins, deps, scratch, "attention_first", 10 * 10**9)


def attention_second_kernel(
    parts, wo_late, h_late, g_late, q_ref, key_ref, value_ref, relkey_ref, mask_ref, half_ref, att_first_ref,
    bias_ref, seg_ref, gain_ref, shift_ref,
    resid_ref, mid_ref, prob_out, att_out, left_att_out,
    raw_ref,
):
    length, width = key_ref.shape
    att_ref = att_out.ref
    att_ref[:, : FIRST_PAIRS * LANES] = att_first_ref[...]

    def pair_step(pair, carry):
        attend_pair(
            pair, FIRST_PAIRS, q_ref, key_ref, value_ref, relkey_ref, mask_ref, half_ref, bias_ref, seg_ref, prob_out.ref, att_ref
        )
        return carry

    for first in range(FIRST_PAIRS, PAIRS, 2):
        lax.fori_loop(first, first + 2, pair_step, 0)
        prob_out.send(pl.ds(2 * (first - FIRST_PAIRS), 4))
    att_out.send()
    wo_ref, h_ref, g_ref = wo_late.get(), h_late.get(), g_late.get()
    for col in range(0, width, 256):
        cols = slice(col, col + 256)
        total = nn(att_ref[...], wo_ref[:, cols])
        resid_ref[:length, cols] = h_ref[:, cols].astype(F32) + total[:length]
        resid_ref[length:, cols] = g_ref[:, cols].astype(F32) + total[length:]
    turn_rows(lambda col: att_ref[:, col : col + 256], raw_ref, left_att_out.ref, parts)
    left_att_out.send()
    for row in range(0, 2 * length, 64):
        xhat, _ = norm_stats(resid_ref[row : row + 64, :])
        mid_ref[row : row + 64, :] = (xhat * gain_ref[0:1, :width] + shift_ref[0:1, :width]).astype(BF)


def attention_second(parts, wo, h, g, q, key, value, relkey, mask, half, att, bias, table, gain, shift, deps):
    length, width = h.shape
    two = 2 * length
    outs = [
        ("v", (two, width), F32), ("v", (two, width), BF), ("e", (HEADS - 2 * FIRST_PAIRS, two, length), BF),
        ("e", (two, width), BF), ("e", (width, two), BF),
    ]
    ins = [("l", value) for value in (wo, h, g)]
    ins += [("v", value) for value in (q, key, value, relkey, mask, half, att, bias, table, gain, shift)]
    return call(
        functools.partial(attention_second_kernel, parts), outs, ins, deps, [pltpu.VMEM((width, two), BF)],
        "attention_second", 10 * 10**9,
    )


def place_rows(raw_ref, out_ref, parts):
    rows = raw_ref.shape[0] // parts
    me = lax.axis_index("dp") if parts > 1 else 0
    order = [low | (rest << 1) for low in (0, 1) for rest in range(parts // 2)] if parts > 1 else [0]
    for at, block in enumerate(order):
        source = pl.multiple_of((me ^ block) * rows, rows)
        out_ref[at * rows : (at + 1) * rows, :] = raw_ref[pl.ds(source, rows), :]


def turn_rows(source, raw_ref, out_ref, parts):
    for col in range(0, raw_ref.shape[0], 256):
        raw_ref[col : col + 256, :] = source(col).astype(F32).T.astype(BF)
    place_rows(raw_ref, out_ref, parts)


def attention_back_kernel(
    pairs, with_out, wo_late, dproj_ref, q_ref, att_ref, key_ref, value_ref, prob_one, prob_two, relrev_ref, half_ref, left_x_ref,
    left_rev_ref, *refs,
):
    left_att_ref, *refs = refs if with_out else (None, *refs)
    bias_ref, seg_ref, dq_ref, dkey_ref, dvalue_ref, vec_ref, keep_out, send_out, datt_ref, drel_ref = refs
    length, width = key_ref.shape
    block = length // 2
    split = width // 2
    wo_ref = wo_late.get()
    for at, pair in enumerate(pairs):
        rows = slice(pair * LANES, (pair + 1) * LANES)
        datt_ref[:, at * LANES : (at + 1) * LANES] = nt(dproj_ref[...], wo_ref[rows, :]).astype(BF)
    vec_ref[...] = jnp.zeros_like(vec_ref)

    def pair_step(at, pair):
        lanes = slice(pair * LANES, (pair + 1) * LANES)
        own = slice(at * LANES, (at + 1) * LANES)
        prob_ref, prob_at = (prob_one, 2 * pair) if pair < FIRST_PAIRS else (prob_two, 2 * (pair - FIRST_PAIRS))
        lane_q = lane_index(2 * length)
        lane_k = lane_index(length)
        low_q = lane_q < HEAD_DIM
        low_k = lane_k < HEAD_DIM
        half_w = half_ref[...]
        flip_row = lax.broadcasted_iota(jnp.int32, (length, length), 0)
        flip_col = lax.broadcasted_iota(jnp.int32, (length, length), 1)
        flip = jnp.where(flip_row + flip_col == length - 1, 1.0, 0.0).astype(BF)
        sel_row = lax.broadcasted_iota(jnp.int32, (2 * LANES, LANES), 0) % LANES
        sel_col = lax.broadcasted_iota(jnp.int32, (2 * LANES, LANES), 1)
        select = jnp.where(
            ((sel_row < HEAD_DIM) & ((sel_col == HEAD_DIM) | (sel_col == HEAD_DIM + 1)))
            | ((sel_row >= HEAD_DIM) & (sel_col < 2)),
            1.0,
            0.0,
        ).astype(BF)
        query = q_ref[:, lanes]
        word = query + bias_ref[0:1, lanes]
        relq = query + bias_ref[0:1, row_lanes(1, pair, width)]
        segq = (query + bias_ref[0:1, row_lanes(2, pair, width)]).astype(BF)
        word_t = word.T.astype(BF)
        relq_t = relq.T.astype(BF)
        datt = datt_ref[:, own]
        datt_wide = datt.astype(F32)
        datt_t = datt_wide.T.astype(BF)
        datt_scaled = datt_wide * (1.0 / math.sqrt(HEAD_DIM))
        product = datt_scaled * att_ref[:, lanes].astype(F32)
        product_high = product.astype(BF)
        product_low = (product - product_high.astype(F32)).astype(BF)
        delta = nn(jnp.concatenate([product_high, product_low], axis=1), select)
        delta_high = delta.astype(BF).astype(F32)
        minus = jnp.where(lane_q % HEAD_DIM == 0, -delta_high, delta_high - delta).astype(BF)
        datt_low = datt_scaled.astype(BF)
        key_extra = seg_keys(half_w, lane_k).astype(BF)
        ones_extra = jnp.where(lane_k % HEAD_DIM < 2, 1.0, 0.0).astype(BF)
        key = key_ref[:, lanes]
        value = value_ref[:, lanes]
        dword, drel = [], []
        for head in (0, 1):
            rows_t = slice(HEAD_DIM * head, HEAD_DIM * head + HEAD_DIM)
            if head == 0:
                datt_one = jnp.where(low_q, datt_low, minus)
                value_one = jnp.where(low_k, value, ones_extra)
                key_one = jnp.where(low_k, key, key_extra)
            else:
                datt_one = jnp.where(low_q, minus, datt_low)
                value_one = jnp.where(low_k, ones_extra, value)
                key_one = jnp.where(low_k, key_extra, key)
            prob = prob_ref[prob_at + head]
            dprob = nt(datt_one, value_one)
            dscore = (prob.astype(F32) * dprob).astype(BF)
            dword.append(nn(dscore, key_one))
            rows_out = slice(at * LANES + HEAD_DIM * head, at * LANES + HEAD_DIM * (head + 1))
            dkey_ref[rows_out, :] = nn(word_t[rows_t], dscore).astype(BF)
            dvalue_ref[rows_out, :] = nn(datt_t[rows_t], prob).astype(BF)
            flipped = nn(dscore, flip).astype(BF)
            pad = jnp.zeros((block, block), BF)
            rel_parts, drel_t = [], []
            for part in (0, 1):
                rows_h = slice(block * part, block * part + block)
                rows_g = slice(length + block * part, length + block * part + block)
                draw = jnp.concatenate(
                    [
                        pltpu.roll(jnp.concatenate([flipped[rows], pad], axis=1), 0, 1, stride=1, stride_axis=0)
                        for rows in (rows_h, rows_g)
                    ],
                    axis=0,
                )
                rel_parts.append(nn(draw, relrev_ref[block * part : block * part + 3 * block, lanes]))
                rel_cols = jnp.concatenate([relq_t[rows_t, rows_h], relq_t[rows_t, rows_g]], axis=1)
                drel_t.append(nn(rel_cols, draw))
            drel.append(
                jnp.concatenate(
                    [rel_parts[0][:block], rel_parts[1][:block], rel_parts[0][block:], rel_parts[1][block:]], axis=0
                )
            )
            drel_ref[rows_out, :] = jnp.concatenate(
                [
                    drel_t[0][:, :block],
                    drel_t[0][:, block:] + drel_t[1][:, : 2 * block],
                    drel_t[1][:, 2 * block :],
                ],
                axis=1,
            ).astype(BF)
        extra = jnp.where(low_q, dword[1], dword[0])
        dword_all = jnp.where(low_q, dword[0], dword[1])
        drel_all = jnp.where(low_q, drel[0], drel[1])
        coef = seg_coefficients(jnp.concatenate([half_w, half_w], axis=0), lane_q)
        dterms = jnp.concatenate([extra, extra * coef], axis=1).astype(BF)
        dsegq = nt(dterms, seg_table(seg_ref, pair, width))
        dtable = tn(dterms, segq)
        dq_ref[:, own] = (dword_all + drel_all + dsegq).astype(BF)
        low_one = lane_index(1) < HEAD_DIM
        first = jnp.where(low_one, dtable[HEAD_DIM : HEAD_DIM + 1], dtable[0:1])
        far = LANES + HEAD_DIM
        second = jnp.where(
            low_one, dtable[far : far + 1] + dtable[far + 1 : far + 2], dtable[LANES : LANES + 1] + dtable[LANES + 1 : LANES + 2]
        )
        vec_ref[0:1, own] = jnp.sum(dword_all, axis=0, keepdims=True)
        vec_ref[1:2, own] = jnp.sum(drel_all, axis=0, keepdims=True)
        vec_ref[2:3, own] = jnp.sum(dsegq, axis=0, keepdims=True)
        vec_ref[3:4, own] = first - second
        vec_ref[4:5, own] = second
    for at, pair in enumerate(pairs):
        pair_step(at, pair)
    size = len(pairs) * LANES
    todo = [
        (left_x_ref[...], dq_ref, nn), (left_x_ref[:, :length], dkey_ref, nt), (left_x_ref[:, :length], dvalue_ref, nt),
        (left_rev_ref[...], drel_ref, nt),
    ]
    if with_out:
        todo.append((left_att_ref[...], dproj_ref, nn))
    at = 0
    for left, right, dot in todo:
        count = right.shape[1] if dot is nn else right.shape[0]
        for col in range(0, count, 256):
            cols = slice(col, col + 256)
            piece = dot(left, right[:, cols] if dot is nn else right[cols, :]).astype(BF)
            keep_out.ref[:, at + col : at + col + 256] = piece[:split]
            send_out.ref[:, at + col : at + col + 256] = piece[split:]
        done = pl.ds(at, count)
        send_out.send(slice(None), done)
        keep_out.send(slice(None), done)
        at += count


def attention_back(name, pairs, wo, dproj, q, att, key, value, prob_one, prob_two, relrev, half, left_x, left_rev, left_att, bias, table, deps):
    length, width = key.shape
    two, size = 2 * length, len(pairs) * LANES
    total = 4 * size + (width if left_att is not None else 0)
    outs = [
        ("v", (two, size), BF), ("v", (size, length), BF), ("v", (size, length), BF), ("v", (8, size), F32),
        ("e", (width // 2, total), BF), ("e", (width // 2, total), BF),
    ]
    ins = [("l", wo)] + [("v", x) for x in (dproj, q, att, key, value, prob_one, prob_two, relrev, half, left_x, left_rev)]
    ins += [("v", left_att)] if left_att is not None else []
    ins += [("v", bias), ("v", table)]
    kernel = functools.partial(attention_back_kernel, pairs, left_att is not None)
    scratch = [pltpu.VMEM((two, size), BF), pltpu.VMEM((size, two), BF)]
    return call(kernel, outs, ins, deps, scratch, name, 12 * 10**9)


def share_kernel(parts, up_hbm, down_hbm, bias_ref, up_ref, down_ref, sem):
    rows = up_hbm.shape[0] // parts
    start = pl.multiple_of(lax.axis_index("dp") * rows, rows) if parts > 1 else 0
    one = pltpu.make_async_copy(up_hbm.at[pl.ds(start, rows)], up_ref, sem.at[0])
    two = pltpu.make_async_copy(down_hbm.at[pl.ds(start, rows)], down_ref.at[pl.ds(0, rows)], sem.at[1])
    one.start()
    two.start()
    down_ref[rows:, :] = jnp.broadcast_to(bias_ref[...], (16, bias_ref.shape[1]))
    one.wait()
    two.wait()


def share_slices(parts, up, down, bias):
    rows, width = up.shape[0] // parts, up.shape[1]
    return call(
        functools.partial(share_kernel, parts), [("v", (rows, width), BF), ("v", (rows + 16, width), BF)],
        [("b", up), ("b", down), ("v", bias)], (), [pltpu.SemaphoreType.DMA((2,))], "share_slices", 10**7,
    )


def start_pieces(pieces, piece_refs, target_ref, sem):
    copies = {}
    for count, ((shard, block, rows, source_at), source) in enumerate(zip(pieces, piece_refs, strict=True)):
        where = 0
        if rows < target_ref.shape[1]:
            where = pl.multiple_of((lax.axis_index("dp") ^ block) * rows, rows)
        copy = pltpu.make_async_copy(
            source.at[pl.ds(source_at, rows)], target_ref.at[shard, pl.ds(where, rows)], sem.at[count]
        )
        copy.start()
        copies.setdefault(shard, []).append(copy)
    return copies


def gelu_parts(pre):
    root = math.sqrt(2.0 / math.pi)
    square = pre * pre
    bend = jnp.tanh(root * pre * (1.0 + 0.044715 * square))
    upper = 0.5 + 0.5 * bend
    slope = upper + (0.5 * root) * pre * (1.0 - bend * bend) * (1.0 + (3 * 0.044715) * square)
    return (pre * upper).astype(BF), slope.astype(BF)


def feed_up_own_kernel(mid_ref, up_late, bias_ref, act_ref, slope_ref):
    width = mid_ref.shape[1]
    up_ref = up_late.get()
    for col in range(0, width, 256):
        cols = slice(col, col + 256)
        bias = bias_ref[0:1, cols].astype(F32)
        act_ref[:, cols], slope_ref[:, cols] = gelu_parts(nn(mid_ref[...], up_ref[:, cols]) + bias)


def feed_up_own(mid, up, bias, deps):
    outs = [("v", mid.shape, BF), ("v", mid.shape, BF)]
    return call(feed_up_own_kernel, outs, [("v", mid), ("l", up), ("v", bias)], deps, [], "feed_up_own", 3 * 10**9)


def feed_up_kernel(shards, pieces, rows, mid_ref, *refs):
    bias_refs, piece_refs = refs[: shards - 1], refs[shards - 1 : shards - 1 + len(pieces)]
    act_ref, slope_ref, up_ref, bias_ref, in_sem, bias_sem = refs[shards - 1 + len(pieces) :]
    width = mid_ref.shape[1]
    copies = start_pieces(pieces, piece_refs, up_ref, in_sem)
    biases = [
        pltpu.make_async_copy(ref.at[pl.ds(rows, 16)], bias_ref.at[shard], bias_sem.at[shard])
        for shard, ref in enumerate(bias_refs)
    ]
    for copy in biases:
        copy.start()
    for copy in biases:
        copy.wait()
    for shard in range(shards - 1):
        for copy in copies[shard]:
            copy.wait()
        for col in range(0, width, 256):
            cols = slice(shard * width + col, shard * width + col + 256)
            pre = nn(mid_ref[...], up_ref[shard, :, col : col + 256])
            act_ref[:, cols], slope_ref[:, cols] = gelu_parts(
                pre + bias_ref[shard, 0:1, col : col + 256].astype(F32)
            )


def feed_up(shards, mid, rows, biases, pieces, deps):
    rows_all, width = mid.shape
    hidden = (shards - 1) * width
    names = [entry[:-1] for entry in pieces]
    outs = [("v", (rows_all, hidden), BF), ("v", (rows_all, hidden), BF), ("v", (shards - 1, width, width), BF)]
    ins = [("v", mid)] + [("h", value) for value in biases] + [("h", entry[-1]) for entry in pieces]
    scratch = [
        pltpu.VMEM((shards - 1, 16, width), BF), pltpu.SemaphoreType.DMA((len(names),)), pltpu.SemaphoreType.DMA((shards - 1,)),
    ]
    return call(functools.partial(feed_up_kernel, shards, names, rows), outs, ins, deps, scratch, "feed_up", 6 * 10**9)


def feed_down_kernel(parts, shards, pieces, own_late, dh_late, dg_late, act_own, resid_ref, act_rest, *refs):
    down_bias, gain_ref, shift_ref = refs[:3]
    piece_refs = refs[3 : 3 + len(pieces)]
    out_h, out_g, dresid_ref, dbranch_ref, keep_out, send_out, vec_ref, down_ref, raw_ref, left_ref, in_sem = refs[3 + len(pieces) :]
    rows_all, width = resid_ref.shape
    length = rows_all // 2
    split = width // 2
    copies = start_pieces(pieces, piece_refs, down_ref, in_sem)
    own_down = own_late.get()
    for col in range(0, width, 256):
        cols = slice(col, col + 256)
        dresid_ref[:, cols] = nn(act_own[...], own_down[:, cols])
    for shard in range(shards - 1):
        for copy in copies[shard]:
            copy.wait()
    down_all = down_ref.reshape((shards - 1) * width, width)
    for col in range(0, width, 256):
        cols = slice(col, col + 256)
        dresid_ref[:, cols] += nn(act_rest[...], down_all[:, cols])
    gain_one, gain_two = gain_ref[0:1, :width], gain_ref[0:1, width:]
    shift_one, shift_two = shift_ref[0:1, :width], shift_ref[0:1, width:]
    step_rows = 32
    sums = [jnp.zeros((step_rows, width), F32)] * 3
    for row in range(0, rows_all, step_rows):
        rows = slice(row, row + step_rows)
        grad_ref = dh_late.get() if row < length else dg_late.get()
        near = row % length
        xhat_one, _ = norm_stats(resid_ref[rows, :])
        middle = xhat_one * gain_one + shift_one
        xhat, rstd = norm_stats(middle + dresid_ref[rows, :] + down_bias[...])
        out = out_h if row < length else out_g
        out.ref[near : near + step_rows, :] = (xhat * gain_two + shift_two).astype(BF)
        grad = grad_ref[near : near + step_rows, :].astype(F32)
        dresid = norm_back(grad, xhat, rstd, gain_two)
        dresid_ref[rows, :] = dresid
        dbranch = dresid.astype(BF)
        dbranch_ref[rows, :] = dbranch
        sums = [sums[0] + grad * xhat, sums[1] + grad, sums[2] + dbranch.astype(F32)]
    vec_ref[...] = jnp.zeros_like(vec_ref)
    for at, total in enumerate(sums):
        vec_ref[at : at + 1, :] = jnp.sum(total, axis=0, keepdims=True)
    out_h.send()
    out_g.send()
    turn_rows(lambda col: dbranch_ref[:, col : col + 256], raw_ref, left_ref, parts)
    for source, count, offset in ((act_own, 1, 0), (act_rest, shards - 1, width)):
        for col in range(0, count * width, 256):
            piece = nn(left_ref[...], source[:, col : col + 256]).astype(BF)
            cols = slice(col + offset, col + offset + 256)
            keep_out.ref[:, cols] = piece[:split]
            send_out.ref[:, cols] = piece[split:]
            if (col + 256) % width == 0:
                done = pl.ds(col + offset + 256 - width, width)
                send_out.send(slice(None), done)
                keep_out.send(slice(None), done)


def feed_down(parts, shards, own_down, act_own, act_rest, resid_one, down_bias, gains, shifts, dh, dg, pieces, deps):
    rows_all, width = resid_one.shape
    hidden = shards * width
    names = [entry[:-1] for entry in pieces]
    outs = [
        ("e", dh.shape, BF), ("e", dg.shape, BF), ("v", (rows_all, width), F32), ("v", (rows_all, width), BF),
        ("e", (width // 2, hidden), BF), ("e", (width // 2, hidden), BF), ("v", (8, width), F32), ("v", (shards - 1, width, width), BF),
    ]
    ins = [("l", value) for value in (own_down, dh, dg)]
    ins += [("v", value) for value in (act_own, resid_one, act_rest, down_bias, gains, shifts)] + [("h", entry[-1]) for entry in pieces]
    scratch = [pltpu.VMEM((width, rows_all), BF), pltpu.VMEM((width, rows_all), BF), pltpu.SemaphoreType.DMA((len(names),))]
    return call(functools.partial(feed_down_kernel, parts, shards, names), outs, ins, deps, scratch, "feed_down", 8 * 10**9)


def feed_back_up_kernel(
    parts, shards, own_late, mid_ref, dbranch_ref, down_ref, slope_own, slope_rest,
    dpre_ref, keep_out, send_out, dbias_ref, raw_ref, left_ref,
):
    rows_all, width = mid_ref.shape
    split = width // 2
    turn_rows(lambda col: mid_ref[:, col : col + 256], raw_ref, left_ref, parts)
    own_down = own_late.get()
    for shard in range(shards):
        for col in range(0, width, 256):
            cols = slice(shard * width + col, shard * width + col + 256)
            if shard:
                near = (shard - 1) * width + col
                weight, slope = down_ref[shard - 1, col : col + 256, :], slope_rest[:, near : near + 256]
            else:
                weight, slope = own_down[col : col + 256, :], slope_own[:, col : col + 256]
            dpre = (nt(dbranch_ref[...], weight) * slope.astype(F32)).astype(BF)
            dpre_ref[:, cols] = dpre
            dbias_ref[:, cols] = jnp.sum(dpre.astype(F32), axis=0, keepdims=True)
            piece = nn(left_ref[...], dpre).astype(BF)
            keep_out.ref[:, cols] = piece[:split]
            send_out.ref[:, cols] = piece[split:]
        done = pl.ds(shard * width, width)
        send_out.send(slice(None), done)
        keep_out.send(slice(None), done)


def feed_back_up(parts, shards, own_down, down_rest, dbranch, mid, slope_own, slope_rest, deps):
    rows_all, width = mid.shape
    hidden = shards * width
    outs = [("v", (rows_all, hidden), BF), ("e", (width // 2, hidden), BF), ("e", (width // 2, hidden), BF), ("v", (1, hidden), F32)]
    ins = [("l", own_down)] + [("v", value) for value in (mid, dbranch, down_rest, slope_own, slope_rest)]
    scratch = [pltpu.VMEM((width, rows_all), BF), pltpu.VMEM((width, rows_all), BF)]
    return call(functools.partial(feed_back_up_kernel, parts, shards), outs, ins, deps, scratch, "feed_back_up", 8 * 10**9)


def feed_back_mid_kernel(shards, own_late, dpre_ref, up_ref, dresid_ref, resid_ref, gain_ref, dproj_ref, dresid_one_ref, vec_ref):
    rows_all, width = dresid_one_ref.shape
    own_up = own_late.get()
    for col in range(0, width, 256):
        cols = slice(col, col + 256)
        total = nt(dpre_ref[:, :width], own_up[cols, :])
        for shard in range(1, shards):
            total += nt(dpre_ref[:, shard * width : (shard + 1) * width], up_ref[shard - 1, cols, :])
        dresid_one_ref[:, cols] = total
    gain_one = gain_ref[0:1, :width]
    step_rows = 32
    sums = [jnp.zeros((step_rows, width), F32)] * 2
    for row in range(0, rows_all, step_rows):
        rows = slice(row, row + step_rows)
        xhat, rstd = norm_stats(resid_ref[rows, :])
        grad = dresid_ref[rows, :] + dresid_one_ref[rows, :]
        dresid = norm_back(grad, xhat, rstd, gain_one)
        dresid_one_ref[rows, :] = dresid
        dproj_ref[rows, :] = dresid.astype(BF)
        sums = [sums[0] + grad * xhat, sums[1] + grad]
    vec_ref[...] = jnp.zeros_like(vec_ref)
    for at, total in enumerate(sums):
        vec_ref[at : at + 1, :] = jnp.sum(total, axis=0, keepdims=True)


def feed_back_mid(shards, own_up, up_rest, dpre, dresid, resid_one, gains, deps):
    rows_all, width = resid_one.shape
    outs = [("v", (rows_all, width), BF), ("v", (rows_all, width), F32), ("v", (8, width), F32)]
    ins = [("l", own_up)] + [("v", value) for value in (dpre, up_rest, dresid, resid_one, gains)]
    return call(functools.partial(feed_back_mid_kernel, shards), outs, ins, deps, [], "feed_back_mid", 5 * 10**9)


def pack_vectors_kernel(shards, early_ref, last_ref, one_ref, two_ref, bias_ref, out_ref):
    width = one_ref.shape[1]
    for ref, pairs in ((early_ref, EARLY_PAIRS), (last_ref, LAST_PAIRS)):
        for at, pair in enumerate(pairs):
            out_ref[0:5, pair * LANES : (pair + 1) * LANES] = ref[0:5, at * LANES : (at + 1) * LANES]
    out_ref[5:6, :] = one_ref[0:1, :]
    out_ref[6:7, :] = two_ref[0:1, :]
    out_ref[7:8, :] = one_ref[1:2, :]
    out_ref[8:10, :] = two_ref[1:3, :]
    for shard in range(shards):
        place = 10 + (lax.axis_index("tensor") ^ shard)
        out_ref[pl.ds(place, 1), :] = bias_ref[0:1, shard * width : (shard + 1) * width]


def pack_vectors(shards, early, last, one, two, bias, rows, deps):
    outs = [("v", (rows, one.shape[1]), F32)]
    ins = [("v", value) for value in (early, last, one, two, bias)]
    return call(functools.partial(pack_vectors_kernel, shards), outs, ins, deps, [], "pack_vectors", 10**7)[0]


def pack_rows_kernel(count, rows, *refs):
    out_ref, sem = refs[count:]
    copies = [
        pltpu.make_async_copy(ref.at[pl.ds(0, rows)], out_ref.at[pl.ds(at * rows, rows)], sem.at[at])
        for at, ref in enumerate(refs[:count])
    ]
    for copy in copies:
        copy.start()
    for copy in copies:
        copy.wait()


def pack_rows(arrays, rows, deps):
    outs = [("v", (len(arrays) * rows, arrays[0].shape[1]), BF)]
    scratch = [pltpu.SemaphoreType.DMA((len(arrays),))]
    kernel = functools.partial(pack_rows_kernel, len(arrays), rows)
    return call(kernel, outs, [("h", value) for value in arrays], deps, scratch, "pack_rows", 10**7)[0]


class Exchange:
    def __init__(self, width):
        self.data = lax.axis_size("dp")
        self.tensor = lax.axis_size("tensor")
        self.by_hand = self.data == 8 and width % (32 * self.data) == 0
        self.blocks = self.data if self.by_hand else 1

    def data_swap(self, value, bit):
        pairs = [(at, at ^ bit) for at in range(self.data)]
        return lax.ppermute(value, "dp", pairs)

    def tensor_swap(self, value, bits):
        pairs = [(at, at ^ bits) for at in range(self.tensor)]
        return lax.ppermute(value, "tensor", pairs)


def add_low(left, right):
    return (left.astype(F32) + right.astype(F32)).astype(BF)


class Share:
    def __init__(self, swap, rows, first):
        self.swap, self.rows, self.first = swap, rows, first
        self.count = swap.tensor - 1

    def fetch(self, mine):
        self.raw = [self.swap.tensor_swap(mine, bits) for bits in range(1, self.swap.tensor)]

    def spread(self, deps):
        self.found = [(0, pack_rows(self.raw, self.rows, deps))]
        if self.swap.blocks > 1:
            bits = [1 << at for at in range(1, self.swap.data.bit_length() - 1)]
            mine = self.found[0][1]
            self.near = [(bit, self.swap.data_swap(mine, bit)) for bit in bits]
            self.found += self.near

    def cross(self):
        if self.swap.data == 8 and self.swap.blocks == 8:
            other = 6 - self.first
            self.found.append((6, self.swap.data_swap(dict(self.near)[self.first], other)))

    def finish(self):
        rows, pieces, found = self.rows, [], list(self.found)
        if self.swap.blocks > 1:
            found += [(block | 1, self.swap.data_swap(value, 1)) for block, value in self.found]
        for block, value in found:
            pieces += [(shard, block, rows, shard * rows, value) for shard in range(self.count)]
        return pieces


def add_all(terms):
    total = terms[0].astype(F32)
    for term in terms[1:]:
        total += term.astype(F32)
    return total


class Term:
    def __init__(self, array, take, axes):
        self.array, self.take, self.axes = array, take, axes

    def value(self):
        return self.array[tuple(self.take)]

    def narrow(self, axis, what):
        take = list(self.take)
        take[axis] = what
        return Term(self.array, take, {bit: at for bit, at in self.axes.items() if at != axis})


class Scatter:
    def __init__(self, swap, keep=None, send=None):
        self.swap = swap
        if keep is None:
            return
        if not swap.by_hand:
            whole = jnp.concatenate([keep, send], axis=0)
            self.arrived = lax.psum_scatter(whole, "dp", scatter_dimension=0, tiled=True)
            self.terms = [Term(self.arrived, [slice(None)] * 2, {})]
            return
        bits = [1 << at for at in range(1, swap.data.bit_length() - 1)][::-1]
        rows = keep.shape[0] // (swap.data // 2)
        shape = (2,) * len(bits) + (rows, keep.shape[-1])
        self.arrived = swap.data_swap(send, 1)
        axes = {bit: at for at, bit in enumerate(bits)}
        self.terms = [Term(x.reshape(shape), [slice(None)] * len(shape), axes) for x in (keep, self.arrived)]

    def columns(self, start, stop):
        part = Scatter(self.swap)
        part.arrived = self.arrived
        part.terms = [term.narrow(term.array.ndim - 1, slice(start, stop)) for term in self.terms]
        return part

    def step(self, bit):
        if not self.swap.by_hand:
            return self
        left = sorted((other for other in self.terms[0].axes if other != bit), reverse=True)
        far = add_all([term.narrow(term.axes[bit], 1).value() for term in self.terms]).astype(BF)
        self.arrived = self.swap.data_swap(far, bit)
        self.terms = [term.narrow(term.axes[bit], 0) for term in self.terms]
        axes = {other: at for at, other in enumerate(left)}
        self.terms.append(Term(self.arrived, [slice(None)] * self.arrived.ndim, axes))
        return self

    def total(self):
        return add_all([term.value() for term in self.terms])


def wait_all(*items):
    arrays = lax.optimization_barrier([[term.array for term in item.terms] for item in items])
    for item, values in zip(items, arrays, strict=True):
        for term, value in zip(item.terms, values, strict=True):
            term.array = value


def per_device(
    h_in, g_in, seg_ids, target_flags, perm_order, w_query, w_key, w_value, w_out, w_rel, attn_bias, seg_embed,
    norm_gain, norm_bias, w_up, b_up, w_down, b_down, d_h_out, d_g_out,
):
    seq_count, length, width = h_in.shape
    assert seq_count == 1
    swap = Exchange(width)
    parts, shards = swap.blocks, swap.tensor
    by_hand = swap.by_hand
    dp_at, tensor_at = lax.axis_index("dp"), lax.axis_index("tensor")
    own_part = width // shards
    rel_host = rel_table(length, width)
    rel, rev = jnp.asarray(rel_host), jnp.asarray(np.ascontiguousarray(rel_host[::-1]))
    h, g = h_in[0], g_in[0]
    up, down = w_up[0], w_down[0]
    bias, table = attn_bias.reshape(1, -1), seg_embed.reshape(1, -1)
    gains, shifts = norm_gain.reshape(1, -1), norm_bias.reshape(1, -1)

    mine_up, mine_down = share_slices(parts, up, down, b_up)
    rows = mine_up.shape[0]
    share_up, share_down = Share(swap, rows, 2), Share(swap, rows, 4)
    share_up.fetch(mine_up)
    q, key, value, relkey, mask, half, att_one, relrev, prob_one, left_x, left_rev = attention_first(
        parts, h, g, seg_ids, target_flags, perm_order, w_query[0], w_key[0], w_value[0], w_rel[0], rel, rev, bias, table, ()
    )
    (mine_down, share_up.raw), _ = lax.optimization_barrier(((mine_down, share_up.raw), half))
    share_down.fetch(mine_down)
    share_up.spread(())
    resid_one, mid, prob_two, att, left_att = attention_second(
        parts, w_out[0], h, g, q, key, value, relkey, mask, half, att_one, bias, table, gains, shifts, [share_up.found[0][1]]
    )
    share_up.cross()
    share_down.spread([mid])
    act_own, slope_own = feed_up_own(mid, up, b_up, [share_down.found[0][1]] + [found for _, found in share_up.found])
    act_rest, slope_rest, up_rest = feed_up(
        shards, mid, rows, share_down.raw, share_up.finish(), [found for _, found in share_down.found]
    )
    share_down.cross()
    out_h, out_g, dresid_two, dbranch, keep_down, send_down, vec_two, down_rest = feed_down(
        parts, shards, down, act_own, act_rest, resid_one, b_down, gains, shifts, d_h_out[0], d_g_out[0],
        share_down.finish(), (),
    )

    hidden = shards * width
    sum_down = Scatter(swap, keep_down, send_down)
    core_down = sum_down.arrived
    dpre, keep_up, send_up, dbias_up = feed_back_up(parts, shards, down, down_rest, dbranch, mid, slope_own, slope_rest, ())
    sum_up = Scatter(swap, keep_up, send_up)
    core_up = sum_up.arrived

    def halves(item, size):
        return item.columns(0, size // 2), item.columns(size // 2, size)

    def first_step(pair):
        pair[0].step(2)
        pair[1].step(4)
        return [pair[0].arrived, pair[1].arrived]

    def second_step(pair):
        pair[0].step(4)
        pair[1].step(2)
        return [pair[0].arrived, pair[1].arrived]

    down_pair = halves(sum_down, hidden)
    first_down = first_step(down_pair)
    dproj, dresid_one, vec_one = feed_back_mid(shards, up, up_rest, dpre, dresid_two, resid_one, gains, [core_down])
    up_pair = halves(sum_up, hidden)
    first_up = first_step(up_pair)
    common = (w_out[0], dproj, q, att, key, value, prob_one, prob_two, relrev, half, left_x, left_rev)
    dq_early, dkey_early, dvalue_early, vec_early, keep_early, send_early = attention_back(
        "attention_back_early", EARLY_PAIRS, *common, left_att, bias, table, [core_up]
    )
    second_down = second_step(down_pair)
    sum_early = Scatter(swap, keep_early, send_early)
    dq_last, dkey_last, dvalue_last, vec_last, keep_last, send_last = attention_back(
        "attention_back_last", LAST_PAIRS, *common, None, bias, table, first_down
    )
    sum_last = Scatter(swap, keep_last, send_last)
    early_pair = halves(sum_early, keep_early.shape[1])
    first_step(early_pair)
    second_step(up_pair)

    def over_tensor(pick):
        total = pick(0)
        for bits in range(1, shards):
            total += swap.tensor_swap(pick(bits).astype(BF), bits).astype(F32)
        return total

    def feed_part(item, start):
        part = Scatter(swap)
        part.arrived = item.arrived
        part.terms = []
        for term in item.terms:
            axis = term.array.ndim - 1
            base = term.take[axis].start or 0
            part.terms.append(term.narrow(axis, slice(base + start, base + start + width)))
        return part.total()

    def feed_sum(pair):
        per = shards // 2
        return over_tensor(lambda bits: feed_part(pair[bits // per], bits % per * width))

    d_down = feed_sum(down_pair).T
    wait_all(*early_pair, sum_last)
    last_pair = halves(sum_last, keep_last.shape[1])
    first_step(last_pair)
    second_step(early_pair)
    d_up = feed_sum(up_pair)

    size_early, size_last = len(EARLY_PAIRS) * LANES, len(LAST_PAIRS) * LANES
    own_early, own_last = size_early // shards, size_last // shards

    def regroup(pair, slots):
        total = jnp.concatenate([pair[0].total().astype(BF), pair[1].total().astype(BF)], axis=1)
        groups = []
        for shard in range(shards):
            at, found = 0, []
            for size in slots:
                part = size // shards
                found.append(total[:, at + shard * part : at + (shard + 1) * part])
                at += size
            groups.append(jnp.concatenate(found, axis=1))
        return jnp.stack(groups)

    def picked(stacked):
        return lambda bits: lax.dynamic_index_in_dim(stacked, tensor_at ^ bits, 0, keepdims=False).astype(F32)

    d_early = over_tensor(picked(regroup(early_pair, [size_early] * 4 + [width])))
    second_step(last_pair)
    d_last = over_tensor(picked(regroup(last_pair, [size_last] * 4)))

    def joined(slot):
        early = d_early[:, slot * own_early : (slot + 1) * own_early]
        last = d_last[:, slot * own_last : (slot + 1) * own_last]
        return jnp.where(tensor_at % 2 == 0, jnp.concatenate([early, last], axis=1), jnp.concatenate([last, early], axis=1))

    d_out = d_early[:, 4 * own_early :]

    late = (dq_early, dq_last, dkey_early, dkey_last, dvalue_early, dvalue_last, vec_early, vec_last)
    late, _ = lax.optimization_barrier((late, last_pair[0].arrived))
    dq_early, dq_last, dkey_early, dkey_last, dvalue_early, dvalue_last, vec_early, vec_last = late

    def back_rows(early, last, weight, dims):
        total = 0.0
        for value, pairs in ((early, EARLY_PAIRS), (last, LAST_PAIRS)):
            part = jnp.concatenate([weight[:, pair * LANES : (pair + 1) * LANES] for pair in pairs], axis=1)
            total += lax.dot_general(value, part, ((dims, (1,)), ((), ())), preferred_element_type=F32)
        return total

    low_q = back_rows(dq_early, dq_last, w_query[0], (1,))
    grad_h = (
        dresid_one[:length]
        + low_q[:length]
        + back_rows(dkey_early, dkey_last, w_key[0], (0,))
        + back_rows(dvalue_early, dvalue_last, w_value[0], (0,))
    )
    grad_g = dresid_one[length:] + low_q[length:]
    size = (10 + shards) * width
    block = pack_vectors(shards, vec_early, vec_last, vec_one, vec_two, dbias_up, 10 + shards, ())
    bit = 1
    while bit < swap.data:
        block = block + swap.data_swap(block, bit)
        bit *= 2
    bit = 1
    while bit < shards:
        block = block + swap.tensor_swap(block, bit)
        bit *= 2
    own = size // (swap.data * shards)
    d_vectors = lax.dynamic_slice_in_dim(block.reshape(-1), (dp_at * shards + tensor_at) * own, own, 0)

    return (
        out_h[None], out_g[None], grad_h[None], grad_g[None],
        joined(0)[None], joined(1)[None], joined(2)[None], d_out[None], joined(3)[None],
        d_up[None], d_down[None], d_vectors[None],
    )


def solution(mesh):
    every = P(AXES, None, None)
    rows = P(AXES, None)
    in_specs = (
        every, every, rows, rows, rows, P(), P(), P(), P(), P(), P(), P(), P(), P(),
        P(None, None, "tensor"), P(None, "tensor"), P(None, "tensor", None), P(), every, every,
    )
    grads = P(None, "dp", "tensor")
    out_specs = (
        every, every, every, every, grads, grads, grads, grads, grads, grads,
        P(None, "tensor", "dp"), P(None, AXES),
    )
    return jax.shard_map(per_device, mesh=mesh, in_specs=in_specs, out_specs=out_specs, check_vma=False)
```

```python
import functools
import math

import jax
import jax.numpy as jnp
import numpy as np
from jax import lax
from jax.experimental import pallas as pl
from jax.experimental.pallas import tpu as pltpu
from jax.sharding import PartitionSpec as P

HEADS = 12
HEAD_DIM = 64
LANES = 128
PAIRS = HEADS // 2
NEGATIVE = -1e30
EPSILON = 1e-06
AXES = ("dp", "tensor")
BF = jnp.bfloat16
F32 = jnp.float32
FIRST_PAIRS = 4
VMEM_MIB = {
    "share_slices": 60, "project": 50, "attention_first": 12, "attention_second": 14, "feed_up_own": 6, "feed_up": 14, "feed_down": 22,
    "feed_back_up": 16, "feed_back_mid": 10, "attention_back_first": 18, "attention_back": 26, "input_grads": 14, "pack_rows": 2,
    "combine": 12, "combine_late": 12, "combine_last": 60, "regroup": 8,
}


def rel_table(length, model_width):
    position = (length - np.arange(2 * length)).astype(np.float32)
    frequency = np.float32(1.0) / np.float32(10000.0) ** (
        np.arange(0, model_width, 2).astype(np.float32) / np.float32(model_width)
    )
    angles = position[:, None] * frequency[None, :]
    return np.concatenate([np.sin(angles), np.cos(angles)], axis=1).astype(BF)


class Late:
    def __init__(self, source, target, sem):
        self.target, self.waiting = target, True
        self.copy = pltpu.make_async_copy(source, target, sem)
        self.copy.start()

    def get(self):
        if self.waiting:
            self.copy.wait()
            self.waiting = False
        return self.target


class Early:
    def __init__(self, ref, target, sems):
        self.ref, self.target, self.sems, self.copies = ref, target, sems, []

    def send(self, *where):
        source, target = (self.ref.at[where], self.target.at[where]) if where else (self.ref, self.target)
        copy = pltpu.make_async_copy(source, target, self.sems.at[len(self.copies)])
        copy.start()
        self.copies.append(copy)


SENDS = 16


def call(kernel, outs, ins, deps, scratch, name, flops):
    deps = tuple(deps)
    spaces = {"s": pltpu.SMEM, "v": pltpu.VMEM, "h": pl.ANY, "l": pltpu.HBM, "e": pltpu.HBM, "b": pltpu.HBM}
    late = [value for kind, value in ins if kind == "l"]
    early = [(shape, dtype) for kind, shape, dtype in outs if kind == "e"]
    more = [pltpu.VMEM(value.shape, value.dtype) for value in late] + [pltpu.VMEM(*spec) for spec in early]
    if late:
        more.append(pltpu.SemaphoreType.DMA((len(late),)))
    if early:
        more.append(pltpu.SemaphoreType.DMA((len(early), SENDS)))
    first_out = len(ins) + len(deps)
    first_scratch = first_out + len(outs)

    def wrapped(*refs):
        own = refs[first_scratch + len(scratch) :]
        late_refs, early_refs = own[: len(late)], own[len(late) : len(late) + len(early)]
        sems = list(own[len(late) + len(early) :])
        late_sem = sems.pop(0) if late else None
        early_sem = sems.pop(0) if early else None
        given, at = [], 0
        for (kind, _), ref in zip(ins, refs[: len(ins)], strict=True):
            if kind == "l":
                ref = Late(ref, late_refs[at], late_sem.at[at])
                at += 1
            given.append(ref)
        made, at = [], 0
        for (kind, _, _), ref in zip(outs, refs[first_out:first_scratch], strict=True):
            if kind == "e":
                ref = Early(early_refs[at], ref, early_sem.at[at])
                at += 1
            made.append(ref)
        kernel(*given, *made, *refs[first_scratch : first_scratch + len(scratch)])
        for item in given:
            if isinstance(item, Late):
                item.get()
        for item in made:
            if isinstance(item, Early):
                for copy in item.copies:
                    copy.wait()

    return pl.pallas_call(
        wrapped,
        out_shape=[jax.ShapeDtypeStruct(shape, dtype) for _, shape, dtype in outs],
        in_specs=[pl.BlockSpec(memory_space=spaces[kind]) for kind, _ in ins]
        + [pl.BlockSpec(memory_space=pl.ANY)] * len(deps),
        out_specs=[pl.BlockSpec(memory_space=spaces[kind]) for kind, _, _ in outs],
        scratch_shapes=list(scratch) + more,
        compiler_params=pltpu.CompilerParams(vmem_limit_bytes=VMEM_MIB[name] * 1024 * 1024),
        cost_estimate=pl.CostEstimate(flops=flops * 100, bytes_accessed=flops // 1000, transcendentals=0),
        name=name,
    )(*[value for _, value in ins], *deps)


def nn(left, right):
    return lax.dot_general(left, right, (((1,), (0,)), ((), ())), preferred_element_type=F32)


def nt(left, right):
    return lax.dot_general(left, right, (((1,), (1,)), ((), ())), preferred_element_type=F32)


def tn(left, right):
    return lax.dot_general(left, right, (((0,), (0,)), ((), ())), preferred_element_type=F32)


def lane_index(rows):
    return lax.broadcasted_iota(jnp.int32, (rows, LANES), 1)


def pair_lanes(pair):
    return pl.ds(pl.multiple_of(pair * LANES, LANES), LANES)


def row_lanes(row, pair, width):
    return pl.ds(pl.multiple_of(row * width + pair * LANES, LANES), LANES)


def norm_stats(source):
    mean = jnp.mean(source, axis=-1, keepdims=True)
    centered = source - mean
    variance = jnp.mean(centered * centered, axis=-1, keepdims=True)
    rstd = lax.rsqrt(variance + EPSILON)
    return centered * rstd, rstd


def norm_back(grad, xhat, rstd, gain):
    dxhat = grad * gain
    mean_one = jnp.mean(dxhat, axis=-1, keepdims=True)
    mean_two = jnp.mean(dxhat * xhat, axis=-1, keepdims=True)
    return rstd * (dxhat - mean_one - xhat * mean_two)


def seg_coefficients(half_wide, lane):
    return jnp.where(lane % HEAD_DIM == 0, half_wide, 1.0 - 2.0 * half_wide)


def seg_keys(half_wide, lane):
    place = lane % HEAD_DIM
    return jnp.where(place == 0, 1.0, jnp.where(place == 1, half_wide, 0.0))


def seg_table(seg_ref, pair, width):
    row = lax.broadcasted_iota(jnp.int32, (LANES, LANES), 0)
    lane = lax.broadcasted_iota(jnp.int32, (LANES, LANES), 1)
    one = jnp.broadcast_to(seg_ref[0:1, pair_lanes(pair)], (LANES, LANES)).T
    two = jnp.broadcast_to(seg_ref[0:1, row_lanes(1, pair, width)], (LANES, LANES)).T
    base = jnp.where(row < HEAD_DIM, HEAD_DIM, 0)
    at_one = lane == base
    at_two = at_one | (lane == base + 1)
    return jnp.concatenate([jnp.where(at_one, one, 0.0), jnp.where(at_two, two - one, 0.0)], axis=1).astype(BF)


def attend_pair(pair, first, q_ref, key_ref, value_ref, relkey_ref, mask_ref, half_ref, bias_ref, seg_ref, prob_ref, att_ref):
    length, width = key_ref.shape
    block = length // 2
    lanes = pair_lanes(pair)
    lane_q = lane_index(2 * length)
    lane_k = lane_index(length)
    low_q = lane_q < HEAD_DIM
    low_k = lane_k < HEAD_DIM
    half_w = half_ref[...]
    scale = 1.0 / math.sqrt(HEAD_DIM)
    query = q_ref[:, lanes]
    word = ((query + bias_ref[0:1, lanes]) * scale).astype(BF)
    relq = ((query + bias_ref[0:1, row_lanes(1, pair, width)]) * scale).astype(BF)
    segq = ((query + bias_ref[0:1, row_lanes(2, pair, width)]) * scale).astype(BF)
    terms = nn(segq, seg_table(seg_ref, pair, width))
    coef = seg_coefficients(jnp.concatenate([half_w, half_w], axis=0), lane_q)
    extra = (terms[:, :LANES] + terms[:, LANES:] * coef).astype(BF)
    key_extra = seg_keys(half_w, lane_k).astype(BF)
    key = key_ref[:, lanes]
    value = value_ref[:, lanes]
    zero = jnp.zeros_like(relq)
    attended = []
    for head in (0, 1):
        if head == 0:
            word_one = jnp.where(low_q, word, extra)
            key_one = jnp.where(low_k, key, key_extra)
            rel_one = jnp.where(low_q, relq, zero)
        else:
            word_one = jnp.where(low_q, extra, word)
            key_one = jnp.where(low_k, key_extra, key)
            rel_one = jnp.where(low_q, zero, relq)
        score = nt(word_one, key_one)
        for part in (0, 1):
            base = block - block * part
            rows_h = slice(block * part, block * part + block)
            rows_g = slice(length + block * part, length + block * part + block)
            rel_rows = jnp.concatenate([rel_one[rows_h], rel_one[rows_g]], axis=0)
            raw = nt(rel_rows, relkey_ref[base : base + 3 * block, lanes])
            for place_at, rows in ((0, rows_h), (1, rows_g)):
                shifted = pltpu.roll(
                    raw[place_at * block : (place_at + 1) * block], 2 * block, 1, stride=1, stride_axis=0
                )[:, :length]
                logits = score[rows] + shifted + mask_ref[rows]
                top = jnp.max(logits, axis=1, keepdims=True)
                power = jnp.exp(logits - top)
                total = jnp.sum(power, axis=1, keepdims=True)
                prob_ref[2 * (pair - first) + head, rows, :] = (power * (1.0 / total)).astype(BF)
        attended.append(nn(prob_ref[2 * (pair - first) + head], value))
    att_ref[:, lanes] = jnp.where(low_q, attended[0], attended[1]).astype(BF)


def project_kernel(
    parts, h_late, g_late, wq_late, wk_late, wv_late, rel_late, wr_late, rev_late,
    seg_row, flag_row, order_row,
    q_ref, key_ref, value_ref, relkey_ref, mask_ref, half_ref, relrev_out, left_x_out, left_rev_out,
    x_ref, raw_ref,
):
    h_ref, g_ref = h_late.get(), g_late.get()
    length, width = h_ref.shape
    x_ref[:length] = h_ref[...]
    x_ref[length:] = g_ref[...]

    def project(left, right_late, target):
        right = right_late.get()
        for col in range(0, width, 256):
            cols = slice(col, col + 256)
            target[:, cols] = nn(left[...], right[:, cols]).astype(target.dtype)

    project(x_ref, wq_late, q_ref)
    project(h_ref, wk_late, key_ref)
    project(h_ref, wv_late, value_ref)
    project(rel_late.get(), wr_late, relkey_ref)

    def wide(row_ref):
        return jnp.broadcast_to(row_ref[...].astype(F32), (length, length))

    row_at = lax.broadcasted_iota(jnp.int32, (length, length), 0)
    col_at = lax.broadcasted_iota(jnp.int32, (length, length), 1)
    seg, order = wide(seg_row), wide(order_row)
    same_doc = seg.T == seg
    start = jnp.min(jnp.where(same_doc, col_at.astype(F32), float(length)), axis=1, keepdims=True)
    in_doc = jnp.sum(jnp.where(same_doc, 1.0, 0.0), axis=1, keepdims=True)
    place = lax.broadcasted_iota(jnp.int32, (length, 1), 0).astype(F32)
    half = jnp.where(2.0 * (place - start) >= in_doc, 1.0, 0.0)
    half_ref[...] = jnp.broadcast_to(half, (length, LANES))
    content = same_doc & ((wide(flag_row) == 0.0) | (order <= order.T))
    mask_ref[:length] = jnp.where(content, 0.0, NEGATIVE)
    mask_ref[length:] = jnp.where(content & (row_at != col_at), 0.0, NEGATIVE)

    project(rev_late.get(), wr_late, relrev_out.ref)
    relrev_out.send()
    turn_rows(lambda col: x_ref[:, col : col + 256], raw_ref.at[0], left_x_out.ref, parts)
    left_x_out.send()
    rev_ref = rev_late.get()
    turn_rows(lambda col: rev_ref[:, col : col + 256], raw_ref.at[1], left_rev_out.ref, parts)
    left_rev_out.send()


def project(parts, h, g, seg, flag, order, wq, wk, wv, wr, rel, rev, deps):
    length, width = h.shape
    two = 2 * length
    outs = [
        ("v", (two, width), F32), ("v", (length, width), BF), ("v", (length, width), BF), ("v", (two, width), BF),
        ("v", (two, length), F32), ("v", (length, LANES), F32), ("e", (two, width), BF), ("e", (width, two), BF),
        ("e", (width, two), BF),
    ]
    ins = [("l", value) for value in (h, g, wq, wk, wv, rel, wr, rev)] + [("v", value) for value in (seg, flag, order)]
    scratch = [pltpu.VMEM((two, width), BF), pltpu.VMEM((2, width, two), BF)]
    return call(functools.partial(project_kernel, parts), outs, ins, deps, scratch, "project", 5 * 10**9)


def attention_first_kernel(
    q_ref, key_ref, value_ref, relkey_ref, mask_ref, half_ref, bias_ref, seg_ref, att_ref, prob_out
):
    def pair_step(pair, carry):
        attend_pair(
            pair, 0, q_ref, key_ref, value_ref, relkey_ref, mask_ref, half_ref, bias_ref, seg_ref, prob_out.ref, att_ref
        )
        return carry

    for first in range(0, FIRST_PAIRS, 2):
        lax.fori_loop(first, first + 2, pair_step, 0)
        prob_out.send(pl.ds(2 * first, 4))


def attention_first(q, key, value, relkey, mask, half, bias, table, deps):
    two, length = mask.shape
    outs = [("v", (two, FIRST_PAIRS * LANES), BF), ("e", (2 * FIRST_PAIRS, two, length), BF)]
    ins = [("v", x) for x in (q, key, value, relkey, mask, half, bias, table)]
    return call(attention_first_kernel, outs, ins, deps, [], "attention_first", 5 * 10**9)


def attention_second_kernel(
    parts, wo_late, h_late, g_late, q_ref, key_ref, value_ref, relkey_ref, mask_ref, half_ref, att_first_ref,
    bias_ref, seg_ref, gain_ref, shift_ref,
    resid_ref, mid_ref, prob_out, att_out, left_att_out,
    raw_ref,
):
    length, width = key_ref.shape
    att_ref = att_out.ref
    att_ref[:, : FIRST_PAIRS * LANES] = att_first_ref[...]

    def pair_step(pair, carry):
        attend_pair(
            pair, FIRST_PAIRS, q_ref, key_ref, value_ref, relkey_ref, mask_ref, half_ref, bias_ref, seg_ref, prob_out.ref, att_ref
        )
        return carry

    for first in range(FIRST_PAIRS, PAIRS, 2):
        lax.fori_loop(first, first + 2, pair_step, 0)
        prob_out.send(pl.ds(2 * (first - FIRST_PAIRS), 4))
    att_out.send()
    wo_ref, h_ref, g_ref = wo_late.get(), h_late.get(), g_late.get()
    for col in range(0, width, 256):
        cols = slice(col, col + 256)
        total = nn(att_ref[...], wo_ref[:, cols])
        resid_ref[:length, cols] = h_ref[:, cols].astype(F32) + total[:length]
        resid_ref[length:, cols] = g_ref[:, cols].astype(F32) + total[length:]
    turn_rows(lambda col: att_ref[:, col : col + 256], raw_ref, left_att_out.ref, parts)
    left_att_out.send()
    for row in range(0, 2 * length, 64):
        xhat, _ = norm_stats(resid_ref[row : row + 64, :])
        mid_ref[row : row + 64, :] = (xhat * gain_ref[0:1, :width] + shift_ref[0:1, :width]).astype(BF)


def attention_second(parts, wo, h, g, q, key, value, relkey, mask, half, att, bias, table, gain, shift, deps):
    length, width = h.shape
    two = 2 * length
    outs = [
        ("v", (two, width), F32), ("v", (two, width), BF), ("e", (HEADS - 2 * FIRST_PAIRS, two, length), BF),
        ("e", (two, width), BF), ("e", (width, two), BF),
    ]
    ins = [("l", value) for value in (wo, h, g)]
    ins += [("v", value) for value in (q, key, value, relkey, mask, half, att, bias, table, gain, shift)]
    return call(
        functools.partial(attention_second_kernel, parts), outs, ins, deps, [pltpu.VMEM((width, two), BF)],
        "attention_second", 10 * 10**9,
    )


def place_rows(raw_ref, out_ref, parts):
    rows = raw_ref.shape[0] // parts
    me = lax.axis_index("dp") if parts > 1 else 0
    order = [low | (rest << 1) for low in (0, 1) for rest in range(parts // 2)] if parts > 1 else [0]
    for at, block in enumerate(order):
        source = pl.multiple_of((me ^ block) * rows, rows)
        out_ref[at * rows : (at + 1) * rows, :] = raw_ref[pl.ds(source, rows), :]


def turn_rows(source, raw_ref, out_ref, parts):
    for col in range(0, raw_ref.shape[0], 256):
        raw_ref[col : col + 256, :] = source(col).astype(F32).T.astype(BF)
    place_rows(raw_ref, out_ref, parts)


def back_pairs(
    pairs, dproj_ref, wo_ref, q_ref, att_ref, key_ref, value_ref, prob_one, prob_two, relrev_ref, half_ref, bias_ref, seg_ref,
    dq_ref, dkey_ref, dvalue_ref, drel_ref, vec_ref, datt_ref,
):
    length, width = key_ref.shape
    block = length // 2
    for at, pair in enumerate(pairs):
        rows = slice(pair * LANES, (pair + 1) * LANES)
        datt_ref[:, at * LANES : (at + 1) * LANES] = nt(dproj_ref[...], wo_ref[rows, :]).astype(BF)

    def pair_step(at, pair):
        lanes = slice(pair * LANES, (pair + 1) * LANES)
        own = slice(at * LANES, (at + 1) * LANES)
        prob_ref, prob_at = (prob_one, 2 * pair) if pair < FIRST_PAIRS else (prob_two, 2 * (pair - FIRST_PAIRS))
        lane_q = lane_index(2 * length)
        lane_k = lane_index(length)
        low_q = lane_q < HEAD_DIM
        low_k = lane_k < HEAD_DIM
        half_w = half_ref[...]
        flip_row = lax.broadcasted_iota(jnp.int32, (length, length), 0)
        flip_col = lax.broadcasted_iota(jnp.int32, (length, length), 1)
        flip = jnp.where(flip_row + flip_col == length - 1, 1.0, 0.0).astype(BF)
        sel_row = lax.broadcasted_iota(jnp.int32, (2 * LANES, LANES), 0) % LANES
        sel_col = lax.broadcasted_iota(jnp.int32, (2 * LANES, LANES), 1)
        select = jnp.where(
            ((sel_row < HEAD_DIM) & ((sel_col == HEAD_DIM) | (sel_col == HEAD_DIM + 1)))
            | ((sel_row >= HEAD_DIM) & (sel_col < 2)),
            1.0,
            0.0,
        ).astype(BF)
        query = q_ref[:, lanes]
        word = query + bias_ref[0:1, lanes]
        relq = query + bias_ref[0:1, row_lanes(1, pair, width)]
        segq = (query + bias_ref[0:1, row_lanes(2, pair, width)]).astype(BF)
        word_t = word.T.astype(BF)
        relq_t = relq.T.astype(BF)
        datt = datt_ref[:, own]
        datt_wide = datt.astype(F32)
        datt_t = datt_wide.T.astype(BF)
        datt_scaled = datt_wide * (1.0 / math.sqrt(HEAD_DIM))
        product = datt_scaled * att_ref[:, lanes].astype(F32)
        product_high = product.astype(BF)
        product_low = (product - product_high.astype(F32)).astype(BF)
        delta = nn(jnp.concatenate([product_high, product_low], axis=1), select)
        delta_high = delta.astype(BF).astype(F32)
        minus = jnp.where(lane_q % HEAD_DIM == 0, -delta_high, delta_high - delta).astype(BF)
        datt_low = datt_scaled.astype(BF)
        key_extra = seg_keys(half_w, lane_k).astype(BF)
        ones_extra = jnp.where(lane_k % HEAD_DIM < 2, 1.0, 0.0).astype(BF)
        key = key_ref[:, lanes]
        value = value_ref[:, lanes]
        dword, drel = [], []
        for head in (0, 1):
            rows_t = slice(HEAD_DIM * head, HEAD_DIM * head + HEAD_DIM)
            if head == 0:
                datt_one = jnp.where(low_q, datt_low, minus)
                value_one = jnp.where(low_k, value, ones_extra)
                key_one = jnp.where(low_k, key, key_extra)
            else:
                datt_one = jnp.where(low_q, minus, datt_low)
                value_one = jnp.where(low_k, ones_extra, value)
                key_one = jnp.where(low_k, key_extra, key)
            prob = prob_ref[prob_at + head]
            dprob = nt(datt_one, value_one)
            dscore = (prob.astype(F32) * dprob).astype(BF)
            dword.append(nn(dscore, key_one))
            rows_out = slice(at * LANES + HEAD_DIM * head, at * LANES + HEAD_DIM * (head + 1))
            dkey_ref[rows_out, :] = nn(word_t[rows_t], dscore).astype(BF)
            dvalue_ref[rows_out, :] = nn(datt_t[rows_t], prob).astype(BF)
            flipped = nn(dscore, flip).astype(BF)
            pad = jnp.zeros((block, block), BF)
            rel_parts, drel_t = [], []
            for part in (0, 1):
                rows_h = slice(block * part, block * part + block)
                rows_g = slice(length + block * part, length + block * part + block)
                draw = jnp.concatenate(
                    [
                        pltpu.roll(jnp.concatenate([flipped[rows], pad], axis=1), 0, 1, stride=1, stride_axis=0)
                        for rows in (rows_h, rows_g)
                    ],
                    axis=0,
                )
                rel_parts.append(nn(draw, relrev_ref[block * part : block * part + 3 * block, lanes]))
                rel_cols = jnp.concatenate([relq_t[rows_t, rows_h], relq_t[rows_t, rows_g]], axis=1)
                drel_t.append(nn(rel_cols, draw))
            drel.append(
                jnp.concatenate(
                    [rel_parts[0][:block], rel_parts[1][:block], rel_parts[0][block:], rel_parts[1][block:]], axis=0
                )
            )
            drel_ref[rows_out, :] = jnp.concatenate(
                [
                    drel_t[0][:, :block],
                    drel_t[0][:, block:] + drel_t[1][:, : 2 * block],
                    drel_t[1][:, 2 * block :],
                ],
                axis=1,
            ).astype(BF)
        extra = jnp.where(low_q, dword[1], dword[0])
        dword_all = jnp.where(low_q, dword[0], dword[1])
        drel_all = jnp.where(low_q, drel[0], drel[1])
        coef = seg_coefficients(jnp.concatenate([half_w, half_w], axis=0), lane_q)
        dterms = jnp.concatenate([extra, extra * coef], axis=1).astype(BF)
        dsegq = nt(dterms, seg_table(seg_ref, pair, width))
        dtable = tn(dterms, segq)
        dq_ref[:, own] = (dword_all + drel_all + dsegq).astype(BF)
        low_one = lane_index(1) < HEAD_DIM
        first = jnp.where(low_one, dtable[HEAD_DIM : HEAD_DIM + 1], dtable[0:1])
        far = LANES + HEAD_DIM
        second = jnp.where(
            low_one, dtable[far : far + 1] + dtable[far + 1 : far + 2], dtable[LANES : LANES + 1] + dtable[LANES + 1 : LANES + 2]
        )
        vec_ref[0:1, own] = jnp.sum(dword_all, axis=0, keepdims=True)
        vec_ref[1:2, own] = jnp.sum(drel_all, axis=0, keepdims=True)
        vec_ref[2:3, own] = jnp.sum(dsegq, axis=0, keepdims=True)
        vec_ref[3:4, own] = first - second
        vec_ref[4:5, own] = second
    for at, pair in enumerate(pairs):
        pair_step(at, pair)


def attention_back_first_kernel(
    pairs, wo_late, dproj_ref, q_ref, att_ref, key_ref, value_ref, prob_one, prob_two, relrev_ref, half_ref, bias_ref, seg_ref,
    dq_ref, dkey_ref, dvalue_ref, drel_ref, vec_ref, datt_ref,
):
    vec_ref[...] = jnp.zeros_like(vec_ref)
    back_pairs(
        pairs, dproj_ref, wo_late.get(), q_ref, att_ref, key_ref, value_ref, prob_one, prob_two, relrev_ref, half_ref, bias_ref,
        seg_ref, dq_ref, dkey_ref, dvalue_ref, drel_ref, vec_ref, datt_ref,
    )


def attention_back_first(pairs, common, bias, table, deps):
    two, width = common[1].shape
    length, size = two // 2, len(pairs) * LANES
    outs = [
        ("v", (two, size), BF), ("v", (size, length), BF), ("v", (size, length), BF), ("v", (size, two), BF), ("v", (8, size), F32),
    ]
    ins = [("l", common[0])] + [("v", x) for x in (*common[1:], bias, table)]
    kernel = functools.partial(attention_back_first_kernel, pairs)
    return call(kernel, outs, ins, deps, [pltpu.VMEM((two, size), BF)], "attention_back_first", 12 * 10**9)


def attention_back_kernel(
    pairs, wo_late, dproj_ref, q_ref, att_ref, key_ref, value_ref, prob_one, prob_two, relrev_ref, half_ref, bias_ref, seg_ref,
    left_x_ref, left_rev_ref, left_att_ref, dq_one, dkey_one, dvalue_one, drel_one, vec_one, norm_one, norm_two, hidden_ref,
    dq_ref, dkey_ref, dvalue_ref, keep_out, send_out, datt_ref, drel_ref, vec_ref, packed_ref,
):
    length, width = key_ref.shape
    split = width // 2
    size = dq_one.shape[1]
    dq_ref[:, :size], dkey_ref[:size], dvalue_ref[:size], drel_ref[:size] = dq_one[...], dkey_one[...], dvalue_one[...], drel_one[...]
    vec_ref[...] = jnp.zeros_like(vec_ref)
    vec_ref[:, :size] = vec_one[...]
    back_pairs(
        pairs, dproj_ref, wo_late.get(), q_ref, att_ref, key_ref, value_ref, prob_one, prob_two, relrev_ref, half_ref, bias_ref,
        seg_ref, dq_ref.at[:, size:], dkey_ref.at[size:], dvalue_ref.at[size:], drel_ref.at[size:], vec_ref.at[:, size:], datt_ref,
    )
    shards = hidden_ref.shape[1] // width
    packed_ref[...] = jnp.zeros_like(packed_ref)
    packed_ref[0:5, :] = vec_ref[0:5, :]
    packed_ref[5:6, :] = norm_one[0:1, :]
    packed_ref[6:7, :] = norm_two[0:1, :]
    packed_ref[7:8, :] = norm_one[1:2, :]
    packed_ref[8:10, :] = norm_two[1:3, :]
    for shard in range(shards):
        place = 10 + (lax.axis_index("tensor") ^ shard)
        packed_ref[pl.ds(place, 1), :] = hidden_ref[0:1, shard * width : (shard + 1) * width]
    packed = packed_ref[...].astype(BF)
    for out in (send_out, keep_out):
        out.ref[split:, :width] = packed
        out.ref[split:, width:] = jnp.zeros((16, 4 * width), BF)
        out.send(pl.ds(split, 16))
    todo = [
        (left_x_ref[...], dq_ref, nn), (left_x_ref[:, :length], dkey_ref, nt), (left_x_ref[:, :length], dvalue_ref, nt),
        (left_att_ref[...], dproj_ref, nn), (left_rev_ref[...], drel_ref, nt),
    ]
    at = 0
    for left, right, dot in todo:
        count = right.shape[1] if dot is nn else right.shape[0]
        for col in range(0, count, 256):
            cols = slice(col, col + 256)
            piece = dot(left, right[:, cols] if dot is nn else right[cols, :]).astype(BF)
            keep_out.ref[:split, at + col : at + col + 256] = piece[:split]
            send_out.ref[:split, at + col : at + col + 256] = piece[split:]
        done = pl.ds(at, count)
        send_out.send(pl.ds(0, split), done)
        keep_out.send(pl.ds(0, split), done)
        at += count


def attention_back(pairs, common, lefts, first, vectors, bias, table, deps):
    two, width = common[1].shape
    length, size = two // 2, len(pairs) * LANES
    outs = [
        ("v", (two, width), BF), ("v", (width, length), BF), ("v", (width, length), BF),
        ("e", (width // 2 + 16, 5 * width), BF), ("e", (width // 2 + 16, 5 * width), BF),
    ]
    ins = [("l", common[0])] + [("v", x) for x in (*common[1:], bias, table, *lefts, *first, *vectors)]
    scratch = [
        pltpu.VMEM((two, size), BF), pltpu.VMEM((width, two), BF), pltpu.VMEM((8, width), F32), pltpu.VMEM((16, width), F32),
    ]
    return call(functools.partial(attention_back_kernel, pairs), outs, ins, deps, scratch, "attention_back", 12 * 10**9)


def input_grads_kernel(wq_late, wk_late, wv_late, dq_ref, dkey_ref, dvalue_ref, dresid_ref, grad_h, grad_g, sum_ref):
    length, width = grad_h.ref.shape
    wq_ref = wq_late.get()
    for col in range(0, width, 256):
        cols = slice(col, col + 256)
        low = nt(dq_ref[...], wq_ref[cols, :])
        sum_ref[:, cols] = dresid_ref[:length, cols] + low[:length]
        grad_g.ref[:, cols] = dresid_ref[length:, cols] + low[length:]
    grad_g.send()
    dkey, dvalue = dkey_ref[...].astype(F32).T.astype(BF), dvalue_ref[...].astype(F32).T.astype(BF)
    wk_ref, wv_ref = wk_late.get(), wv_late.get()
    for col in range(0, width, 256):
        cols = slice(col, col + 256)
        grad_h.ref[:, cols] = sum_ref[:, cols] + nt(dkey, wk_ref[cols, :]) + nt(dvalue, wv_ref[cols, :])
    grad_h.send()


def input_grads(wq, wk, wv, dq, dkey, dvalue, dresid, deps):
    two, width = dresid.shape
    outs = [("e", (two // 2, width), F32), ("e", (two // 2, width), F32)]
    ins = [("l", wq), ("l", wk), ("l", wv), ("v", dq), ("v", dkey), ("v", dvalue), ("v", dresid)]
    scratch = [pltpu.VMEM((two // 2, width), F32)]
    return call(input_grads_kernel, outs, ins, deps, scratch, "input_grads", 10**9)


def share_kernel(parts, up_hbm, down_hbm, bias_ref, out_ref, sem):
    rows = up_hbm.shape[0] // parts
    start = pl.multiple_of(lax.axis_index("dp") * rows, rows) if parts > 1 else 0
    one = pltpu.make_async_copy(up_hbm.at[pl.ds(start, rows)], out_ref.at[pl.ds(0, rows)], sem.at[0])
    two = pltpu.make_async_copy(down_hbm.at[pl.ds(start, rows)], out_ref.at[pl.ds(rows, rows)], sem.at[1])
    one.start()
    two.start()
    out_ref[2 * rows :, :] = jnp.broadcast_to(bias_ref[...], (16, bias_ref.shape[1]))
    one.wait()
    two.wait()


def share_slices(parts, up, down, bias):
    rows, width = up.shape[0] // parts, up.shape[1]
    outs = [("v", (2 * rows + 16, width), BF)]
    ins = [("b", up), ("b", down), ("v", bias)]
    return call(functools.partial(share_kernel, parts), outs, ins, (), [pltpu.SemaphoreType.DMA((2,))], "share_slices", 10**7)[0]


def start_pieces(pieces, piece_refs, target_ref, sem):
    copies = {}
    for count, ((shard, block, rows, source_at), source) in enumerate(zip(pieces, piece_refs, strict=True)):
        where = 0
        if rows < target_ref.shape[1]:
            where = pl.multiple_of((lax.axis_index("dp") ^ block) * rows, rows)
        copy = pltpu.make_async_copy(
            source.at[pl.ds(source_at, rows)], target_ref.at[shard, pl.ds(where, rows)], sem.at[count]
        )
        copy.start()
        copies.setdefault(shard, []).append(copy)
    return copies


def gelu_parts(pre):
    root = math.sqrt(2.0 / math.pi)
    square = pre * pre
    bend = jnp.tanh(root * pre * (1.0 + 0.044715 * square))
    upper = 0.5 + 0.5 * bend
    slope = upper + (0.5 * root) * pre * (1.0 - bend * bend) * (1.0 + (3 * 0.044715) * square)
    return (pre * upper).astype(BF), slope.astype(BF)


def feed_up_own_kernel(mid_ref, up_late, bias_ref, act_ref, slope_ref):
    width = mid_ref.shape[1]
    up_ref = up_late.get()
    for col in range(0, width, 256):
        cols = slice(col, col + 256)
        bias = bias_ref[0:1, cols].astype(F32)
        act_ref[:, cols], slope_ref[:, cols] = gelu_parts(nn(mid_ref[...], up_ref[:, cols]) + bias)


def feed_up_own(mid, up, bias, deps):
    outs = [("v", mid.shape, BF), ("v", mid.shape, BF)]
    return call(feed_up_own_kernel, outs, [("v", mid), ("l", up), ("v", bias)], deps, [], "feed_up_own", 3 * 10**9)


def feed_up_kernel(shards, pieces, rows, mid_ref, *refs):
    bias_refs, piece_refs = refs[: shards - 1], refs[shards - 1 : shards - 1 + len(pieces)]
    act_ref, slope_ref, up_ref, bias_ref, in_sem, bias_sem = refs[shards - 1 + len(pieces) :]
    width = mid_ref.shape[1]
    copies = start_pieces(pieces, piece_refs, up_ref, in_sem)
    biases = [
        pltpu.make_async_copy(ref.at[pl.ds(rows, 16)], bias_ref.at[shard], bias_sem.at[shard])
        for shard, ref in enumerate(bias_refs)
    ]
    for copy in biases:
        copy.start()
    for copy in biases:
        copy.wait()
    for shard in range(shards - 1):
        for copy in copies[shard]:
            copy.wait()
        for col in range(0, width, 256):
            cols = slice(shard * width + col, shard * width + col + 256)
            pre = nn(mid_ref[...], up_ref[shard, :, col : col + 256])
            act_ref[:, cols], slope_ref[:, cols] = gelu_parts(
                pre + bias_ref[shard, 0:1, col : col + 256].astype(F32)
            )


def feed_up(shards, mid, rows, biases, pieces, deps):
    rows_all, width = mid.shape
    hidden = (shards - 1) * width
    names = [entry[:-1] for entry in pieces]
    outs = [("v", (rows_all, hidden), BF), ("v", (rows_all, hidden), BF), ("v", (shards - 1, width, width), BF)]
    ins = [("v", mid)] + [("h", value) for value in biases] + [("h", entry[-1]) for entry in pieces]
    scratch = [
        pltpu.VMEM((shards - 1, 16, width), BF), pltpu.SemaphoreType.DMA((len(names),)), pltpu.SemaphoreType.DMA((shards - 1,)),
    ]
    return call(functools.partial(feed_up_kernel, shards, names, rows), outs, ins, deps, scratch, "feed_up", 6 * 10**9)


def feed_down_kernel(parts, shards, pieces, own_late, dh_late, dg_late, act_own, resid_ref, act_rest, *refs):
    down_bias, gain_ref, shift_ref = refs[:3]
    piece_refs = refs[3 : 3 + len(pieces)]
    out_h, out_g, dresid_ref, dbranch_ref, keep_out, send_out, vec_ref, down_ref, raw_ref, left_ref, in_sem = refs[3 + len(pieces) :]
    rows_all, width = resid_ref.shape
    length = rows_all // 2
    split = width // 2
    copies = start_pieces(pieces, piece_refs, down_ref, in_sem)
    own_down = own_late.get()
    for col in range(0, width, 256):
        cols = slice(col, col + 256)
        dresid_ref[:, cols] = nn(act_own[...], own_down[:, cols])
    for shard in range(shards - 1):
        for copy in copies[shard]:
            copy.wait()
    down_all = down_ref.reshape((shards - 1) * width, width)
    for col in range(0, width, 256):
        cols = slice(col, col + 256)
        dresid_ref[:, cols] += nn(act_rest[...], down_all[:, cols])
    gain_one, gain_two = gain_ref[0:1, :width], gain_ref[0:1, width:]
    shift_one, shift_two = shift_ref[0:1, :width], shift_ref[0:1, width:]
    step_rows = 32
    sums = [jnp.zeros((step_rows, width), F32)] * 3
    for row in range(0, rows_all, step_rows):
        rows = slice(row, row + step_rows)
        grad_ref = dh_late.get() if row < length else dg_late.get()
        near = row % length
        xhat_one, _ = norm_stats(resid_ref[rows, :])
        middle = xhat_one * gain_one + shift_one
        xhat, rstd = norm_stats(middle + dresid_ref[rows, :] + down_bias[...])
        out = out_h if row < length else out_g
        out.ref[near : near + step_rows, :] = (xhat * gain_two + shift_two).astype(BF)
        grad = grad_ref[near : near + step_rows, :].astype(F32)
        dresid = norm_back(grad, xhat, rstd, gain_two)
        dresid_ref[rows, :] = dresid
        dbranch = dresid.astype(BF)
        dbranch_ref[rows, :] = dbranch
        sums = [sums[0] + grad * xhat, sums[1] + grad, sums[2] + dbranch.astype(F32)]
    vec_ref[...] = jnp.zeros_like(vec_ref)
    for at, total in enumerate(sums):
        vec_ref[at : at + 1, :] = jnp.sum(total, axis=0, keepdims=True)
    out_h.send()
    out_g.send()
    turn_rows(lambda col: dbranch_ref[:, col : col + 256], raw_ref, left_ref, parts)
    for source, count, offset in ((act_own, 1, 0), (act_rest, shards - 1, width)):
        for col in range(0, count * width, 256):
            piece = nn(left_ref[...], source[:, col : col + 256]).astype(BF)
            cols = slice(col + offset, col + offset + 256)
            keep_out.ref[:, cols] = piece[:split]
            send_out.ref[:, cols] = piece[split:]
            if (col + 256) % width == 0:
                done = pl.ds(col + offset + 256 - width, width)
                send_out.send(slice(None), done)
                keep_out.send(slice(None), done)


def feed_down(parts, shards, own_down, act_own, act_rest, resid_one, down_bias, gains, shifts, dh, dg, pieces, deps):
    rows_all, width = resid_one.shape
    hidden = shards * width
    names = [entry[:-1] for entry in pieces]
    outs = [
        ("e", dh.shape, BF), ("e", dg.shape, BF), ("v", (rows_all, width), F32), ("v", (rows_all, width), BF),
        ("e", (width // 2, hidden), BF), ("e", (width // 2, hidden), BF), ("v", (8, width), F32), ("v", (shards - 1, width, width), BF),
    ]
    ins = [("l", value) for value in (own_down, dh, dg)]
    ins += [("v", value) for value in (act_own, resid_one, act_rest, down_bias, gains, shifts)] + [("h", entry[-1]) for entry in pieces]
    scratch = [pltpu.VMEM((width, rows_all), BF), pltpu.VMEM((width, rows_all), BF), pltpu.SemaphoreType.DMA((len(names),))]
    return call(functools.partial(feed_down_kernel, parts, shards, names), outs, ins, deps, scratch, "feed_down", 8 * 10**9)


def feed_back_up_kernel(
    parts, shards, own_late, mid_ref, dbranch_ref, down_ref, slope_own, slope_rest,
    dpre_ref, keep_out, send_out, dbias_ref, raw_ref, left_ref,
):
    rows_all, width = mid_ref.shape
    split = width // 2
    turn_rows(lambda col: mid_ref[:, col : col + 256], raw_ref, left_ref, parts)
    own_down = own_late.get()
    for shard in range(shards):
        for col in range(0, width, 256):
            cols = slice(shard * width + col, shard * width + col + 256)
            if shard:
                near = (shard - 1) * width + col
                weight, slope = down_ref[shard - 1, col : col + 256, :], slope_rest[:, near : near + 256]
            else:
                weight, slope = own_down[col : col + 256, :], slope_own[:, col : col + 256]
            dpre = (nt(dbranch_ref[...], weight) * slope.astype(F32)).astype(BF)
            dpre_ref[:, cols] = dpre
            dbias_ref[:, cols] = jnp.sum(dpre.astype(F32), axis=0, keepdims=True)
            piece = nn(left_ref[...], dpre).astype(BF)
            keep_out.ref[:, cols] = piece[:split]
            send_out.ref[:, cols] = piece[split:]
        done = pl.ds(shard * width, width)
        send_out.send(slice(None), done)
        keep_out.send(slice(None), done)


def feed_back_up(parts, shards, own_down, down_rest, dbranch, mid, slope_own, slope_rest, deps):
    rows_all, width = mid.shape
    hidden = shards * width
    outs = [("v", (rows_all, hidden), BF), ("e", (width // 2, hidden), BF), ("e", (width // 2, hidden), BF), ("v", (1, hidden), F32)]
    ins = [("l", own_down)] + [("v", value) for value in (mid, dbranch, down_rest, slope_own, slope_rest)]
    scratch = [pltpu.VMEM((width, rows_all), BF), pltpu.VMEM((width, rows_all), BF)]
    return call(functools.partial(feed_back_up_kernel, parts, shards), outs, ins, deps, scratch, "feed_back_up", 8 * 10**9)


def feed_back_mid_kernel(shards, own_late, dpre_ref, up_ref, dresid_ref, resid_ref, gain_ref, dproj_ref, dresid_one_ref, vec_ref):
    rows_all, width = dresid_one_ref.shape
    own_up = own_late.get()
    for col in range(0, width, 256):
        cols = slice(col, col + 256)
        total = nt(dpre_ref[:, :width], own_up[cols, :])
        for shard in range(1, shards):
            total += nt(dpre_ref[:, shard * width : (shard + 1) * width], up_ref[shard - 1, cols, :])
        dresid_one_ref[:, cols] = total
    gain_one = gain_ref[0:1, :width]
    step_rows = 32
    sums = [jnp.zeros((step_rows, width), F32)] * 2
    for row in range(0, rows_all, step_rows):
        rows = slice(row, row + step_rows)
        xhat, rstd = norm_stats(resid_ref[rows, :])
        grad = dresid_ref[rows, :] + dresid_one_ref[rows, :]
        dresid = norm_back(grad, xhat, rstd, gain_one)
        dresid_one_ref[rows, :] = dresid
        dproj_ref[rows, :] = dresid.astype(BF)
        sums = [sums[0] + grad * xhat, sums[1] + grad]
    vec_ref[...] = jnp.zeros_like(vec_ref)
    for at, total in enumerate(sums):
        vec_ref[at : at + 1, :] = jnp.sum(total, axis=0, keepdims=True)


def feed_back_mid(shards, own_up, up_rest, dpre, dresid, resid_one, gains, deps):
    rows_all, width = resid_one.shape
    outs = [("v", (rows_all, width), BF), ("v", (rows_all, width), F32), ("v", (8, width), F32)]
    ins = [("l", own_up)] + [("v", value) for value in (dpre, up_rest, dresid, resid_one, gains)]
    return call(functools.partial(feed_back_mid_kernel, shards), outs, ins, deps, [], "feed_back_mid", 5 * 10**9)


def pack_rows_kernel(count, rows, *refs):
    one_ref, two_ref, sem = refs[count:]
    copies = [
        pltpu.make_async_copy(ref.at[pl.ds(half * rows, rows)], out.at[pl.ds(at * rows, rows)], sem.at[half, at])
        for half, out in enumerate((one_ref, two_ref))
        for at, ref in enumerate(refs[:count])
    ]
    for copy in copies:
        copy.start()
    for copy in copies:
        copy.wait()


def pack_rows(arrays, rows, deps):
    outs = [("v", (len(arrays) * rows, arrays[0].shape[1]), BF)] * 2
    scratch = [pltpu.SemaphoreType.DMA((2, len(arrays)))]
    kernel = functools.partial(pack_rows_kernel, len(arrays), rows)
    return call(kernel, outs, [("h", value) for value in arrays], deps, scratch, "pack_rows", 10**6)


def combine(arrays, outs, deps=(), name="combine_late"):
    buffers = [pltpu.VMEM((count, cols), BF) for _, cols, parts in outs for _, count, sources in parts for _ in sources]

    def kernel(*refs):
        out_refs = refs[len(arrays) : len(arrays) + len(outs)]
        *held, sem = refs[len(arrays) + len(outs) :]
        copies = []
        for _, cols, parts in outs:
            for _, count, sources in parts:
                for source, row, col in sources:
                    at = len(copies)
                    piece = refs[source].at[pl.ds(row, count), pl.ds(col, cols)]
                    copies.append(pltpu.make_async_copy(piece, held[at], sem.at[at]))
                    copies[-1].start()
        at = 0
        for (_, _, parts), out_ref in zip(outs, out_refs, strict=True):
            for first, count, sources in parts:
                total = None
                for _ in sources:
                    copies[at].wait()
                    value = held[at][...].astype(F32)
                    total = value if total is None else total + value
                    at += 1
                out_ref[first : first + count, :] = total.astype(BF)

    shapes = [("v", (rows, cols), BF) for rows, cols, _ in outs]
    scratch = [*buffers, pltpu.SemaphoreType.DMA((len(buffers),))]
    return call(kernel, shapes, [("b", value) for value in arrays], deps, scratch, name, 10**6)


def regroup_kernel(shards, keep_ref, core_ref, first_a, first_b, second_a, second_b, *refs):
    outs, (held_wide, held_a, held_b, group_ref, sem, out_sem) = refs[:shards], refs[shards:]
    rows, total = held_wide.shape[1] - 16, held_wide.shape[2]
    width = total // 5
    part = width // shards
    copies = [
        pltpu.make_async_copy(ref.at[pl.ds(0, rows)], held.at[pl.ds(0, rows)], sem.at[at])
        for at, (ref, held) in enumerate(
            (
                (keep_ref, held_wide.at[0]), (core_ref, held_wide.at[1]), (first_a, held_a.at[0]), (first_b, held_b.at[0]),
                (second_a, held_a.at[1]), (second_b, held_b.at[1]),
            )
        )
    ]
    copies += [
        pltpu.make_async_copy(ref.at[pl.ds(ref.shape[0] - 16, 16)], held.at[pl.ds(rows, 16)], sem.at[6 + at])
        for at, (ref, held) in enumerate(
            ((keep_ref, held_wide.at[0]), (core_ref, held_wide.at[1]), (first_a, held_a.at[0]), (second_a, held_a.at[1]))
        )
    ]
    for copy in copies:
        copy.start()
    for copy in copies:
        copy.wait()
    sums = []
    for half, held in enumerate((held_a, held_b)):
        cols = slice(half * total // 2, (half + 1) * total // 2)
        value = held_wide[0, :rows, cols].astype(F32) + held_wide[1, :rows, cols].astype(F32)
        sums.append(value + held[0, :rows].astype(F32) + held[1, :rows].astype(F32))
    whole = jnp.concatenate(sums, axis=1)
    vectors = [held[at, rows:, :width].astype(F32) for held in (held_wide, held_a) for at in (0, 1)]
    vectors = add_all(vectors).astype(BF)
    for shard in range(shards):
        for slot in range(5):
            at = slot * width + shard * part
            group_ref[shard, :rows, slot * part : (slot + 1) * part] = whole[:, at : at + part].astype(BF)
        group_ref[shard, rows:, :width] = vectors
        group_ref[shard, rows:, width:] = jnp.zeros((16, 5 * part - width), BF)
    me = lax.axis_index("tensor")
    backs = [pltpu.make_async_copy(group_ref.at[me ^ bits], outs[bits], out_sem.at[bits]) for bits in range(shards)]
    for back in backs:
        back.start()
    for back in backs:
        back.wait()


def regroup(shards, keep, core, first, second, deps=()):
    total = keep.shape[1]
    rows = second[0].shape[0]
    shape = (rows, total // shards)
    scratch = [
        pltpu.VMEM((2, rows, total), BF), pltpu.VMEM((2, rows, total // 2), BF), pltpu.VMEM((2, rows, total // 2), BF),
        pltpu.VMEM((shards, *shape), BF), pltpu.SemaphoreType.DMA((10,)), pltpu.SemaphoreType.DMA((shards,)),
    ]
    ins = [("b", value) for value in (keep, core, *first, *second)]
    outs = [("v", shape, BF)] * shards
    return call(functools.partial(regroup_kernel, shards), outs, ins, deps, scratch, "regroup", 10**6)


class Exchange:
    def __init__(self, width):
        self.data = lax.axis_size("dp")
        self.tensor = lax.axis_size("tensor")
        self.by_hand = self.data == 8 and width % (32 * self.data) == 0
        self.blocks = self.data if self.by_hand else 1

    def data_swap(self, value, bit):
        pairs = [(at, at ^ bit) for at in range(self.data)]
        return lax.ppermute(value, "dp", pairs)

    def tensor_swap(self, value, bits):
        pairs = [(at, at ^ bits) for at in range(self.tensor)]
        return lax.ppermute(value, "tensor", pairs)


def add_low(left, right):
    return (left.astype(F32) + right.astype(F32)).astype(BF)


class Share:
    def __init__(self, swap, rows, first):
        self.swap, self.rows, self.first = swap, rows, first
        self.count = swap.tensor - 1

    def spread(self, packed):
        self.found = [(0, packed)]
        if self.swap.blocks > 1:
            bits = [1 << at for at in range(1, self.swap.data.bit_length() - 1)]
            mine = self.found[0][1]
            self.near = [(bit, self.swap.data_swap(mine, bit)) for bit in bits]
            self.found += self.near

    def cross(self):
        if self.swap.data == 8 and self.swap.blocks == 8:
            other = 6 - self.first
            self.found.append((6, self.swap.data_swap(dict(self.near)[self.first], other)))

    def finish(self):
        rows, pieces, found = self.rows, [], list(self.found)
        if self.swap.blocks > 1:
            found += [(block | 1, self.swap.data_swap(value, 1)) for block, value in self.found]
        for block, value in found:
            pieces += [(shard, block, rows, shard * rows, value) for shard in range(self.count)]
        return pieces


def add_all(terms):
    total = terms[0].astype(F32)
    for term in terms[1:]:
        total += term.astype(F32)
    return total


def tensor_sum(swap, parts):
    return add_all([parts[0]] + [swap.tensor_swap(parts[bits], bits) for bits in range(1, swap.tensor)])


def per_device(
    h_in, g_in, seg_ids, target_flags, perm_order, w_query, w_key, w_value, w_out, w_rel, attn_bias, seg_embed,
    norm_gain, norm_bias, w_up, b_up, w_down, b_down, d_h_out, d_g_out,
):
    seq_count, length, width = h_in.shape
    assert seq_count == 1
    swap = Exchange(width)
    parts, shards = swap.blocks, swap.tensor
    by_hand = swap.by_hand
    dp_at, tensor_at = lax.axis_index("dp"), lax.axis_index("tensor")
    own_part = width // shards
    rel_host = rel_table(length, width)
    rel, rev = jnp.asarray(rel_host), jnp.asarray(np.ascontiguousarray(rel_host[::-1]))
    h, g = h_in[0], g_in[0]
    up, down = w_up[0], w_down[0]
    bias, table = attn_bias.reshape(1, -1), seg_embed.reshape(1, -1)
    gains, shifts = norm_gain.reshape(1, -1), norm_bias.reshape(1, -1)

    mine = share_slices(parts, up, down, b_up)
    rows = (mine.shape[0] - 16) // 2
    fetched = [swap.tensor_swap(mine, bits) for bits in range(1, shards)]
    share_up, share_down = Share(swap, rows, 2), Share(swap, rows, 4)
    q, key, value, relkey, mask, half, relrev, left_x, left_rev = project(
        parts, h, g, seg_ids, target_flags, perm_order, w_query[0], w_key[0], w_value[0], w_rel[0], rel, rev, ()
    )
    att_one, prob_one = attention_first(q, key, value, relkey, mask, half, bias, table, ())
    packed_up, packed_down = pack_rows(fetched, rows, [att_one])
    share_up.spread(packed_up)
    share_down.spread(packed_down)
    resid_one, mid, prob_two, att, left_att = attention_second(
        parts, w_out[0], h, g, q, key, value, relkey, mask, half, att_one, bias, table, gains, shifts,
        [share_up.found[0][1], share_down.found[0][1]],
    )
    share_up.cross()
    act_own, slope_own = feed_up_own(mid, up, b_up, [found for _, found in share_up.found[:3]])
    share_down.cross()
    act_rest, slope_rest, up_rest = feed_up(
        shards, mid, 2 * rows, fetched, share_up.finish(), [found for _, found in share_down.found]
    )
    out_h, out_g, dresid_two, dbranch, keep_down, send_down, vec_two, down_rest = feed_down(
        parts, shards, down, act_own, act_rest, resid_one, b_down, gains, shifts, d_h_out[0], d_g_out[0],
        share_down.finish(), (),
    )

    hidden, wide = shards * width, 5 * width
    block, middle = width // 8, width // 4
    size = (10 + shards) * width

    def first_far(keep, core, deps, name):
        cut = keep.shape[1] // 2
        odd = [(at, block, [(0, block + 2 * at, 0), (1, block + 2 * at, 0)]) for at in (0, block)]
        upper = [(0, middle, [(0, middle, cut), (1, middle, cut)])]
        more = keep.shape[0] - 2 * middle
        if more:
            odd.append((middle, more, [(0, 2 * middle, 0), (1, 2 * middle, 0)]))
        return combine([keep, core], [(middle + more, cut, odd), (middle, cut, upper)], deps, name)

    def first_swap(far):
        return swap.data_swap(far[0], 2), swap.data_swap(far[1], 4)

    def second_far(keep, core, first, deps, name):
        cut = keep.shape[1] // 2
        more = keep.shape[0] - 2 * middle
        upper = [(0, block, [(0, middle, 0), (1, middle, 0), (2, block, 0)])]
        if more:
            upper.append((block, more, [(0, 2 * middle, 0), (1, 2 * middle, 0), (2, middle, 0)]))
        return combine(
            [keep, core, *first],
            [
                (block + more, cut, upper),
                (block, cut, [(0, block, [(0, block, cut), (1, block, cut), (3, block, 0)])]),
            ],
            deps,
            name,
        )

    def second_swap(far):
        return swap.data_swap(far[0], 4), swap.data_swap(far[1], 2)

    def feed_parts_of(sides, deps):
        per = shards // 2
        outs, arrays = [], []
        for keep, core, first, second in sides:
            arrays += [keep, core, *first, *second]
        for shard in range(shards):
            half, near, rows = shard // per, shard % per * width, []
            for side in range(len(sides)):
                at = 6 * side
                sources = [(at, 0, shard * width), (at + 1, 0, shard * width), (at + 2 + half, 0, near), (at + 4 + half, 0, near)]
                rows.append((side * block, block, sources))
            outs.append((len(sides) * block, width, rows))
        return combine(arrays, outs, deps)

    if by_hand:
        core_down = swap.data_swap(send_down, 1)
    dpre, keep_up, send_up, dbias_up = feed_back_up(parts, shards, down, down_rest, dbranch, mid, slope_own, slope_rest, ())
    deps = ()
    if by_hand:
        core_up = swap.data_swap(send_up, 1)
        far_down = first_far(keep_down, core_down, (), "combine")
        first_down = first_swap(far_down)
        far_up = first_far(keep_up, core_up, far_down, "combine")
        first_up = first_swap(far_up)
        deps = far_up
    dproj, dresid_one, vec_one = feed_back_mid(shards, up, up_rest, dpre, dresid_two, resid_one, gains, deps)
    common = (w_out[0], dproj, q, att, key, value, prob_one, prob_two, relrev, half)
    back_first = attention_back_first(tuple(range(PAIRS // 2)), common, bias, table, ())
    deps = ()
    if by_hand:
        far_down = second_far(keep_down, core_down, first_down, back_first[-1:], "combine")
        second_down = second_swap(far_down)
        deps = far_down
    dq, dkey, dvalue, keep_att, send_att = attention_back(
        tuple(range(PAIRS // 2, PAIRS)), common, (left_x, left_rev, left_att), back_first, (vec_one, vec_two, dbias_up),
        bias, table, deps,
    )
    if by_hand:
        (send_att, keep_att), (first_up, second_down) = lax.optimization_barrier(
            ((send_att, keep_att), (first_up, second_down))
        )
        core_att = swap.data_swap(send_att, 1)
        far_up = second_far(keep_up, core_up, first_up, (), "combine_late")
        second_up = second_swap(far_up)
        grad_h, grad_g = input_grads(w_query[0], w_key[0], w_value[0], dq, dkey, dvalue, dresid_one, far_up)
        far_att = first_far(keep_att, core_att, [grad_h, *second_up], "combine_late")
        first_att = first_swap(far_att)
        feed_parts = feed_parts_of(
            [(keep_up, core_up, first_up, second_up), (keep_down, core_down, first_down, second_down)], far_att
        )
        came = [swap.tensor_swap(feed_parts[bits], bits) for bits in range(1, shards)]
        far_att = second_far(keep_att, core_att, first_att, came[:2], "combine_late")
        second_att = second_swap(far_att)
        att_parts = regroup(shards, keep_att, core_att, first_att, second_att, came)
    else:
        grad_h, grad_g = input_grads(w_query[0], w_key[0], w_value[0], dq, dkey, dvalue, dresid_one, ())
        vectors = lax.psum(keep_att[width // 2 : width // 2 + 10 + shards, :width].astype(F32), AXES)
        keep_att, send_att = keep_att[: width // 2], send_att[: width // 2]

        def rows_sum(keep, send):
            whole = jnp.concatenate([keep, send], axis=0)
            return lax.psum_scatter(whole, "dp", scatter_dimension=0, tiled=True)

        sum_up, sum_down, sum_att = (
            rows_sum(keep, send) for keep, send in ((keep_up, send_up), (keep_down, send_down), (keep_att, send_att))
        )
        cols = [slice(shard * width, (shard + 1) * width) for shard in range(shards)]
        d_up = tensor_sum(swap, [sum_up[:, part] for part in cols])
        d_down = tensor_sum(swap, [sum_down[:, part] for part in cols]).T
        split = sum_att.reshape(-1, 5, shards, own_part).transpose(2, 0, 1, 3).reshape(shards, -1, 5 * own_part)
        att_parts = [lax.dynamic_index_in_dim(split, tensor_at ^ bits, 0, keepdims=False) for bits in range(shards)]
    att_parts = [att_parts[0]] + [swap.tensor_swap(att_parts[bits], bits) for bits in range(1, shards)]
    if by_hand:
        came, _ = lax.optimization_barrier((came, att_parts[1]))
        d_feed = add_all([feed_parts[0], *came])
        d_up, d_down = d_feed[:block], d_feed[block:].T
    d_att = add_all(att_parts)
    if by_hand:
        d_att, vectors = d_att[:block], d_att[block : block + 10 + shards, :width]
    d_att = [d_att[:, slot * own_part : (slot + 1) * own_part] for slot in range(5)]

    own = size // (swap.data * shards)
    d_vectors = lax.dynamic_slice_in_dim(vectors.reshape(-1), (dp_at * shards + tensor_at) * own, own, 0)

    return (
        out_h[None], out_g[None], grad_h[None], grad_g[None],
        d_att[0][None], d_att[1][None], d_att[2][None], d_att[3][None], d_att[4][None],
        d_up[None], d_down[None], d_vectors[None],
    )


def solution(mesh):
    every = P(AXES, None, None)
    rows = P(AXES, None)
    in_specs = (
        every, every, rows, rows, rows, P(), P(), P(), P(), P(), P(), P(), P(), P(),
        P(None, None, "tensor"), P(None, "tensor"), P(None, "tensor", None), P(), every, every,
    )
    grads = P(None, "dp", "tensor")
    out_specs = (
        every, every, every, every, grads, grads, grads, grads, grads, grads,
        P(None, "tensor", "dp"), P(None, AXES),
    )
    return jax.shard_map(per_device, mesh=mesh, in_specs=in_specs, out_specs=out_specs, check_vma=False)
```

```python
import functools
import math

import jax
import jax.numpy as jnp
import numpy as np
from jax import lax
from jax.experimental import pallas as pl
from jax.experimental.pallas import tpu as pltpu
from jax.sharding import PartitionSpec as P

HEADS = 12
HEAD_DIM = 64
LANES = 128
PAIRS = HEADS // 2
NEGATIVE = -1e30
EPSILON = 1e-06
AXES = ("dp", "tensor")
BF = jnp.bfloat16
F32 = jnp.float32
FIRST_PAIRS = 4
VMEM_MIB = {
    "share_slices": 60, "project": 50, "attention_first": 12, "attention_second": 14, "feed_up_own": 6, "feed_up": 14, "feed_down": 22,
    "feed_back_up": 16, "feed_back_mid": 10, "attention_back_first": 18, "attention_back": 26, "input_grads": 14, "pack_rows": 2,
    "combine": 12, "combine_late": 12, "combine_att": 59, "combine_left": 59, "regroup": 59,
}


def rel_table(length, model_width):
    position = (length - np.arange(2 * length)).astype(np.float32)
    frequency = np.float32(1.0) / np.float32(10000.0) ** (
        np.arange(0, model_width, 2).astype(np.float32) / np.float32(model_width)
    )
    angles = position[:, None] * frequency[None, :]
    return np.concatenate([np.sin(angles), np.cos(angles)], axis=1).astype(BF)


class Late:
    def __init__(self, source, target, sem):
        self.target, self.waiting = target, True
        self.copy = pltpu.make_async_copy(source, target, sem)
        self.copy.start()

    def get(self):
        if self.waiting:
            self.copy.wait()
            self.waiting = False
        return self.target


class Early:
    def __init__(self, ref, target, sems):
        self.ref, self.target, self.sems, self.copies = ref, target, sems, []

    def send(self, *where):
        source, target = (self.ref.at[where], self.target.at[where]) if where else (self.ref, self.target)
        copy = pltpu.make_async_copy(source, target, self.sems.at[len(self.copies)])
        copy.start()
        self.copies.append(copy)


SENDS = 16


def call(kernel, outs, ins, deps, scratch, name, flops):
    deps = tuple(deps)
    spaces = {"s": pltpu.SMEM, "v": pltpu.VMEM, "h": pl.ANY, "l": pltpu.HBM, "e": pltpu.HBM, "b": pltpu.HBM}
    late = [value for kind, value in ins if kind == "l"]
    early = [(shape, dtype) for kind, shape, dtype in outs if kind == "e"]
    more = [pltpu.VMEM(value.shape, value.dtype) for value in late] + [pltpu.VMEM(*spec) for spec in early]
    if late:
        more.append(pltpu.SemaphoreType.DMA((len(late),)))
    if early:
        more.append(pltpu.SemaphoreType.DMA((len(early), SENDS)))
    first_out = len(ins) + len(deps)
    first_scratch = first_out + len(outs)

    def wrapped(*refs):
        own = refs[first_scratch + len(scratch) :]
        late_refs, early_refs = own[: len(late)], own[len(late) : len(late) + len(early)]
        sems = list(own[len(late) + len(early) :])
        late_sem = sems.pop(0) if late else None
        early_sem = sems.pop(0) if early else None
        given, at = [], 0
        for (kind, _), ref in zip(ins, refs[: len(ins)], strict=True):
            if kind == "l":
                ref = Late(ref, late_refs[at], late_sem.at[at])
                at += 1
            given.append(ref)
        made, at = [], 0
        for (kind, _, _), ref in zip(outs, refs[first_out:first_scratch], strict=True):
            if kind == "e":
                ref = Early(early_refs[at], ref, early_sem.at[at])
                at += 1
            made.append(ref)
        kernel(*given, *made, *refs[first_scratch : first_scratch + len(scratch)])
        for item in given:
            if isinstance(item, Late):
                item.get()
        for item in made:
            if isinstance(item, Early):
                for copy in item.copies:
                    copy.wait()

    return pl.pallas_call(
        wrapped,
        out_shape=[jax.ShapeDtypeStruct(shape, dtype) for _, shape, dtype in outs],
        in_specs=[pl.BlockSpec(memory_space=spaces[kind]) for kind, _ in ins]
        + [pl.BlockSpec(memory_space=pl.ANY)] * len(deps),
        out_specs=[pl.BlockSpec(memory_space=spaces[kind]) for kind, _, _ in outs],
        scratch_shapes=list(scratch) + more,
        compiler_params=pltpu.CompilerParams(vmem_limit_bytes=VMEM_MIB[name] * 1024 * 1024),
        cost_estimate=pl.CostEstimate(flops=flops * 100, bytes_accessed=flops // 1000, transcendentals=0),
        name=name,
    )(*[value for _, value in ins], *deps)


def nn(left, right):
    return lax.dot_general(left, right, (((1,), (0,)), ((), ())), preferred_element_type=F32)


def nt(left, right):
    return lax.dot_general(left, right, (((1,), (1,)), ((), ())), preferred_element_type=F32)


def tn(left, right):
    return lax.dot_general(left, right, (((0,), (0,)), ((), ())), preferred_element_type=F32)


def lane_index(rows):
    return lax.broadcasted_iota(jnp.int32, (rows, LANES), 1)


def pair_lanes(pair):
    return pl.ds(pl.multiple_of(pair * LANES, LANES), LANES)


def row_lanes(row, pair, width):
    return pl.ds(pl.multiple_of(row * width + pair * LANES, LANES), LANES)


def norm_stats(source):
    mean = jnp.mean(source, axis=-1, keepdims=True)
    centered = source - mean
    variance = jnp.mean(centered * centered, axis=-1, keepdims=True)
    rstd = lax.rsqrt(variance + EPSILON)
    return centered * rstd, rstd


def norm_back(grad, xhat, rstd, gain):
    dxhat = grad * gain
    mean_one = jnp.mean(dxhat, axis=-1, keepdims=True)
    mean_two = jnp.mean(dxhat * xhat, axis=-1, keepdims=True)
    return rstd * (dxhat - mean_one - xhat * mean_two)


def seg_coefficients(half_wide, lane):
    return jnp.where(lane % HEAD_DIM == 0, half_wide, 1.0 - 2.0 * half_wide)


def seg_keys(half_wide, lane):
    place = lane % HEAD_DIM
    return jnp.where(place == 0, 1.0, jnp.where(place == 1, half_wide, 0.0))


def seg_table(seg_ref, pair, width):
    row = lax.broadcasted_iota(jnp.int32, (LANES, LANES), 0)
    lane = lax.broadcasted_iota(jnp.int32, (LANES, LANES), 1)
    one = jnp.broadcast_to(seg_ref[0:1, pair_lanes(pair)], (LANES, LANES)).T
    two = jnp.broadcast_to(seg_ref[0:1, row_lanes(1, pair, width)], (LANES, LANES)).T
    base = jnp.where(row < HEAD_DIM, HEAD_DIM, 0)
    at_one = lane == base
    at_two = at_one | (lane == base + 1)
    return jnp.concatenate([jnp.where(at_one, one, 0.0), jnp.where(at_two, two - one, 0.0)], axis=1).astype(BF)


def attend_pair(pair, first, q_ref, key_ref, value_ref, relkey_ref, mask_ref, half_ref, bias_ref, seg_ref, prob_ref, att_ref):
    length, width = key_ref.shape
    block = length // 2
    lanes = pair_lanes(pair)
    lane_q = lane_index(2 * length)
    lane_k = lane_index(length)
    low_q = lane_q < HEAD_DIM
    low_k = lane_k < HEAD_DIM
    half_w = half_ref[...]
    scale = 1.0 / math.sqrt(HEAD_DIM)
    query = q_ref[:, lanes]
    word = ((query + bias_ref[0:1, lanes]) * scale).astype(BF)
    relq = ((query + bias_ref[0:1, row_lanes(1, pair, width)]) * scale).astype(BF)
    segq = ((query + bias_ref[0:1, row_lanes(2, pair, width)]) * scale).astype(BF)
    terms = nn(segq, seg_table(seg_ref, pair, width))
    coef = seg_coefficients(jnp.concatenate([half_w, half_w], axis=0), lane_q)
    extra = (terms[:, :LANES] + terms[:, LANES:] * coef).astype(BF)
    key_extra = seg_keys(half_w, lane_k).astype(BF)
    key = key_ref[:, lanes]
    value = value_ref[:, lanes]
    zero = jnp.zeros_like(relq)
    attended = []
    for head in (0, 1):
        if head == 0:
            word_one = jnp.where(low_q, word, extra)
            key_one = jnp.where(low_k, key, key_extra)
            rel_one = jnp.where(low_q, relq, zero)
        else:
            word_one = jnp.where(low_q, extra, word)
            key_one = jnp.where(low_k, key_extra, key)
            rel_one = jnp.where(low_q, zero, relq)
        score = nt(word_one, key_one)
        for part in (0, 1):
            base = block - block * part
            rows_h = slice(block * part, block * part + block)
            rows_g = slice(length + block * part, length + block * part + block)
            rel_rows = jnp.concatenate([rel_one[rows_h], rel_one[rows_g]], axis=0)
            raw = nt(rel_rows, relkey_ref[base : base + 3 * block, lanes])
            for place_at, rows in ((0, rows_h), (1, rows_g)):
                shifted = pltpu.roll(
                    raw[place_at * block : (place_at + 1) * block], 2 * block, 1, stride=1, stride_axis=0
                )[:, :length]
                logits = score[rows] + shifted + mask_ref[rows]
                top = jnp.max(logits, axis=1, keepdims=True)
                power = jnp.exp(logits - top)
                total = jnp.sum(power, axis=1, keepdims=True)
                prob_ref[2 * (pair - first) + head, rows, :] = (power * (1.0 / total)).astype(BF)
        attended.append(nn(prob_ref[2 * (pair - first) + head], value))
    att_ref[:, lanes] = jnp.where(low_q, attended[0], attended[1]).astype(BF)


def project_kernel(
    parts, h_late, g_late, wq_late, wk_late, wv_late, rel_late, wr_late, rev_late,
    seg_row, flag_row, order_row,
    q_ref, key_ref, value_ref, relkey_ref, mask_ref, half_ref, relrev_out, left_x_out, left_rev_out,
    x_ref, raw_ref,
):
    h_ref, g_ref = h_late.get(), g_late.get()
    length, width = h_ref.shape
    x_ref[:length] = h_ref[...]
    x_ref[length:] = g_ref[...]

    def project(left, right_late, target):
        right = right_late.get()
        for col in range(0, width, 256):
            cols = slice(col, col + 256)
            target[:, cols] = nn(left[...], right[:, cols]).astype(target.dtype)

    project(x_ref, wq_late, q_ref)
    project(h_ref, wk_late, key_ref)
    project(h_ref, wv_late, value_ref)
    project(rel_late.get(), wr_late, relkey_ref)

    def wide(row_ref):
        return jnp.broadcast_to(row_ref[...].astype(F32), (length, length))

    row_at = lax.broadcasted_iota(jnp.int32, (length, length), 0)
    col_at = lax.broadcasted_iota(jnp.int32, (length, length), 1)
    seg, order = wide(seg_row), wide(order_row)
    same_doc = seg.T == seg
    start = jnp.min(jnp.where(same_doc, col_at.astype(F32), float(length)), axis=1, keepdims=True)
    in_doc = jnp.sum(jnp.where(same_doc, 1.0, 0.0), axis=1, keepdims=True)
    place = lax.broadcasted_iota(jnp.int32, (length, 1), 0).astype(F32)
    half = jnp.where(2.0 * (place - start) >= in_doc, 1.0, 0.0)
    half_ref[...] = jnp.broadcast_to(half, (length, LANES))
    content = same_doc & ((wide(flag_row) == 0.0) | (order <= order.T))
    mask_ref[:length] = jnp.where(content, 0.0, NEGATIVE)
    mask_ref[length:] = jnp.where(content & (row_at != col_at), 0.0, NEGATIVE)

    project(rev_late.get(), wr_late, relrev_out.ref)
    relrev_out.send()
    turn_rows(lambda col: x_ref[:, col : col + 256], raw_ref.at[0], left_x_out.ref, parts)
    left_x_out.send()
    rev_ref = rev_late.get()
    turn_rows(lambda col: rev_ref[:, col : col + 256], raw_ref.at[1], left_rev_out.ref, parts)
    left_rev_out.send()


def project(parts, h, g, seg, flag, order, wq, wk, wv, wr, rel, rev, deps):
    length, width = h.shape
    two = 2 * length
    outs = [
        ("v", (two, width), F32), ("v", (length, width), BF), ("v", (length, width), BF), ("v", (two, width), BF),
        ("v", (two, length), F32), ("v", (length, LANES), F32), ("e", (two, width), BF), ("e", (width, two), BF),
        ("e", (width, two), BF),
    ]
    ins = [("l", value) for value in (h, g, wq, wk, wv, rel, wr, rev)] + [("v", value) for value in (seg, flag, order)]
    scratch = [pltpu.VMEM((two, width), BF), pltpu.VMEM((2, width, two), BF)]
    return call(functools.partial(project_kernel, parts), outs, ins, deps, scratch, "project", 5 * 10**9)


def attention_first_kernel(
    q_ref, key_ref, value_ref, relkey_ref, mask_ref, half_ref, bias_ref, seg_ref, att_ref, prob_out
):
    def pair_step(pair, carry):
        attend_pair(
            pair, 0, q_ref, key_ref, value_ref, relkey_ref, mask_ref, half_ref, bias_ref, seg_ref, prob_out.ref, att_ref
        )
        return carry

    for first in range(0, FIRST_PAIRS, 2):
        lax.fori_loop(first, first + 2, pair_step, 0)
        prob_out.send(pl.ds(2 * first, 4))


def attention_first(q, key, value, relkey, mask, half, bias, table, deps):
    two, length = mask.shape
    outs = [("v", (two, FIRST_PAIRS * LANES), BF), ("e", (2 * FIRST_PAIRS, two, length), BF)]
    ins = [("v", x) for x in (q, key, value, relkey, mask, half, bias, table)]
    return call(attention_first_kernel, outs, ins, deps, [], "attention_first", 5 * 10**9)


def attention_second_kernel(
    parts, wo_late, h_late, g_late, q_ref, key_ref, value_ref, relkey_ref, mask_ref, half_ref, att_first_ref,
    bias_ref, seg_ref, gain_ref, shift_ref,
    resid_ref, mid_ref, prob_out, att_out, left_att_out,
    raw_ref,
):
    length, width = key_ref.shape
    att_ref = att_out.ref
    att_ref[:, : FIRST_PAIRS * LANES] = att_first_ref[...]

    def pair_step(pair, carry):
        attend_pair(
            pair, FIRST_PAIRS, q_ref, key_ref, value_ref, relkey_ref, mask_ref, half_ref, bias_ref, seg_ref, prob_out.ref, att_ref
        )
        return carry

    for first in range(FIRST_PAIRS, PAIRS, 2):
        lax.fori_loop(first, first + 2, pair_step, 0)
        prob_out.send(pl.ds(2 * (first - FIRST_PAIRS), 4))
    att_out.send()
    wo_ref, h_ref, g_ref = wo_late.get(), h_late.get(), g_late.get()
    for col in range(0, width, 256):
        cols = slice(col, col + 256)
        total = nn(att_ref[...], wo_ref[:, cols])
        resid_ref[:length, cols] = h_ref[:, cols].astype(F32) + total[:length]
        resid_ref[length:, cols] = g_ref[:, cols].astype(F32) + total[length:]
    turn_rows(lambda col: att_ref[:, col : col + 256], raw_ref, left_att_out.ref, parts)
    left_att_out.send()
    for row in range(0, 2 * length, 64):
        xhat, _ = norm_stats(resid_ref[row : row + 64, :])
        mid_ref[row : row + 64, :] = (xhat * gain_ref[0:1, :width] + shift_ref[0:1, :width]).astype(BF)


def attention_second(parts, wo, h, g, q, key, value, relkey, mask, half, att, bias, table, gain, shift, deps):
    length, width = h.shape
    two = 2 * length
    outs = [
        ("v", (two, width), F32), ("v", (two, width), BF), ("e", (HEADS - 2 * FIRST_PAIRS, two, length), BF),
        ("e", (two, width), BF), ("e", (width, two), BF),
    ]
    ins = [("l", value) for value in (wo, h, g)]
    ins += [("v", value) for value in (q, key, value, relkey, mask, half, att, bias, table, gain, shift)]
    return call(
        functools.partial(attention_second_kernel, parts), outs, ins, deps, [pltpu.VMEM((width, two), BF)],
        "attention_second", 10 * 10**9,
    )


def place_rows(raw_ref, out_ref, parts):
    rows = raw_ref.shape[0] // parts
    me = lax.axis_index("dp") if parts > 1 else 0
    order = [low | (rest << 1) for low in (0, 1) for rest in range(parts // 2)] if parts > 1 else [0]
    for at, block in enumerate(order):
        source = pl.multiple_of((me ^ block) * rows, rows)
        out_ref[at * rows : (at + 1) * rows, :] = raw_ref[pl.ds(source, rows), :]


def turn_rows(source, raw_ref, out_ref, parts):
    for col in range(0, raw_ref.shape[0], 256):
        raw_ref[col : col + 256, :] = source(col).astype(F32).T.astype(BF)
    place_rows(raw_ref, out_ref, parts)


def back_pairs(
    pairs, dproj_ref, wo_ref, q_ref, att_ref, key_ref, value_ref, prob_one, prob_two, relrev_ref, half_ref, bias_ref, seg_ref,
    dq_ref, dkey_ref, dvalue_ref, drel_ref, vec_ref, datt_ref,
):
    length, width = key_ref.shape
    block = length // 2
    for at, pair in enumerate(pairs):
        rows = slice(pair * LANES, (pair + 1) * LANES)
        datt_ref[:, at * LANES : (at + 1) * LANES] = nt(dproj_ref[...], wo_ref[rows, :]).astype(BF)

    def pair_step(at, pair):
        lanes = slice(pair * LANES, (pair + 1) * LANES)
        own = slice(at * LANES, (at + 1) * LANES)
        prob_ref, prob_at = (prob_one, 2 * pair) if pair < FIRST_PAIRS else (prob_two, 2 * (pair - FIRST_PAIRS))
        lane_q = lane_index(2 * length)
        lane_k = lane_index(length)
        low_q = lane_q < HEAD_DIM
        low_k = lane_k < HEAD_DIM
        half_w = half_ref[...]
        flip_row = lax.broadcasted_iota(jnp.int32, (length, length), 0)
        flip_col = lax.broadcasted_iota(jnp.int32, (length, length), 1)
        flip = jnp.where(flip_row + flip_col == length - 1, 1.0, 0.0).astype(BF)
        sel_row = lax.broadcasted_iota(jnp.int32, (2 * LANES, LANES), 0) % LANES
        sel_col = lax.broadcasted_iota(jnp.int32, (2 * LANES, LANES), 1)
        select = jnp.where(
            ((sel_row < HEAD_DIM) & ((sel_col == HEAD_DIM) | (sel_col == HEAD_DIM + 1)))
            | ((sel_row >= HEAD_DIM) & (sel_col < 2)),
            1.0,
            0.0,
        ).astype(BF)
        query = q_ref[:, lanes]
        word = query + bias_ref[0:1, lanes]
        relq = query + bias_ref[0:1, row_lanes(1, pair, width)]
        segq = (query + bias_ref[0:1, row_lanes(2, pair, width)]).astype(BF)
        word_t = word.T.astype(BF)
        relq_t = relq.T.astype(BF)
        datt = datt_ref[:, own]
        datt_wide = datt.astype(F32)
        datt_t = datt_wide.T.astype(BF)
        datt_scaled = datt_wide * (1.0 / math.sqrt(HEAD_DIM))
        product = datt_scaled * att_ref[:, lanes].astype(F32)
        product_high = product.astype(BF)
        product_low = (product - product_high.astype(F32)).astype(BF)
        delta = nn(jnp.concatenate([product_high, product_low], axis=1), select)
        delta_high = delta.astype(BF).astype(F32)
        minus = jnp.where(lane_q % HEAD_DIM == 0, -delta_high, delta_high - delta).astype(BF)
        datt_low = datt_scaled.astype(BF)
        key_extra = seg_keys(half_w, lane_k).astype(BF)
        ones_extra = jnp.where(lane_k % HEAD_DIM < 2, 1.0, 0.0).astype(BF)
        key = key_ref[:, lanes]
        value = value_ref[:, lanes]
        dword, drel = [], []
        for head in (0, 1):
            rows_t = slice(HEAD_DIM * head, HEAD_DIM * head + HEAD_DIM)
            if head == 0:
                datt_one = jnp.where(low_q, datt_low, minus)
                value_one = jnp.where(low_k, value, ones_extra)
                key_one = jnp.where(low_k, key, key_extra)
            else:
                datt_one = jnp.where(low_q, minus, datt_low)
                value_one = jnp.where(low_k, ones_extra, value)
                key_one = jnp.where(low_k, key_extra, key)
            prob = prob_ref[prob_at + head]
            dprob = nt(datt_one, value_one)
            dscore = (prob.astype(F32) * dprob).astype(BF)
            dword.append(nn(dscore, key_one))
            rows_out = slice(at * LANES + HEAD_DIM * head, at * LANES + HEAD_DIM * (head + 1))
            dkey_ref[rows_out, :] = nn(word_t[rows_t], dscore).astype(BF)
            dvalue_ref[rows_out, :] = nn(datt_t[rows_t], prob).astype(BF)
            flipped = nn(dscore, flip).astype(BF)
            pad = jnp.zeros((block, block), BF)
            rel_parts, drel_t = [], []
            for part in (0, 1):
                rows_h = slice(block * part, block * part + block)
                rows_g = slice(length + block * part, length + block * part + block)
                draw = jnp.concatenate(
                    [
                        pltpu.roll(jnp.concatenate([flipped[rows], pad], axis=1), 0, 1, stride=1, stride_axis=0)
                        for rows in (rows_h, rows_g)
                    ],
                    axis=0,
                )
                rel_parts.append(nn(draw, relrev_ref[block * part : block * part + 3 * block, lanes]))
                rel_cols = jnp.concatenate([relq_t[rows_t, rows_h], relq_t[rows_t, rows_g]], axis=1)
                drel_t.append(nn(rel_cols, draw))
            drel.append(
                jnp.concatenate(
                    [rel_parts[0][:block], rel_parts[1][:block], rel_parts[0][block:], rel_parts[1][block:]], axis=0
                )
            )
            drel_ref[rows_out, :] = jnp.concatenate(
                [
                    drel_t[0][:, :block],
                    drel_t[0][:, block:] + drel_t[1][:, : 2 * block],
                    drel_t[1][:, 2 * block :],
                ],
                axis=1,
            ).astype(BF)
        extra = jnp.where(low_q, dword[1], dword[0])
        dword_all = jnp.where(low_q, dword[0], dword[1])
        drel_all = jnp.where(low_q, drel[0], drel[1])
        coef = seg_coefficients(jnp.concatenate([half_w, half_w], axis=0), lane_q)
        dterms = jnp.concatenate([extra, extra * coef], axis=1).astype(BF)
        dsegq = nt(dterms, seg_table(seg_ref, pair, width))
        dtable = tn(dterms, segq)
        dq_ref[:, own] = (dword_all + drel_all + dsegq).astype(BF)
        low_one = lane_index(1) < HEAD_DIM
        first = jnp.where(low_one, dtable[HEAD_DIM : HEAD_DIM + 1], dtable[0:1])
        far = LANES + HEAD_DIM
        second = jnp.where(
            low_one, dtable[far : far + 1] + dtable[far + 1 : far + 2], dtable[LANES : LANES + 1] + dtable[LANES + 1 : LANES + 2]
        )
        vec_ref[0:1, own] = jnp.sum(dword_all, axis=0, keepdims=True)
        vec_ref[1:2, own] = jnp.sum(drel_all, axis=0, keepdims=True)
        vec_ref[2:3, own] = jnp.sum(dsegq, axis=0, keepdims=True)
        vec_ref[3:4, own] = first - second
        vec_ref[4:5, own] = second
    for at, pair in enumerate(pairs):
        pair_step(at, pair)


def attention_back_first_kernel(
    pairs, wo_late, dproj_ref, q_ref, att_ref, key_ref, value_ref, prob_one, prob_two, relrev_ref, half_ref, bias_ref, seg_ref,
    dq_ref, dkey_ref, dvalue_ref, drel_ref, vec_ref, datt_ref,
):
    vec_ref[...] = jnp.zeros_like(vec_ref)
    back_pairs(
        pairs, dproj_ref, wo_late.get(), q_ref, att_ref, key_ref, value_ref, prob_one, prob_two, relrev_ref, half_ref, bias_ref,
        seg_ref, dq_ref, dkey_ref, dvalue_ref, drel_ref, vec_ref, datt_ref,
    )


def attention_back_first(pairs, common, bias, table, deps):
    two, width = common[1].shape
    length, size = two // 2, len(pairs) * LANES
    outs = [
        ("v", (two, size), BF), ("v", (size, length), BF), ("v", (size, length), BF), ("v", (size, two), BF), ("v", (8, size), F32),
    ]
    ins = [("l", common[0])] + [("v", x) for x in (*common[1:], bias, table)]
    kernel = functools.partial(attention_back_first_kernel, pairs)
    return call(kernel, outs, ins, deps, [pltpu.VMEM((two, size), BF)], "attention_back_first", 12 * 10**9)


def attention_back_kernel(
    pairs, wo_late, dproj_ref, q_ref, att_ref, key_ref, value_ref, prob_one, prob_two, relrev_ref, half_ref, bias_ref, seg_ref,
    left_x_ref, left_rev_ref, left_att_ref, dq_one, dkey_one, dvalue_one, drel_one, vec_one, norm_one, norm_two, hidden_ref,
    dq_ref, dkey_ref, dvalue_ref, keep_out, send_out, datt_ref, drel_ref, vec_ref, packed_ref,
):
    length, width = key_ref.shape
    split = width // 2
    size = dq_one.shape[1]
    dq_ref[:, :size], dkey_ref[:size], dvalue_ref[:size], drel_ref[:size] = dq_one[...], dkey_one[...], dvalue_one[...], drel_one[...]
    vec_ref[...] = jnp.zeros_like(vec_ref)
    vec_ref[:, :size] = vec_one[...]
    back_pairs(
        pairs, dproj_ref, wo_late.get(), q_ref, att_ref, key_ref, value_ref, prob_one, prob_two, relrev_ref, half_ref, bias_ref,
        seg_ref, dq_ref.at[:, size:], dkey_ref.at[size:], dvalue_ref.at[size:], drel_ref.at[size:], vec_ref.at[:, size:], datt_ref,
    )
    shards = hidden_ref.shape[1] // width
    packed_ref[...] = jnp.zeros_like(packed_ref)
    packed_ref[0:5, :] = vec_ref[0:5, :]
    packed_ref[5:6, :] = norm_one[0:1, :]
    packed_ref[6:7, :] = norm_two[0:1, :]
    packed_ref[7:8, :] = norm_one[1:2, :]
    packed_ref[8:10, :] = norm_two[1:3, :]
    for shard in range(shards):
        place = 10 + (lax.axis_index("tensor") ^ shard)
        packed_ref[pl.ds(place, 1), :] = hidden_ref[0:1, shard * width : (shard + 1) * width]
    packed = packed_ref[...].astype(BF)
    for out in (send_out, keep_out):
        out.ref[split:, :width] = packed
        out.ref[split:, width:] = jnp.zeros((16, 4 * width), BF)
        out.send(pl.ds(split, 16))
    todo = [
        (left_x_ref[...], dq_ref, nn), (left_x_ref[:, :length], dkey_ref, nt), (left_x_ref[:, :length], dvalue_ref, nt),
        (left_att_ref[...], dproj_ref, nn), (left_rev_ref[...], drel_ref, nt),
    ]
    at = 0
    for left, right, dot in todo:
        count = right.shape[1] if dot is nn else right.shape[0]
        for col in range(0, count, 256):
            cols = slice(col, col + 256)
            piece = dot(left, right[:, cols] if dot is nn else right[cols, :]).astype(BF)
            keep_out.ref[:split, at + col : at + col + 256] = piece[:split]
            send_out.ref[:split, at + col : at + col + 256] = piece[split:]
        done = pl.ds(at, count)
        send_out.send(pl.ds(0, split), done)
        keep_out.send(pl.ds(0, split), done)
        at += count


def attention_back(pairs, common, lefts, first, vectors, bias, table, deps):
    two, width = common[1].shape
    length, size = two // 2, len(pairs) * LANES
    outs = [
        ("v", (two, width), BF), ("v", (width, length), BF), ("v", (width, length), BF),
        ("e", (width // 2 + 16, 5 * width), BF), ("e", (width // 2 + 16, 5 * width), BF),
    ]
    ins = [("l", common[0])] + [("v", x) for x in (*common[1:], bias, table, *lefts, *first, *vectors)]
    scratch = [
        pltpu.VMEM((two, size), BF), pltpu.VMEM((width, two), BF), pltpu.VMEM((8, width), F32), pltpu.VMEM((16, width), F32),
    ]
    return call(functools.partial(attention_back_kernel, pairs), outs, ins, deps, scratch, "attention_back", 12 * 10**9)


def input_grads_kernel(wq_late, wk_late, wv_late, dq_ref, dkey_ref, dvalue_ref, dresid_ref, grad_h, grad_g, sum_ref):
    length, width = grad_h.ref.shape
    wq_ref = wq_late.get()
    for col in range(0, width, 256):
        cols = slice(col, col + 256)
        low = nt(dq_ref[...], wq_ref[cols, :])
        sum_ref[:, cols] = dresid_ref[:length, cols] + low[:length]
        grad_g.ref[:, cols] = dresid_ref[length:, cols] + low[length:]
    grad_g.send()
    dkey, dvalue = dkey_ref[...].astype(F32).T.astype(BF), dvalue_ref[...].astype(F32).T.astype(BF)
    wk_ref, wv_ref = wk_late.get(), wv_late.get()
    for col in range(0, width, 256):
        cols = slice(col, col + 256)
        grad_h.ref[:, cols] = sum_ref[:, cols] + nt(dkey, wk_ref[cols, :]) + nt(dvalue, wv_ref[cols, :])
    grad_h.send()


def input_grads(wq, wk, wv, dq, dkey, dvalue, dresid, deps):
    two, width = dresid.shape
    outs = [("e", (two // 2, width), F32), ("e", (two // 2, width), F32)]
    ins = [("l", wq), ("l", wk), ("l", wv), ("v", dq), ("v", dkey), ("v", dvalue), ("v", dresid)]
    scratch = [pltpu.VMEM((two // 2, width), F32)]
    return call(input_grads_kernel, outs, ins, deps, scratch, "input_grads", 10**9)


def share_kernel(parts, up_hbm, down_hbm, bias_ref, out_ref, sem):
    rows = up_hbm.shape[0] // parts
    start = pl.multiple_of(lax.axis_index("dp") * rows, rows) if parts > 1 else 0
    one = pltpu.make_async_copy(up_hbm.at[pl.ds(start, rows)], out_ref.at[pl.ds(0, rows)], sem.at[0])
    two = pltpu.make_async_copy(down_hbm.at[pl.ds(start, rows)], out_ref.at[pl.ds(rows, rows)], sem.at[1])
    one.start()
    two.start()
    out_ref[2 * rows :, :] = jnp.broadcast_to(bias_ref[...], (16, bias_ref.shape[1]))
    one.wait()
    two.wait()


def share_slices(parts, up, down, bias):
    rows, width = up.shape[0] // parts, up.shape[1]
    outs = [("v", (2 * rows + 16, width), BF)]
    ins = [("b", up), ("b", down), ("v", bias)]
    return call(functools.partial(share_kernel, parts), outs, ins, (), [pltpu.SemaphoreType.DMA((2,))], "share_slices", 10**7)[0]


def start_pieces(pieces, piece_refs, target_ref, sem):
    copies = []
    for count, ((block, rows), source) in enumerate(zip(pieces, piece_refs, strict=True)):
        where = 0
        if rows < target_ref.shape[1]:
            where = pl.multiple_of((lax.axis_index("dp") ^ block) * rows, rows)
        copies.append(pltpu.make_async_copy(source, target_ref.at[:, pl.ds(where, rows)], sem.at[count]))
        copies[-1].start()
    return copies


def gelu_parts(pre):
    root = math.sqrt(2.0 / math.pi)
    square = pre * pre
    bend = jnp.tanh(root * pre * (1.0 + 0.044715 * square))
    upper = 0.5 + 0.5 * bend
    slope = upper + (0.5 * root) * pre * (1.0 - bend * bend) * (1.0 + (3 * 0.044715) * square)
    return (pre * upper).astype(BF), slope.astype(BF)


def feed_up_own_kernel(mid_ref, up_late, bias_ref, act_ref, slope_ref):
    width = mid_ref.shape[1]
    up_ref = up_late.get()
    for col in range(0, width, 256):
        cols = slice(col, col + 256)
        bias = bias_ref[0:1, cols].astype(F32)
        act_ref[:, cols], slope_ref[:, cols] = gelu_parts(nn(mid_ref[...], up_ref[:, cols]) + bias)


def feed_up_own(mid, up, bias, deps):
    outs = [("v", mid.shape, BF), ("v", mid.shape, BF)]
    return call(feed_up_own_kernel, outs, [("v", mid), ("l", up), ("v", bias)], deps, [], "feed_up_own", 3 * 10**9)


def feed_up_kernel(shards, pieces, rows, mid_ref, *refs):
    bias_refs, piece_refs = refs[: shards - 1], refs[shards - 1 : shards - 1 + len(pieces)]
    act_ref, slope_ref, up_ref, bias_ref, in_sem, bias_sem = refs[shards - 1 + len(pieces) :]
    width = mid_ref.shape[1]
    copies = start_pieces(pieces, piece_refs, up_ref, in_sem)
    biases = [
        pltpu.make_async_copy(ref.at[pl.ds(rows, 16)], bias_ref.at[shard], bias_sem.at[shard])
        for shard, ref in enumerate(bias_refs)
    ]
    for copy in biases:
        copy.start()
    for copy in biases:
        copy.wait()
    for copy in copies:
        copy.wait()
    for shard in range(shards - 1):
        for col in range(0, width, 256):
            cols = slice(shard * width + col, shard * width + col + 256)
            pre = nn(mid_ref[...], up_ref[shard, :, col : col + 256])
            act_ref[:, cols], slope_ref[:, cols] = gelu_parts(
                pre + bias_ref[shard, 0:1, col : col + 256].astype(F32)
            )


def feed_up(shards, mid, rows, biases, pieces, deps):
    rows_all, width = mid.shape
    hidden = (shards - 1) * width
    names = [entry[:-1] for entry in pieces]
    outs = [("v", (rows_all, hidden), BF), ("v", (rows_all, hidden), BF), ("v", (shards - 1, width, width), BF)]
    ins = [("v", mid)] + [("h", value) for value in biases] + [("h", entry[-1]) for entry in pieces]
    scratch = [
        pltpu.VMEM((shards - 1, 16, width), BF), pltpu.SemaphoreType.DMA((len(names),)), pltpu.SemaphoreType.DMA((shards - 1,)),
    ]
    return call(functools.partial(feed_up_kernel, shards, names, rows), outs, ins, deps, scratch, "feed_up", 6 * 10**9)


def feed_down_kernel(parts, shards, pieces, own_late, dh_late, dg_late, act_own, resid_ref, act_rest, *refs):
    down_bias, gain_ref, shift_ref = refs[:3]
    piece_refs = refs[3 : 3 + len(pieces)]
    out_h, out_g, dresid_ref, dbranch_ref, keep_out, send_out, vec_ref, down_ref, raw_ref, left_ref, in_sem = refs[3 + len(pieces) :]
    rows_all, width = resid_ref.shape
    length = rows_all // 2
    split = width // 2
    copies = start_pieces(pieces, piece_refs, down_ref, in_sem)
    own_down = own_late.get()
    for col in range(0, width, 256):
        cols = slice(col, col + 256)
        dresid_ref[:, cols] = nn(act_own[...], own_down[:, cols])
    for copy in copies:
        copy.wait()
    down_all = down_ref.reshape((shards - 1) * width, width)
    for col in range(0, width, 256):
        cols = slice(col, col + 256)
        dresid_ref[:, cols] += nn(act_rest[...], down_all[:, cols])
    gain_one, gain_two = gain_ref[0:1, :width], gain_ref[0:1, width:]
    shift_one, shift_two = shift_ref[0:1, :width], shift_ref[0:1, width:]
    step_rows = 32
    sums = [jnp.zeros((step_rows, width), F32)] * 3
    for row in range(0, rows_all, step_rows):
        rows = slice(row, row + step_rows)
        grad_ref = dh_late.get() if row < length else dg_late.get()
        near = row % length
        xhat_one, _ = norm_stats(resid_ref[rows, :])
        middle = xhat_one * gain_one + shift_one
        xhat, rstd = norm_stats(middle + dresid_ref[rows, :] + down_bias[...])
        out = out_h if row < length else out_g
        out.ref[near : near + step_rows, :] = (xhat * gain_two + shift_two).astype(BF)
        grad = grad_ref[near : near + step_rows, :].astype(F32)
        dresid = norm_back(grad, xhat, rstd, gain_two)
        dresid_ref[rows, :] = dresid
        dbranch = dresid.astype(BF)
        dbranch_ref[rows, :] = dbranch
        sums = [sums[0] + grad * xhat, sums[1] + grad, sums[2] + dbranch.astype(F32)]
    vec_ref[...] = jnp.zeros_like(vec_ref)
    for at, total in enumerate(sums):
        vec_ref[at : at + 1, :] = jnp.sum(total, axis=0, keepdims=True)
    out_h.send()
    out_g.send()
    turn_rows(lambda col: dbranch_ref[:, col : col + 256], raw_ref, left_ref, parts)
    for source, count, offset in ((act_own, 1, 0), (act_rest, shards - 1, width)):
        for col in range(0, count * width, 256):
            piece = nn(left_ref[...], source[:, col : col + 256]).astype(BF)
            cols = slice(col + offset, col + offset + 256)
            keep_out.ref[:, cols] = piece[:split]
            send_out.ref[:, cols] = piece[split:]
            if (col + 256) % width == 0:
                done = pl.ds(col + offset + 256 - width, width)
                send_out.send(slice(None), done)
                keep_out.send(slice(None), done)


def feed_down(parts, shards, own_down, act_own, act_rest, resid_one, down_bias, gains, shifts, dh, dg, pieces, deps):
    rows_all, width = resid_one.shape
    hidden = shards * width
    names = [entry[:-1] for entry in pieces]
    outs = [
        ("e", dh.shape, BF), ("e", dg.shape, BF), ("v", (rows_all, width), F32), ("v", (rows_all, width), BF),
        ("e", (width // 2, hidden), BF), ("e", (width // 2, hidden), BF), ("v", (8, width), F32), ("v", (shards - 1, width, width), BF),
    ]
    ins = [("l", value) for value in (own_down, dh, dg)]
    ins += [("v", value) for value in (act_own, resid_one, act_rest, down_bias, gains, shifts)] + [("h", entry[-1]) for entry in pieces]
    scratch = [pltpu.VMEM((width, rows_all), BF), pltpu.VMEM((width, rows_all), BF), pltpu.SemaphoreType.DMA((len(names),))]
    return call(functools.partial(feed_down_kernel, parts, shards, names), outs, ins, deps, scratch, "feed_down", 8 * 10**9)


def left_columns(width):
    return width // 3


def feed_back_up_kernel(
    parts, shards, own_late, mid_ref, dbranch_ref, down_ref, slope_own, slope_rest,
    dpre_ref, keep_out, send_out, dbias_ref, raw_ref, left_ref,
):
    rows_all, width = mid_ref.shape
    split, side = width // 2, left_columns(width)
    turn_rows(lambda col: mid_ref[:, col : col + 256], raw_ref, left_ref, parts)
    own_down = own_late.get()
    for shard in range(shards):
        for col in range(0, width, 256):
            cols = slice(shard * width + col, shard * width + col + 256)
            if shard:
                near = (shard - 1) * width + col
                weight, slope = down_ref[shard - 1, col : col + 256, :], slope_rest[:, near : near + 256]
            else:
                weight, slope = own_down[col : col + 256, :], slope_own[:, col : col + 256]
            dpre = (nt(dbranch_ref[...], weight) * slope.astype(F32)).astype(BF)
            dpre_ref[:, cols] = dpre
            dbias_ref[:, cols] = jnp.sum(dpre.astype(F32), axis=0, keepdims=True)
            piece = nn(left_ref[...], dpre).astype(BF)
            for at in range(col, col + 256, LANES):
                if at < side:
                    to = shard * side + at
                else:
                    to = shards * side + shard * (width - side) + at - side
                part = slice(at - col, at - col + LANES)
                keep_out.ref[:, to : to + LANES] = piece[:split, part]
                send_out.ref[:, to : to + LANES] = piece[split:, part]
        for start, size in ((shard * side, side), (shards * side + shard * (width - side), width - side)):
            done = pl.ds(start, size)
            send_out.send(slice(None), done)
            keep_out.send(slice(None), done)


def feed_back_up(parts, shards, own_down, down_rest, dbranch, mid, slope_own, slope_rest, deps):
    rows_all, width = mid.shape
    hidden = shards * width
    outs = [("v", (rows_all, hidden), BF), ("e", (width // 2, hidden), BF), ("e", (width // 2, hidden), BF), ("v", (1, hidden), F32)]
    ins = [("l", own_down)] + [("v", value) for value in (mid, dbranch, down_rest, slope_own, slope_rest)]
    scratch = [pltpu.VMEM((width, rows_all), BF), pltpu.VMEM((width, rows_all), BF)]
    return call(functools.partial(feed_back_up_kernel, parts, shards), outs, ins, deps, scratch, "feed_back_up", 8 * 10**9)


def feed_back_mid_kernel(shards, own_late, dpre_ref, up_ref, dresid_ref, resid_ref, gain_ref, dproj_ref, dresid_one_ref, vec_ref):
    rows_all, width = dresid_one_ref.shape
    own_up = own_late.get()
    for col in range(0, width, 256):
        cols = slice(col, col + 256)
        total = nt(dpre_ref[:, :width], own_up[cols, :])
        for shard in range(1, shards):
            total += nt(dpre_ref[:, shard * width : (shard + 1) * width], up_ref[shard - 1, cols, :])
        dresid_one_ref[:, cols] = total
    gain_one = gain_ref[0:1, :width]
    step_rows = 32
    sums = [jnp.zeros((step_rows, width), F32)] * 2
    for row in range(0, rows_all, step_rows):
        rows = slice(row, row + step_rows)
        xhat, rstd = norm_stats(resid_ref[rows, :])
        grad = dresid_ref[rows, :] + dresid_one_ref[rows, :]
        dresid = norm_back(grad, xhat, rstd, gain_one)
        dresid_one_ref[rows, :] = dresid
        dproj_ref[rows, :] = dresid.astype(BF)
        sums = [sums[0] + grad * xhat, sums[1] + grad]
    vec_ref[...] = jnp.zeros_like(vec_ref)
    for at, total in enumerate(sums):
        vec_ref[at : at + 1, :] = jnp.sum(total, axis=0, keepdims=True)


def feed_back_mid(shards, own_up, up_rest, dpre, dresid, resid_one, gains, deps):
    rows_all, width = resid_one.shape
    outs = [("v", (rows_all, width), BF), ("v", (rows_all, width), F32), ("v", (8, width), F32)]
    ins = [("l", own_up)] + [("v", value) for value in (dpre, up_rest, dresid, resid_one, gains)]
    return call(functools.partial(feed_back_mid_kernel, shards), outs, ins, deps, [], "feed_back_mid", 5 * 10**9)


def pack_rows_kernel(count, rows, *refs):
    one_ref, two_ref, sem = refs[count:]
    copies = [
        pltpu.make_async_copy(ref.at[pl.ds(half * rows, rows)], out.at[at], sem.at[half, at])
        for half, out in enumerate((one_ref, two_ref))
        for at, ref in enumerate(refs[:count])
    ]
    for copy in copies:
        copy.start()
    for copy in copies:
        copy.wait()


def pack_rows(arrays, rows, deps):
    outs = [("v", (len(arrays), rows, arrays[0].shape[1]), BF)] * 2
    scratch = [pltpu.SemaphoreType.DMA((2, len(arrays)))]
    kernel = functools.partial(pack_rows_kernel, len(arrays), rows)
    return call(kernel, outs, [("h", value) for value in arrays], deps, scratch, "pack_rows", 10**6)


def combine(arrays, outs, deps=(), name="combine_late"):
    outs = [(rows, cols, [(*part, 0, cols)[:5] for part in parts]) for rows, cols, parts in outs]
    ranges = {}
    for _, _, parts in outs:
        for _, count, sources, _, cols in parts:
            for source, row, col in sources:
                low, high = ranges.get((source, row, count), (col, col + cols))
                ranges[source, row, count] = (min(low, col), max(high, col + cols))
    buffers = [pltpu.VMEM((count, high - low), BF) for (_, _, count), (low, high) in ranges.items()]

    def kernel(*refs):
        out_refs = refs[len(arrays) : len(arrays) + len(outs)]
        *held, sem = refs[len(arrays) + len(outs) :]
        copies = {}
        for at, ((source, row, count), (low, high)) in enumerate(ranges.items()):
            piece = refs[source].at[pl.ds(row, count), pl.ds(low, high - low)]
            copies[source, row, count] = (pltpu.make_async_copy(piece, held[at], sem.at[at]), held[at], low)
            copies[source, row, count][0].start()
        waited = set()
        for (_, _, parts), out_ref in zip(outs, out_refs, strict=True):
            for first, count, sources, to, cols in parts:
                values = []
                for source, row, col in sources:
                    copy, buffer, low = copies[source, row, count]
                    if (source, row, count) not in waited:
                        copy.wait()
                        waited.add((source, row, count))
                    values.append(buffer[:, col - low : col - low + cols])
                out_ref[first : first + count, to : to + cols] = add_all(values).astype(BF)

    shapes = [("v", (rows, cols), BF) for rows, cols, _ in outs]
    scratch = [*buffers, pltpu.SemaphoreType.DMA((len(buffers),))]
    return call(kernel, shapes, [("b", value) for value in arrays], deps, scratch, name, 10**9 if name == "combine_left" else 10**6)


def regroup_kernel(shards, keep_ref, core_ref, first_a, first_b, second_a, second_b, *refs):
    outs, (held_wide, held_a, held_b, group_ref, sem, out_sem) = refs[:shards], refs[shards:]
    rows, total = held_wide.shape[1] - 16, held_wide.shape[2]
    width = total // 5
    part = width // shards
    copies = [
        pltpu.make_async_copy(ref.at[pl.ds(0, rows)], held.at[pl.ds(0, rows)], sem.at[at])
        for at, (ref, held) in enumerate(
            (
                (keep_ref, held_wide.at[0]), (core_ref, held_wide.at[1]), (first_a, held_a.at[0]), (first_b, held_b.at[0]),
                (second_a, held_a.at[1]), (second_b, held_b.at[1]),
            )
        )
    ]
    copies += [
        pltpu.make_async_copy(ref.at[pl.ds(ref.shape[0] - 16, 16)], held.at[pl.ds(rows, 16)], sem.at[6 + at])
        for at, (ref, held) in enumerate(
            ((keep_ref, held_wide.at[0]), (core_ref, held_wide.at[1]), (first_a, held_a.at[0]), (second_a, held_a.at[1]))
        )
    ]
    for copy in copies:
        copy.start()
    for copy in copies:
        copy.wait()
    sums = []
    for half, held in enumerate((held_a, held_b)):
        cols = slice(half * total // 2, (half + 1) * total // 2)
        value = held_wide[0, :rows, cols].astype(F32) + held_wide[1, :rows, cols].astype(F32)
        sums.append(value + held[0, :rows].astype(F32) + held[1, :rows].astype(F32))
    whole = jnp.concatenate(sums, axis=1)
    vectors = [held[at, rows:, :width].astype(F32) for held in (held_wide, held_a) for at in (0, 1)]
    vectors = add_all(vectors).astype(BF)
    for shard in range(shards):
        for slot in range(5):
            at = slot * width + shard * part
            group_ref[shard, :rows, slot * part : (slot + 1) * part] = whole[:, at : at + part].astype(BF)
        group_ref[shard, rows:, :width] = vectors
        group_ref[shard, rows:, width:] = jnp.zeros((16, 5 * part - width), BF)
    me = lax.axis_index("tensor")
    backs = [pltpu.make_async_copy(group_ref.at[me ^ bits], outs[bits], out_sem.at[bits]) for bits in range(shards)]
    for back in backs:
        back.start()
    for back in backs:
        back.wait()


def regroup(shards, keep, core, first, second, deps=()):
    total = keep.shape[1]
    rows = second[0].shape[0]
    shape = (rows, total // shards)
    scratch = [
        pltpu.VMEM((2, rows, total), BF), pltpu.VMEM((2, rows, total // 2), BF), pltpu.VMEM((2, rows, total // 2), BF),
        pltpu.VMEM((shards, *shape), BF), pltpu.SemaphoreType.DMA((10,)), pltpu.SemaphoreType.DMA((shards,)),
    ]
    ins = [("b", value) for value in (keep, core, *first, *second)]
    outs = [("v", shape, BF)] * shards
    return call(functools.partial(regroup_kernel, shards), outs, ins, deps, scratch, "regroup", 10**6)


class Exchange:
    def __init__(self, width):
        self.data = lax.axis_size("dp")
        self.tensor = lax.axis_size("tensor")
        self.by_hand = self.data == 8 and width % (32 * self.data) == 0
        self.blocks = self.data if self.by_hand else 1

    def data_swap(self, value, bit):
        pairs = [(at, at ^ bit) for at in range(self.data)]
        return lax.ppermute(value, "dp", pairs)

    def tensor_swap(self, value, bits):
        pairs = [(at, at ^ bits) for at in range(self.tensor)]
        return lax.ppermute(value, "tensor", pairs)


def add_low(left, right):
    return (left.astype(F32) + right.astype(F32)).astype(BF)


class Share:
    def __init__(self, swap, rows, first):
        self.swap, self.rows, self.first = swap, rows, first
        self.count = swap.tensor - 1

    def spread(self, packed):
        self.found = [(0, packed)]
        if self.swap.blocks > 1:
            bits = [1 << at for at in range(1, self.swap.data.bit_length() - 1)]
            mine = self.found[0][1]
            self.near = [(bit, self.swap.data_swap(mine, bit)) for bit in bits]
            self.found += self.near

    def cross(self):
        if self.swap.data == 8 and self.swap.blocks == 8:
            other = 6 - self.first
            self.found.append((6, self.swap.data_swap(dict(self.near)[self.first], other)))

    def finish(self):
        found = list(self.found)
        if self.swap.blocks > 1:
            found += [(block | 1, self.swap.data_swap(value, 1)) for block, value in self.found]
        return [(block, self.rows, value) for block, value in found]


def add_all(terms):
    total = terms[0].astype(F32)
    for term in terms[1:]:
        total += term.astype(F32)
    return total


def tensor_sum(swap, parts):
    return add_all([parts[0]] + [swap.tensor_swap(parts[bits], bits) for bits in range(1, swap.tensor)])


def per_device(
    h_in, g_in, seg_ids, target_flags, perm_order, w_query, w_key, w_value, w_out, w_rel, attn_bias, seg_embed,
    norm_gain, norm_bias, w_up, b_up, w_down, b_down, d_h_out, d_g_out,
):
    seq_count, length, width = h_in.shape
    assert seq_count == 1
    swap = Exchange(width)
    parts, shards = swap.blocks, swap.tensor
    by_hand = swap.by_hand
    dp_at, tensor_at = lax.axis_index("dp"), lax.axis_index("tensor")
    own_part = width // shards
    rel_host = rel_table(length, width)
    rel, rev = jnp.asarray(rel_host), jnp.asarray(np.ascontiguousarray(rel_host[::-1]))
    h, g = h_in[0], g_in[0]
    up, down = w_up[0], w_down[0]
    bias, table = attn_bias.reshape(1, -1), seg_embed.reshape(1, -1)
    gains, shifts = norm_gain.reshape(1, -1), norm_bias.reshape(1, -1)

    mine = share_slices(parts, up, down, b_up)
    rows = (mine.shape[0] - 16) // 2
    fetched = [swap.tensor_swap(mine, bits) for bits in range(1, shards)]
    share_up, share_down = Share(swap, rows, 2), Share(swap, rows, 4)
    q, key, value, relkey, mask, half, relrev, left_x, left_rev = project(
        parts, h, g, seg_ids, target_flags, perm_order, w_query[0], w_key[0], w_value[0], w_rel[0], rel, rev, ()
    )
    att_one, prob_one = attention_first(q, key, value, relkey, mask, half, bias, table, ())
    packed_up, packed_down = pack_rows(fetched, rows, [att_one])
    share_up.spread(packed_up)
    share_down.spread(packed_down)
    resid_one, mid, prob_two, att, left_att = attention_second(
        parts, w_out[0], h, g, q, key, value, relkey, mask, half, att_one, bias, table, gains, shifts,
        [share_up.found[0][1], share_down.found[0][1]],
    )
    share_up.cross()
    act_own, slope_own = feed_up_own(mid, up, b_up, [found for _, found in share_up.found[:3]])
    share_down.cross()
    act_rest, slope_rest, up_rest = feed_up(
        shards, mid, 2 * rows, fetched, share_up.finish(), [found for _, found in share_down.found]
    )
    out_h, out_g, dresid_two, dbranch, keep_down, send_down, vec_two, down_rest = feed_down(
        parts, shards, down, act_own, act_rest, resid_one, b_down, gains, shifts, d_h_out[0], d_g_out[0],
        share_down.finish(), (),
    )

    hidden, wide = shards * width, 5 * width
    block, middle = width // 8, width // 4
    size = (10 + shards) * width

    def first_far(keep, core, deps, name):
        cut = keep.shape[1] // 2
        odd = [(at, block, [(0, block + 2 * at, 0), (1, block + 2 * at, 0)]) for at in (0, block)]
        upper = [(0, middle, [(0, middle, cut), (1, middle, cut)])]
        more = keep.shape[0] - 2 * middle
        if more:
            odd.append((middle, more, [(0, 2 * middle, 0), (1, 2 * middle, 0)]))
        return combine([keep, core], [(middle + more, cut, odd), (middle, cut, upper)], deps, name)

    def first_swap(far):
        return swap.data_swap(far[0], 2), swap.data_swap(far[1], 4)

    def second_far(keep, core, first, deps, name):
        cut = keep.shape[1] // 2
        more = keep.shape[0] - 2 * middle
        upper = [(0, block, [(0, middle, 0), (1, middle, 0), (2, block, 0)])]
        if more:
            upper.append((block, more, [(0, 2 * middle, 0), (1, 2 * middle, 0), (2, middle, 0)]))
        return combine(
            [keep, core, *first],
            [
                (block + more, cut, upper),
                (block, cut, [(0, block, [(0, block, cut), (1, block, cut), (3, block, 0)])]),
            ],
            deps,
            name,
        )

    def second_swap(far):
        return swap.data_swap(far[0], 4), swap.data_swap(far[1], 2)

    if by_hand:
        core_down = swap.data_swap(send_down, 1)
    dpre, keep_up, send_up, dbias_up = feed_back_up(parts, shards, down, down_rest, dbranch, mid, slope_own, slope_rest, ())
    deps = ()
    if by_hand:
        core_up = swap.data_swap(send_up, 1)
        far_down = first_far(keep_down, core_down, (), "combine")
        first_down = first_swap(far_down)
        side = left_columns(width)
        rest = width - side
        cut, quarter = shards * side, shards * rest // 2
        odd = [(at, block, [(0, block + 2 * at, cut), (1, block + 2 * at, cut)]) for at in (0, block)]
        far_up = combine(
            [keep_up, core_up],
            [
                *((2 * middle, side, [(0, 2 * middle, [(0, 0, k * side), (1, 0, k * side)])]) for k in range(1, shards)),
                (middle, quarter, odd),
                (middle, quarter, [(0, middle, [(0, middle, cut + quarter), (1, middle, cut + quarter)])]),
            ],
            far_down,
            "combine",
        )
        came_up = [swap.tensor_swap(far_up[bits - 1], bits) for bits in range(1, shards)]
        first_up = first_swap(far_up[-2:])
        deps = far_up[-1:]
    dproj, dresid_one, vec_one = feed_back_mid(shards, up, up_rest, dpre, dresid_two, resid_one, gains, deps)
    common = (w_out[0], dproj, q, att, key, value, prob_one, prob_two, relrev, half)
    back_first = attention_back_first(tuple(range(PAIRS // 2)), common, bias, table, ())
    deps = ()
    if by_hand:
        far_down = second_far(keep_down, core_down, first_down, back_first[-1:], "combine")
        second_down = second_swap(far_down)
        deps = far_down
    dq, dkey, dvalue, keep_att, send_att = attention_back(
        tuple(range(PAIRS // 2, PAIRS)), common, (left_x, left_rev, left_att), back_first, (vec_one, vec_two, dbias_up),
        bias, table, [*deps, *came_up] if by_hand else deps,
    )
    if by_hand:
        (send_att, keep_att), (first_up, second_down) = lax.optimization_barrier(
            ((send_att, keep_att), (first_up, second_down))
        )
        core_att = swap.data_swap(send_att, 1)
        all_up = [keep_up, core_up, *came_up]
        left = range(len(all_up))
        far_up = combine(
            [*all_up, *first_up],
            [
                (block, quarter, [(0, block, [(0, middle, cut), (1, middle, cut), (shards + 1, block, 0)])]),
                (block, quarter, [(0, block, [(0, block, cut + quarter), (1, block, cut + quarter), (shards + 2, block, 0)])]),
                (middle, side, [(0, middle, [(at, middle, 0) for at in left])]),
            ],
        )
        second_up = second_swap(far_up[:2])
        left_y = swap.data_swap(far_up[2], 4)
        far_att = first_far(keep_att, core_att, second_up, "combine_late")
        first_att = first_swap(far_att)
        arrays = [keep_down, core_down, *first_down, *second_down, *all_up, *first_up, *second_up]
        up_at, per, outs = 6, shards // 2, []
        half_at = up_at + len(all_up)
        for k in range(shards):
            half, near = k // per, k % per
            outs.append(
                (
                    block,
                    width + rest,
                    [
                        (0, block, [(0, 0, k * width), (1, 0, k * width), (2 + half, 0, near * width), (4 + half, 0, near * width)],
                         0, width),
                        (0, block, [(up_at, 0, cut + k * rest), (up_at + 1, 0, cut + k * rest), (half_at + half, 0, near * rest),
                                    (half_at + 2 + half, 0, near * rest)], width, rest),
                    ],
                )
            )
        feed_parts = combine(arrays, outs, far_att)
        came = [swap.tensor_swap(feed_parts[bits], bits) for bits in range(1, shards)]
        grad_h, grad_g = input_grads(w_query[0], w_key[0], w_value[0], dq, dkey, dvalue, dresid_one, feed_parts[:1])
        far_att = second_far(keep_att, core_att, first_att, [*came[:1], grad_h], "combine_att")
        second_att = second_swap(far_att)
        left_own, far_left = combine(
            [*all_up, left_y],
            [(block, side, [(0, block, [(at, row, 0) for at in range(shards + 2)])]) for row in (0, block)],
            [*far_att],
            "combine_left",
        )
        left_x = swap.data_swap(far_left, 2)
        att_parts = regroup(shards, keep_att, core_att, first_att, second_att, came)
    else:
        grad_h, grad_g = input_grads(w_query[0], w_key[0], w_value[0], dq, dkey, dvalue, dresid_one, ())
        vectors = lax.psum(keep_att[width // 2 : width // 2 + 10 + shards, :width].astype(F32), AXES)
        keep_att, send_att = keep_att[: width // 2], send_att[: width // 2]

        def rows_sum(keep, send):
            whole = jnp.concatenate([keep, send], axis=0)
            return lax.psum_scatter(whole, "dp", scatter_dimension=0, tiled=True)

        sum_up, sum_down, sum_att = (
            rows_sum(keep, send) for keep, send in ((keep_up, send_up), (keep_down, send_down), (keep_att, send_att))
        )
        cols = [slice(shard * width, (shard + 1) * width) for shard in range(shards)]
        side = left_columns(width)
        left, right = sum_up[:, : shards * side], sum_up[:, shards * side :]
        rest = width - side
        d_up = [
            jnp.concatenate([left[:, k * side : (k + 1) * side], right[:, k * rest : (k + 1) * rest]], axis=1)
            for k in range(shards)
        ]
        d_up = tensor_sum(swap, d_up)
        d_down = tensor_sum(swap, [sum_down[:, part] for part in cols]).T
        split = sum_att.reshape(-1, 5, shards, own_part).transpose(2, 0, 1, 3).reshape(shards, -1, 5 * own_part)
        att_parts = [lax.dynamic_index_in_dim(split, tensor_at ^ bits, 0, keepdims=False) for bits in range(shards)]
    att_parts = [att_parts[0]] + [swap.tensor_swap(att_parts[bits], bits) for bits in range(1, shards)]
    if by_hand:
        came, _ = lax.optimization_barrier((came, att_parts[1]))
        d_feed = add_all([feed_parts[0], *came])
        d_up = jnp.concatenate([add_all([left_own, left_x]), d_feed[:, width:]], axis=1)
        d_down = d_feed[:, :width].T
    d_att = add_all(att_parts)
    if by_hand:
        d_att, vectors = d_att[:block], d_att[block : block + 10 + shards, :width]
    d_att = [d_att[:, slot * own_part : (slot + 1) * own_part] for slot in range(5)]

    own = size // (swap.data * shards)
    d_vectors = lax.dynamic_slice_in_dim(vectors.reshape(-1), (dp_at * shards + tensor_at) * own, own, 0)

    return (
        out_h[None], out_g[None], grad_h[None], grad_g[None],
        d_att[0][None], d_att[1][None], d_att[2][None], d_att[3][None], d_att[4][None],
        d_up[None], d_down[None], d_vectors[None],
    )


def solution(mesh):
    every = P(AXES, None, None)
    rows = P(AXES, None)
    in_specs = (
        every, every, rows, rows, rows, P(), P(), P(), P(), P(), P(), P(), P(), P(),
        P(None, None, "tensor"), P(None, "tensor"), P(None, "tensor", None), P(), every, every,
    )
    grads = P(None, "dp", "tensor")
    out_specs = (
        every, every, every, every, grads, grads, grads, grads, grads, grads,
        P(None, "tensor", "dp"), P(None, AXES),
    )
    return jax.shard_map(per_device, mesh=mesh, in_specs=in_specs, out_specs=out_specs, check_vma=False)
```

```python
import functools
import math

import jax
import jax.numpy as jnp
import numpy as np
from jax import lax
from jax.experimental import pallas as pl
from jax.experimental.pallas import tpu as pltpu
from jax.sharding import PartitionSpec as P

HEADS = 12
HEAD_DIM = 64
LANES = 128
PAIRS = HEADS // 2
NEGATIVE = -1e30
EPSILON = 1e-06
AXES = ("dp", "tensor")
BF = jnp.bfloat16
F32 = jnp.float32
FIRST_PAIRS = 4
VMEM_MIB = {
    "share_slices": 60, "project": 50, "attention_first": 12, "attention_second": 14, "feed_up_own": 6, "feed_up": 14, "feed_down": 22,
    "feed_back_up": 16, "feed_back_mid": 10, "attention_back_first": 18, "attention_back": 26, "input_grads": 14, "pack_rows": 2,
    "combine": 12, "combine_late": 12, "combine_att": 59, "combine_left": 59, "regroup": 59,
}


def rel_table(length, model_width):
    position = (length - np.arange(2 * length)).astype(np.float32)
    frequency = np.float32(1.0) / np.float32(10000.0) ** (
        np.arange(0, model_width, 2).astype(np.float32) / np.float32(model_width)
    )
    angles = position[:, None] * frequency[None, :]
    return np.concatenate([np.sin(angles), np.cos(angles)], axis=1).astype(BF)


class Late:
    def __init__(self, source, target, sem):
        self.target, self.waiting = target, True
        self.copy = pltpu.make_async_copy(source, target, sem)
        self.copy.start()

    def get(self):
        if self.waiting:
            self.copy.wait()
            self.waiting = False
        return self.target


class Early:
    def __init__(self, ref, target, sems):
        self.ref, self.target, self.sems, self.copies = ref, target, sems, []

    def send(self, *where):
        source, target = (self.ref.at[where], self.target.at[where]) if where else (self.ref, self.target)
        copy = pltpu.make_async_copy(source, target, self.sems.at[len(self.copies)])
        copy.start()
        self.copies.append(copy)


SENDS = 16


def call(kernel, outs, ins, deps, scratch, name, flops):
    deps = tuple(deps)
    spaces = {"s": pltpu.SMEM, "v": pltpu.VMEM, "h": pl.ANY, "l": pltpu.HBM, "e": pltpu.HBM, "b": pltpu.HBM}
    late = [value for kind, value in ins if kind == "l"]
    early = [(shape, dtype) for kind, shape, dtype in outs if kind == "e"]
    more = [pltpu.VMEM(value.shape, value.dtype) for value in late] + [pltpu.VMEM(*spec) for spec in early]
    if late:
        more.append(pltpu.SemaphoreType.DMA((len(late),)))
    if early:
        more.append(pltpu.SemaphoreType.DMA((len(early), SENDS)))
    first_out = len(ins) + len(deps)
    first_scratch = first_out + len(outs)

    def wrapped(*refs):
        own = refs[first_scratch + len(scratch) :]
        late_refs, early_refs = own[: len(late)], own[len(late) : len(late) + len(early)]
        sems = list(own[len(late) + len(early) :])
        late_sem = sems.pop(0) if late else None
        early_sem = sems.pop(0) if early else None
        given, at = [], 0
        for (kind, _), ref in zip(ins, refs[: len(ins)], strict=True):
            if kind == "l":
                ref = Late(ref, late_refs[at], late_sem.at[at])
                at += 1
            given.append(ref)
        made, at = [], 0
        for (kind, _, _), ref in zip(outs, refs[first_out:first_scratch], strict=True):
            if kind == "e":
                ref = Early(early_refs[at], ref, early_sem.at[at])
                at += 1
            made.append(ref)
        kernel(*given, *made, *refs[first_scratch : first_scratch + len(scratch)])
        for item in given:
            if isinstance(item, Late):
                item.get()
        for item in made:
            if isinstance(item, Early):
                for copy in item.copies:
                    copy.wait()

    return pl.pallas_call(
        wrapped,
        out_shape=[jax.ShapeDtypeStruct(shape, dtype) for _, shape, dtype in outs],
        in_specs=[pl.BlockSpec(memory_space=spaces[kind]) for kind, _ in ins]
        + [pl.BlockSpec(memory_space=pl.ANY)] * len(deps),
        out_specs=[pl.BlockSpec(memory_space=spaces[kind]) for kind, _, _ in outs],
        scratch_shapes=list(scratch) + more,
        compiler_params=pltpu.CompilerParams(vmem_limit_bytes=VMEM_MIB[name] * 1024 * 1024),
        cost_estimate=pl.CostEstimate(flops=flops * 100, bytes_accessed=flops // 1000, transcendentals=0),
        name=name,
    )(*[value for _, value in ins], *deps)


def nn(left, right):
    return lax.dot_general(left, right, (((1,), (0,)), ((), ())), preferred_element_type=F32)


def nt(left, right):
    return lax.dot_general(left, right, (((1,), (1,)), ((), ())), preferred_element_type=F32)


def tn(left, right):
    return lax.dot_general(left, right, (((0,), (0,)), ((), ())), preferred_element_type=F32)


def lane_index(rows):
    return lax.broadcasted_iota(jnp.int32, (rows, LANES), 1)


def pair_lanes(pair):
    return pl.ds(pl.multiple_of(pair * LANES, LANES), LANES)


def row_lanes(row, pair, width):
    return pl.ds(pl.multiple_of(row * width + pair * LANES, LANES), LANES)


def norm_stats(source):
    mean = jnp.mean(source, axis=-1, keepdims=True)
    centered = source - mean
    variance = jnp.mean(centered * centered, axis=-1, keepdims=True)
    rstd = lax.rsqrt(variance + EPSILON)
    return centered * rstd, rstd


def norm_back(grad, xhat, rstd, gain):
    dxhat = grad * gain
    mean_one = jnp.mean(dxhat, axis=-1, keepdims=True)
    mean_two = jnp.mean(dxhat * xhat, axis=-1, keepdims=True)
    return rstd * (dxhat - mean_one - xhat * mean_two)


def seg_coefficients(half_wide, lane):
    return jnp.where(lane % HEAD_DIM == 0, half_wide, 1.0 - 2.0 * half_wide)


def seg_keys(half_wide, lane):
    place = lane % HEAD_DIM
    return jnp.where(place == 0, 1.0, jnp.where(place == 1, half_wide, 0.0))


def seg_table(seg_ref, pair, width):
    row = lax.broadcasted_iota(jnp.int32, (LANES, LANES), 0)
    lane = lax.broadcasted_iota(jnp.int32, (LANES, LANES), 1)
    one = jnp.broadcast_to(seg_ref[0:1, pair_lanes(pair)], (LANES, LANES)).T
    two = jnp.broadcast_to(seg_ref[0:1, row_lanes(1, pair, width)], (LANES, LANES)).T
    base = jnp.where(row < HEAD_DIM, HEAD_DIM, 0)
    at_one = lane == base
    at_two = at_one | (lane == base + 1)
    return jnp.concatenate([jnp.where(at_one, one, 0.0), jnp.where(at_two, two - one, 0.0)], axis=1).astype(BF)


def attend_pair(pair, first, q_ref, key_ref, value_ref, relkey_ref, mask_ref, half_ref, bias_ref, seg_ref, prob_ref, att_ref):
    length, width = key_ref.shape
    block = length // 2
    lanes = pair_lanes(pair)
    lane_q = lane_index(2 * length)
    lane_k = lane_index(length)
    low_q = lane_q < HEAD_DIM
    low_k = lane_k < HEAD_DIM
    half_w = half_ref[...]
    scale = 1.0 / math.sqrt(HEAD_DIM)
    query = q_ref[:, lanes]
    word = ((query + bias_ref[0:1, lanes]) * scale).astype(BF)
    relq = ((query + bias_ref[0:1, row_lanes(1, pair, width)]) * scale).astype(BF)
    segq = ((query + bias_ref[0:1, row_lanes(2, pair, width)]) * scale).astype(BF)
    terms = nn(segq, seg_table(seg_ref, pair, width))
    coef = seg_coefficients(jnp.concatenate([half_w, half_w], axis=0), lane_q)
    extra = (terms[:, :LANES] + terms[:, LANES:] * coef).astype(BF)
    key_extra = seg_keys(half_w, lane_k).astype(BF)
    key = key_ref[:, lanes]
    value = value_ref[:, lanes]
    zero = jnp.zeros_like(relq)
    attended = []
    for head in (0, 1):
        if head == 0:
            word_one = jnp.where(low_q, word, extra)
            key_one = jnp.where(low_k, key, key_extra)
            rel_one = jnp.where(low_q, relq, zero)
        else:
            word_one = jnp.where(low_q, extra, word)
            key_one = jnp.where(low_k, key_extra, key)
            rel_one = jnp.where(low_q, zero, relq)
        score = nt(word_one, key_one)
        for part in (0, 1):
            base = block - block * part
            rows_h = slice(block * part, block * part + block)
            rows_g = slice(length + block * part, length + block * part + block)
            rel_rows = jnp.concatenate([rel_one[rows_h], rel_one[rows_g]], axis=0)
            raw = nt(rel_rows, relkey_ref[base : base + 3 * block, lanes])
            for place_at, rows in ((0, rows_h), (1, rows_g)):
                shifted = pltpu.roll(
                    raw[place_at * block : (place_at + 1) * block], 2 * block, 1, stride=1, stride_axis=0
                )[:, :length]
                logits = score[rows] + shifted + mask_ref[rows]
                top = jnp.max(logits, axis=1, keepdims=True)
                power = jnp.exp(logits - top)
                total = jnp.sum(power, axis=1, keepdims=True)
                prob_ref[2 * (pair - first) + head, rows, :] = (power * (1.0 / total)).astype(BF)
        attended.append(nn(prob_ref[2 * (pair - first) + head], value))
    att_ref[:, lanes] = jnp.where(low_q, attended[0], attended[1]).astype(BF)


def project_kernel(
    parts, h_late, g_late, wq_late, wk_late, wv_late, rel_late, wr_late, rev_late,
    seg_row, flag_row, order_row,
    q_ref, key_ref, value_ref, relkey_ref, mask_ref, half_ref, relrev_out, left_x_out, left_rev_out,
    x_ref, raw_ref,
):
    h_ref, g_ref = h_late.get(), g_late.get()
    length, width = h_ref.shape
    x_ref[:length] = h_ref[...]
    x_ref[length:] = g_ref[...]

    def project(left, right_late, target):
        right = right_late.get()
        for col in range(0, width, 256):
            cols = slice(col, col + 256)
            target[:, cols] = nn(left[...], right[:, cols]).astype(target.dtype)

    project(x_ref, wq_late, q_ref)
    project(h_ref, wk_late, key_ref)
    project(h_ref, wv_late, value_ref)
    project(rel_late.get(), wr_late, relkey_ref)

    def wide(row_ref):
        return jnp.broadcast_to(row_ref[...].astype(F32), (length, length))

    row_at = lax.broadcasted_iota(jnp.int32, (length, length), 0)
    col_at = lax.broadcasted_iota(jnp.int32, (length, length), 1)
    seg, order = wide(seg_row), wide(order_row)
    same_doc = seg.T == seg
    start = jnp.min(jnp.where(same_doc, col_at.astype(F32), float(length)), axis=1, keepdims=True)
    in_doc = jnp.sum(jnp.where(same_doc, 1.0, 0.0), axis=1, keepdims=True)
    place = lax.broadcasted_iota(jnp.int32, (length, 1), 0).astype(F32)
    half = jnp.where(2.0 * (place - start) >= in_doc, 1.0, 0.0)
    half_ref[...] = jnp.broadcast_to(half, (length, LANES))
    content = same_doc & ((wide(flag_row) == 0.0) | (order <= order.T))
    mask_ref[:length] = jnp.where(content, 0.0, NEGATIVE)
    mask_ref[length:] = jnp.where(content & (row_at != col_at), 0.0, NEGATIVE)

    project(rev_late.get(), wr_late, relrev_out.ref)
    relrev_out.send()
    turn_rows(lambda col: x_ref[:, col : col + 256], raw_ref.at[0], left_x_out.ref, parts)
    left_x_out.send()
    rev_ref = rev_late.get()
    turn_rows(lambda col: rev_ref[:, col : col + 256], raw_ref.at[1], left_rev_out.ref, parts)
    left_rev_out.send()


def project(parts, h, g, seg, flag, order, wq, wk, wv, wr, rel, rev, deps):
    length, width = h.shape
    two = 2 * length
    outs = [
        ("v", (two, width), F32), ("v", (length, width), BF), ("v", (length, width), BF), ("v", (two, width), BF),
        ("v", (two, length), F32), ("v", (length, LANES), F32), ("e", (two, width), BF), ("e", (width, two), BF),
        ("e", (width, two), BF),
    ]
    ins = [("l", value) for value in (h, g, wq, wk, wv, rel, wr, rev)] + [("v", value) for value in (seg, flag, order)]
    scratch = [pltpu.VMEM((two, width), BF), pltpu.VMEM((2, width, two), BF)]
    return call(functools.partial(project_kernel, parts), outs, ins, deps, scratch, "project", 5 * 10**9)


def attention_first_kernel(
    q_ref, key_ref, value_ref, relkey_ref, mask_ref, half_ref, bias_ref, seg_ref, att_ref, prob_out
):
    def pair_step(pair, carry):
        attend_pair(
            pair, 0, q_ref, key_ref, value_ref, relkey_ref, mask_ref, half_ref, bias_ref, seg_ref, prob_out.ref, att_ref
        )
        return carry

    for first in range(0, FIRST_PAIRS, 2):
        lax.fori_loop(first, first + 2, pair_step, 0)
        prob_out.send(pl.ds(2 * first, 4))


def attention_first(q, key, value, relkey, mask, half, bias, table, deps):
    two, length = mask.shape
    outs = [("v", (two, FIRST_PAIRS * LANES), BF), ("e", (2 * FIRST_PAIRS, two, length), BF)]
    ins = [("v", x) for x in (q, key, value, relkey, mask, half, bias, table)]
    return call(attention_first_kernel, outs, ins, deps, [], "attention_first", 5 * 10**9)


def attention_second_kernel(
    parts, wo_late, h_late, g_late, q_ref, key_ref, value_ref, relkey_ref, mask_ref, half_ref, att_first_ref,
    bias_ref, seg_ref, gain_ref, shift_ref,
    resid_ref, mid_ref, prob_out, att_out, left_att_out,
    raw_ref,
):
    length, width = key_ref.shape
    att_ref = att_out.ref
    att_ref[:, : FIRST_PAIRS * LANES] = att_first_ref[...]

    def pair_step(pair, carry):
        attend_pair(
            pair, FIRST_PAIRS, q_ref, key_ref, value_ref, relkey_ref, mask_ref, half_ref, bias_ref, seg_ref, prob_out.ref, att_ref
        )
        return carry

    for first in range(FIRST_PAIRS, PAIRS, 2):
        lax.fori_loop(first, first + 2, pair_step, 0)
        prob_out.send(pl.ds(2 * (first - FIRST_PAIRS), 4))
    att_out.send()
    wo_ref, h_ref, g_ref = wo_late.get(), h_late.get(), g_late.get()
    for col in range(0, width, 256):
        cols = slice(col, col + 256)
        total = nn(att_ref[...], wo_ref[:, cols])
        resid_ref[:length, cols] = h_ref[:, cols].astype(F32) + total[:length]
        resid_ref[length:, cols] = g_ref[:, cols].astype(F32) + total[length:]
    turn_rows(lambda col: att_ref[:, col : col + 256], raw_ref, left_att_out.ref, parts)
    left_att_out.send()
    for row in range(0, 2 * length, 64):
        xhat, _ = norm_stats(resid_ref[row : row + 64, :])
        mid_ref[row : row + 64, :] = (xhat * gain_ref[0:1, :width] + shift_ref[0:1, :width]).astype(BF)


def attention_second(parts, wo, h, g, q, key, value, relkey, mask, half, att, bias, table, gain, shift, deps):
    length, width = h.shape
    two = 2 * length
    outs = [
        ("v", (two, width), F32), ("v", (two, width), BF), ("e", (HEADS - 2 * FIRST_PAIRS, two, length), BF),
        ("e", (two, width), BF), ("e", (width, two), BF),
    ]
    ins = [("l", value) for value in (wo, h, g)]
    ins += [("v", value) for value in (q, key, value, relkey, mask, half, att, bias, table, gain, shift)]
    return call(
        functools.partial(attention_second_kernel, parts), outs, ins, deps, [pltpu.VMEM((width, two), BF)],
        "attention_second", 10 * 10**9,
    )


def place_rows(raw_ref, out_ref, parts):
    rows = raw_ref.shape[0] // parts
    me = lax.axis_index("dp") if parts > 1 else 0
    order = [low | (rest << 1) for low in (0, 1) for rest in range(parts // 2)] if parts > 1 else [0]
    for at, block in enumerate(order):
        source = pl.multiple_of((me ^ block) * rows, rows)
        out_ref[at * rows : (at + 1) * rows, :] = raw_ref[pl.ds(source, rows), :]


def turn_rows(source, raw_ref, out_ref, parts):
    for col in range(0, raw_ref.shape[0], 256):
        raw_ref[col : col + 256, :] = source(col).astype(F32).T.astype(BF)
    place_rows(raw_ref, out_ref, parts)


def back_pairs(
    pairs, dproj_ref, wo_ref, q_ref, att_ref, key_ref, value_ref, prob_one, prob_two, relrev_ref, half_ref, bias_ref, seg_ref,
    dq_ref, dkey_ref, dvalue_ref, drel_ref, vec_ref, datt_ref,
):
    length, width = key_ref.shape
    block = length // 2
    for at, pair in enumerate(pairs):
        rows = slice(pair * LANES, (pair + 1) * LANES)
        datt_ref[:, at * LANES : (at + 1) * LANES] = nt(dproj_ref[...], wo_ref[rows, :]).astype(BF)

    def pair_step(at, pair):
        lanes = slice(pair * LANES, (pair + 1) * LANES)
        own = slice(at * LANES, (at + 1) * LANES)
        prob_ref, prob_at = (prob_one, 2 * pair) if pair < FIRST_PAIRS else (prob_two, 2 * (pair - FIRST_PAIRS))
        lane_q = lane_index(2 * length)
        lane_k = lane_index(length)
        low_q = lane_q < HEAD_DIM
        low_k = lane_k < HEAD_DIM
        half_w = half_ref[...]
        flip_row = lax.broadcasted_iota(jnp.int32, (length, length), 0)
        flip_col = lax.broadcasted_iota(jnp.int32, (length, length), 1)
        flip = jnp.where(flip_row + flip_col == length - 1, 1.0, 0.0).astype(BF)
        sel_row = lax.broadcasted_iota(jnp.int32, (2 * LANES, LANES), 0) % LANES
        sel_col = lax.broadcasted_iota(jnp.int32, (2 * LANES, LANES), 1)
        select = jnp.where(
            ((sel_row < HEAD_DIM) & ((sel_col == HEAD_DIM) | (sel_col == HEAD_DIM + 1)))
            | ((sel_row >= HEAD_DIM) & (sel_col < 2)),
            1.0,
            0.0,
        ).astype(BF)
        query = q_ref[:, lanes]
        word = query + bias_ref[0:1, lanes]
        relq = query + bias_ref[0:1, row_lanes(1, pair, width)]
        segq = (query + bias_ref[0:1, row_lanes(2, pair, width)]).astype(BF)
        word_t = word.T.astype(BF)
        relq_t = relq.T.astype(BF)
        datt = datt_ref[:, own]
        datt_wide = datt.astype(F32)
        datt_t = datt_wide.T.astype(BF)
        datt_scaled = datt_wide * (1.0 / math.sqrt(HEAD_DIM))
        product = datt_scaled * att_ref[:, lanes].astype(F32)
        product_high = product.astype(BF)
        product_low = (product - product_high.astype(F32)).astype(BF)
        delta = nn(jnp.concatenate([product_high, product_low], axis=1), select)
        delta_high = delta.astype(BF).astype(F32)
        minus = jnp.where(lane_q % HEAD_DIM == 0, -delta_high, delta_high - delta).astype(BF)
        datt_low = datt_scaled.astype(BF)
        key_extra = seg_keys(half_w, lane_k).astype(BF)
        ones_extra = jnp.where(lane_k % HEAD_DIM < 2, 1.0, 0.0).astype(BF)
        key = key_ref[:, lanes]
        value = value_ref[:, lanes]
        dword, drel = [], []
        for head in (0, 1):
            rows_t = slice(HEAD_DIM * head, HEAD_DIM * head + HEAD_DIM)
            if head == 0:
                datt_one = jnp.where(low_q, datt_low, minus)
                value_one = jnp.where(low_k, value, ones_extra)
                key_one = jnp.where(low_k, key, key_extra)
            else:
                datt_one = jnp.where(low_q, minus, datt_low)
                value_one = jnp.where(low_k, ones_extra, value)
                key_one = jnp.where(low_k, key_extra, key)
            prob = prob_ref[prob_at + head]
            dprob = nt(datt_one, value_one)
            dscore = (prob.astype(F32) * dprob).astype(BF)
            dword.append(nn(dscore, key_one))
            rows_out = slice(at * LANES + HEAD_DIM * head, at * LANES + HEAD_DIM * (head + 1))
            dkey_ref[rows_out, :] = nn(word_t[rows_t], dscore).astype(BF)
            dvalue_ref[rows_out, :] = nn(datt_t[rows_t], prob).astype(BF)
            flipped = nn(dscore, flip).astype(BF)
            pad = jnp.zeros((block, block), BF)
            rel_parts, drel_t = [], []
            for part in (0, 1):
                rows_h = slice(block * part, block * part + block)
                rows_g = slice(length + block * part, length + block * part + block)
                draw = jnp.concatenate(
                    [
                        pltpu.roll(jnp.concatenate([flipped[rows], pad], axis=1), 0, 1, stride=1, stride_axis=0)
                        for rows in (rows_h, rows_g)
                    ],
                    axis=0,
                )
                rel_parts.append(nn(draw, relrev_ref[block * part : block * part + 3 * block, lanes]))
                rel_cols = jnp.concatenate([relq_t[rows_t, rows_h], relq_t[rows_t, rows_g]], axis=1)
                drel_t.append(nn(rel_cols, draw))
            drel.append(
                jnp.concatenate(
                    [rel_parts[0][:block], rel_parts[1][:block], rel_parts[0][block:], rel_parts[1][block:]], axis=0
                )
            )
            drel_ref[rows_out, :] = jnp.concatenate(
                [
                    drel_t[0][:, :block],
                    drel_t[0][:, block:] + drel_t[1][:, : 2 * block],
                    drel_t[1][:, 2 * block :],
                ],
                axis=1,
            ).astype(BF)
        extra = jnp.where(low_q, dword[1], dword[0])
        dword_all = jnp.where(low_q, dword[0], dword[1])
        drel_all = jnp.where(low_q, drel[0], drel[1])
        coef = seg_coefficients(jnp.concatenate([half_w, half_w], axis=0), lane_q)
        dterms = jnp.concatenate([extra, extra * coef], axis=1).astype(BF)
        dsegq = nt(dterms, seg_table(seg_ref, pair, width))
        dtable = tn(dterms, segq)
        dq_ref[:, own] = (dword_all + drel_all + dsegq).astype(BF)
        low_one = lane_index(1) < HEAD_DIM
        first = jnp.where(low_one, dtable[HEAD_DIM : HEAD_DIM + 1], dtable[0:1])
        far = LANES + HEAD_DIM
        second = jnp.where(
            low_one, dtable[far : far + 1] + dtable[far + 1 : far + 2], dtable[LANES : LANES + 1] + dtable[LANES + 1 : LANES + 2]
        )
        vec_ref[0:1, own] = jnp.sum(dword_all, axis=0, keepdims=True)
        vec_ref[1:2, own] = jnp.sum(drel_all, axis=0, keepdims=True)
        vec_ref[2:3, own] = jnp.sum(dsegq, axis=0, keepdims=True)
        vec_ref[3:4, own] = first - second
        vec_ref[4:5, own] = second
    for at, pair in enumerate(pairs):
        pair_step(at, pair)


def attention_back_first_kernel(
    pairs, wo_late, dproj_ref, q_ref, att_ref, key_ref, value_ref, prob_one, prob_two, relrev_ref, half_ref, bias_ref, seg_ref,
    dq_ref, dkey_ref, dvalue_ref, drel_ref, vec_ref, datt_ref,
):
    vec_ref[...] = jnp.zeros_like(vec_ref)
    back_pairs(
        pairs, dproj_ref, wo_late.get(), q_ref, att_ref, key_ref, value_ref, prob_one, prob_two, relrev_ref, half_ref, bias_ref,
        seg_ref, dq_ref, dkey_ref, dvalue_ref, drel_ref, vec_ref, datt_ref,
    )


def attention_back_first(pairs, common, bias, table, deps):
    two, width = common[1].shape
    length, size = two // 2, len(pairs) * LANES
    outs = [
        ("v", (two, size), BF), ("v", (size, length), BF), ("v", (size, length), BF), ("v", (size, two), BF), ("v", (8, size), F32),
    ]
    ins = [("l", common[0])] + [("v", x) for x in (*common[1:], bias, table)]
    kernel = functools.partial(attention_back_first_kernel, pairs)
    return call(kernel, outs, ins, deps, [pltpu.VMEM((two, size), BF)], "attention_back_first", 12 * 10**9)


def attention_back_kernel(
    pairs, wo_late, dproj_ref, q_ref, att_ref, key_ref, value_ref, prob_one, prob_two, relrev_ref, half_ref, bias_ref, seg_ref,
    left_x_ref, left_rev_ref, left_att_ref, dq_one, dkey_one, dvalue_one, drel_one, vec_one, norm_one, norm_two, hidden_ref,
    dq_ref, dkey_ref, dvalue_ref, keep_out, send_out, datt_ref, drel_ref, vec_ref, packed_ref,
):
    length, width = key_ref.shape
    split = width // 2
    size = dq_one.shape[1]
    dq_ref[:, :size], dkey_ref[:size], dvalue_ref[:size], drel_ref[:size] = dq_one[...], dkey_one[...], dvalue_one[...], drel_one[...]
    vec_ref[...] = jnp.zeros_like(vec_ref)
    vec_ref[:, :size] = vec_one[...]
    back_pairs(
        pairs, dproj_ref, wo_late.get(), q_ref, att_ref, key_ref, value_ref, prob_one, prob_two, relrev_ref, half_ref, bias_ref,
        seg_ref, dq_ref.at[:, size:], dkey_ref.at[size:], dvalue_ref.at[size:], drel_ref.at[size:], vec_ref.at[:, size:], datt_ref,
    )
    shards = hidden_ref.shape[1] // width
    packed_ref[...] = jnp.zeros_like(packed_ref)
    packed_ref[0:5, :] = vec_ref[0:5, :]
    packed_ref[5:6, :] = norm_one[0:1, :]
    packed_ref[6:7, :] = norm_two[0:1, :]
    packed_ref[7:8, :] = norm_one[1:2, :]
    packed_ref[8:10, :] = norm_two[1:3, :]
    for shard in range(shards):
        place = 10 + (lax.axis_index("tensor") ^ shard)
        packed_ref[pl.ds(place, 1), :] = hidden_ref[0:1, shard * width : (shard + 1) * width]
    packed = packed_ref[...].astype(BF)
    for out in (send_out, keep_out):
        out.ref[split:, :width] = packed
        out.ref[split:, width:] = jnp.zeros((16, 4 * width), BF)
        out.send(pl.ds(split, 16))
    todo = [
        (left_x_ref[...], dq_ref, nn), (left_x_ref[:, :length], dkey_ref, nt), (left_x_ref[:, :length], dvalue_ref, nt),
        (left_att_ref[...], dproj_ref, nn), (left_rev_ref[...], drel_ref, nt),
    ]
    at = 0
    for left, right, dot in todo:
        count = right.shape[1] if dot is nn else right.shape[0]
        for col in range(0, count, 256):
            cols = slice(col, col + 256)
            piece = dot(left, right[:, cols] if dot is nn else right[cols, :]).astype(BF)
            keep_out.ref[:split, at + col : at + col + 256] = piece[:split]
            send_out.ref[:split, at + col : at + col + 256] = piece[split:]
        done = pl.ds(at, count)
        send_out.send(pl.ds(0, split), done)
        keep_out.send(pl.ds(0, split), done)
        at += count


def attention_back(pairs, common, lefts, first, vectors, bias, table, deps):
    two, width = common[1].shape
    length, size = two // 2, len(pairs) * LANES
    outs = [
        ("v", (two, width), BF), ("v", (width, length), BF), ("v", (width, length), BF),
        ("e", (width // 2 + 16, 5 * width), BF), ("e", (width // 2 + 16, 5 * width), BF),
    ]
    ins = [("l", common[0])] + [("v", x) for x in (*common[1:], bias, table, *lefts, *first, *vectors)]
    scratch = [
        pltpu.VMEM((two, size), BF), pltpu.VMEM((width, two), BF), pltpu.VMEM((8, width), F32), pltpu.VMEM((16, width), F32),
    ]
    return call(functools.partial(attention_back_kernel, pairs), outs, ins, deps, scratch, "attention_back", 12 * 10**9)


def input_grads_kernel(wq_late, wk_late, wv_late, dq_ref, dkey_ref, dvalue_ref, dresid_ref, grad_h, grad_g, sum_ref):
    length, width = grad_h.ref.shape
    wq_ref = wq_late.get()
    for col in range(0, width, 256):
        cols = slice(col, col + 256)
        low = nt(dq_ref[...], wq_ref[cols, :])
        sum_ref[:, cols] = dresid_ref[:length, cols] + low[:length]
        grad_g.ref[:, cols] = dresid_ref[length:, cols] + low[length:]
    grad_g.send()
    dkey, dvalue = dkey_ref[...].astype(F32).T.astype(BF), dvalue_ref[...].astype(F32).T.astype(BF)
    wk_ref, wv_ref = wk_late.get(), wv_late.get()
    for col in range(0, width, 256):
        cols = slice(col, col + 256)
        grad_h.ref[:, cols] = sum_ref[:, cols] + nt(dkey, wk_ref[cols, :]) + nt(dvalue, wv_ref[cols, :])
    grad_h.send()


def input_grads(wq, wk, wv, dq, dkey, dvalue, dresid, deps):
    two, width = dresid.shape
    outs = [("e", (two // 2, width), F32), ("e", (two // 2, width), F32)]
    ins = [("l", wq), ("l", wk), ("l", wv), ("v", dq), ("v", dkey), ("v", dvalue), ("v", dresid)]
    scratch = [pltpu.VMEM((two // 2, width), F32)]
    return call(input_grads_kernel, outs, ins, deps, scratch, "input_grads", 10**9)


def share_kernel(parts, up_hbm, down_hbm, bias_ref, out_ref, sem):
    rows = up_hbm.shape[0] // parts
    start = pl.multiple_of(lax.axis_index("dp") * rows, rows) if parts > 1 else 0
    one = pltpu.make_async_copy(up_hbm.at[pl.ds(start, rows)], out_ref.at[pl.ds(0, rows)], sem.at[0])
    two = pltpu.make_async_copy(down_hbm.at[pl.ds(start, rows)], out_ref.at[pl.ds(rows, rows)], sem.at[1])
    one.start()
    two.start()
    out_ref[2 * rows :, :] = jnp.broadcast_to(bias_ref[...], (16, bias_ref.shape[1]))
    one.wait()
    two.wait()


def share_slices(parts, up, down, bias):
    rows, width = up.shape[0] // parts, up.shape[1]
    outs = [("v", (2 * rows + 16, width), BF)]
    ins = [("b", up), ("b", down), ("v", bias)]
    return call(functools.partial(share_kernel, parts), outs, ins, (), [pltpu.SemaphoreType.DMA((2,))], "share_slices", 10**7)[0]


def start_pieces(pieces, piece_refs, target_ref, sem):
    copies = []
    for count, ((block, rows), source) in enumerate(zip(pieces, piece_refs, strict=True)):
        where = 0
        if rows < target_ref.shape[1]:
            where = pl.multiple_of((lax.axis_index("dp") ^ block) * rows, rows)
        copies.append(pltpu.make_async_copy(source, target_ref.at[:, pl.ds(where, rows)], sem.at[count]))
        copies[-1].start()
    return copies


def gelu_parts(pre):
    root = math.sqrt(2.0 / math.pi)
    square = pre * pre
    bend = jnp.tanh(root * pre * (1.0 + 0.044715 * square))
    upper = 0.5 + 0.5 * bend
    slope = upper + (0.5 * root) * pre * (1.0 - bend * bend) * (1.0 + (3 * 0.044715) * square)
    return (pre * upper).astype(BF), slope.astype(BF)


def feed_up_own_kernel(mid_ref, up_late, bias_ref, act_ref, slope_ref):
    width = mid_ref.shape[1]
    up_ref = up_late.get()
    for col in range(0, width, 256):
        cols = slice(col, col + 256)
        bias = bias_ref[0:1, cols].astype(F32)
        act_ref[:, cols], slope_ref[:, cols] = gelu_parts(nn(mid_ref[...], up_ref[:, cols]) + bias)


def feed_up_own(mid, up, bias, deps):
    outs = [("v", mid.shape, BF), ("v", mid.shape, BF)]
    return call(feed_up_own_kernel, outs, [("v", mid), ("l", up), ("v", bias)], deps, [], "feed_up_own", 3 * 10**9)


def feed_up_kernel(shards, pieces, rows, mid_ref, *refs):
    bias_refs, piece_refs = refs[: shards - 1], refs[shards - 1 : shards - 1 + len(pieces)]
    act_ref, slope_ref, up_ref, bias_ref, in_sem, bias_sem = refs[shards - 1 + len(pieces) :]
    width = mid_ref.shape[1]
    copies = start_pieces(pieces, piece_refs, up_ref, in_sem)
    biases = [
        pltpu.make_async_copy(ref.at[pl.ds(rows, 16)], bias_ref.at[shard], bias_sem.at[shard])
        for shard, ref in enumerate(bias_refs)
    ]
    for copy in biases:
        copy.start()
    for copy in biases:
        copy.wait()
    for copy in copies:
        copy.wait()
    for shard in range(shards - 1):
        for col in range(0, width, 256):
            cols = slice(shard * width + col, shard * width + col + 256)
            pre = nn(mid_ref[...], up_ref[shard, :, col : col + 256])
            act_ref[:, cols], slope_ref[:, cols] = gelu_parts(
                pre + bias_ref[shard, 0:1, col : col + 256].astype(F32)
            )


def feed_up(shards, mid, rows, biases, pieces, deps):
    rows_all, width = mid.shape
    hidden = (shards - 1) * width
    names = [entry[:-1] for entry in pieces]
    outs = [("v", (rows_all, hidden), BF), ("v", (rows_all, hidden), BF), ("v", (shards - 1, width, width), BF)]
    ins = [("v", mid)] + [("h", value) for value in biases] + [("h", entry[-1]) for entry in pieces]
    scratch = [
        pltpu.VMEM((shards - 1, 16, width), BF), pltpu.SemaphoreType.DMA((len(names),)), pltpu.SemaphoreType.DMA((shards - 1,)),
    ]
    return call(functools.partial(feed_up_kernel, shards, names, rows), outs, ins, deps, scratch, "feed_up", 6 * 10**9)


def feed_down_kernel(parts, shards, pieces, own_down, dh_ref, dg_ref, act_own, resid_ref, act_rest, *refs):
    down_bias, gain_ref, shift_ref = refs[:3]
    piece_refs = refs[3 : 3 + len(pieces)]
    out_h, out_g, dresid_ref, dbranch_ref, keep_out, send_out, vec_ref, down_ref, raw_ref, left_ref, in_sem = refs[3 + len(pieces) :]
    rows_all, width = resid_ref.shape
    length = rows_all // 2
    split = width // 2
    copies = start_pieces(pieces, piece_refs, down_ref, in_sem)
    for col in range(0, width, 256):
        cols = slice(col, col + 256)
        dresid_ref[:, cols] = nn(act_own[...], own_down[:, cols])
    for copy in copies:
        copy.wait()
    down_all = down_ref.reshape((shards - 1) * width, width)
    for col in range(0, width, 256):
        cols = slice(col, col + 256)
        dresid_ref[:, cols] += nn(act_rest[...], down_all[:, cols])
    gain_one, gain_two = gain_ref[0:1, :width], gain_ref[0:1, width:]
    shift_one, shift_two = shift_ref[0:1, :width], shift_ref[0:1, width:]
    step_rows = 32
    sums = [jnp.zeros((step_rows, width), F32)] * 3
    for row in range(0, rows_all, step_rows):
        rows = slice(row, row + step_rows)
        grad_ref = dh_ref if row < length else dg_ref
        near = row % length
        xhat_one, _ = norm_stats(resid_ref[rows, :])
        middle = xhat_one * gain_one + shift_one
        xhat, rstd = norm_stats(middle + dresid_ref[rows, :] + down_bias[...])
        out = out_h if row < length else out_g
        out.ref[near : near + step_rows, :] = (xhat * gain_two + shift_two).astype(BF)
        grad = grad_ref[near : near + step_rows, :].astype(F32)
        dresid = norm_back(grad, xhat, rstd, gain_two)
        dresid_ref[rows, :] = dresid
        dbranch = dresid.astype(BF)
        dbranch_ref[rows, :] = dbranch
        sums = [sums[0] + grad * xhat, sums[1] + grad, sums[2] + dbranch.astype(F32)]
    vec_ref[...] = jnp.zeros_like(vec_ref)
    for at, total in enumerate(sums):
        vec_ref[at : at + 1, :] = jnp.sum(total, axis=0, keepdims=True)
    out_h.send()
    out_g.send()
    turn_rows(lambda col: dbranch_ref[:, col : col + 256], raw_ref, left_ref, parts)
    for source, count, offset in ((act_own, 1, 0), (act_rest, shards - 1, width)):
        for col in range(0, count * width, 256):
            piece = nn(left_ref[...], source[:, col : col + 256]).astype(BF)
            cols = slice(col + offset, col + offset + 256)
            keep_out.ref[:, cols] = piece[:split]
            send_out.ref[:, cols] = piece[split:]
            if (col + 256) % width == 0:
                done = pl.ds(col + offset + 256 - width, width)
                send_out.send(slice(None), done)
                keep_out.send(slice(None), done)


def feed_down(parts, shards, own_down, act_own, act_rest, resid_one, down_bias, gains, shifts, dh, dg, pieces, deps):
    rows_all, width = resid_one.shape
    hidden = shards * width
    names = [entry[:-1] for entry in pieces]
    outs = [
        ("e", dh.shape, BF), ("e", dg.shape, BF), ("v", (rows_all, width), F32), ("v", (rows_all, width), BF),
        ("e", (width // 2, hidden), BF), ("e", (width // 2, hidden), BF), ("v", (8, width), F32), ("v", (shards - 1, width, width), BF),
    ]
    ins = [("v", own_down), ("v", dh), ("v", dg)]
    ins += [("v", value) for value in (act_own, resid_one, act_rest, down_bias, gains, shifts)] + [("h", entry[-1]) for entry in pieces]
    scratch = [pltpu.VMEM((width, rows_all), BF), pltpu.VMEM((width, rows_all), BF), pltpu.SemaphoreType.DMA((len(names),))]
    return call(functools.partial(feed_down_kernel, parts, shards, names), outs, ins, deps, scratch, "feed_down", 8 * 10**9)


def left_columns(width):
    return width // 3


def feed_back_up_kernel(
    parts, shards, own_down, mid_ref, dbranch_ref, down_ref, slope_own, slope_rest,
    dpre_ref, keep_out, send_out, dbias_ref, raw_ref, left_ref,
):
    rows_all, width = mid_ref.shape
    split, side = width // 2, left_columns(width)
    turn_rows(lambda col: mid_ref[:, col : col + 256], raw_ref, left_ref, parts)
    for shard in range(shards):
        for col in range(0, width, 256):
            cols = slice(shard * width + col, shard * width + col + 256)
            if shard:
                near = (shard - 1) * width + col
                weight, slope = down_ref[shard - 1, col : col + 256, :], slope_rest[:, near : near + 256]
            else:
                weight, slope = own_down[col : col + 256, :], slope_own[:, col : col + 256]
            dpre = (nt(dbranch_ref[...], weight) * slope.astype(F32)).astype(BF)
            dpre_ref[:, cols] = dpre
            dbias_ref[:, cols] = jnp.sum(dpre.astype(F32), axis=0, keepdims=True)
            piece = nn(left_ref[...], dpre).astype(BF)
            for at in range(col, col + 256, LANES):
                if at < side:
                    to = shard * side + at
                else:
                    to = shards * side + shard * (width - side) + at - side
                part = slice(at - col, at - col + LANES)
                keep_out.ref[:, to : to + LANES] = piece[:split, part]
                send_out.ref[:, to : to + LANES] = piece[split:, part]
        for start, size in ((shard * side, side), (shards * side + shard * (width - side), width - side)):
            done = pl.ds(start, size)
            send_out.send(slice(None), done)
            keep_out.send(slice(None), done)


def feed_back_up(parts, shards, own_down, down_rest, dbranch, mid, slope_own, slope_rest, deps):
    rows_all, width = mid.shape
    hidden = shards * width
    outs = [("v", (rows_all, hidden), BF), ("e", (width // 2, hidden), BF), ("e", (width // 2, hidden), BF), ("v", (1, hidden), F32)]
    ins = [("v", own_down)] + [("v", value) for value in (mid, dbranch, down_rest, slope_own, slope_rest)]
    scratch = [pltpu.VMEM((width, rows_all), BF), pltpu.VMEM((width, rows_all), BF)]
    return call(functools.partial(feed_back_up_kernel, parts, shards), outs, ins, deps, scratch, "feed_back_up", 8 * 10**9)


def feed_back_mid_kernel(shards, own_late, dpre_ref, up_ref, dresid_ref, resid_ref, gain_ref, dproj_ref, dresid_one_ref, vec_ref):
    rows_all, width = dresid_one_ref.shape
    own_up = own_late.get()
    for col in range(0, width, 256):
        cols = slice(col, col + 256)
        total = nt(dpre_ref[:, :width], own_up[cols, :])
        for shard in range(1, shards):
            total += nt(dpre_ref[:, shard * width : (shard + 1) * width], up_ref[shard - 1, cols, :])
        dresid_one_ref[:, cols] = total
    gain_one = gain_ref[0:1, :width]
    step_rows = 32
    sums = [jnp.zeros((step_rows, width), F32)] * 2
    for row in range(0, rows_all, step_rows):
        rows = slice(row, row + step_rows)
        xhat, rstd = norm_stats(resid_ref[rows, :])
        grad = dresid_ref[rows, :] + dresid_one_ref[rows, :]
        dresid = norm_back(grad, xhat, rstd, gain_one)
        dresid_one_ref[rows, :] = dresid
        dproj_ref[rows, :] = dresid.astype(BF)
        sums = [sums[0] + grad * xhat, sums[1] + grad]
    vec_ref[...] = jnp.zeros_like(vec_ref)
    for at, total in enumerate(sums):
        vec_ref[at : at + 1, :] = jnp.sum(total, axis=0, keepdims=True)


def feed_back_mid(shards, own_up, up_rest, dpre, dresid, resid_one, gains, deps):
    rows_all, width = resid_one.shape
    outs = [("v", (rows_all, width), BF), ("v", (rows_all, width), F32), ("v", (8, width), F32)]
    ins = [("l", own_up)] + [("v", value) for value in (dpre, up_rest, dresid, resid_one, gains)]
    return call(functools.partial(feed_back_mid_kernel, shards), outs, ins, deps, [], "feed_back_mid", 5 * 10**9)


def pack_rows_kernel(count, rows, *refs):
    one_ref, two_ref, sem = refs[count:]
    copies = [
        pltpu.make_async_copy(ref.at[pl.ds(half * rows, rows)], out.at[at], sem.at[half, at])
        for half, out in enumerate((one_ref, two_ref))
        for at, ref in enumerate(refs[:count])
    ]
    for copy in copies:
        copy.start()
    for copy in copies:
        copy.wait()


def pack_rows(arrays, rows, deps):
    outs = [("v", (len(arrays), rows, arrays[0].shape[1]), BF)] * 2
    scratch = [pltpu.SemaphoreType.DMA((2, len(arrays)))]
    kernel = functools.partial(pack_rows_kernel, len(arrays), rows)
    return call(kernel, outs, [("h", value) for value in arrays], deps, scratch, "pack_rows", 10**6)


def combine(arrays, outs, deps=(), name="combine_late"):
    outs = [(rows, cols, [(*part, 0, cols)[:5] for part in parts]) for rows, cols, parts in outs]
    ranges = {}
    for _, _, parts in outs:
        for _, count, sources, _, cols in parts:
            for source, row, col in sources:
                low, high = ranges.get((source, row, count), (col, col + cols))
                ranges[source, row, count] = (min(low, col), max(high, col + cols))
    buffers = [pltpu.VMEM((count, high - low), BF) for (_, _, count), (low, high) in ranges.items()]

    def kernel(*refs):
        out_refs = refs[len(arrays) : len(arrays) + len(outs)]
        *held, sem = refs[len(arrays) + len(outs) :]
        copies = {}
        for at, ((source, row, count), (low, high)) in enumerate(ranges.items()):
            piece = refs[source].at[pl.ds(row, count), pl.ds(low, high - low)]
            copies[source, row, count] = (pltpu.make_async_copy(piece, held[at], sem.at[at]), held[at], low)
            copies[source, row, count][0].start()
        waited = set()
        for (_, _, parts), out_ref in zip(outs, out_refs, strict=True):
            for first, count, sources, to, cols in parts:
                values = []
                for source, row, col in sources:
                    copy, buffer, low = copies[source, row, count]
                    if (source, row, count) not in waited:
                        copy.wait()
                        waited.add((source, row, count))
                    values.append(buffer[:, col - low : col - low + cols])
                out_ref[first : first + count, to : to + cols] = add_all(values).astype(BF)

    shapes = [("v", (rows, cols), BF) for rows, cols, _ in outs]
    scratch = [*buffers, pltpu.SemaphoreType.DMA((len(buffers),))]
    return call(kernel, shapes, [("b", value) for value in arrays], deps, scratch, name, 10**9 if name == "combine_left" else 10**6)


def regroup_kernel(shards, keep_ref, core_ref, first_a, first_b, second_a, second_b, *refs):
    outs, (held_wide, held_a, held_b, group_ref, sem, out_sem) = refs[:shards], refs[shards:]
    rows, total = held_wide.shape[1] - 16, held_wide.shape[2]
    width = total // 5
    part = width // shards
    copies = [
        pltpu.make_async_copy(ref.at[pl.ds(0, rows)], held.at[pl.ds(0, rows)], sem.at[at])
        for at, (ref, held) in enumerate(
            (
                (keep_ref, held_wide.at[0]), (core_ref, held_wide.at[1]), (first_a, held_a.at[0]), (first_b, held_b.at[0]),
                (second_a, held_a.at[1]), (second_b, held_b.at[1]),
            )
        )
    ]
    copies += [
        pltpu.make_async_copy(ref.at[pl.ds(ref.shape[0] - 16, 16)], held.at[pl.ds(rows, 16)], sem.at[6 + at])
        for at, (ref, held) in enumerate(
            ((keep_ref, held_wide.at[0]), (core_ref, held_wide.at[1]), (first_a, held_a.at[0]), (second_a, held_a.at[1]))
        )
    ]
    for copy in copies:
        copy.start()
    for copy in copies:
        copy.wait()
    sums = []
    for half, held in enumerate((held_a, held_b)):
        cols = slice(half * total // 2, (half + 1) * total // 2)
        value = held_wide[0, :rows, cols].astype(F32) + held_wide[1, :rows, cols].astype(F32)
        sums.append(value + held[0, :rows].astype(F32) + held[1, :rows].astype(F32))
    whole = jnp.concatenate(sums, axis=1)
    vectors = [held[at, rows:, :width].astype(F32) for held in (held_wide, held_a) for at in (0, 1)]
    vectors = add_all(vectors).astype(BF)
    for shard in range(shards):
        for slot in range(5):
            at = slot * width + shard * part
            group_ref[shard, :rows, slot * part : (slot + 1) * part] = whole[:, at : at + part].astype(BF)
        group_ref[shard, rows:, :width] = vectors
        group_ref[shard, rows:, width:] = jnp.zeros((16, 5 * part - width), BF)
    me = lax.axis_index("tensor")
    backs = [pltpu.make_async_copy(group_ref.at[me ^ bits], outs[bits], out_sem.at[bits]) for bits in range(shards)]
    for back in backs:
        back.start()
    for back in backs:
        back.wait()


def regroup(shards, keep, core, first, second, deps=()):
    total = keep.shape[1]
    rows = second[0].shape[0]
    shape = (rows, total // shards)
    scratch = [
        pltpu.VMEM((2, rows, total), BF), pltpu.VMEM((2, rows, total // 2), BF), pltpu.VMEM((2, rows, total // 2), BF),
        pltpu.VMEM((shards, *shape), BF), pltpu.SemaphoreType.DMA((10,)), pltpu.SemaphoreType.DMA((shards,)),
    ]
    ins = [("b", value) for value in (keep, core, *first, *second)]
    outs = [("b", shape, BF)] * shards
    return call(functools.partial(regroup_kernel, shards), outs, ins, deps, scratch, "regroup", 10**6)


class Exchange:
    def __init__(self, width):
        self.data = lax.axis_size("dp")
        self.tensor = lax.axis_size("tensor")
        self.by_hand = self.data == 8 and width % (32 * self.data) == 0
        self.blocks = self.data if self.by_hand else 1

    def data_swap(self, value, bit):
        pairs = [(at, at ^ bit) for at in range(self.data)]
        return lax.ppermute(value, "dp", pairs)

    def tensor_swap(self, value, bits):
        pairs = [(at, at ^ bits) for at in range(self.tensor)]
        return lax.ppermute(value, "tensor", pairs)


def add_low(left, right):
    return (left.astype(F32) + right.astype(F32)).astype(BF)


class Share:
    def __init__(self, swap, rows, first):
        self.swap, self.rows, self.first = swap, rows, first
        self.count = swap.tensor - 1

    def spread(self, packed):
        self.found = [(0, packed)]
        if self.swap.blocks > 1:
            bits = [1 << at for at in range(1, self.swap.data.bit_length() - 1)]
            mine = self.found[0][1]
            self.near = [(bit, self.swap.data_swap(mine, bit)) for bit in bits]
            self.found += self.near

    def cross(self):
        if self.swap.data == 8 and self.swap.blocks == 8:
            other = 6 - self.first
            self.found.append((6, self.swap.data_swap(dict(self.near)[self.first], other)))

    def finish(self):
        found = list(self.found)
        if self.swap.blocks > 1:
            found += [(block | 1, self.swap.data_swap(value, 1)) for block, value in self.found]
        return [(block, self.rows, value) for block, value in found]


def add_all(terms):
    total = terms[0].astype(F32)
    for term in terms[1:]:
        total += term.astype(F32)
    return total


def tensor_sum(swap, parts):
    return add_all([parts[0]] + [swap.tensor_swap(parts[bits], bits) for bits in range(1, swap.tensor)])


def per_device(
    h_in, g_in, seg_ids, target_flags, perm_order, w_query, w_key, w_value, w_out, w_rel, attn_bias, seg_embed,
    norm_gain, norm_bias, w_up, b_up, w_down, b_down, d_h_out, d_g_out,
):
    seq_count, length, width = h_in.shape
    assert seq_count == 1
    swap = Exchange(width)
    parts, shards = swap.blocks, swap.tensor
    by_hand = swap.by_hand
    dp_at, tensor_at = lax.axis_index("dp"), lax.axis_index("tensor")
    own_part = width // shards
    rel_host = rel_table(length, width)
    rel, rev = jnp.asarray(rel_host), jnp.asarray(np.ascontiguousarray(rel_host[::-1]))
    h, g = h_in[0], g_in[0]
    up, down = w_up[0], w_down[0]
    bias, table = attn_bias.reshape(1, -1), seg_embed.reshape(1, -1)
    gains, shifts = norm_gain.reshape(1, -1), norm_bias.reshape(1, -1)

    mine = share_slices(parts, up, down, b_up)
    rows = (mine.shape[0] - 16) // 2
    fetched = [swap.tensor_swap(mine, bits) for bits in range(1, shards)]
    share_up, share_down = Share(swap, rows, 2), Share(swap, rows, 4)
    q, key, value, relkey, mask, half, relrev, left_x, left_rev = project(
        parts, h, g, seg_ids, target_flags, perm_order, w_query[0], w_key[0], w_value[0], w_rel[0], rel, rev, ()
    )
    att_one, prob_one = attention_first(q, key, value, relkey, mask, half, bias, table, ())
    packed_up, packed_down = pack_rows(fetched, rows, [att_one])
    share_up.spread(packed_up)
    share_down.spread(packed_down)
    resid_one, mid, prob_two, att, left_att = attention_second(
        parts, w_out[0], h, g, q, key, value, relkey, mask, half, att_one, bias, table, gains, shifts,
        [share_up.found[0][1], share_down.found[0][1]],
    )
    share_up.cross()
    act_own, slope_own = feed_up_own(mid, up, b_up, [found for _, found in share_up.found[:3]])
    share_down.cross()
    act_rest, slope_rest, up_rest = feed_up(
        shards, mid, 2 * rows, fetched, share_up.finish(), [found for _, found in share_down.found]
    )
    out_h, out_g, dresid_two, dbranch, keep_down, send_down, vec_two, down_rest = feed_down(
        parts, shards, down, act_own, act_rest, resid_one, b_down, gains, shifts, d_h_out[0], d_g_out[0],
        share_down.finish(), (),
    )

    hidden, wide = shards * width, 5 * width
    block, middle = width // 8, width // 4
    size = (10 + shards) * width

    def first_far(keep, core, deps, name):
        cut = keep.shape[1] // 2
        odd = [(at, block, [(0, block + 2 * at, 0), (1, block + 2 * at, 0)]) for at in (0, block)]
        upper = [(0, middle, [(0, middle, cut), (1, middle, cut)])]
        more = keep.shape[0] - 2 * middle
        if more:
            odd.append((middle, more, [(0, 2 * middle, 0), (1, 2 * middle, 0)]))
        return combine([keep, core], [(middle + more, cut, odd), (middle, cut, upper)], deps, name)

    def first_swap(far):
        return swap.data_swap(far[0], 2), swap.data_swap(far[1], 4)

    def second_far(keep, core, first, deps, name):
        cut = keep.shape[1] // 2
        more = keep.shape[0] - 2 * middle
        upper = [(0, block, [(0, middle, 0), (1, middle, 0), (2, block, 0)])]
        if more:
            upper.append((block, more, [(0, 2 * middle, 0), (1, 2 * middle, 0), (2, middle, 0)]))
        return combine(
            [keep, core, *first],
            [
                (block + more, cut, upper),
                (block, cut, [(0, block, [(0, block, cut), (1, block, cut), (3, block, 0)])]),
            ],
            deps,
            name,
        )

    def second_swap(far):
        return swap.data_swap(far[0], 4), swap.data_swap(far[1], 2)

    if by_hand:
        core_down = swap.data_swap(send_down, 1)
    dpre, keep_up, send_up, dbias_up = feed_back_up(parts, shards, down, down_rest, dbranch, mid, slope_own, slope_rest, ())
    deps = ()
    if by_hand:
        core_up = swap.data_swap(send_up, 1)
        far_down = first_far(keep_down, core_down, (), "combine")
        first_down = first_swap(far_down)
        side = left_columns(width)
        rest = width - side
        cut, quarter = shards * side, shards * rest // 2
        odd = [(at, block, [(0, block + 2 * at, cut), (1, block + 2 * at, cut)]) for at in (0, block)]
        far_up = combine(
            [keep_up, core_up],
            [
                *((2 * middle, side, [(0, 2 * middle, [(0, 0, k * side), (1, 0, k * side)])]) for k in range(1, shards)),
                (middle, quarter, odd),
                (middle, quarter, [(0, middle, [(0, middle, cut + quarter), (1, middle, cut + quarter)])]),
            ],
            far_down,
            "combine",
        )
        came_up = [swap.tensor_swap(far_up[bits - 1], bits) for bits in range(1, shards)]
        first_up = first_swap(far_up[-2:])
        deps = far_up[-1:]
    dproj, dresid_one, vec_one = feed_back_mid(shards, up, up_rest, dpre, dresid_two, resid_one, gains, deps)
    common = (w_out[0], dproj, q, att, key, value, prob_one, prob_two, relrev, half)
    back_first = attention_back_first(tuple(range(PAIRS // 2)), common, bias, table, ())
    deps = ()
    if by_hand:
        far_down = second_far(keep_down, core_down, first_down, back_first[-1:], "combine")
        second_down = second_swap(far_down)
        deps = far_down
    dq, dkey, dvalue, keep_att, send_att = attention_back(
        tuple(range(PAIRS // 2, PAIRS)), common, (left_x, left_rev, left_att), back_first, (vec_one, vec_two, dbias_up),
        bias, table, [*deps, *came_up] if by_hand else deps,
    )
    if by_hand:
        (send_att, keep_att), (first_up, second_down) = lax.optimization_barrier(
            ((send_att, keep_att), (first_up, second_down))
        )
        core_att = swap.data_swap(send_att, 1)
        all_up = [keep_up, core_up, *came_up]
        left = range(len(all_up))
        far_up = combine(
            [*all_up, *first_up],
            [
                (block, quarter, [(0, block, [(0, middle, cut), (1, middle, cut), (shards + 1, block, 0)])]),
                (block, quarter, [(0, block, [(0, block, cut + quarter), (1, block, cut + quarter), (shards + 2, block, 0)])]),
                (middle, side, [(0, middle, [(at, middle, 0) for at in left])]),
            ],
        )
        second_up = second_swap(far_up[:2])
        left_y = swap.data_swap(far_up[2], 4)
        far_att = first_far(keep_att, core_att, second_up, "combine_late")
        first_att = first_swap(far_att)
        arrays = [keep_down, core_down, *first_down, *second_down, *all_up, *first_up, *second_up]
        up_at, per, outs = 6, shards // 2, []
        half_at = up_at + len(all_up)
        for k in range(shards):
            half, near = k // per, k % per
            outs.append(
                (
                    block,
                    width + rest,
                    [
                        (0, block, [(0, 0, k * width), (1, 0, k * width), (2 + half, 0, near * width), (4 + half, 0, near * width)],
                         0, width),
                        (0, block, [(up_at, 0, cut + k * rest), (up_at + 1, 0, cut + k * rest), (half_at + half, 0, near * rest),
                                    (half_at + 2 + half, 0, near * rest)], width, rest),
                    ],
                )
            )
        feed_parts = combine(arrays, outs, far_att)
        came = [swap.tensor_swap(feed_parts[bits], bits) for bits in range(1, shards)]
        grad_h, grad_g = input_grads(w_query[0], w_key[0], w_value[0], dq, dkey, dvalue, dresid_one, feed_parts[:1])
        far_att = second_far(keep_att, core_att, first_att, [*came[:1], grad_h], "combine_att")
        second_att = second_swap(far_att)
        left_own, far_left = combine(
            [*all_up, left_y],
            [(block, side, [(0, block, [(at, row, 0) for at in range(shards + 2)])]) for row in (0, block)],
            [*far_att],
            "combine_left",
        )
        left_x = swap.data_swap(far_left, 2)
        att_parts = regroup(shards, keep_att, core_att, first_att, second_att, came)
    else:
        grad_h, grad_g = input_grads(w_query[0], w_key[0], w_value[0], dq, dkey, dvalue, dresid_one, ())
        vectors = lax.psum(keep_att[width // 2 : width // 2 + 10 + shards, :width].astype(F32), AXES)
        keep_att, send_att = keep_att[: width // 2], send_att[: width // 2]

        def rows_sum(keep, send):
            whole = jnp.concatenate([keep, send], axis=0)
            return lax.psum_scatter(whole, "dp", scatter_dimension=0, tiled=True)

        sum_up, sum_down, sum_att = (
            rows_sum(keep, send) for keep, send in ((keep_up, send_up), (keep_down, send_down), (keep_att, send_att))
        )
        cols = [slice(shard * width, (shard + 1) * width) for shard in range(shards)]
        side = left_columns(width)
        left, right = sum_up[:, : shards * side], sum_up[:, shards * side :]
        rest = width - side
        d_up = [
            jnp.concatenate([left[:, k * side : (k + 1) * side], right[:, k * rest : (k + 1) * rest]], axis=1)
            for k in range(shards)
        ]
        d_up = tensor_sum(swap, d_up)
        d_down = tensor_sum(swap, [sum_down[:, part] for part in cols]).T
        split = sum_att.reshape(-1, 5, shards, own_part).transpose(2, 0, 1, 3).reshape(shards, -1, 5 * own_part)
        att_parts = [lax.dynamic_index_in_dim(split, tensor_at ^ bits, 0, keepdims=False) for bits in range(shards)]
    att_parts = [att_parts[0]] + [swap.tensor_swap(att_parts[bits], bits) for bits in range(1, shards)]
    if by_hand:
        came, _ = lax.optimization_barrier((came, att_parts[1]))
        d_feed = add_all([feed_parts[0], *came])
        d_up = jnp.concatenate([add_all([left_own, left_x]), d_feed[:, width:]], axis=1)
        d_down = d_feed[:, :width].T
    d_att = add_all(att_parts)
    if by_hand:
        d_att, vectors = d_att[:block], d_att[block : block + 10 + shards, :width]
    d_att = [d_att[:, slot * own_part : (slot + 1) * own_part] for slot in range(5)]

    own = size // (swap.data * shards)
    d_vectors = lax.dynamic_slice_in_dim(vectors.reshape(-1), (dp_at * shards + tensor_at) * own, own, 0)

    return (
        out_h[None], out_g[None], grad_h[None], grad_g[None],
        d_att[0][None], d_att[1][None], d_att[2][None], d_att[3][None], d_att[4][None],
        d_up[None], d_down[None], d_vectors[None],
    )


def solution(mesh):
    every = P(AXES, None, None)
    rows = P(AXES, None)
    in_specs = (
        every, every, rows, rows, rows, P(), P(), P(), P(), P(), P(), P(), P(), P(),
        P(None, None, "tensor"), P(None, "tensor"), P(None, "tensor", None), P(), every, every,
    )
    grads = P(None, "dp", "tensor")
    out_specs = (
        every, every, every, every, grads, grads, grads, grads, grads, grads,
        P(None, "tensor", "dp"), P(None, AXES),
    )
    return jax.shard_map(per_device, mesh=mesh, in_specs=in_specs, out_specs=out_specs, check_vma=False)
```

```python
import functools
import math

import jax
import jax.numpy as jnp
import numpy as np
from jax import lax
from jax.experimental import pallas as pl
from jax.experimental.pallas import tpu as pltpu
from jax.sharding import PartitionSpec as P

HEADS = 12
HEAD_DIM = 64
LANES = 128
PAIRS = HEADS // 2
NEGATIVE = -1e30
EPSILON = 1e-06
AXES = ("dp", "tensor")
BF = jnp.bfloat16
F32 = jnp.float32
FIRST_PAIRS = 4
VMEM_MIB = {
    "share_slices": 60, "project": 50, "attention_first": 12, "attention_second": 14, "feed_up_own": 6, "feed_up": 14, "feed_down": 22,
    "feed_back_up": 16, "feed_back_mid": 10, "attention_back_first": 18, "attention_back": 26, "input_grads": 14, "pack_rows": 2,
    "combine": 12, "combine_late": 12, "combine_att": 59, "combine_left": 59, "regroup": 59,
}


def rel_table(length, model_width):
    position = (length - np.arange(2 * length)).astype(np.float32)
    frequency = np.float32(1.0) / np.float32(10000.0) ** (
        np.arange(0, model_width, 2).astype(np.float32) / np.float32(model_width)
    )
    angles = position[:, None] * frequency[None, :]
    return np.concatenate([np.sin(angles), np.cos(angles)], axis=1).astype(BF)


class Late:
    def __init__(self, source, target, sem):
        self.target, self.waiting = target, True
        self.copy = pltpu.make_async_copy(source, target, sem)
        self.copy.start()

    def get(self):
        if self.waiting:
            self.copy.wait()
            self.waiting = False
        return self.target


class Early:
    def __init__(self, ref, target, sems):
        self.ref, self.target, self.sems, self.copies = ref, target, sems, []

    def send(self, *where):
        source, target = (self.ref.at[where], self.target.at[where]) if where else (self.ref, self.target)
        copy = pltpu.make_async_copy(source, target, self.sems.at[len(self.copies)])
        copy.start()
        self.copies.append(copy)


SENDS = 16


def call(kernel, outs, ins, deps, scratch, name, flops):
    deps = tuple(deps)
    spaces = {"s": pltpu.SMEM, "v": pltpu.VMEM, "h": pl.ANY, "l": pltpu.HBM, "e": pltpu.HBM, "b": pltpu.HBM}
    late = [value for kind, value in ins if kind == "l"]
    early = [(shape, dtype) for kind, shape, dtype in outs if kind == "e"]
    more = [pltpu.VMEM(value.shape, value.dtype) for value in late] + [pltpu.VMEM(*spec) for spec in early]
    if late:
        more.append(pltpu.SemaphoreType.DMA((len(late),)))
    if early:
        more.append(pltpu.SemaphoreType.DMA((len(early), SENDS)))
    first_out = len(ins) + len(deps)
    first_scratch = first_out + len(outs)

    def wrapped(*refs):
        own = refs[first_scratch + len(scratch) :]
        late_refs, early_refs = own[: len(late)], own[len(late) : len(late) + len(early)]
        sems = list(own[len(late) + len(early) :])
        late_sem = sems.pop(0) if late else None
        early_sem = sems.pop(0) if early else None
        given, at = [], 0
        for (kind, _), ref in zip(ins, refs[: len(ins)], strict=True):
            if kind == "l":
                ref = Late(ref, late_refs[at], late_sem.at[at])
                at += 1
            given.append(ref)
        made, at = [], 0
        for (kind, _, _), ref in zip(outs, refs[first_out:first_scratch], strict=True):
            if kind == "e":
                ref = Early(early_refs[at], ref, early_sem.at[at])
                at += 1
            made.append(ref)
        kernel(*given, *made, *refs[first_scratch : first_scratch + len(scratch)])
        for item in given:
            if isinstance(item, Late):
                item.get()
        for item in made:
            if isinstance(item, Early):
                for copy in item.copies:
                    copy.wait()

    return pl.pallas_call(
        wrapped,
        out_shape=[jax.ShapeDtypeStruct(shape, dtype) for _, shape, dtype in outs],
        in_specs=[pl.BlockSpec(memory_space=spaces[kind]) for kind, _ in ins]
        + [pl.BlockSpec(memory_space=pl.ANY)] * len(deps),
        out_specs=[pl.BlockSpec(memory_space=spaces[kind]) for kind, _, _ in outs],
        scratch_shapes=list(scratch) + more,
        compiler_params=pltpu.CompilerParams(vmem_limit_bytes=VMEM_MIB[name] * 1024 * 1024),
        cost_estimate=pl.CostEstimate(flops=flops * 100, bytes_accessed=flops // 1000, transcendentals=0),
        name=name,
    )(*[value for _, value in ins], *deps)


def nn(left, right):
    return lax.dot_general(left, right, (((1,), (0,)), ((), ())), preferred_element_type=F32)


def nt(left, right):
    return lax.dot_general(left, right, (((1,), (1,)), ((), ())), preferred_element_type=F32)


def tn(left, right):
    return lax.dot_general(left, right, (((0,), (0,)), ((), ())), preferred_element_type=F32)


def lane_index(rows):
    return lax.broadcasted_iota(jnp.int32, (rows, LANES), 1)


def pair_lanes(pair):
    return pl.ds(pl.multiple_of(pair * LANES, LANES), LANES)


def row_lanes(row, pair, width):
    return pl.ds(pl.multiple_of(row * width + pair * LANES, LANES), LANES)


def norm_stats(source):
    mean = jnp.mean(source, axis=-1, keepdims=True)
    centered = source - mean
    variance = jnp.mean(centered * centered, axis=-1, keepdims=True)
    rstd = lax.rsqrt(variance + EPSILON)
    return centered * rstd, rstd


def norm_back(grad, xhat, rstd, gain):
    dxhat = grad * gain
    mean_one = jnp.mean(dxhat, axis=-1, keepdims=True)
    mean_two = jnp.mean(dxhat * xhat, axis=-1, keepdims=True)
    return rstd * (dxhat - mean_one - xhat * mean_two)


def seg_coefficients(half_wide, lane):
    return jnp.where(lane % HEAD_DIM == 0, half_wide, 1.0 - 2.0 * half_wide)


def seg_keys(half_wide, lane):
    place = lane % HEAD_DIM
    return jnp.where(place == 0, 1.0, jnp.where(place == 1, half_wide, 0.0))


def seg_table(seg_ref, pair, width):
    row = lax.broadcasted_iota(jnp.int32, (LANES, LANES), 0)
    lane = lax.broadcasted_iota(jnp.int32, (LANES, LANES), 1)
    one = jnp.broadcast_to(seg_ref[0:1, pair_lanes(pair)], (LANES, LANES)).T
    two = jnp.broadcast_to(seg_ref[0:1, row_lanes(1, pair, width)], (LANES, LANES)).T
    base = jnp.where(row < HEAD_DIM, HEAD_DIM, 0)
    at_one = lane == base
    at_two = at_one | (lane == base + 1)
    return jnp.concatenate([jnp.where(at_one, one, 0.0), jnp.where(at_two, two - one, 0.0)], axis=1).astype(BF)


def attend_pair(pair, first, q_ref, key_ref, value_ref, relkey_ref, mask_ref, half_ref, bias_ref, seg_ref, prob_ref, att_ref):
    length, width = key_ref.shape
    block = length // 2
    lanes = pair_lanes(pair)
    lane_q = lane_index(2 * length)
    lane_k = lane_index(length)
    low_q = lane_q < HEAD_DIM
    low_k = lane_k < HEAD_DIM
    half_w = half_ref[...]
    scale = 1.0 / math.sqrt(HEAD_DIM)
    query = q_ref[:, lanes]
    word = ((query + bias_ref[0:1, lanes]) * scale).astype(BF)
    relq = ((query + bias_ref[0:1, row_lanes(1, pair, width)]) * scale).astype(BF)
    segq = ((query + bias_ref[0:1, row_lanes(2, pair, width)]) * scale).astype(BF)
    terms = nn(segq, seg_table(seg_ref, pair, width))
    coef = seg_coefficients(jnp.concatenate([half_w, half_w], axis=0), lane_q)
    extra = (terms[:, :LANES] + terms[:, LANES:] * coef).astype(BF)
    key_extra = seg_keys(half_w, lane_k).astype(BF)
    key = key_ref[:, lanes]
    value = value_ref[:, lanes]
    zero = jnp.zeros_like(relq)
    attended = []
    for head in (0, 1):
        if head == 0:
            word_one = jnp.where(low_q, word, extra)
            key_one = jnp.where(low_k, key, key_extra)
            rel_one = jnp.where(low_q, relq, zero)
        else:
            word_one = jnp.where(low_q, extra, word)
            key_one = jnp.where(low_k, key_extra, key)
            rel_one = jnp.where(low_q, zero, relq)
        score = nt(word_one, key_one)
        for part in (0, 1):
            base = block - block * part
            rows_h = slice(block * part, block * part + block)
            rows_g = slice(length + block * part, length + block * part + block)
            rel_rows = jnp.concatenate([rel_one[rows_h], rel_one[rows_g]], axis=0)
            raw = nt(rel_rows, relkey_ref[base : base + 3 * block, lanes])
            for place_at, rows in ((0, rows_h), (1, rows_g)):
                shifted = pltpu.roll(
                    raw[place_at * block : (place_at + 1) * block], 2 * block, 1, stride=1, stride_axis=0
                )[:, :length]
                logits = score[rows] + shifted + mask_ref[rows]
                top = jnp.max(logits, axis=1, keepdims=True)
                power = jnp.exp(logits - top)
                total = jnp.sum(power, axis=1, keepdims=True)
                prob_ref[2 * (pair - first) + head, rows, :] = (power * (1.0 / total)).astype(BF)
        attended.append(nn(prob_ref[2 * (pair - first) + head], value))
    att_ref[:, lanes] = jnp.where(low_q, attended[0], attended[1]).astype(BF)


def project_kernel(
    parts, h_late, g_late, wq_late, wk_late, wv_late, rel_late, wr_late, rev_late,
    seg_row, flag_row, order_row,
    q_ref, key_ref, value_ref, relkey_ref, mask_ref, half_ref, relrev_out, left_x_out, left_rev_out,
    x_ref, raw_ref,
):
    h_ref, g_ref = h_late.get(), g_late.get()
    length, width = h_ref.shape
    x_ref[:length] = h_ref[...]
    x_ref[length:] = g_ref[...]

    def project(left, right_late, target):
        right = right_late.get()
        for col in range(0, width, 256):
            cols = slice(col, col + 256)
            target[:, cols] = nn(left[...], right[:, cols]).astype(target.dtype)

    project(x_ref, wq_late, q_ref)
    project(h_ref, wk_late, key_ref)
    project(h_ref, wv_late, value_ref)
    project(rel_late.get(), wr_late, relkey_ref)

    def wide(row_ref):
        return jnp.broadcast_to(row_ref[...].astype(F32), (length, length))

    row_at = lax.broadcasted_iota(jnp.int32, (length, length), 0)
    col_at = lax.broadcasted_iota(jnp.int32, (length, length), 1)
    seg, order = wide(seg_row), wide(order_row)
    same_doc = seg.T == seg
    start = jnp.min(jnp.where(same_doc, col_at.astype(F32), float(length)), axis=1, keepdims=True)
    in_doc = jnp.sum(jnp.where(same_doc, 1.0, 0.0), axis=1, keepdims=True)
    place = lax.broadcasted_iota(jnp.int32, (length, 1), 0).astype(F32)
    half = jnp.where(2.0 * (place - start) >= in_doc, 1.0, 0.0)
    half_ref[...] = jnp.broadcast_to(half, (length, LANES))
    content = same_doc & ((wide(flag_row) == 0.0) | (order <= order.T))
    mask_ref[:length] = jnp.where(content, 0.0, NEGATIVE)
    mask_ref[length:] = jnp.where(content & (row_at != col_at), 0.0, NEGATIVE)

    project(rev_late.get(), wr_late, relrev_out.ref)
    relrev_out.send()
    turn_rows(lambda col: x_ref[:, col : col + 256], raw_ref.at[0], left_x_out.ref, parts)
    left_x_out.send()
    rev_ref = rev_late.get()
    turn_rows(lambda col: rev_ref[:, col : col + 256], raw_ref.at[1], left_rev_out.ref, parts)
    left_rev_out.send()


def project(parts, h, g, seg, flag, order, wq, wk, wv, wr, rel, rev, deps):
    length, width = h.shape
    two = 2 * length
    outs = [
        ("v", (two, width), F32), ("v", (length, width), BF), ("v", (length, width), BF), ("v", (two, width), BF),
        ("v", (two, length), F32), ("v", (length, LANES), F32), ("e", (two, width), BF), ("e", (width, two), BF),
        ("e", (width, two), BF),
    ]
    ins = [("l", value) for value in (h, g, wq, wk, wv, rel, wr, rev)] + [("v", value) for value in (seg, flag, order)]
    scratch = [pltpu.VMEM((two, width), BF), pltpu.VMEM((2, width, two), BF)]
    return call(functools.partial(project_kernel, parts), outs, ins, deps, scratch, "project", 5 * 10**9)


def attention_first_kernel(
    q_ref, key_ref, value_ref, relkey_ref, mask_ref, half_ref, bias_ref, seg_ref, att_ref, prob_out
):
    def pair_step(pair, carry):
        attend_pair(
            pair, 0, q_ref, key_ref, value_ref, relkey_ref, mask_ref, half_ref, bias_ref, seg_ref, prob_out.ref, att_ref
        )
        return carry

    for first in range(0, FIRST_PAIRS, 2):
        lax.fori_loop(first, first + 2, pair_step, 0)
        prob_out.send(pl.ds(2 * first, 4))


def attention_first(q, key, value, relkey, mask, half, bias, table, deps):
    two, length = mask.shape
    outs = [("v", (two, FIRST_PAIRS * LANES), BF), ("e", (2 * FIRST_PAIRS, two, length), BF)]
    ins = [("v", x) for x in (q, key, value, relkey, mask, half, bias, table)]
    return call(attention_first_kernel, outs, ins, deps, [], "attention_first", 5 * 10**9)


def attention_second_kernel(
    parts, wo_late, h_late, g_late, q_ref, key_ref, value_ref, relkey_ref, mask_ref, half_ref, att_first_ref,
    bias_ref, seg_ref, gain_ref, shift_ref,
    resid_ref, mid_ref, prob_out, att_out, left_att_out,
    raw_ref,
):
    length, width = key_ref.shape
    att_ref = att_out.ref
    att_ref[:, : FIRST_PAIRS * LANES] = att_first_ref[...]

    def pair_step(pair, carry):
        attend_pair(
            pair, FIRST_PAIRS, q_ref, key_ref, value_ref, relkey_ref, mask_ref, half_ref, bias_ref, seg_ref, prob_out.ref, att_ref
        )
        return carry

    for first in range(FIRST_PAIRS, PAIRS, 2):
        lax.fori_loop(first, first + 2, pair_step, 0)
        prob_out.send(pl.ds(2 * (first - FIRST_PAIRS), 4))
    att_out.send()
    wo_ref, h_ref, g_ref = wo_late.get(), h_late.get(), g_late.get()
    for col in range(0, width, 256):
        cols = slice(col, col + 256)
        total = nn(att_ref[...], wo_ref[:, cols])
        resid_ref[:length, cols] = h_ref[:, cols].astype(F32) + total[:length]
        resid_ref[length:, cols] = g_ref[:, cols].astype(F32) + total[length:]
    turn_rows(lambda col: att_ref[:, col : col + 256], raw_ref, left_att_out.ref, parts)
    left_att_out.send()
    for row in range(0, 2 * length, 64):
        xhat, _ = norm_stats(resid_ref[row : row + 64, :])
        mid_ref[row : row + 64, :] = (xhat * gain_ref[0:1, :width] + shift_ref[0:1, :width]).astype(BF)


def attention_second(parts, wo, h, g, q, key, value, relkey, mask, half, att, bias, table, gain, shift, deps):
    length, width = h.shape
    two = 2 * length
    outs = [
        ("v", (two, width), F32), ("v", (two, width), BF), ("e", (HEADS - 2 * FIRST_PAIRS, two, length), BF),
        ("e", (two, width), BF), ("e", (width, two), BF),
    ]
    ins = [("l", value) for value in (wo, h, g)]
    ins += [("v", value) for value in (q, key, value, relkey, mask, half, att, bias, table, gain, shift)]
    return call(
        functools.partial(attention_second_kernel, parts), outs, ins, deps, [pltpu.VMEM((width, two), BF)],
        "attention_second", 10 * 10**9,
    )


def place_rows(raw_ref, out_ref, parts):
    rows = raw_ref.shape[0] // parts
    me = lax.axis_index("dp") if parts > 1 else 0
    order = [low | (rest << 1) for low in (0, 1) for rest in range(parts // 2)] if parts > 1 else [0]
    for at, block in enumerate(order):
        source = pl.multiple_of((me ^ block) * rows, rows)
        out_ref[at * rows : (at + 1) * rows, :] = raw_ref[pl.ds(source, rows), :]


def turn_rows(source, raw_ref, out_ref, parts):
    for col in range(0, raw_ref.shape[0], 256):
        raw_ref[col : col + 256, :] = source(col).astype(F32).T.astype(BF)
    place_rows(raw_ref, out_ref, parts)


def back_pairs(
    pairs, dproj_ref, wo_ref, q_ref, att_ref, key_ref, value_ref, prob_one, prob_two, relrev_ref, half_ref, bias_ref, seg_ref,
    dq_ref, dkey_ref, dvalue_ref, drel_ref, vec_ref, datt_ref,
):
    length, width = key_ref.shape
    block = length // 2
    for at, pair in enumerate(pairs):
        rows = slice(pair * LANES, (pair + 1) * LANES)
        datt_ref[:, at * LANES : (at + 1) * LANES] = nt(dproj_ref[...], wo_ref[rows, :]).astype(BF)

    def pair_step(at, pair):
        lanes = slice(pair * LANES, (pair + 1) * LANES)
        own = slice(at * LANES, (at + 1) * LANES)
        prob_ref, prob_at = (prob_one, 2 * pair) if pair < FIRST_PAIRS else (prob_two, 2 * (pair - FIRST_PAIRS))
        lane_q = lane_index(2 * length)
        lane_k = lane_index(length)
        low_q = lane_q < HEAD_DIM
        low_k = lane_k < HEAD_DIM
        half_w = half_ref[...]
        flip_row = lax.broadcasted_iota(jnp.int32, (length, length), 0)
        flip_col = lax.broadcasted_iota(jnp.int32, (length, length), 1)
        flip = jnp.where(flip_row + flip_col == length - 1, 1.0, 0.0).astype(BF)
        sel_row = lax.broadcasted_iota(jnp.int32, (2 * LANES, LANES), 0) % LANES
        sel_col = lax.broadcasted_iota(jnp.int32, (2 * LANES, LANES), 1)
        select = jnp.where(
            ((sel_row < HEAD_DIM) & ((sel_col == HEAD_DIM) | (sel_col == HEAD_DIM + 1)))
            | ((sel_row >= HEAD_DIM) & (sel_col < 2)),
            1.0,
            0.0,
        ).astype(BF)
        query = q_ref[:, lanes]
        word = query + bias_ref[0:1, lanes]
        relq = query + bias_ref[0:1, row_lanes(1, pair, width)]
        segq = (query + bias_ref[0:1, row_lanes(2, pair, width)]).astype(BF)
        word_t = word.T.astype(BF)
        relq_t = relq.T.astype(BF)
        datt = datt_ref[:, own]
        datt_wide = datt.astype(F32)
        datt_t = datt_wide.T.astype(BF)
        datt_scaled = datt_wide * (1.0 / math.sqrt(HEAD_DIM))
        product = datt_scaled * att_ref[:, lanes].astype(F32)
        product_high = product.astype(BF)
        product_low = (product - product_high.astype(F32)).astype(BF)
        delta = nn(jnp.concatenate([product_high, product_low], axis=1), select)
        delta_high = delta.astype(BF).astype(F32)
        minus = jnp.where(lane_q % HEAD_DIM == 0, -delta_high, delta_high - delta).astype(BF)
        datt_low = datt_scaled.astype(BF)
        key_extra = seg_keys(half_w, lane_k).astype(BF)
        ones_extra = jnp.where(lane_k % HEAD_DIM < 2, 1.0, 0.0).astype(BF)
        key = key_ref[:, lanes]
        value = value_ref[:, lanes]
        dword, drel = [], []
        for head in (0, 1):
            rows_t = slice(HEAD_DIM * head, HEAD_DIM * head + HEAD_DIM)
            if head == 0:
                datt_one = jnp.where(low_q, datt_low, minus)
                value_one = jnp.where(low_k, value, ones_extra)
                key_one = jnp.where(low_k, key, key_extra)
            else:
                datt_one = jnp.where(low_q, minus, datt_low)
                value_one = jnp.where(low_k, ones_extra, value)
                key_one = jnp.where(low_k, key_extra, key)
            prob = prob_ref[prob_at + head]
            dprob = nt(datt_one, value_one)
            dscore = (prob.astype(F32) * dprob).astype(BF)
            dword.append(nn(dscore, key_one))
            rows_out = slice(at * LANES + HEAD_DIM * head, at * LANES + HEAD_DIM * (head + 1))
            dkey_ref[rows_out, :] = nn(word_t[rows_t], dscore).astype(BF)
            dvalue_ref[rows_out, :] = nn(datt_t[rows_t], prob).astype(BF)
            flipped = nn(dscore, flip).astype(BF)
            pad = jnp.zeros((block, block), BF)
            rel_parts, drel_t = [], []
            for part in (0, 1):
                rows_h = slice(block * part, block * part + block)
                rows_g = slice(length + block * part, length + block * part + block)
                draw = jnp.concatenate(
                    [
                        pltpu.roll(jnp.concatenate([flipped[rows], pad], axis=1), 0, 1, stride=1, stride_axis=0)
                        for rows in (rows_h, rows_g)
                    ],
                    axis=0,
                )
                rel_parts.append(nn(draw, relrev_ref[block * part : block * part + 3 * block, lanes]))
                rel_cols = jnp.concatenate([relq_t[rows_t, rows_h], relq_t[rows_t, rows_g]], axis=1)
                drel_t.append(nn(rel_cols, draw))
            drel.append(
                jnp.concatenate(
                    [rel_parts[0][:block], rel_parts[1][:block], rel_parts[0][block:], rel_parts[1][block:]], axis=0
                )
            )
            drel_ref[rows_out, :] = jnp.concatenate(
                [
                    drel_t[0][:, :block],
                    drel_t[0][:, block:] + drel_t[1][:, : 2 * block],
                    drel_t[1][:, 2 * block :],
                ],
                axis=1,
            ).astype(BF)
        extra = jnp.where(low_q, dword[1], dword[0])
        dword_all = jnp.where(low_q, dword[0], dword[1])
        drel_all = jnp.where(low_q, drel[0], drel[1])
        coef = seg_coefficients(jnp.concatenate([half_w, half_w], axis=0), lane_q)
        dterms = jnp.concatenate([extra, extra * coef], axis=1).astype(BF)
        dsegq = nt(dterms, seg_table(seg_ref, pair, width))
        dtable = tn(dterms, segq)
        dq_ref[:, own] = (dword_all + drel_all + dsegq).astype(BF)
        low_one = lane_index(1) < HEAD_DIM
        first = jnp.where(low_one, dtable[HEAD_DIM : HEAD_DIM + 1], dtable[0:1])
        far = LANES + HEAD_DIM
        second = jnp.where(
            low_one, dtable[far : far + 1] + dtable[far + 1 : far + 2], dtable[LANES : LANES + 1] + dtable[LANES + 1 : LANES + 2]
        )
        vec_ref[0:1, own] = jnp.sum(dword_all, axis=0, keepdims=True)
        vec_ref[1:2, own] = jnp.sum(drel_all, axis=0, keepdims=True)
        vec_ref[2:3, own] = jnp.sum(dsegq, axis=0, keepdims=True)
        vec_ref[3:4, own] = first - second
        vec_ref[4:5, own] = second
    for at, pair in enumerate(pairs):
        pair_step(at, pair)


def attention_back_first_kernel(
    pairs, wo_late, dproj_ref, q_ref, att_ref, key_ref, value_ref, prob_one, prob_two, relrev_ref, half_ref, bias_ref, seg_ref,
    dq_ref, dkey_ref, dvalue_ref, drel_ref, vec_ref, datt_ref,
):
    vec_ref[...] = jnp.zeros_like(vec_ref)
    back_pairs(
        pairs, dproj_ref, wo_late.get(), q_ref, att_ref, key_ref, value_ref, prob_one, prob_two, relrev_ref, half_ref, bias_ref,
        seg_ref, dq_ref, dkey_ref, dvalue_ref, drel_ref, vec_ref, datt_ref,
    )


def attention_back_first(pairs, common, bias, table, deps):
    two, width = common[1].shape
    length, size = two // 2, len(pairs) * LANES
    outs = [
        ("v", (two, size), BF), ("v", (size, length), BF), ("v", (size, length), BF), ("v", (size, two), BF), ("v", (8, size), F32),
    ]
    ins = [("l", common[0])] + [("v", x) for x in (*common[1:], bias, table)]
    kernel = functools.partial(attention_back_first_kernel, pairs)
    return call(kernel, outs, ins, deps, [pltpu.VMEM((two, size), BF)], "attention_back_first", 12 * 10**9)


def attention_back_kernel(
    pairs, wo_late, dproj_ref, q_ref, att_ref, key_ref, value_ref, prob_one, prob_two, relrev_ref, half_ref, bias_ref, seg_ref,
    left_x_ref, left_rev_ref, left_att_ref, dq_one, dkey_one, dvalue_one, drel_one, vec_one, norm_one, norm_two, hidden_ref,
    dq_ref, dkey_ref, dvalue_ref, keep_out, send_out, datt_ref, drel_ref, vec_ref, packed_ref,
):
    length, width = key_ref.shape
    split = width // 2
    size = dq_one.shape[1]
    dq_ref[:, :size], dkey_ref[:size], dvalue_ref[:size], drel_ref[:size] = dq_one[...], dkey_one[...], dvalue_one[...], drel_one[...]
    vec_ref[...] = jnp.zeros_like(vec_ref)
    vec_ref[:, :size] = vec_one[...]
    back_pairs(
        pairs, dproj_ref, wo_late.get(), q_ref, att_ref, key_ref, value_ref, prob_one, prob_two, relrev_ref, half_ref, bias_ref,
        seg_ref, dq_ref.at[:, size:], dkey_ref.at[size:], dvalue_ref.at[size:], drel_ref.at[size:], vec_ref.at[:, size:], datt_ref,
    )
    shards = hidden_ref.shape[1] // width
    packed_ref[...] = jnp.zeros_like(packed_ref)
    packed_ref[0:5, :] = vec_ref[0:5, :]
    packed_ref[5:6, :] = norm_one[0:1, :]
    packed_ref[6:7, :] = norm_two[0:1, :]
    packed_ref[7:8, :] = norm_one[1:2, :]
    packed_ref[8:10, :] = norm_two[1:3, :]
    for shard in range(shards):
        place = 10 + (lax.axis_index("tensor") ^ shard)
        packed_ref[pl.ds(place, 1), :] = hidden_ref[0:1, shard * width : (shard + 1) * width]
    packed = packed_ref[...].astype(BF)
    for out in (send_out, keep_out):
        out.ref[split:, :width] = packed
        out.ref[split:, width:] = jnp.zeros((16, 4 * width), BF)
        out.send(pl.ds(split, 16))
    todo = [
        (left_x_ref[...], dq_ref, nn), (left_x_ref[:, :length], dkey_ref, nt), (left_x_ref[:, :length], dvalue_ref, nt),
        (left_att_ref[...], dproj_ref, nn), (left_rev_ref[...], drel_ref, nt),
    ]
    at = 0
    for left, right, dot in todo:
        count = right.shape[1] if dot is nn else right.shape[0]
        for col in range(0, count, 256):
            cols = slice(col, col + 256)
            piece = dot(left, right[:, cols] if dot is nn else right[cols, :]).astype(BF)
            keep_out.ref[:split, at + col : at + col + 256] = piece[:split]
            send_out.ref[:split, at + col : at + col + 256] = piece[split:]
        done = pl.ds(at, count)
        send_out.send(pl.ds(0, split), done)
        keep_out.send(pl.ds(0, split), done)
        at += count


def attention_back(pairs, common, lefts, first, vectors, bias, table, deps):
    two, width = common[1].shape
    length, size = two // 2, len(pairs) * LANES
    outs = [
        ("v", (two, width), BF), ("v", (width, length), BF), ("v", (width, length), BF),
        ("e", (width // 2 + 16, 5 * width), BF), ("e", (width // 2 + 16, 5 * width), BF),
    ]
    ins = [("l", common[0])] + [("v", x) for x in (*common[1:], bias, table, *lefts, *first, *vectors)]
    scratch = [
        pltpu.VMEM((two, size), BF), pltpu.VMEM((width, two), BF), pltpu.VMEM((8, width), F32), pltpu.VMEM((16, width), F32),
    ]
    return call(functools.partial(attention_back_kernel, pairs), outs, ins, deps, scratch, "attention_back", 12 * 10**9)


def input_grads_kernel(wq_late, wk_late, wv_late, dq_ref, dkey_ref, dvalue_ref, dresid_ref, grad_h, grad_g, sum_ref):
    length, width = grad_h.ref.shape
    wq_ref = wq_late.get()
    for col in range(0, width, 256):
        cols = slice(col, col + 256)
        low = nt(dq_ref[...], wq_ref[cols, :])
        sum_ref[:, cols] = dresid_ref[:length, cols] + low[:length]
        grad_g.ref[:, cols] = dresid_ref[length:, cols] + low[length:]
    grad_g.send()
    dkey, dvalue = dkey_ref[...].astype(F32).T.astype(BF), dvalue_ref[...].astype(F32).T.astype(BF)
    wk_ref, wv_ref = wk_late.get(), wv_late.get()
    for col in range(0, width, 256):
        cols = slice(col, col + 256)
        grad_h.ref[:, cols] = sum_ref[:, cols] + nt(dkey, wk_ref[cols, :]) + nt(dvalue, wv_ref[cols, :])
    grad_h.send()


def input_grads(wq, wk, wv, dq, dkey, dvalue, dresid, deps):
    two, width = dresid.shape
    outs = [("e", (two // 2, width), F32), ("e", (two // 2, width), F32)]
    ins = [("l", wq), ("l", wk), ("l", wv), ("v", dq), ("v", dkey), ("v", dvalue), ("v", dresid)]
    scratch = [pltpu.VMEM((two // 2, width), F32)]
    return call(input_grads_kernel, outs, ins, deps, scratch, "input_grads", 10**9)


def share_kernel(parts, up_hbm, down_hbm, bias_ref, out_ref, sem):
    rows = up_hbm.shape[0] // parts
    start = pl.multiple_of(lax.axis_index("dp") * rows, rows) if parts > 1 else 0
    one = pltpu.make_async_copy(up_hbm.at[pl.ds(start, rows)], out_ref.at[pl.ds(0, rows)], sem.at[0])
    two = pltpu.make_async_copy(down_hbm.at[pl.ds(start, rows)], out_ref.at[pl.ds(rows, rows)], sem.at[1])
    one.start()
    two.start()
    out_ref[2 * rows :, :] = jnp.broadcast_to(bias_ref[...], (16, bias_ref.shape[1]))
    one.wait()
    two.wait()


def share_slices(parts, up, down, bias):
    rows, width = up.shape[0] // parts, up.shape[1]
    outs = [("v", (2 * rows + 16, width), BF)]
    ins = [("b", up), ("b", down), ("v", bias)]
    return call(functools.partial(share_kernel, parts), outs, ins, (), [pltpu.SemaphoreType.DMA((2,))], "share_slices", 10**7)[0]


def start_pieces(pieces, piece_refs, target_ref, sem):
    copies = []
    for count, ((block, rows), source) in enumerate(zip(pieces, piece_refs, strict=True)):
        where = 0
        if rows < target_ref.shape[1]:
            where = pl.multiple_of((lax.axis_index("dp") ^ block) * rows, rows)
        copies.append(pltpu.make_async_copy(source, target_ref.at[:, pl.ds(where, rows)], sem.at[count]))
        copies[-1].start()
    return copies


def gelu_parts(pre):
    root = math.sqrt(2.0 / math.pi)
    square = pre * pre
    bend = jnp.tanh(root * pre * (1.0 + 0.044715 * square))
    upper = 0.5 + 0.5 * bend
    slope = upper + (0.5 * root) * pre * (1.0 - bend * bend) * (1.0 + (3 * 0.044715) * square)
    return (pre * upper).astype(BF), slope.astype(BF)


def feed_up_own_kernel(mid_ref, up_late, bias_ref, act_ref, slope_ref):
    width = mid_ref.shape[1]
    up_ref = up_late.get()
    for col in range(0, width, 256):
        cols = slice(col, col + 256)
        bias = bias_ref[0:1, cols].astype(F32)
        act_ref[:, cols], slope_ref[:, cols] = gelu_parts(nn(mid_ref[...], up_ref[:, cols]) + bias)


def feed_up_own(mid, up, bias, deps):
    outs = [("v", mid.shape, BF), ("v", mid.shape, BF)]
    return call(feed_up_own_kernel, outs, [("v", mid), ("l", up), ("v", bias)], deps, [], "feed_up_own", 3 * 10**9)


def feed_up_kernel(shards, pieces, rows, mid_ref, *refs):
    bias_refs, piece_refs = refs[: shards - 1], refs[shards - 1 : shards - 1 + len(pieces)]
    act_ref, slope_ref, up_ref, bias_ref, in_sem, bias_sem = refs[shards - 1 + len(pieces) :]
    width = mid_ref.shape[1]
    copies = start_pieces(pieces, piece_refs, up_ref, in_sem)
    biases = [
        pltpu.make_async_copy(ref.at[pl.ds(rows, 16)], bias_ref.at[shard], bias_sem.at[shard])
        for shard, ref in enumerate(bias_refs)
    ]
    for copy in biases:
        copy.start()
    for copy in biases:
        copy.wait()
    for copy in copies:
        copy.wait()
    for shard in range(shards - 1):
        for col in range(0, width, 256):
            cols = slice(shard * width + col, shard * width + col + 256)
            pre = nn(mid_ref[...], up_ref[shard, :, col : col + 256])
            act_ref[:, cols], slope_ref[:, cols] = gelu_parts(
                pre + bias_ref[shard, 0:1, col : col + 256].astype(F32)
            )


def feed_up(shards, mid, rows, biases, pieces, deps):
    rows_all, width = mid.shape
    hidden = (shards - 1) * width
    names = [entry[:-1] for entry in pieces]
    outs = [("v", (rows_all, hidden), BF), ("v", (rows_all, hidden), BF), ("v", (shards - 1, width, width), BF)]
    ins = [("v", mid)] + [("h", value) for value in biases] + [("h", entry[-1]) for entry in pieces]
    scratch = [
        pltpu.VMEM((shards - 1, 16, width), BF), pltpu.SemaphoreType.DMA((len(names),)), pltpu.SemaphoreType.DMA((shards - 1,)),
    ]
    return call(functools.partial(feed_up_kernel, shards, names, rows), outs, ins, deps, scratch, "feed_up", 6 * 10**9)


def feed_down_kernel(parts, shards, pieces, own_down, dh_ref, dg_ref, act_own, resid_ref, act_rest, *refs):
    down_bias, gain_ref, shift_ref = refs[:3]
    piece_refs = refs[3 : 3 + len(pieces)]
    out_h, out_g, dresid_ref, dbranch_ref, keep_out, send_out, vec_ref, down_ref, raw_ref, left_ref, in_sem = refs[3 + len(pieces) :]
    rows_all, width = resid_ref.shape
    length = rows_all // 2
    split = width // 2
    copies = start_pieces(pieces, piece_refs, down_ref, in_sem)
    for col in range(0, width, 256):
        cols = slice(col, col + 256)
        dresid_ref[:, cols] = nn(act_own[...], own_down[:, cols])
    for copy in copies:
        copy.wait()
    down_all = down_ref.reshape((shards - 1) * width, width)
    for col in range(0, width, 256):
        cols = slice(col, col + 256)
        dresid_ref[:, cols] += nn(act_rest[...], down_all[:, cols])
    gain_one, gain_two = gain_ref[0:1, :width], gain_ref[0:1, width:]
    shift_one, shift_two = shift_ref[0:1, :width], shift_ref[0:1, width:]
    step_rows = 32
    sums = [jnp.zeros((step_rows, width), F32)] * 3
    for row in range(0, rows_all, step_rows):
        rows = slice(row, row + step_rows)
        grad_ref = dh_ref if row < length else dg_ref
        near = row % length
        xhat_one, _ = norm_stats(resid_ref[rows, :])
        middle = xhat_one * gain_one + shift_one
        xhat, rstd = norm_stats(middle + dresid_ref[rows, :] + down_bias[...])
        out = out_h if row < length else out_g
        out.ref[near : near + step_rows, :] = (xhat * gain_two + shift_two).astype(BF)
        grad = grad_ref[near : near + step_rows, :].astype(F32)
        dresid = norm_back(grad, xhat, rstd, gain_two)
        dresid_ref[rows, :] = dresid
        dbranch = dresid.astype(BF)
        dbranch_ref[rows, :] = dbranch
        sums = [sums[0] + grad * xhat, sums[1] + grad, sums[2] + dbranch.astype(F32)]
    vec_ref[...] = jnp.zeros_like(vec_ref)
    for at, total in enumerate(sums):
        vec_ref[at : at + 1, :] = jnp.sum(total, axis=0, keepdims=True)
    out_h.send()
    out_g.send()
    turn_rows(lambda col: dbranch_ref[:, col : col + 256], raw_ref, left_ref, parts)
    for source, count, offset in ((act_own, 1, 0), (act_rest, shards - 1, width)):
        for col in range(0, count * width, 256):
            piece = nn(left_ref[...], source[:, col : col + 256]).astype(BF)
            cols = slice(col + offset, col + offset + 256)
            keep_out.ref[:, cols] = piece[:split]
            send_out.ref[:, cols] = piece[split:]
            if (col + 256) % width == 0:
                done = pl.ds(col + offset + 256 - width, width)
                send_out.send(slice(None), done)
                keep_out.send(slice(None), done)


def feed_down(parts, shards, own_down, act_own, act_rest, resid_one, down_bias, gains, shifts, dh, dg, pieces, deps):
    rows_all, width = resid_one.shape
    hidden = shards * width
    names = [entry[:-1] for entry in pieces]
    outs = [
        ("e", dh.shape, BF), ("e", dg.shape, BF), ("v", (rows_all, width), F32), ("v", (rows_all, width), BF),
        ("e", (width // 2, hidden), BF), ("e", (width // 2, hidden), BF), ("v", (8, width), F32), ("v", (shards - 1, width, width), BF),
    ]
    ins = [("v", own_down), ("v", dh), ("v", dg)]
    ins += [("v", value) for value in (act_own, resid_one, act_rest, down_bias, gains, shifts)] + [("h", entry[-1]) for entry in pieces]
    scratch = [pltpu.VMEM((width, rows_all), BF), pltpu.VMEM((width, rows_all), BF), pltpu.SemaphoreType.DMA((len(names),))]
    return call(functools.partial(feed_down_kernel, parts, shards, names), outs, ins, deps, scratch, "feed_down", 8 * 10**9)


def left_columns(width):
    return width // 3


def feed_back_up_kernel(
    parts, shards, own_down, mid_ref, dbranch_ref, down_ref, slope_own, slope_rest,
    dpre_ref, keep_out, send_out, dbias_ref, raw_ref, left_ref,
):
    rows_all, width = mid_ref.shape
    split, side = width // 2, left_columns(width)
    turn_rows(lambda col: mid_ref[:, col : col + 256], raw_ref, left_ref, parts)
    for shard in range(shards):
        for col in range(0, width, 256):
            cols = slice(shard * width + col, shard * width + col + 256)
            if shard:
                near = (shard - 1) * width + col
                weight, slope = down_ref[shard - 1, col : col + 256, :], slope_rest[:, near : near + 256]
            else:
                weight, slope = own_down[col : col + 256, :], slope_own[:, col : col + 256]
            dpre = (nt(dbranch_ref[...], weight) * slope.astype(F32)).astype(BF)
            dpre_ref[:, cols] = dpre
            dbias_ref[:, cols] = jnp.sum(dpre.astype(F32), axis=0, keepdims=True)
            piece = nn(left_ref[...], dpre).astype(BF)
            for at in range(col, col + 256, LANES):
                if at < side:
                    to = shard * side + at
                else:
                    to = shards * side + shard * (width - side) + at - side
                part = slice(at - col, at - col + LANES)
                keep_out.ref[:, to : to + LANES] = piece[:split, part]
                send_out.ref[:, to : to + LANES] = piece[split:, part]
        for start, size in ((shard * side, side), (shards * side + shard * (width - side), width - side)):
            done = pl.ds(start, size)
            send_out.send(slice(None), done)
            keep_out.send(slice(None), done)


def feed_back_up(parts, shards, own_down, down_rest, dbranch, mid, slope_own, slope_rest, deps):
    rows_all, width = mid.shape
    hidden = shards * width
    outs = [("v", (rows_all, hidden), BF), ("e", (width // 2, hidden), BF), ("e", (width // 2, hidden), BF), ("v", (1, hidden), F32)]
    ins = [("v", own_down)] + [("v", value) for value in (mid, dbranch, down_rest, slope_own, slope_rest)]
    scratch = [pltpu.VMEM((width, rows_all), BF), pltpu.VMEM((width, rows_all), BF)]
    return call(functools.partial(feed_back_up_kernel, parts, shards), outs, ins, deps, scratch, "feed_back_up", 8 * 10**9)


def feed_back_mid_kernel(shards, own_late, dpre_ref, up_ref, dresid_ref, resid_ref, gain_ref, dproj_ref, dresid_one_ref, vec_ref):
    rows_all, width = dresid_one_ref.shape
    own_up = own_late.get()
    for col in range(0, width, 256):
        cols = slice(col, col + 256)
        total = nt(dpre_ref[:, :width], own_up[cols, :])
        for shard in range(1, shards):
            total += nt(dpre_ref[:, shard * width : (shard + 1) * width], up_ref[shard - 1, cols, :])
        dresid_one_ref[:, cols] = total
    gain_one = gain_ref[0:1, :width]
    step_rows = 32
    sums = [jnp.zeros((step_rows, width), F32)] * 2
    for row in range(0, rows_all, step_rows):
        rows = slice(row, row + step_rows)
        xhat, rstd = norm_stats(resid_ref[rows, :])
        grad = dresid_ref[rows, :] + dresid_one_ref[rows, :]
        dresid = norm_back(grad, xhat, rstd, gain_one)
        dresid_one_ref[rows, :] = dresid
        dproj_ref[rows, :] = dresid.astype(BF)
        sums = [sums[0] + grad * xhat, sums[1] + grad]
    vec_ref[...] = jnp.zeros_like(vec_ref)
    for at, total in enumerate(sums):
        vec_ref[at : at + 1, :] = jnp.sum(total, axis=0, keepdims=True)


def feed_back_mid(shards, own_up, up_rest, dpre, dresid, resid_one, gains, deps):
    rows_all, width = resid_one.shape
    outs = [("v", (rows_all, width), BF), ("v", (rows_all, width), F32), ("v", (8, width), F32)]
    ins = [("l", own_up)] + [("v", value) for value in (dpre, up_rest, dresid, resid_one, gains)]
    return call(functools.partial(feed_back_mid_kernel, shards), outs, ins, deps, [], "feed_back_mid", 5 * 10**9)


def pack_rows_kernel(count, rows, *refs):
    one_ref, two_ref, sem = refs[count:]
    copies = [
        pltpu.make_async_copy(ref.at[pl.ds(half * rows, rows)], out.at[at], sem.at[half, at])
        for half, out in enumerate((one_ref, two_ref))
        for at, ref in enumerate(refs[:count])
    ]
    for copy in copies:
        copy.start()
    for copy in copies:
        copy.wait()


def pack_rows(arrays, rows, deps):
    outs = [("v", (len(arrays), rows, arrays[0].shape[1]), BF)] * 2
    scratch = [pltpu.SemaphoreType.DMA((2, len(arrays)))]
    kernel = functools.partial(pack_rows_kernel, len(arrays), rows)
    return call(kernel, outs, [("h", value) for value in arrays], deps, scratch, "pack_rows", 10**6)


def combine(arrays, outs, deps=(), name="combine_late"):
    outs = [(rows, cols, [(*part, 0, cols)[:5] for part in parts]) for rows, cols, parts in outs]
    ranges = {}
    for _, _, parts in outs:
        for _, count, sources, _, cols in parts:
            for source, row, col in sources:
                low, high = ranges.get((source, row, count), (col, col + cols))
                ranges[source, row, count] = (min(low, col), max(high, col + cols))
    buffers = [pltpu.VMEM((count, high - low), BF) for (_, _, count), (low, high) in ranges.items()]

    def kernel(*refs):
        out_refs = refs[len(arrays) : len(arrays) + len(outs)]
        *held, sem = refs[len(arrays) + len(outs) :]
        copies = {}
        for at, ((source, row, count), (low, high)) in enumerate(ranges.items()):
            piece = refs[source].at[pl.ds(row, count), pl.ds(low, high - low)]
            copies[source, row, count] = (pltpu.make_async_copy(piece, held[at], sem.at[at]), held[at], low)
            copies[source, row, count][0].start()
        waited = set()
        for (_, _, parts), out_ref in zip(outs, out_refs, strict=True):
            for first, count, sources, to, cols in parts:
                values = []
                for source, row, col in sources:
                    copy, buffer, low = copies[source, row, count]
                    if (source, row, count) not in waited:
                        copy.wait()
                        waited.add((source, row, count))
                    values.append(buffer[:, col - low : col - low + cols])
                out_ref[first : first + count, to : to + cols] = add_all(values).astype(BF)

    shapes = [("v", (rows, cols), BF) for rows, cols, _ in outs]
    scratch = [*buffers, pltpu.SemaphoreType.DMA((len(buffers),))]
    return call(kernel, shapes, [("b", value) for value in arrays], deps, scratch, name, 10**9 if name == "combine_left" else 10**6)


def regroup_kernel(shards, keep_ref, core_ref, first_a, first_b, second_a, second_b, *refs):
    outs, (held_wide, held_a, held_b, group_ref, sem, out_sem) = refs[:shards], refs[shards:]
    rows, total = held_wide.shape[1] - 16, held_wide.shape[2]
    width = total // 5
    part = width // shards
    copies = [
        pltpu.make_async_copy(ref.at[pl.ds(0, rows)], held.at[pl.ds(0, rows)], sem.at[at])
        for at, (ref, held) in enumerate(
            (
                (keep_ref, held_wide.at[0]), (core_ref, held_wide.at[1]), (first_a, held_a.at[0]), (first_b, held_b.at[0]),
                (second_a, held_a.at[1]), (second_b, held_b.at[1]),
            )
        )
    ]
    copies += [
        pltpu.make_async_copy(ref.at[pl.ds(ref.shape[0] - 16, 16)], held.at[pl.ds(rows, 16)], sem.at[6 + at])
        for at, (ref, held) in enumerate(
            ((keep_ref, held_wide.at[0]), (core_ref, held_wide.at[1]), (first_a, held_a.at[0]), (second_a, held_a.at[1]))
        )
    ]
    for copy in copies:
        copy.start()
    for copy in copies:
        copy.wait()
    sums = []
    for half, held in enumerate((held_a, held_b)):
        cols = slice(half * total // 2, (half + 1) * total // 2)
        value = held_wide[0, :rows, cols].astype(F32) + held_wide[1, :rows, cols].astype(F32)
        sums.append(value + held[0, :rows].astype(F32) + held[1, :rows].astype(F32))
    whole = jnp.concatenate(sums, axis=1)
    vectors = [held[at, rows:, :width].astype(F32) for held in (held_wide, held_a) for at in (0, 1)]
    vectors = add_all(vectors).astype(BF)
    for shard in range(shards):
        for slot in range(5):
            at = slot * width + shard * part
            group_ref[shard, :rows, slot * part : (slot + 1) * part] = whole[:, at : at + part].astype(BF)
        group_ref[shard, rows:, :width] = vectors
        group_ref[shard, rows:, width:] = jnp.zeros((16, 5 * part - width), BF)
    me = lax.axis_index("tensor")
    backs = [pltpu.make_async_copy(group_ref.at[me ^ bits], outs[bits], out_sem.at[bits]) for bits in range(shards)]
    for back in backs:
        back.start()
    for back in backs:
        back.wait()


def regroup(shards, keep, core, first, second, deps=()):
    total = keep.shape[1]
    rows = second[0].shape[0]
    shape = (rows, total // shards)
    scratch = [
        pltpu.VMEM((2, rows, total), BF), pltpu.VMEM((2, rows, total // 2), BF), pltpu.VMEM((2, rows, total // 2), BF),
        pltpu.VMEM((shards, *shape), BF), pltpu.SemaphoreType.DMA((10,)), pltpu.SemaphoreType.DMA((shards,)),
    ]
    ins = [("b", value) for value in (keep, core, *first, *second)]
    outs = [("b", shape, BF)] * shards
    return call(functools.partial(regroup_kernel, shards), outs, ins, deps, scratch, "regroup", 10**6)


class Exchange:
    def __init__(self, width):
        self.data = lax.axis_size("dp")
        self.tensor = lax.axis_size("tensor")
        self.by_hand = self.data == 8 and width % (32 * self.data) == 0
        self.blocks = self.data if self.by_hand else 1

    def data_swap(self, value, bit):
        pairs = [(at, at ^ bit) for at in range(self.data)]
        return lax.ppermute(value, "dp", pairs)

    def tensor_swap(self, value, bits):
        pairs = [(at, at ^ bits) for at in range(self.tensor)]
        return lax.ppermute(value, "tensor", pairs)


def add_low(left, right):
    return (left.astype(F32) + right.astype(F32)).astype(BF)


class Share:
    def __init__(self, swap, rows, first):
        self.swap, self.rows, self.first = swap, rows, first
        self.count = swap.tensor - 1

    def spread(self, packed):
        self.found = [(0, packed)]
        if self.swap.blocks > 1:
            bits = [1 << at for at in range(1, self.swap.data.bit_length() - 1)]
            mine = self.found[0][1]
            self.near = [(bit, self.swap.data_swap(mine, bit)) for bit in bits]
            self.found += self.near

    def cross(self):
        if self.swap.data == 8 and self.swap.blocks == 8:
            other = 6 - self.first
            self.found.append((6, self.swap.data_swap(dict(self.near)[self.first], other)))

    def finish(self):
        found = list(self.found)
        if self.swap.blocks > 1:
            found += [(block | 1, self.swap.data_swap(value, 1)) for block, value in self.found]
        return [(block, self.rows, value) for block, value in found]


def add_all(terms):
    total = terms[0].astype(F32)
    for term in terms[1:]:
        total += term.astype(F32)
    return total


def tensor_sum(swap, parts):
    return add_all([parts[0]] + [swap.tensor_swap(parts[bits], bits) for bits in range(1, swap.tensor)])


def per_device(
    h_in, g_in, seg_ids, target_flags, perm_order, w_query, w_key, w_value, w_out, w_rel, attn_bias, seg_embed,
    norm_gain, norm_bias, w_up, b_up, w_down, b_down, d_h_out, d_g_out,
):
    seq_count, length, width = h_in.shape
    assert seq_count == 1
    swap = Exchange(width)
    parts, shards = swap.blocks, swap.tensor
    by_hand = swap.by_hand
    dp_at, tensor_at = lax.axis_index("dp"), lax.axis_index("tensor")
    own_part = width // shards
    rel_host = rel_table(length, width)
    rel, rev = jnp.asarray(rel_host), jnp.asarray(np.ascontiguousarray(rel_host[::-1]))
    h, g = h_in[0], g_in[0]
    up, down = w_up[0], w_down[0]
    bias, table = attn_bias.reshape(1, -1), seg_embed.reshape(1, -1)
    gains, shifts = norm_gain.reshape(1, -1), norm_bias.reshape(1, -1)

    mine = share_slices(parts, up, down, b_up)
    rows = (mine.shape[0] - 16) // 2
    fetched = [swap.tensor_swap(mine, bits) for bits in range(1, shards)]
    share_up, share_down = Share(swap, rows, 2), Share(swap, rows, 4)
    q, key, value, relkey, mask, half, relrev, left_x, left_rev = project(
        parts, h, g, seg_ids, target_flags, perm_order, w_query[0], w_key[0], w_value[0], w_rel[0], rel, rev, ()
    )
    att_one, prob_one = attention_first(q, key, value, relkey, mask, half, bias, table, ())
    packed_up, packed_down = pack_rows(fetched, rows, [att_one])
    share_up.spread(packed_up)
    share_down.spread(packed_down)
    resid_one, mid, prob_two, att, left_att = attention_second(
        parts, w_out[0], h, g, q, key, value, relkey, mask, half, att_one, bias, table, gains, shifts,
        [share_up.found[0][1], share_down.found[0][1]],
    )
    share_up.cross()
    act_own, slope_own = feed_up_own(mid, up, b_up, [found for _, found in share_up.found[:3]])
    share_down.cross()
    act_rest, slope_rest, up_rest = feed_up(
        shards, mid, 2 * rows, fetched, share_up.finish(), [found for _, found in share_down.found]
    )
    out_h, out_g, dresid_two, dbranch, keep_down, send_down, vec_two, down_rest = feed_down(
        parts, shards, down, act_own, act_rest, resid_one, b_down, gains, shifts, d_h_out[0], d_g_out[0],
        share_down.finish(), (),
    )

    hidden, wide = shards * width, 5 * width
    block, middle = width // 8, width // 4
    size = (10 + shards) * width

    def first_far(keep, core, deps, name):
        cut = keep.shape[1] // 2
        odd = [(at, block, [(0, block + 2 * at, 0), (1, block + 2 * at, 0)]) for at in (0, block)]
        upper = [(0, middle, [(0, middle, cut), (1, middle, cut)])]
        more = keep.shape[0] - 2 * middle
        if more:
            odd.append((middle, more, [(0, 2 * middle, 0), (1, 2 * middle, 0)]))
        return combine([keep, core], [(middle + more, cut, odd), (middle, cut, upper)], deps, name)

    def first_swap(far):
        return swap.data_swap(far[0], 2), swap.data_swap(far[1], 4)

    def second_far(keep, core, first, deps, name):
        cut = keep.shape[1] // 2
        more = keep.shape[0] - 2 * middle
        upper = [(0, block, [(0, middle, 0), (1, middle, 0), (2, block, 0)])]
        if more:
            upper.append((block, more, [(0, 2 * middle, 0), (1, 2 * middle, 0), (2, middle, 0)]))
        return combine(
            [keep, core, *first],
            [
                (block + more, cut, upper),
                (block, cut, [(0, block, [(0, block, cut), (1, block, cut), (3, block, 0)])]),
            ],
            deps,
            name,
        )

    def second_swap(far):
        return swap.data_swap(far[0], 4), swap.data_swap(far[1], 2)

    if by_hand:
        core_down = swap.data_swap(send_down, 1)
    dpre, keep_up, send_up, dbias_up = feed_back_up(parts, shards, down, down_rest, dbranch, mid, slope_own, slope_rest, ())
    deps = ()
    if by_hand:
        core_up = swap.data_swap(send_up, 1)
        far_down = first_far(keep_down, core_down, (), "combine")
        first_down = first_swap(far_down)
        side = left_columns(width)
        rest = width - side
        cut, quarter = shards * side, shards * rest // 2
        odd = [(at, block, [(0, block + 2 * at, cut), (1, block + 2 * at, cut)]) for at in (0, block)]
        far_up = combine(
            [keep_up, core_up],
            [
                *((2 * middle, side, [(0, 2 * middle, [(0, 0, k * side), (1, 0, k * side)])]) for k in range(1, shards)),
                (middle, quarter, odd),
                (middle, quarter, [(0, middle, [(0, middle, cut + quarter), (1, middle, cut + quarter)])]),
            ],
            far_down,
            "combine",
        )
        came_up = [swap.tensor_swap(far_up[bits - 1], bits) for bits in range(1, shards)]
        first_up = first_swap(far_up[-2:])
        deps = far_up[-1:]
    dproj, dresid_one, vec_one = feed_back_mid(shards, up, up_rest, dpre, dresid_two, resid_one, gains, deps)
    common = (w_out[0], dproj, q, att, key, value, prob_one, prob_two, relrev, half)
    back_first = attention_back_first(tuple(range(PAIRS // 2)), common, bias, table, ())
    deps = ()
    if by_hand:
        far_down = second_far(keep_down, core_down, first_down, back_first[-1:], "combine")
        second_down = second_swap(far_down)
        deps = far_down
    dq, dkey, dvalue, keep_att, send_att = attention_back(
        tuple(range(PAIRS // 2, PAIRS)), common, (left_x, left_rev, left_att), back_first, (vec_one, vec_two, dbias_up),
        bias, table, [*deps, *came_up] if by_hand else deps,
    )
    if by_hand:
        (send_att, keep_att), (first_up, second_down) = lax.optimization_barrier(
            ((send_att, keep_att), (first_up, second_down))
        )
        core_att = swap.data_swap(send_att, 1)
        all_up = [keep_up, core_up, *came_up]
        left = range(len(all_up))
        far_up = combine(
            [*all_up, *first_up],
            [
                (block, quarter, [(0, block, [(0, middle, cut), (1, middle, cut), (shards + 1, block, 0)])]),
                (block, quarter, [(0, block, [(0, block, cut + quarter), (1, block, cut + quarter), (shards + 2, block, 0)])]),
                (middle, side, [(0, middle, [(at, middle, 0) for at in left])]),
            ],
        )
        second_up = second_swap(far_up[:2])
        left_y = swap.data_swap(far_up[2], 4)
        far_att = first_far(keep_att, core_att, second_up, "combine_late")
        first_att = first_swap(far_att)
        arrays = [keep_down, core_down, *first_down, *second_down, *all_up, *first_up, *second_up]
        up_at, per, outs = 6, shards // 2, []
        half_at = up_at + len(all_up)
        for k in range(shards):
            half, near = k // per, k % per
            outs.append(
                (
                    block,
                    width + rest,
                    [
                        (0, block, [(0, 0, k * width), (1, 0, k * width), (2 + half, 0, near * width), (4 + half, 0, near * width)],
                         0, width),
                        (0, block, [(up_at, 0, cut + k * rest), (up_at + 1, 0, cut + k * rest), (half_at + half, 0, near * rest),
                                    (half_at + 2 + half, 0, near * rest)], width, rest),
                    ],
                )
            )
        feed_parts = combine(arrays, outs, far_att)
        came = [swap.tensor_swap(feed_parts[bits], bits) for bits in range(1, shards)]
        grad_h, grad_g = input_grads(w_query[0], w_key[0], w_value[0], dq, dkey, dvalue, dresid_one, feed_parts[:1])
        far_att = second_far(keep_att, core_att, first_att, [*came[:1], grad_h], "combine_att")
        second_att = second_swap(far_att)
        left_own, far_left = combine(
            [*all_up, left_y],
            [(block, side, [(0, block, [(at, row, 0) for at in range(shards + 2)])]) for row in (0, block)],
            [*far_att],
            "combine_left",
        )
        left_x = swap.data_swap(far_left, 2)
        att_parts = regroup(shards, keep_att, core_att, first_att, second_att, came)
    else:
        grad_h, grad_g = input_grads(w_query[0], w_key[0], w_value[0], dq, dkey, dvalue, dresid_one, ())
        vectors = lax.psum(keep_att[width // 2 : width // 2 + 10 + shards, :width].astype(F32), AXES)
        keep_att, send_att = keep_att[: width // 2], send_att[: width // 2]

        def rows_sum(keep, send):
            whole = jnp.concatenate([keep, send], axis=0)
            return lax.psum_scatter(whole, "dp", scatter_dimension=0, tiled=True)

        sum_up, sum_down, sum_att = (
            rows_sum(keep, send) for keep, send in ((keep_up, send_up), (keep_down, send_down), (keep_att, send_att))
        )
        cols = [slice(shard * width, (shard + 1) * width) for shard in range(shards)]
        side = left_columns(width)
        left, right = sum_up[:, : shards * side], sum_up[:, shards * side :]
        rest = width - side
        d_up = [
            jnp.concatenate([left[:, k * side : (k + 1) * side], right[:, k * rest : (k + 1) * rest]], axis=1)
            for k in range(shards)
        ]
        d_up = tensor_sum(swap, d_up)
        d_down = tensor_sum(swap, [sum_down[:, part] for part in cols]).T
        split = sum_att.reshape(-1, 5, shards, own_part).transpose(2, 0, 1, 3).reshape(shards, -1, 5 * own_part)
        att_parts = [lax.dynamic_index_in_dim(split, tensor_at ^ bits, 0, keepdims=False) for bits in range(shards)]
    att_parts = [att_parts[0]] + [swap.tensor_swap(att_parts[bits], bits) for bits in range(1, shards)]
    if by_hand:
        came, _ = lax.optimization_barrier((came, att_parts[1]))
        d_feed = add_all([feed_parts[0], *came])
        d_up = jnp.concatenate([add_all([left_own, left_x]), d_feed[:, width:]], axis=1)
        d_down = d_feed[:, :width].T
        (d_up, d_down), att_parts = lax.optimization_barrier(((d_up, d_down), att_parts))
    d_att = add_all(att_parts)
    if by_hand:
        d_att, vectors = d_att[:block], d_att[block : block + 10 + shards, :width]
    d_att = [d_att[:, slot * own_part : (slot + 1) * own_part] for slot in range(5)]

    own = size // (swap.data * shards)
    d_vectors = lax.dynamic_slice_in_dim(vectors.reshape(-1), (dp_at * shards + tensor_at) * own, own, 0)

    return (
        out_h[None], out_g[None], grad_h[None], grad_g[None],
        d_att[0][None], d_att[1][None], d_att[2][None], d_att[3][None], d_att[4][None],
        d_up[None], d_down[None], d_vectors[None],
    )


def solution(mesh):
    every = P(AXES, None, None)
    rows = P(AXES, None)
    in_specs = (
        every, every, rows, rows, rows, P(), P(), P(), P(), P(), P(), P(), P(), P(),
        P(None, None, "tensor"), P(None, "tensor"), P(None, "tensor", None), P(), every, every,
    )
    grads = P(None, "dp", "tensor")
    out_specs = (
        every, every, every, every, grads, grads, grads, grads, grads, grads,
        P(None, "tensor", "dp"), P(None, AXES),
    )
    return jax.shard_map(per_device, mesh=mesh, in_specs=in_specs, out_specs=out_specs, check_vma=False)
```

```python
import functools
import math

import jax
import jax.numpy as jnp
import numpy as np
from jax import lax
from jax.experimental import pallas as pl
from jax.experimental.pallas import tpu as pltpu
from jax.sharding import PartitionSpec as P

HEADS = 12
HEAD_DIM = 64
LANES = 128
PAIRS = HEADS // 2
NEGATIVE = -1e30
EPSILON = 1e-06
AXES = ("dp", "tensor")
BF = jnp.bfloat16
F32 = jnp.float32
FIRST_PAIRS = 4
VMEM_MIB = {
    "share_slices": 60, "project": 50, "attention_first": 12, "attention_second": 14, "feed_up_own": 6, "feed_up": 14, "feed_down": 22,
    "feed_back_up": 16, "feed_back_mid": 10, "attention_back_first": 18, "attention_back": 26, "input_grads": 14, "pack_rows": 2,
    "combine": 12, "combine_late": 12, "combine_att": 59, "combine_left": 59, "regroup": 59,
}


def rel_table(length, model_width):
    position = (length - np.arange(2 * length)).astype(np.float32)
    frequency = np.float32(1.0) / np.float32(10000.0) ** (
        np.arange(0, model_width, 2).astype(np.float32) / np.float32(model_width)
    )
    angles = position[:, None] * frequency[None, :]
    return np.concatenate([np.sin(angles), np.cos(angles)], axis=1).astype(BF)


class Late:
    def __init__(self, source, target, sem):
        self.target, self.waiting = target, True
        self.copy = pltpu.make_async_copy(source, target, sem)
        self.copy.start()

    def get(self):
        if self.waiting:
            self.copy.wait()
            self.waiting = False
        return self.target


class Early:
    def __init__(self, ref, target, sems):
        self.ref, self.target, self.sems, self.copies = ref, target, sems, []

    def send(self, *where):
        source, target = (self.ref.at[where], self.target.at[where]) if where else (self.ref, self.target)
        copy = pltpu.make_async_copy(source, target, self.sems.at[len(self.copies)])
        copy.start()
        self.copies.append(copy)


SENDS = 16


def call(kernel, outs, ins, deps, scratch, name, flops):
    deps = tuple(deps)
    spaces = {"s": pltpu.SMEM, "v": pltpu.VMEM, "h": pl.ANY, "l": pltpu.HBM, "e": pltpu.HBM, "b": pltpu.HBM}
    late = [value for kind, value in ins if kind == "l"]
    early = [(shape, dtype) for kind, shape, dtype in outs if kind == "e"]
    more = [pltpu.VMEM(value.shape, value.dtype) for value in late] + [pltpu.VMEM(*spec) for spec in early]
    if late:
        more.append(pltpu.SemaphoreType.DMA((len(late),)))
    if early:
        more.append(pltpu.SemaphoreType.DMA((len(early), SENDS)))
    first_out = len(ins) + len(deps)
    first_scratch = first_out + len(outs)

    def wrapped(*refs):
        own = refs[first_scratch + len(scratch) :]
        late_refs, early_refs = own[: len(late)], own[len(late) : len(late) + len(early)]
        sems = list(own[len(late) + len(early) :])
        late_sem = sems.pop(0) if late else None
        early_sem = sems.pop(0) if early else None
        given, at = [], 0
        for (kind, _), ref in zip(ins, refs[: len(ins)], strict=True):
            if kind == "l":
                ref = Late(ref, late_refs[at], late_sem.at[at])
                at += 1
            given.append(ref)
        made, at = [], 0
        for (kind, _, _), ref in zip(outs, refs[first_out:first_scratch], strict=True):
            if kind == "e":
                ref = Early(early_refs[at], ref, early_sem.at[at])
                at += 1
            made.append(ref)
        kernel(*given, *made, *refs[first_scratch : first_scratch + len(scratch)])
        for item in given:
            if isinstance(item, Late):
                item.get()
        for item in made:
            if isinstance(item, Early):
                for copy in item.copies:
                    copy.wait()

    return pl.pallas_call(
        wrapped,
        out_shape=[jax.ShapeDtypeStruct(shape, dtype) for _, shape, dtype in outs],
        in_specs=[pl.BlockSpec(memory_space=spaces[kind]) for kind, _ in ins]
        + [pl.BlockSpec(memory_space=pl.ANY)] * len(deps),
        out_specs=[pl.BlockSpec(memory_space=spaces[kind]) for kind, _, _ in outs],
        scratch_shapes=list(scratch) + more,
        compiler_params=pltpu.CompilerParams(vmem_limit_bytes=VMEM_MIB[name] * 1024 * 1024),
        cost_estimate=pl.CostEstimate(flops=flops * 100, bytes_accessed=flops // 1000, transcendentals=0),
        name=name,
    )(*[value for _, value in ins], *deps)


def nn(left, right):
    return lax.dot_general(left, right, (((1,), (0,)), ((), ())), preferred_element_type=F32)


def nt(left, right):
    return lax.dot_general(left, right, (((1,), (1,)), ((), ())), preferred_element_type=F32)


def tn(left, right):
    return lax.dot_general(left, right, (((0,), (0,)), ((), ())), preferred_element_type=F32)


def lane_index(rows):
    return lax.broadcasted_iota(jnp.int32, (rows, LANES), 1)


def pair_lanes(pair):
    return pl.ds(pl.multiple_of(pair * LANES, LANES), LANES)


def row_lanes(row, pair, width):
    return pl.ds(pl.multiple_of(row * width + pair * LANES, LANES), LANES)


def norm_stats(source):
    mean = jnp.mean(source, axis=-1, keepdims=True)
    centered = source - mean
    variance = jnp.mean(centered * centered, axis=-1, keepdims=True)
    rstd = lax.rsqrt(variance + EPSILON)
    return centered * rstd, rstd


def norm_back(grad, xhat, rstd, gain):
    dxhat = grad * gain
    mean_one = jnp.mean(dxhat, axis=-1, keepdims=True)
    mean_two = jnp.mean(dxhat * xhat, axis=-1, keepdims=True)
    return rstd * (dxhat - mean_one - xhat * mean_two)


def seg_coefficients(half_wide, lane):
    return jnp.where(lane % HEAD_DIM == 0, half_wide, 1.0 - 2.0 * half_wide)


def seg_keys(half_wide, lane):
    place = lane % HEAD_DIM
    return jnp.where(place == 0, 1.0, jnp.where(place == 1, half_wide, 0.0))


def seg_table(seg_ref, pair, width):
    row = lax.broadcasted_iota(jnp.int32, (LANES, LANES), 0)
    lane = lax.broadcasted_iota(jnp.int32, (LANES, LANES), 1)
    one = jnp.broadcast_to(seg_ref[0:1, pair_lanes(pair)], (LANES, LANES)).T
    two = jnp.broadcast_to(seg_ref[0:1, row_lanes(1, pair, width)], (LANES, LANES)).T
    base = jnp.where(row < HEAD_DIM, HEAD_DIM, 0)
    at_one = lane == base
    at_two = at_one | (lane == base + 1)
    return jnp.concatenate([jnp.where(at_one, one, 0.0), jnp.where(at_two, two - one, 0.0)], axis=1).astype(BF)


def attend_pair(pair, first, q_ref, key_ref, value_ref, relkey_ref, mask_ref, half_ref, bias_ref, seg_ref, prob_ref, att_ref):
    length, width = key_ref.shape
    block = length // 2
    lanes = pair_lanes(pair)
    lane_q = lane_index(2 * length)
    lane_k = lane_index(length)
    low_q = lane_q < HEAD_DIM
    low_k = lane_k < HEAD_DIM
    half_w = half_ref[...]
    scale = 1.0 / math.sqrt(HEAD_DIM)
    query = q_ref[:, lanes]
    word = ((query + bias_ref[0:1, lanes]) * scale).astype(BF)
    relq = ((query + bias_ref[0:1, row_lanes(1, pair, width)]) * scale).astype(BF)
    segq = ((query + bias_ref[0:1, row_lanes(2, pair, width)]) * scale).astype(BF)
    terms = nn(segq, seg_table(seg_ref, pair, width))
    coef = seg_coefficients(jnp.concatenate([half_w, half_w], axis=0), lane_q)
    extra = (terms[:, :LANES] + terms[:, LANES:] * coef).astype(BF)
    key_extra = seg_keys(half_w, lane_k).astype(BF)
    key = key_ref[:, lanes]
    value = value_ref[:, lanes]
    zero = jnp.zeros_like(relq)
    attended = []
    for head in (0, 1):
        if head == 0:
            word_one = jnp.where(low_q, word, extra)
            key_one = jnp.where(low_k, key, key_extra)
            rel_one = jnp.where(low_q, relq, zero)
        else:
            word_one = jnp.where(low_q, extra, word)
            key_one = jnp.where(low_k, key_extra, key)
            rel_one = jnp.where(low_q, zero, relq)
        score = nt(word_one, key_one)
        for part in (0, 1):
            base = block - block * part
            rows_h = slice(block * part, block * part + block)
            rows_g = slice(length + block * part, length + block * part + block)
            rel_rows = jnp.concatenate([rel_one[rows_h], rel_one[rows_g]], axis=0)
            raw = nt(rel_rows, relkey_ref[base : base + 3 * block, lanes])
            for place_at, rows in ((0, rows_h), (1, rows_g)):
                shifted = pltpu.roll(
                    raw[place_at * block : (place_at + 1) * block], 2 * block, 1, stride=1, stride_axis=0
                )[:, :length]
                logits = score[rows] + shifted + mask_ref[rows]
                top = jnp.max(logits, axis=1, keepdims=True)
                power = jnp.exp(logits - top)
                total = jnp.sum(power, axis=1, keepdims=True)
                prob_ref[2 * (pair - first) + head, rows, :] = (power * (1.0 / total)).astype(BF)
        attended.append(nn(prob_ref[2 * (pair - first) + head], value))
    att_ref[:, lanes] = jnp.where(low_q, attended[0], attended[1]).astype(BF)


def project_kernel(
    parts, h_late, g_late, wq_late, wk_late, wv_late, rel_late, wr_late, rev_late,
    seg_row, flag_row, order_row,
    q_ref, key_ref, value_ref, relkey_ref, mask_ref, half_ref, relrev_out, left_x_out, left_rev_out,
    x_ref, raw_ref,
):
    h_ref, g_ref = h_late.get(), g_late.get()
    length, width = h_ref.shape
    x_ref[:length] = h_ref[...]
    x_ref[length:] = g_ref[...]

    def project(left, right_late, target):
        right = right_late.get()
        for col in range(0, width, 256):
            cols = slice(col, col + 256)
            target[:, cols] = nn(left[...], right[:, cols]).astype(target.dtype)

    project(x_ref, wq_late, q_ref)
    project(h_ref, wk_late, key_ref)
    project(h_ref, wv_late, value_ref)
    project(rel_late.get(), wr_late, relkey_ref)

    def wide(row_ref):
        return jnp.broadcast_to(row_ref[...].astype(F32), (length, length))

    row_at = lax.broadcasted_iota(jnp.int32, (length, length), 0)
    col_at = lax.broadcasted_iota(jnp.int32, (length, length), 1)
    seg, order = wide(seg_row), wide(order_row)
    same_doc = seg.T == seg
    start = jnp.min(jnp.where(same_doc, col_at.astype(F32), float(length)), axis=1, keepdims=True)
    in_doc = jnp.sum(jnp.where(same_doc, 1.0, 0.0), axis=1, keepdims=True)
    place = lax.broadcasted_iota(jnp.int32, (length, 1), 0).astype(F32)
    half = jnp.where(2.0 * (place - start) >= in_doc, 1.0, 0.0)
    half_ref[...] = jnp.broadcast_to(half, (length, LANES))
    content = same_doc & ((wide(flag_row) == 0.0) | (order <= order.T))
    mask_ref[:length] = jnp.where(content, 0.0, NEGATIVE)
    mask_ref[length:] = jnp.where(content & (row_at != col_at), 0.0, NEGATIVE)

    project(rev_late.get(), wr_late, relrev_out.ref)
    relrev_out.send()
    turn_rows(lambda col: x_ref[:, col : col + 256], raw_ref.at[0], left_x_out.ref, parts)
    left_x_out.send()
    rev_ref = rev_late.get()
    turn_rows(lambda col: rev_ref[:, col : col + 256], raw_ref.at[1], left_rev_out.ref, parts)
    left_rev_out.send()


def project(parts, h, g, seg, flag, order, wq, wk, wv, wr, rel, rev, deps):
    length, width = h.shape
    two = 2 * length
    outs = [
        ("v", (two, width), F32), ("v", (length, width), BF), ("v", (length, width), BF), ("v", (two, width), BF),
        ("v", (two, length), F32), ("v", (length, LANES), F32), ("e", (two, width), BF), ("e", (width, two), BF),
        ("e", (width, two), BF),
    ]
    ins = [("l", value) for value in (h, g, wq, wk, wv, rel, wr, rev)] + [("v", value) for value in (seg, flag, order)]
    scratch = [pltpu.VMEM((two, width), BF), pltpu.VMEM((2, width, two), BF)]
    return call(functools.partial(project_kernel, parts), outs, ins, deps, scratch, "project", 5 * 10**9)


def attention_first_kernel(
    q_ref, key_ref, value_ref, relkey_ref, mask_ref, half_ref, bias_ref, seg_ref, att_ref, prob_out
):
    def pair_step(pair, carry):
        attend_pair(
            pair, 0, q_ref, key_ref, value_ref, relkey_ref, mask_ref, half_ref, bias_ref, seg_ref, prob_out.ref, att_ref
        )
        return carry

    for first in range(0, FIRST_PAIRS, 2):
        lax.fori_loop(first, first + 2, pair_step, 0)
        prob_out.send(pl.ds(2 * first, 4))


def attention_first(q, key, value, relkey, mask, half, bias, table, deps):
    two, length = mask.shape
    outs = [("v", (two, FIRST_PAIRS * LANES), BF), ("e", (2 * FIRST_PAIRS, two, length), BF)]
    ins = [("v", x) for x in (q, key, value, relkey, mask, half, bias, table)]
    return call(attention_first_kernel, outs, ins, deps, [], "attention_first", 5 * 10**9)


def attention_second_kernel(
    parts, wo_late, h_late, g_late, q_ref, key_ref, value_ref, relkey_ref, mask_ref, half_ref, att_first_ref,
    bias_ref, seg_ref, gain_ref, shift_ref,
    resid_ref, mid_ref, prob_out, att_out, left_att_out,
    raw_ref,
):
    length, width = key_ref.shape
    att_ref = att_out.ref
    att_ref[:, : FIRST_PAIRS * LANES] = att_first_ref[...]

    def pair_step(pair, carry):
        attend_pair(
            pair, FIRST_PAIRS, q_ref, key_ref, value_ref, relkey_ref, mask_ref, half_ref, bias_ref, seg_ref, prob_out.ref, att_ref
        )
        return carry

    for first in range(FIRST_PAIRS, PAIRS, 2):
        lax.fori_loop(first, first + 2, pair_step, 0)
        prob_out.send(pl.ds(2 * (first - FIRST_PAIRS), 4))
    att_out.send()
    wo_ref, h_ref, g_ref = wo_late.get(), h_late.get(), g_late.get()
    for col in range(0, width, 256):
        cols = slice(col, col + 256)
        total = nn(att_ref[...], wo_ref[:, cols])
        resid_ref[:length, cols] = h_ref[:, cols].astype(F32) + total[:length]
        resid_ref[length:, cols] = g_ref[:, cols].astype(F32) + total[length:]
    turn_rows(lambda col: att_ref[:, col : col + 256], raw_ref, left_att_out.ref, parts)
    left_att_out.send()
    for row in range(0, 2 * length, 64):
        xhat, _ = norm_stats(resid_ref[row : row + 64, :])
        mid_ref[row : row + 64, :] = (xhat * gain_ref[0:1, :width] + shift_ref[0:1, :width]).astype(BF)


def attention_second(parts, wo, h, g, q, key, value, relkey, mask, half, att, bias, table, gain, shift, deps):
    length, width = h.shape
    two = 2 * length
    outs = [
        ("v", (two, width), F32), ("v", (two, width), BF), ("e", (HEADS - 2 * FIRST_PAIRS, two, length), BF),
        ("e", (two, width), BF), ("e", (width, two), BF),
    ]
    ins = [("l", value) for value in (wo, h, g)]
    ins += [("v", value) for value in (q, key, value, relkey, mask, half, att, bias, table, gain, shift)]
    return call(
        functools.partial(attention_second_kernel, parts), outs, ins, deps, [pltpu.VMEM((width, two), BF)],
        "attention_second", 10 * 10**9,
    )


def place_rows(raw_ref, out_ref, parts):
    rows = raw_ref.shape[0] // parts
    me = lax.axis_index("dp") if parts > 1 else 0
    order = [low | (rest << 1) for low in (0, 1) for rest in range(parts // 2)] if parts > 1 else [0]
    for at, block in enumerate(order):
        source = pl.multiple_of((me ^ block) * rows, rows)
        out_ref[at * rows : (at + 1) * rows, :] = raw_ref[pl.ds(source, rows), :]


def turn_rows(source, raw_ref, out_ref, parts):
    for col in range(0, raw_ref.shape[0], 256):
        raw_ref[col : col + 256, :] = source(col).astype(F32).T.astype(BF)
    place_rows(raw_ref, out_ref, parts)


def back_pairs(
    pairs, dproj_ref, wo_ref, q_ref, att_ref, key_ref, value_ref, prob_one, prob_two, relrev_ref, half_ref, bias_ref, seg_ref,
    dq_ref, dkey_ref, dvalue_ref, drel_ref, vec_ref, datt_ref,
):
    length, width = key_ref.shape
    block = length // 2
    for at, pair in enumerate(pairs):
        rows = slice(pair * LANES, (pair + 1) * LANES)
        datt_ref[:, at * LANES : (at + 1) * LANES] = nt(dproj_ref[...], wo_ref[rows, :]).astype(BF)

    def pair_step(at, pair):
        lanes = slice(pair * LANES, (pair + 1) * LANES)
        own = slice(at * LANES, (at + 1) * LANES)
        prob_ref, prob_at = (prob_one, 2 * pair) if pair < FIRST_PAIRS else (prob_two, 2 * (pair - FIRST_PAIRS))
        lane_q = lane_index(2 * length)
        lane_k = lane_index(length)
        low_q = lane_q < HEAD_DIM
        low_k = lane_k < HEAD_DIM
        half_w = half_ref[...]
        flip_row = lax.broadcasted_iota(jnp.int32, (length, length), 0)
        flip_col = lax.broadcasted_iota(jnp.int32, (length, length), 1)
        flip = jnp.where(flip_row + flip_col == length - 1, 1.0, 0.0).astype(BF)
        sel_row = lax.broadcasted_iota(jnp.int32, (2 * LANES, LANES), 0) % LANES
        sel_col = lax.broadcasted_iota(jnp.int32, (2 * LANES, LANES), 1)
        select = jnp.where(
            ((sel_row < HEAD_DIM) & ((sel_col == HEAD_DIM) | (sel_col == HEAD_DIM + 1)))
            | ((sel_row >= HEAD_DIM) & (sel_col < 2)),
            1.0,
            0.0,
        ).astype(BF)
        query = q_ref[:, lanes]
        word = query + bias_ref[0:1, lanes]
        relq = query + bias_ref[0:1, row_lanes(1, pair, width)]
        segq = (query + bias_ref[0:1, row_lanes(2, pair, width)]).astype(BF)
        word_t = word.T.astype(BF)
        relq_t = relq.T.astype(BF)
        datt = datt_ref[:, own]
        datt_wide = datt.astype(F32)
        datt_t = datt_wide.T.astype(BF)
        datt_scaled = datt_wide * (1.0 / math.sqrt(HEAD_DIM))
        product = datt_scaled * att_ref[:, lanes].astype(F32)
        product_high = product.astype(BF)
        product_low = (product - product_high.astype(F32)).astype(BF)
        delta = nn(jnp.concatenate([product_high, product_low], axis=1), select)
        delta_high = delta.astype(BF).astype(F32)
        minus = jnp.where(lane_q % HEAD_DIM == 0, -delta_high, delta_high - delta).astype(BF)
        datt_low = datt_scaled.astype(BF)
        key_extra = seg_keys(half_w, lane_k).astype(BF)
        ones_extra = jnp.where(lane_k % HEAD_DIM < 2, 1.0, 0.0).astype(BF)
        key = key_ref[:, lanes]
        value = value_ref[:, lanes]
        dword, drel = [], []
        for head in (0, 1):
            rows_t = slice(HEAD_DIM * head, HEAD_DIM * head + HEAD_DIM)
            if head == 0:
                datt_one = jnp.where(low_q, datt_low, minus)
                value_one = jnp.where(low_k, value, ones_extra)
                key_one = jnp.where(low_k, key, key_extra)
            else:
                datt_one = jnp.where(low_q, minus, datt_low)
                value_one = jnp.where(low_k, ones_extra, value)
                key_one = jnp.where(low_k, key_extra, key)
            prob = prob_ref[prob_at + head]
            dprob = nt(datt_one, value_one)
            dscore = (prob.astype(F32) * dprob).astype(BF)
            dword.append(nn(dscore, key_one))
            rows_out = slice(at * LANES + HEAD_DIM * head, at * LANES + HEAD_DIM * (head + 1))
            dkey_ref[rows_out, :] = nn(word_t[rows_t], dscore).astype(BF)
            dvalue_ref[rows_out, :] = nn(datt_t[rows_t], prob).astype(BF)
            flipped = nn(dscore, flip).astype(BF)
            pad = jnp.zeros((block, block), BF)
            rel_parts, drel_t = [], []
            for part in (0, 1):
                rows_h = slice(block * part, block * part + block)
                rows_g = slice(length + block * part, length + block * part + block)
                draw = jnp.concatenate(
                    [
                        pltpu.roll(jnp.concatenate([flipped[rows], pad], axis=1), 0, 1, stride=1, stride_axis=0)
                        for rows in (rows_h, rows_g)
                    ],
                    axis=0,
                )
                rel_parts.append(nn(draw, relrev_ref[block * part : block * part + 3 * block, lanes]))
                rel_cols = jnp.concatenate([relq_t[rows_t, rows_h], relq_t[rows_t, rows_g]], axis=1)
                drel_t.append(nn(rel_cols, draw))
            drel.append(
                jnp.concatenate(
                    [rel_parts[0][:block], rel_parts[1][:block], rel_parts[0][block:], rel_parts[1][block:]], axis=0
                )
            )
            drel_ref[rows_out, :] = jnp.concatenate(
                [
                    drel_t[0][:, :block],
                    drel_t[0][:, block:] + drel_t[1][:, : 2 * block],
                    drel_t[1][:, 2 * block :],
                ],
                axis=1,
            ).astype(BF)
        extra = jnp.where(low_q, dword[1], dword[0])
        dword_all = jnp.where(low_q, dword[0], dword[1])
        drel_all = jnp.where(low_q, drel[0], drel[1])
        coef = seg_coefficients(jnp.concatenate([half_w, half_w], axis=0), lane_q)
        dterms = jnp.concatenate([extra, extra * coef], axis=1).astype(BF)
        dsegq = nt(dterms, seg_table(seg_ref, pair, width))
        dtable = tn(dterms, segq)
        dq_ref[:, own] = (dword_all + drel_all + dsegq).astype(BF)
        low_one = lane_index(1) < HEAD_DIM
        first = jnp.where(low_one, dtable[HEAD_DIM : HEAD_DIM + 1], dtable[0:1])
        far = LANES + HEAD_DIM
        second = jnp.where(
            low_one, dtable[far : far + 1] + dtable[far + 1 : far + 2], dtable[LANES : LANES + 1] + dtable[LANES + 1 : LANES + 2]
        )
        vec_ref[0:1, own] = jnp.sum(dword_all, axis=0, keepdims=True)
        vec_ref[1:2, own] = jnp.sum(drel_all, axis=0, keepdims=True)
        vec_ref[2:3, own] = jnp.sum(dsegq, axis=0, keepdims=True)
        vec_ref[3:4, own] = first - second
        vec_ref[4:5, own] = second
    for at, pair in enumerate(pairs):
        pair_step(at, pair)


def attention_back_first_kernel(
    pairs, wo_late, dproj_ref, q_ref, att_ref, key_ref, value_ref, prob_one, prob_two, relrev_ref, half_ref, bias_ref, seg_ref,
    dq_ref, dkey_ref, dvalue_ref, drel_ref, vec_ref, datt_ref,
):
    vec_ref[...] = jnp.zeros_like(vec_ref)
    back_pairs(
        pairs, dproj_ref, wo_late.get(), q_ref, att_ref, key_ref, value_ref, prob_one, prob_two, relrev_ref, half_ref, bias_ref,
        seg_ref, dq_ref, dkey_ref, dvalue_ref, drel_ref, vec_ref, datt_ref,
    )


def attention_back_first(pairs, common, bias, table, deps):
    two, width = common[1].shape
    length, size = two // 2, len(pairs) * LANES
    outs = [
        ("v", (two, size), BF), ("v", (size, length), BF), ("v", (size, length), BF), ("v", (size, two), BF), ("v", (8, size), F32),
    ]
    ins = [("l", common[0])] + [("v", x) for x in (*common[1:], bias, table)]
    kernel = functools.partial(attention_back_first_kernel, pairs)
    return call(kernel, outs, ins, deps, [pltpu.VMEM((two, size), BF)], "attention_back_first", 12 * 10**9)


def attention_back_kernel(
    pairs, wo_late, dproj_ref, q_ref, att_ref, key_ref, value_ref, prob_one, prob_two, relrev_ref, half_ref, bias_ref, seg_ref,
    left_x_ref, left_rev_ref, left_att_ref, dq_one, dkey_one, dvalue_one, drel_one, vec_one, norm_one, norm_two, hidden_ref,
    dq_ref, dkey_ref, dvalue_ref, keep_out, send_out, datt_ref, drel_ref, vec_ref, packed_ref,
):
    length, width = key_ref.shape
    split = width // 2
    size = dq_one.shape[1]
    dq_ref[:, :size], dkey_ref[:size], dvalue_ref[:size], drel_ref[:size] = dq_one[...], dkey_one[...], dvalue_one[...], drel_one[...]
    vec_ref[...] = jnp.zeros_like(vec_ref)
    vec_ref[:, :size] = vec_one[...]
    back_pairs(
        pairs, dproj_ref, wo_late.get(), q_ref, att_ref, key_ref, value_ref, prob_one, prob_two, relrev_ref, half_ref, bias_ref,
        seg_ref, dq_ref.at[:, size:], dkey_ref.at[size:], dvalue_ref.at[size:], drel_ref.at[size:], vec_ref.at[:, size:], datt_ref,
    )
    shards = hidden_ref.shape[1] // width
    packed_ref[...] = jnp.zeros_like(packed_ref)
    packed_ref[0:5, :] = vec_ref[0:5, :]
    packed_ref[5:6, :] = norm_one[0:1, :]
    packed_ref[6:7, :] = norm_two[0:1, :]
    packed_ref[7:8, :] = norm_one[1:2, :]
    packed_ref[8:10, :] = norm_two[1:3, :]
    for shard in range(shards):
        place = 10 + (lax.axis_index("tensor") ^ shard)
        packed_ref[pl.ds(place, 1), :] = hidden_ref[0:1, shard * width : (shard + 1) * width]
    packed = packed_ref[...].astype(BF)
    for out in (send_out, keep_out):
        out.ref[split:, :width] = packed
        out.ref[split:, width:] = jnp.zeros((16, 4 * width), BF)
        out.send(pl.ds(split, 16))
    todo = [
        (left_x_ref[...], dq_ref, nn), (left_x_ref[:, :length], dkey_ref, nt), (left_x_ref[:, :length], dvalue_ref, nt),
        (left_att_ref[...], dproj_ref, nn), (left_rev_ref[...], drel_ref, nt),
    ]
    at = 0
    for left, right, dot in todo:
        count = right.shape[1] if dot is nn else right.shape[0]
        for col in range(0, count, 256):
            cols = slice(col, col + 256)
            piece = dot(left, right[:, cols] if dot is nn else right[cols, :]).astype(BF)
            keep_out.ref[:split, at + col : at + col + 256] = piece[:split]
            send_out.ref[:split, at + col : at + col + 256] = piece[split:]
        done = pl.ds(at, count)
        send_out.send(pl.ds(0, split), done)
        keep_out.send(pl.ds(0, split), done)
        at += count


def attention_back(pairs, common, lefts, first, vectors, bias, table, deps):
    two, width = common[1].shape
    length, size = two // 2, len(pairs) * LANES
    outs = [
        ("v", (two, width), BF), ("v", (width, length), BF), ("v", (width, length), BF),
        ("e", (width // 2 + 16, 5 * width), BF), ("e", (width // 2 + 16, 5 * width), BF),
    ]
    ins = [("l", common[0])] + [("v", x) for x in (*common[1:], bias, table, *lefts, *first, *vectors)]
    scratch = [
        pltpu.VMEM((two, size), BF), pltpu.VMEM((width, two), BF), pltpu.VMEM((8, width), F32), pltpu.VMEM((16, width), F32),
    ]
    return call(functools.partial(attention_back_kernel, pairs), outs, ins, deps, scratch, "attention_back", 12 * 10**9)


def input_grads_kernel(wq_late, wk_late, wv_late, dq_ref, dkey_ref, dvalue_ref, dresid_ref, grad_h, grad_g, sum_ref):
    length, width = grad_h.ref.shape
    wq_ref = wq_late.get()
    for col in range(0, width, 256):
        cols = slice(col, col + 256)
        low = nt(dq_ref[...], wq_ref[cols, :])
        sum_ref[:, cols] = dresid_ref[:length, cols] + low[:length]
        grad_g.ref[:, cols] = dresid_ref[length:, cols] + low[length:]
    grad_g.send()
    dkey, dvalue = dkey_ref[...].astype(F32).T.astype(BF), dvalue_ref[...].astype(F32).T.astype(BF)
    wk_ref, wv_ref = wk_late.get(), wv_late.get()
    for col in range(0, width, 256):
        cols = slice(col, col + 256)
        grad_h.ref[:, cols] = sum_ref[:, cols] + nt(dkey, wk_ref[cols, :]) + nt(dvalue, wv_ref[cols, :])
    grad_h.send()


def input_grads(wq, wk, wv, dq, dkey, dvalue, dresid, deps):
    two, width = dresid.shape
    outs = [("e", (two // 2, width), F32), ("e", (two // 2, width), F32)]
    ins = [("l", wq), ("l", wk), ("l", wv), ("v", dq), ("v", dkey), ("v", dvalue), ("v", dresid)]
    scratch = [pltpu.VMEM((two // 2, width), F32)]
    return call(input_grads_kernel, outs, ins, deps, scratch, "input_grads", 10**9)


def share_kernel(parts, up_hbm, down_hbm, bias_ref, out_ref, sem):
    rows = up_hbm.shape[0] // parts
    start = pl.multiple_of(lax.axis_index("dp") * rows, rows) if parts > 1 else 0
    one = pltpu.make_async_copy(up_hbm.at[pl.ds(start, rows)], out_ref.at[pl.ds(0, rows)], sem.at[0])
    two = pltpu.make_async_copy(down_hbm.at[pl.ds(start, rows)], out_ref.at[pl.ds(rows, rows)], sem.at[1])
    one.start()
    two.start()
    out_ref[2 * rows :, :] = jnp.broadcast_to(bias_ref[...], (16, bias_ref.shape[1]))
    one.wait()
    two.wait()


def share_slices(parts, up, down, bias):
    rows, width = up.shape[0] // parts, up.shape[1]
    outs = [("v", (2 * rows + 16, width), BF)]
    ins = [("b", up), ("b", down), ("v", bias)]
    return call(functools.partial(share_kernel, parts), outs, ins, (), [pltpu.SemaphoreType.DMA((2,))], "share_slices", 10**7)[0]


def start_pieces(pieces, piece_refs, target_ref, sem):
    copies = []
    for count, ((block, rows), source) in enumerate(zip(pieces, piece_refs, strict=True)):
        where = 0
        if rows < target_ref.shape[1]:
            where = pl.multiple_of((lax.axis_index("dp") ^ block) * rows, rows)
        copies.append(pltpu.make_async_copy(source, target_ref.at[:, pl.ds(where, rows)], sem.at[count]))
        copies[-1].start()
    return copies


def gelu_parts(pre):
    root = math.sqrt(2.0 / math.pi)
    square = pre * pre
    bend = jnp.tanh(root * pre * (1.0 + 0.044715 * square))
    upper = 0.5 + 0.5 * bend
    slope = upper + (0.5 * root) * pre * (1.0 - bend * bend) * (1.0 + (3 * 0.044715) * square)
    return (pre * upper).astype(BF), slope.astype(BF)


def feed_up_own_kernel(mid_ref, up_late, bias_ref, act_ref, slope_ref):
    width = mid_ref.shape[1]
    up_ref = up_late.get()
    for col in range(0, width, 256):
        cols = slice(col, col + 256)
        bias = bias_ref[0:1, cols].astype(F32)
        act_ref[:, cols], slope_ref[:, cols] = gelu_parts(nn(mid_ref[...], up_ref[:, cols]) + bias)


def feed_up_own(mid, up, bias, deps):
    outs = [("v", mid.shape, BF), ("v", mid.shape, BF)]
    return call(feed_up_own_kernel, outs, [("v", mid), ("l", up), ("v", bias)], deps, [], "feed_up_own", 3 * 10**9)


def feed_up_kernel(shards, pieces, rows, mid_ref, *refs):
    bias_refs, piece_refs = refs[: shards - 1], refs[shards - 1 : shards - 1 + len(pieces)]
    act_ref, slope_ref, up_ref, bias_ref, in_sem, bias_sem = refs[shards - 1 + len(pieces) :]
    width = mid_ref.shape[1]
    copies = start_pieces(pieces, piece_refs, up_ref, in_sem)
    biases = [
        pltpu.make_async_copy(ref.at[pl.ds(rows, 16)], bias_ref.at[shard], bias_sem.at[shard])
        for shard, ref in enumerate(bias_refs)
    ]
    for copy in biases:
        copy.start()
    for copy in biases:
        copy.wait()
    for copy in copies:
        copy.wait()
    for shard in range(shards - 1):
        for col in range(0, width, 256):
            cols = slice(shard * width + col, shard * width + col + 256)
            pre = nn(mid_ref[...], up_ref[shard, :, col : col + 256])
            act_ref[:, cols], slope_ref[:, cols] = gelu_parts(
                pre + bias_ref[shard, 0:1, col : col + 256].astype(F32)
            )


def feed_up(shards, mid, rows, biases, pieces, deps):
    rows_all, width = mid.shape
    hidden = (shards - 1) * width
    names = [entry[:-1] for entry in pieces]
    outs = [("v", (rows_all, hidden), BF), ("v", (rows_all, hidden), BF), ("v", (shards - 1, width, width), BF)]
    ins = [("v", mid)] + [("h", value) for value in biases] + [("h", entry[-1]) for entry in pieces]
    scratch = [
        pltpu.VMEM((shards - 1, 16, width), BF), pltpu.SemaphoreType.DMA((len(names),)), pltpu.SemaphoreType.DMA((shards - 1,)),
    ]
    return call(functools.partial(feed_up_kernel, shards, names, rows), outs, ins, deps, scratch, "feed_up", 6 * 10**9)


def feed_down_kernel(parts, shards, pieces, own_down, dh_ref, dg_ref, act_own, resid_ref, act_rest, *refs):
    down_bias, gain_ref, shift_ref = refs[:3]
    piece_refs = refs[3 : 3 + len(pieces)]
    out_h, out_g, dresid_ref, dbranch_ref, keep_out, send_out, vec_ref, down_ref, raw_ref, left_ref, in_sem = refs[3 + len(pieces) :]
    rows_all, width = resid_ref.shape
    length = rows_all // 2
    split = width // 2
    copies = start_pieces(pieces, piece_refs, down_ref, in_sem)
    for col in range(0, width, 256):
        cols = slice(col, col + 256)
        dresid_ref[:, cols] = nn(act_own[...], own_down[:, cols])
    for copy in copies:
        copy.wait()
    down_all = down_ref.reshape((shards - 1) * width, width)
    for col in range(0, width, 256):
        cols = slice(col, col + 256)
        dresid_ref[:, cols] += nn(act_rest[...], down_all[:, cols])
    gain_one, gain_two = gain_ref[0:1, :width], gain_ref[0:1, width:]
    shift_one, shift_two = shift_ref[0:1, :width], shift_ref[0:1, width:]
    step_rows = 32
    sums = [jnp.zeros((step_rows, width), F32)] * 3
    for row in range(0, rows_all, step_rows):
        rows = slice(row, row + step_rows)
        grad_ref = dh_ref if row < length else dg_ref
        near = row % length
        xhat_one, _ = norm_stats(resid_ref[rows, :])
        middle = xhat_one * gain_one + shift_one
        xhat, rstd = norm_stats(middle + dresid_ref[rows, :] + down_bias[...])
        out = out_h if row < length else out_g
        out.ref[near : near + step_rows, :] = (xhat * gain_two + shift_two).astype(BF)
        grad = grad_ref[near : near + step_rows, :].astype(F32)
        dresid = norm_back(grad, xhat, rstd, gain_two)
        dresid_ref[rows, :] = dresid
        dbranch = dresid.astype(BF)
        dbranch_ref[rows, :] = dbranch
        sums = [sums[0] + grad * xhat, sums[1] + grad, sums[2] + dbranch.astype(F32)]
    vec_ref[...] = jnp.zeros_like(vec_ref)
    for at, total in enumerate(sums):
        vec_ref[at : at + 1, :] = jnp.sum(total, axis=0, keepdims=True)
    out_h.send()
    out_g.send()
    turn_rows(lambda col: dbranch_ref[:, col : col + 256], raw_ref, left_ref, parts)
    for source, count, offset in ((act_own, 1, 0), (act_rest, shards - 1, width)):
        for col in range(0, count * width, 256):
            piece = nn(left_ref[...], source[:, col : col + 256]).astype(BF)
            cols = slice(col + offset, col + offset + 256)
            keep_out.ref[:, cols] = piece[:split]
            send_out.ref[:, cols] = piece[split:]
            if (col + 256) % width == 0:
                done = pl.ds(col + offset + 256 - width, width)
                send_out.send(slice(None), done)
                keep_out.send(slice(None), done)


def feed_down(parts, shards, own_down, act_own, act_rest, resid_one, down_bias, gains, shifts, dh, dg, pieces, deps):
    rows_all, width = resid_one.shape
    hidden = shards * width
    names = [entry[:-1] for entry in pieces]
    outs = [
        ("e", dh.shape, BF), ("e", dg.shape, BF), ("v", (rows_all, width), F32), ("v", (rows_all, width), BF),
        ("e", (width // 2, hidden), BF), ("e", (width // 2, hidden), BF), ("v", (8, width), F32), ("v", (shards - 1, width, width), BF),
    ]
    ins = [("v", own_down), ("v", dh), ("v", dg)]
    ins += [("v", value) for value in (act_own, resid_one, act_rest, down_bias, gains, shifts)] + [("h", entry[-1]) for entry in pieces]
    scratch = [pltpu.VMEM((width, rows_all), BF), pltpu.VMEM((width, rows_all), BF), pltpu.SemaphoreType.DMA((len(names),))]
    return call(functools.partial(feed_down_kernel, parts, shards, names), outs, ins, deps, scratch, "feed_down", 8 * 10**9)


def left_columns(width):
    return width // 3


def feed_back_up_kernel(
    parts, shards, own_down, mid_ref, dbranch_ref, down_ref, slope_own, slope_rest,
    dpre_ref, keep_out, send_out, dbias_ref, raw_ref, left_ref,
):
    rows_all, width = mid_ref.shape
    split, side = width // 2, left_columns(width)
    turn_rows(lambda col: mid_ref[:, col : col + 256], raw_ref, left_ref, parts)
    for shard in range(shards):
        for col in range(0, width, 256):
            cols = slice(shard * width + col, shard * width + col + 256)
            if shard:
                near = (shard - 1) * width + col
                weight, slope = down_ref[shard - 1, col : col + 256, :], slope_rest[:, near : near + 256]
            else:
                weight, slope = own_down[col : col + 256, :], slope_own[:, col : col + 256]
            dpre = (nt(dbranch_ref[...], weight) * slope.astype(F32)).astype(BF)
            dpre_ref[:, cols] = dpre
            dbias_ref[:, cols] = jnp.sum(dpre.astype(F32), axis=0, keepdims=True)
            piece = nn(left_ref[...], dpre).astype(BF)
            for at in range(col, col + 256, LANES):
                if at < side:
                    to = shard * side + at
                else:
                    to = shards * side + shard * (width - side) + at - side
                part = slice(at - col, at - col + LANES)
                keep_out.ref[:, to : to + LANES] = piece[:split, part]
                send_out.ref[:, to : to + LANES] = piece[split:, part]
        for start, size in ((shard * side, side), (shards * side + shard * (width - side), width - side)):
            done = pl.ds(start, size)
            send_out.send(slice(None), done)
            keep_out.send(slice(None), done)


def feed_back_up(parts, shards, own_down, down_rest, dbranch, mid, slope_own, slope_rest, deps):
    rows_all, width = mid.shape
    hidden = shards * width
    outs = [("v", (rows_all, hidden), BF), ("e", (width // 2, hidden), BF), ("e", (width // 2, hidden), BF), ("v", (1, hidden), F32)]
    ins = [("v", own_down)] + [("v", value) for value in (mid, dbranch, down_rest, slope_own, slope_rest)]
    scratch = [pltpu.VMEM((width, rows_all), BF), pltpu.VMEM((width, rows_all), BF)]
    return call(functools.partial(feed_back_up_kernel, parts, shards), outs, ins, deps, scratch, "feed_back_up", 8 * 10**9)


def feed_back_mid_kernel(shards, own_late, dpre_ref, up_ref, dresid_ref, resid_ref, gain_ref, dproj_ref, dresid_one_ref, vec_ref):
    rows_all, width = dresid_one_ref.shape
    own_up = own_late.get()
    for col in range(0, width, 256):
        cols = slice(col, col + 256)
        total = nt(dpre_ref[:, :width], own_up[cols, :])
        for shard in range(1, shards):
            total += nt(dpre_ref[:, shard * width : (shard + 1) * width], up_ref[shard - 1, cols, :])
        dresid_one_ref[:, cols] = total
    gain_one = gain_ref[0:1, :width]
    step_rows = 32
    sums = [jnp.zeros((step_rows, width), F32)] * 2
    for row in range(0, rows_all, step_rows):
        rows = slice(row, row + step_rows)
        xhat, rstd = norm_stats(resid_ref[rows, :])
        grad = dresid_ref[rows, :] + dresid_one_ref[rows, :]
        dresid = norm_back(grad, xhat, rstd, gain_one)
        dresid_one_ref[rows, :] = dresid
        dproj_ref[rows, :] = dresid.astype(BF)
        sums = [sums[0] + grad * xhat, sums[1] + grad]
    vec_ref[...] = jnp.zeros_like(vec_ref)
    for at, total in enumerate(sums):
        vec_ref[at : at + 1, :] = jnp.sum(total, axis=0, keepdims=True)


def feed_back_mid(shards, own_up, up_rest, dpre, dresid, resid_one, gains, deps):
    rows_all, width = resid_one.shape
    outs = [("v", (rows_all, width), BF), ("v", (rows_all, width), F32), ("v", (8, width), F32)]
    ins = [("l", own_up)] + [("v", value) for value in (dpre, up_rest, dresid, resid_one, gains)]
    return call(functools.partial(feed_back_mid_kernel, shards), outs, ins, deps, [], "feed_back_mid", 5 * 10**9)


def pack_rows_kernel(count, rows, *refs):
    one_ref, two_ref, sem = refs[count:]
    copies = [
        pltpu.make_async_copy(ref.at[pl.ds(half * rows, rows)], out.at[at], sem.at[half, at])
        for half, out in enumerate((one_ref, two_ref))
        for at, ref in enumerate(refs[:count])
    ]
    for copy in copies:
        copy.start()
    for copy in copies:
        copy.wait()


def pack_rows(arrays, rows, deps):
    outs = [("v", (len(arrays), rows, arrays[0].shape[1]), BF)] * 2
    scratch = [pltpu.SemaphoreType.DMA((2, len(arrays)))]
    kernel = functools.partial(pack_rows_kernel, len(arrays), rows)
    return call(kernel, outs, [("h", value) for value in arrays], deps, scratch, "pack_rows", 10**6)


def combine(arrays, outs, deps=(), name="combine_late"):
    outs = [(rows, cols, [(*part, 0, cols)[:5] for part in parts]) for rows, cols, parts in outs]
    ranges = {}
    for _, _, parts in outs:
        for _, count, sources, _, cols in parts:
            for source, row, col in sources:
                low, high = ranges.get((source, row, count), (col, col + cols))
                ranges[source, row, count] = (min(low, col), max(high, col + cols))
    buffers = [pltpu.VMEM((count, high - low), BF) for (_, _, count), (low, high) in ranges.items()]

    def kernel(*refs):
        out_refs = refs[len(arrays) : len(arrays) + len(outs)]
        *held, sem = refs[len(arrays) + len(outs) :]
        copies = {}
        for at, ((source, row, count), (low, high)) in enumerate(ranges.items()):
            piece = refs[source].at[pl.ds(row, count), pl.ds(low, high - low)]
            copies[source, row, count] = (pltpu.make_async_copy(piece, held[at], sem.at[at]), held[at], low)
            copies[source, row, count][0].start()
        waited = set()
        for (_, _, parts), out_ref in zip(outs, out_refs, strict=True):
            for first, count, sources, to, cols in parts:
                values = []
                for source, row, col in sources:
                    copy, buffer, low = copies[source, row, count]
                    if (source, row, count) not in waited:
                        copy.wait()
                        waited.add((source, row, count))
                    values.append(buffer[:, col - low : col - low + cols])
                out_ref[first : first + count, to : to + cols] = add_all(values).astype(BF)

    shapes = [("v", (rows, cols), BF) for rows, cols, _ in outs]
    scratch = [*buffers, pltpu.SemaphoreType.DMA((len(buffers),))]
    return call(kernel, shapes, [("b", value) for value in arrays], deps, scratch, name, 10**9 if name == "combine_left" else 10**6)


def regroup_kernel(shards, keep_ref, core_ref, first_a, first_b, second_a, second_b, *refs):
    outs, (held_wide, held_a, held_b, group_ref, sem, out_sem) = refs[:shards], refs[shards:]
    rows, total = held_wide.shape[1] - 16, held_wide.shape[2]
    width = total // 5
    part = width // shards
    copies = [
        pltpu.make_async_copy(ref.at[pl.ds(0, rows)], held.at[pl.ds(0, rows)], sem.at[at])
        for at, (ref, held) in enumerate(
            (
                (keep_ref, held_wide.at[0]), (core_ref, held_wide.at[1]), (first_a, held_a.at[0]), (first_b, held_b.at[0]),
                (second_a, held_a.at[1]), (second_b, held_b.at[1]),
            )
        )
    ]
    copies += [
        pltpu.make_async_copy(ref.at[pl.ds(ref.shape[0] - 16, 16)], held.at[pl.ds(rows, 16)], sem.at[6 + at])
        for at, (ref, held) in enumerate(
            ((keep_ref, held_wide.at[0]), (core_ref, held_wide.at[1]), (first_a, held_a.at[0]), (second_a, held_a.at[1]))
        )
    ]
    for copy in copies:
        copy.start()
    for copy in copies:
        copy.wait()
    sums = []
    for half, held in enumerate((held_a, held_b)):
        cols = slice(half * total // 2, (half + 1) * total // 2)
        value = held_wide[0, :rows, cols].astype(F32) + held_wide[1, :rows, cols].astype(F32)
        sums.append(value + held[0, :rows].astype(F32) + held[1, :rows].astype(F32))
    whole = jnp.concatenate(sums, axis=1)
    vectors = [held[at, rows:, :width].astype(F32) for held in (held_wide, held_a) for at in (0, 1)]
    vectors = add_all(vectors).astype(BF)
    for shard in range(shards):
        for slot in range(5):
            at = slot * width + shard * part
            group_ref[shard, :rows, slot * part : (slot + 1) * part] = whole[:, at : at + part].astype(BF)
        group_ref[shard, rows:, :width] = vectors
        group_ref[shard, rows:, width:] = jnp.zeros((16, 5 * part - width), BF)
    me = lax.axis_index("tensor")
    backs = [pltpu.make_async_copy(group_ref.at[me ^ bits], outs[bits], out_sem.at[bits]) for bits in range(shards)]
    for back in backs:
        back.start()
    for back in backs:
        back.wait()


def regroup(shards, keep, core, first, second, deps=()):
    total = keep.shape[1]
    rows = second[0].shape[0]
    shape = (rows, total // shards)
    scratch = [
        pltpu.VMEM((2, rows, total), BF), pltpu.VMEM((2, rows, total // 2), BF), pltpu.VMEM((2, rows, total // 2), BF),
        pltpu.VMEM((shards, *shape), BF), pltpu.SemaphoreType.DMA((10,)), pltpu.SemaphoreType.DMA((shards,)),
    ]
    ins = [("b", value) for value in (keep, core, *first, *second)]
    outs = [("b", shape, BF)] * shards
    return call(functools.partial(regroup_kernel, shards), outs, ins, deps, scratch, "regroup", 10**6)


class Exchange:
    def __init__(self, width):
        self.data = lax.axis_size("dp")
        self.tensor = lax.axis_size("tensor")
        self.by_hand = self.data == 8 and width % (32 * self.data) == 0
        self.blocks = self.data if self.by_hand else 1

    def data_swap(self, value, bit):
        pairs = [(at, at ^ bit) for at in range(self.data)]
        return lax.ppermute(value, "dp", pairs)

    def tensor_swap(self, value, bits):
        pairs = [(at, at ^ bits) for at in range(self.tensor)]
        return lax.ppermute(value, "tensor", pairs)


def add_low(left, right):
    return (left.astype(F32) + right.astype(F32)).astype(BF)


class Share:
    def __init__(self, swap, rows, first):
        self.swap, self.rows, self.first = swap, rows, first
        self.count = swap.tensor - 1

    def spread(self, packed):
        self.found = [(0, packed)]
        if self.swap.blocks > 1:
            bits = [1 << at for at in range(1, self.swap.data.bit_length() - 1)]
            mine = self.found[0][1]
            self.near = [(bit, self.swap.data_swap(mine, bit)) for bit in bits]
            self.found += self.near

    def cross(self):
        if self.swap.data == 8 and self.swap.blocks == 8:
            other = 6 - self.first
            self.found.append((6, self.swap.data_swap(dict(self.near)[self.first], other)))

    def finish(self):
        found = list(self.found)
        if self.swap.blocks > 1:
            found += [(block | 1, self.swap.data_swap(value, 1)) for block, value in self.found]
        return [(block, self.rows, value) for block, value in found]


def add_all(terms):
    total = terms[0].astype(F32)
    for term in terms[1:]:
        total += term.astype(F32)
    return total


def tensor_sum(swap, parts):
    return add_all([parts[0]] + [swap.tensor_swap(parts[bits], bits) for bits in range(1, swap.tensor)])


def per_device(
    h_in, g_in, seg_ids, target_flags, perm_order, w_query, w_key, w_value, w_out, w_rel, attn_bias, seg_embed,
    norm_gain, norm_bias, w_up, b_up, w_down, b_down, d_h_out, d_g_out,
):
    seq_count, length, width = h_in.shape
    assert seq_count == 1
    swap = Exchange(width)
    parts, shards = swap.blocks, swap.tensor
    by_hand = swap.by_hand
    dp_at, tensor_at = lax.axis_index("dp"), lax.axis_index("tensor")
    own_part = width // shards
    rel_host = rel_table(length, width)
    rel, rev = jnp.asarray(rel_host), jnp.asarray(np.ascontiguousarray(rel_host[::-1]))
    h, g = h_in[0], g_in[0]
    up, down = w_up[0], w_down[0]
    bias, table = attn_bias.reshape(1, -1), seg_embed.reshape(1, -1)
    gains, shifts = norm_gain.reshape(1, -1), norm_bias.reshape(1, -1)

    mine = share_slices(parts, up, down, b_up)
    rows = (mine.shape[0] - 16) // 2
    fetched = [swap.tensor_swap(mine, bits) for bits in range(1, shards)]
    share_up, share_down = Share(swap, rows, 2), Share(swap, rows, 4)
    q, key, value, relkey, mask, half, relrev, left_x, left_rev = project(
        parts, h, g, seg_ids, target_flags, perm_order, w_query[0], w_key[0], w_value[0], w_rel[0], rel, rev, ()
    )
    att_one, prob_one = attention_first(q, key, value, relkey, mask, half, bias, table, ())
    packed_up, packed_down = pack_rows(fetched, rows, [att_one])
    share_up.spread(packed_up)
    share_down.spread(packed_down)
    resid_one, mid, prob_two, att, left_att = attention_second(
        parts, w_out[0], h, g, q, key, value, relkey, mask, half, att_one, bias, table, gains, shifts,
        [share_up.found[0][1], share_down.found[0][1]],
    )
    if by_hand:
        share_up.near = [(bit, lax.optimization_barrier((value, mid))[0]) for bit, value in share_up.near]
    share_up.cross()
    act_own, slope_own = feed_up_own(mid, up, b_up, [found for _, found in share_up.found[:3]])
    share_down.cross()
    act_rest, slope_rest, up_rest = feed_up(
        shards, mid, 2 * rows, fetched, share_up.finish(), [found for _, found in share_down.found]
    )
    out_h, out_g, dresid_two, dbranch, keep_down, send_down, vec_two, down_rest = feed_down(
        parts, shards, down, act_own, act_rest, resid_one, b_down, gains, shifts, d_h_out[0], d_g_out[0],
        share_down.finish(), (),
    )

    hidden, wide = shards * width, 5 * width
    block, middle = width // 8, width // 4
    size = (10 + shards) * width

    def first_far(keep, core, deps, name):
        cut = keep.shape[1] // 2
        odd = [(at, block, [(0, block + 2 * at, 0), (1, block + 2 * at, 0)]) for at in (0, block)]
        upper = [(0, middle, [(0, middle, cut), (1, middle, cut)])]
        more = keep.shape[0] - 2 * middle
        if more:
            odd.append((middle, more, [(0, 2 * middle, 0), (1, 2 * middle, 0)]))
        return combine([keep, core], [(middle + more, cut, odd), (middle, cut, upper)], deps, name)

    def first_swap(far):
        return swap.data_swap(far[0], 2), swap.data_swap(far[1], 4)

    def second_far(keep, core, first, deps, name):
        cut = keep.shape[1] // 2
        more = keep.shape[0] - 2 * middle
        upper = [(0, block, [(0, middle, 0), (1, middle, 0), (2, block, 0)])]
        if more:
            upper.append((block, more, [(0, 2 * middle, 0), (1, 2 * middle, 0), (2, middle, 0)]))
        return combine(
            [keep, core, *first],
            [
                (block + more, cut, upper),
                (block, cut, [(0, block, [(0, block, cut), (1, block, cut), (3, block, 0)])]),
            ],
            deps,
            name,
        )

    def second_swap(far):
        return swap.data_swap(far[0], 4), swap.data_swap(far[1], 2)

    if by_hand:
        core_down = swap.data_swap(send_down, 1)
    dpre, keep_up, send_up, dbias_up = feed_back_up(parts, shards, down, down_rest, dbranch, mid, slope_own, slope_rest, ())
    deps = ()
    if by_hand:
        core_up = swap.data_swap(send_up, 1)
        far_down = first_far(keep_down, core_down, (), "combine")
        first_down = first_swap(far_down)
        side = left_columns(width)
        rest = width - side
        cut, quarter = shards * side, shards * rest // 2
        odd = [(at, block, [(0, block + 2 * at, cut), (1, block + 2 * at, cut)]) for at in (0, block)]
        far_up = combine(
            [keep_up, core_up],
            [
                *((2 * middle, side, [(0, 2 * middle, [(0, 0, k * side), (1, 0, k * side)])]) for k in range(1, shards)),
                (middle, quarter, odd),
                (middle, quarter, [(0, middle, [(0, middle, cut + quarter), (1, middle, cut + quarter)])]),
            ],
            far_down,
            "combine",
        )
        came_up = [swap.tensor_swap(far_up[bits - 1], bits) for bits in range(1, shards)]
        first_up = first_swap(far_up[-2:])
        deps = far_up[-1:]
    dproj, dresid_one, vec_one = feed_back_mid(shards, up, up_rest, dpre, dresid_two, resid_one, gains, deps)
    common = (w_out[0], dproj, q, att, key, value, prob_one, prob_two, relrev, half)
    back_first = attention_back_first(tuple(range(PAIRS // 2)), common, bias, table, ())
    deps = ()
    if by_hand:
        far_down = second_far(keep_down, core_down, first_down, back_first[-1:], "combine")
        second_down = second_swap(far_down)
        deps = far_down
    dq, dkey, dvalue, keep_att, send_att = attention_back(
        tuple(range(PAIRS // 2, PAIRS)), common, (left_x, left_rev, left_att), back_first, (vec_one, vec_two, dbias_up),
        bias, table, [*deps, *came_up] if by_hand else deps,
    )
    if by_hand:
        (send_att, keep_att), (first_up, second_down) = lax.optimization_barrier(
            ((send_att, keep_att), (first_up, second_down))
        )
        core_att = swap.data_swap(send_att, 1)
        all_up = [keep_up, core_up, *came_up]
        left = range(len(all_up))
        far_up = combine(
            [*all_up, *first_up],
            [
                (block, quarter, [(0, block, [(0, middle, cut), (1, middle, cut), (shards + 1, block, 0)])]),
                (block, quarter, [(0, block, [(0, block, cut + quarter), (1, block, cut + quarter), (shards + 2, block, 0)])]),
                (middle, side, [(0, middle, [(at, middle, 0) for at in left])]),
            ],
        )
        second_up = second_swap(far_up[:2])
        left_y = swap.data_swap(far_up[2], 4)
        far_att = first_far(keep_att, core_att, second_up, "combine_late")
        first_att = first_swap(far_att)
        arrays = [keep_down, core_down, *first_down, *second_down, *all_up, *first_up, *second_up]
        up_at, per, outs = 6, shards // 2, []
        half_at = up_at + len(all_up)
        for k in range(shards):
            half, near = k // per, k % per
            outs.append(
                (
                    block,
                    width + rest,
                    [
                        (0, block, [(0, 0, k * width), (1, 0, k * width), (2 + half, 0, near * width), (4 + half, 0, near * width)],
                         0, width),
                        (0, block, [(up_at, 0, cut + k * rest), (up_at + 1, 0, cut + k * rest), (half_at + half, 0, near * rest),
                                    (half_at + 2 + half, 0, near * rest)], width, rest),
                    ],
                )
            )
        feed_parts = combine(arrays, outs, far_att)
        came = [swap.tensor_swap(feed_parts[bits], bits) for bits in range(1, shards)]
        grad_h, grad_g = input_grads(w_query[0], w_key[0], w_value[0], dq, dkey, dvalue, dresid_one, feed_parts[:1])
        far_att = second_far(keep_att, core_att, first_att, [*came[:1], grad_h], "combine_att")
        second_att = second_swap(far_att)
        left_own, far_left = combine(
            [*all_up, left_y],
            [(block, side, [(0, block, [(at, row, 0) for at in range(shards + 2)])]) for row in (0, block)],
            [*far_att],
            "combine_left",
        )
        left_x = swap.data_swap(far_left, 2)
        att_parts = regroup(shards, keep_att, core_att, first_att, second_att, came)
    else:
        grad_h, grad_g = input_grads(w_query[0], w_key[0], w_value[0], dq, dkey, dvalue, dresid_one, ())
        vectors = lax.psum(keep_att[width // 2 : width // 2 + 10 + shards, :width].astype(F32), AXES)
        keep_att, send_att = keep_att[: width // 2], send_att[: width // 2]

        def rows_sum(keep, send):
            whole = jnp.concatenate([keep, send], axis=0)
            return lax.psum_scatter(whole, "dp", scatter_dimension=0, tiled=True)

        sum_up, sum_down, sum_att = (
            rows_sum(keep, send) for keep, send in ((keep_up, send_up), (keep_down, send_down), (keep_att, send_att))
        )
        cols = [slice(shard * width, (shard + 1) * width) for shard in range(shards)]
        side = left_columns(width)
        left, right = sum_up[:, : shards * side], sum_up[:, shards * side :]
        rest = width - side
        d_up = [
            jnp.concatenate([left[:, k * side : (k + 1) * side], right[:, k * rest : (k + 1) * rest]], axis=1)
            for k in range(shards)
        ]
        d_up = tensor_sum(swap, d_up)
        d_down = tensor_sum(swap, [sum_down[:, part] for part in cols]).T
        split = sum_att.reshape(-1, 5, shards, own_part).transpose(2, 0, 1, 3).reshape(shards, -1, 5 * own_part)
        att_parts = [lax.dynamic_index_in_dim(split, tensor_at ^ bits, 0, keepdims=False) for bits in range(shards)]
    att_parts = [att_parts[0]] + [swap.tensor_swap(att_parts[bits], bits) for bits in range(1, shards)]
    if by_hand:
        came, _ = lax.optimization_barrier((came, att_parts[1]))
        d_feed = add_all([feed_parts[0], *came])
        d_up = jnp.concatenate([add_all([left_own, left_x]), d_feed[:, width:]], axis=1)
        d_down = d_feed[:, :width].T
        (d_up, d_down), att_parts = lax.optimization_barrier(((d_up, d_down), att_parts))
    d_att = add_all(att_parts)
    if by_hand:
        d_att, vectors = d_att[:block], d_att[block : block + 10 + shards, :width]
    d_att = [d_att[:, slot * own_part : (slot + 1) * own_part] for slot in range(5)]

    own = size // (swap.data * shards)
    d_vectors = lax.dynamic_slice_in_dim(vectors.reshape(-1), (dp_at * shards + tensor_at) * own, own, 0)

    return (
        out_h[None], out_g[None], grad_h[None], grad_g[None],
        d_att[0][None], d_att[1][None], d_att[2][None], d_att[3][None], d_att[4][None],
        d_up[None], d_down[None], d_vectors[None],
    )


def solution(mesh):
    every = P(AXES, None, None)
    rows = P(AXES, None)
    in_specs = (
        every, every, rows, rows, rows, P(), P(), P(), P(), P(), P(), P(), P(), P(),
        P(None, None, "tensor"), P(None, "tensor"), P(None, "tensor", None), P(), every, every,
    )
    grads = P(None, "dp", "tensor")
    out_specs = (
        every, every, every, every, grads, grads, grads, grads, grads, grads,
        P(None, "tensor", "dp"), P(None, AXES),
    )
    return jax.shard_map(per_device, mesh=mesh, in_specs=in_specs, out_specs=out_specs, check_vma=False)
```

```python
import functools
import math

import jax
import jax.numpy as jnp
import numpy as np
from jax import lax
from jax.experimental import pallas as pl
from jax.experimental.pallas import tpu as pltpu
from jax.sharding import PartitionSpec as P

HEADS = 12
HEAD_DIM = 64
LANES = 128
PAIRS = HEADS // 2
NEGATIVE = -1e30
EPSILON = 1e-06
AXES = ("dp", "tensor")
BF = jnp.bfloat16
F32 = jnp.float32
FIRST_PAIRS = 4
VMEM_MIB = {
    "share_slices": 60, "project": 50, "attention_first": 12, "attention_second": 14, "feed_up_own": 6, "feed_up": 14, "feed_down": 22,
    "feed_back_up": 16, "feed_back_mid": 10, "attention_back_first": 18, "attention_back": 26, "input_grads": 14, "pack_rows": 2,
    "combine": 12, "combine_late": 12, "combine_att": 59, "combine_left": 59, "regroup": 59,
}


def rel_table(length, model_width):
    position = (length - np.arange(2 * length)).astype(np.float32)
    frequency = np.float32(1.0) / np.float32(10000.0) ** (
        np.arange(0, model_width, 2).astype(np.float32) / np.float32(model_width)
    )
    angles = position[:, None] * frequency[None, :]
    return np.concatenate([np.sin(angles), np.cos(angles)], axis=1).astype(BF)


class Late:
    def __init__(self, source, target, sem):
        self.target, self.waiting = target, True
        self.copy = pltpu.make_async_copy(source, target, sem)
        self.copy.start()

    def get(self):
        if self.waiting:
            self.copy.wait()
            self.waiting = False
        return self.target


class Early:
    def __init__(self, ref, target, sems):
        self.ref, self.target, self.sems, self.copies = ref, target, sems, []

    def send(self, *where):
        source, target = (self.ref.at[where], self.target.at[where]) if where else (self.ref, self.target)
        copy = pltpu.make_async_copy(source, target, self.sems.at[len(self.copies)])
        copy.start()
        self.copies.append(copy)


SENDS = 16


def call(kernel, outs, ins, deps, scratch, name, flops):
    deps = tuple(deps)
    spaces = {"s": pltpu.SMEM, "v": pltpu.VMEM, "h": pl.ANY, "l": pltpu.HBM, "e": pltpu.HBM, "b": pltpu.HBM}
    late = [value for kind, value in ins if kind == "l"]
    early = [(shape, dtype) for kind, shape, dtype in outs if kind == "e"]
    more = [pltpu.VMEM(value.shape, value.dtype) for value in late] + [pltpu.VMEM(*spec) for spec in early]
    if late:
        more.append(pltpu.SemaphoreType.DMA((len(late),)))
    if early:
        more.append(pltpu.SemaphoreType.DMA((len(early), SENDS)))
    first_out = len(ins) + len(deps)
    first_scratch = first_out + len(outs)

    def wrapped(*refs):
        own = refs[first_scratch + len(scratch) :]
        late_refs, early_refs = own[: len(late)], own[len(late) : len(late) + len(early)]
        sems = list(own[len(late) + len(early) :])
        late_sem = sems.pop(0) if late else None
        early_sem = sems.pop(0) if early else None
        given, at = [], 0
        for (kind, _), ref in zip(ins, refs[: len(ins)], strict=True):
            if kind == "l":
                ref = Late(ref, late_refs[at], late_sem.at[at])
                at += 1
            given.append(ref)
        made, at = [], 0
        for (kind, _, _), ref in zip(outs, refs[first_out:first_scratch], strict=True):
            if kind == "e":
                ref = Early(early_refs[at], ref, early_sem.at[at])
                at += 1
            made.append(ref)
        kernel(*given, *made, *refs[first_scratch : first_scratch + len(scratch)])
        for item in given:
            if isinstance(item, Late):
                item.get()
        for item in made:
            if isinstance(item, Early):
                for copy in item.copies:
                    copy.wait()

    return pl.pallas_call(
        wrapped,
        out_shape=[jax.ShapeDtypeStruct(shape, dtype) for _, shape, dtype in outs],
        in_specs=[pl.BlockSpec(memory_space=spaces[kind]) for kind, _ in ins]
        + [pl.BlockSpec(memory_space=pl.ANY)] * len(deps),
        out_specs=[pl.BlockSpec(memory_space=spaces[kind]) for kind, _, _ in outs],
        scratch_shapes=list(scratch) + more,
        compiler_params=pltpu.CompilerParams(vmem_limit_bytes=VMEM_MIB[name] * 1024 * 1024),
        cost_estimate=pl.CostEstimate(flops=flops * 100, bytes_accessed=flops // 1000, transcendentals=0),
        name=name,
    )(*[value for _, value in ins], *deps)


def nn(left, right):
    return lax.dot_general(left, right, (((1,), (0,)), ((), ())), preferred_element_type=F32)


def nt(left, right):
    return lax.dot_general(left, right, (((1,), (1,)), ((), ())), preferred_element_type=F32)


def tn(left, right):
    return lax.dot_general(left, right, (((0,), (0,)), ((), ())), preferred_element_type=F32)


def lane_index(rows):
    return lax.broadcasted_iota(jnp.int32, (rows, LANES), 1)


def pair_lanes(pair):
    return pl.ds(pl.multiple_of(pair * LANES, LANES), LANES)


def row_lanes(row, pair, width):
    return pl.ds(pl.multiple_of(row * width + pair * LANES, LANES), LANES)


def norm_stats(source):
    mean = jnp.mean(source, axis=-1, keepdims=True)
    centered = source - mean
    variance = jnp.mean(centered * centered, axis=-1, keepdims=True)
    rstd = lax.rsqrt(variance + EPSILON)
    return centered * rstd, rstd


def norm_back(grad, xhat, rstd, gain):
    dxhat = grad * gain
    mean_one = jnp.mean(dxhat, axis=-1, keepdims=True)
    mean_two = jnp.mean(dxhat * xhat, axis=-1, keepdims=True)
    return rstd * (dxhat - mean_one - xhat * mean_two)


def seg_coefficients(half_wide, lane):
    return jnp.where(lane % HEAD_DIM == 0, half_wide, 1.0 - 2.0 * half_wide)


def seg_keys(half_wide, lane):
    place = lane % HEAD_DIM
    return jnp.where(place == 0, 1.0, jnp.where(place == 1, half_wide, 0.0))


def seg_table(seg_ref, pair, width):
    row = lax.broadcasted_iota(jnp.int32, (LANES, LANES), 0)
    lane = lax.broadcasted_iota(jnp.int32, (LANES, LANES), 1)
    one = jnp.broadcast_to(seg_ref[0:1, pair_lanes(pair)], (LANES, LANES)).T
    two = jnp.broadcast_to(seg_ref[0:1, row_lanes(1, pair, width)], (LANES, LANES)).T
    base = jnp.where(row < HEAD_DIM, HEAD_DIM, 0)
    at_one = lane == base
    at_two = at_one | (lane == base + 1)
    return jnp.concatenate([jnp.where(at_one, one, 0.0), jnp.where(at_two, two - one, 0.0)], axis=1).astype(BF)


def attend_pair(pair, first, q_ref, key_ref, value_ref, relkey_ref, mask_ref, half_ref, bias_ref, seg_ref, prob_ref, att_ref):
    length, width = key_ref.shape
    block = length // 2
    lanes = pair_lanes(pair)
    lane_q = lane_index(2 * length)
    lane_k = lane_index(length)
    low_q = lane_q < HEAD_DIM
    low_k = lane_k < HEAD_DIM
    half_w = half_ref[...]
    scale = 1.0 / math.sqrt(HEAD_DIM)
    query = q_ref[:, lanes]
    word = ((query + bias_ref[0:1, lanes]) * scale).astype(BF)
    relq = ((query + bias_ref[0:1, row_lanes(1, pair, width)]) * scale).astype(BF)
    segq = ((query + bias_ref[0:1, row_lanes(2, pair, width)]) * scale).astype(BF)
    terms = nn(segq, seg_table(seg_ref, pair, width))
    coef = seg_coefficients(jnp.concatenate([half_w, half_w], axis=0), lane_q)
    extra = (terms[:, :LANES] + terms[:, LANES:] * coef).astype(BF)
    key_extra = seg_keys(half_w, lane_k).astype(BF)
    key = key_ref[:, lanes]
    value = value_ref[:, lanes]
    zero = jnp.zeros_like(relq)
    attended = []
    for head in (0, 1):
        if head == 0:
            word_one = jnp.where(low_q, word, extra)
            key_one = jnp.where(low_k, key, key_extra)
            rel_one = jnp.where(low_q, relq, zero)
        else:
            word_one = jnp.where(low_q, extra, word)
            key_one = jnp.where(low_k, key_extra, key)
            rel_one = jnp.where(low_q, zero, relq)
        score = nt(word_one, key_one)
        for part in (0, 1):
            base = block - block * part
            rows_h = slice(block * part, block * part + block)
            rows_g = slice(length + block * part, length + block * part + block)
            rel_rows = jnp.concatenate([rel_one[rows_h], rel_one[rows_g]], axis=0)
            raw = nt(rel_rows, relkey_ref[base : base + 3 * block, lanes])
            for place_at, rows in ((0, rows_h), (1, rows_g)):
                shifted = pltpu.roll(
                    raw[place_at * block : (place_at + 1) * block], 2 * block, 1, stride=1, stride_axis=0
                )[:, :length]
                logits = score[rows] + shifted + mask_ref[rows]
                top = jnp.max(logits, axis=1, keepdims=True)
                power = jnp.exp(logits - top)
                total = jnp.sum(power, axis=1, keepdims=True)
                prob_ref[2 * (pair - first) + head, rows, :] = (power * (1.0 / total)).astype(BF)
        attended.append(nn(prob_ref[2 * (pair - first) + head], value))
    att_ref[:, lanes] = jnp.where(low_q, attended[0], attended[1]).astype(BF)


def project_kernel(
    parts, h_late, g_late, wq_late, wk_late, wv_late, rel_late, wr_late, rev_late,
    seg_row, flag_row, order_row,
    q_ref, key_ref, value_ref, relkey_ref, mask_ref, half_ref, relrev_out, left_x_out, left_rev_out,
    x_ref, raw_ref,
):
    h_ref, g_ref = h_late.get(), g_late.get()
    length, width = h_ref.shape
    x_ref[:length] = h_ref[...]
    x_ref[length:] = g_ref[...]

    def project(left, right_late, target):
        right = right_late.get()
        for col in range(0, width, 256):
            cols = slice(col, col + 256)
            target[:, cols] = nn(left[...], right[:, cols]).astype(target.dtype)

    project(x_ref, wq_late, q_ref)
    project(h_ref, wk_late, key_ref)
    project(h_ref, wv_late, value_ref)
    project(rel_late.get(), wr_late, relkey_ref)

    def wide(row_ref):
        return jnp.broadcast_to(row_ref[...].astype(F32), (length, length))

    row_at = lax.broadcasted_iota(jnp.int32, (length, length), 0)
    col_at = lax.broadcasted_iota(jnp.int32, (length, length), 1)
    seg, order = wide(seg_row), wide(order_row)
    same_doc = seg.T == seg
    start = jnp.min(jnp.where(same_doc, col_at.astype(F32), float(length)), axis=1, keepdims=True)
    in_doc = jnp.sum(jnp.where(same_doc, 1.0, 0.0), axis=1, keepdims=True)
    place = lax.broadcasted_iota(jnp.int32, (length, 1), 0).astype(F32)
    half = jnp.where(2.0 * (place - start) >= in_doc, 1.0, 0.0)
    half_ref[...] = jnp.broadcast_to(half, (length, LANES))
    content = same_doc & ((wide(flag_row) == 0.0) | (order <= order.T))
    mask_ref[:length] = jnp.where(content, 0.0, NEGATIVE)
    mask_ref[length:] = jnp.where(content & (row_at != col_at), 0.0, NEGATIVE)

    project(rev_late.get(), wr_late, relrev_out.ref)
    relrev_out.send()
    turn_rows(lambda col: x_ref[:, col : col + 256], raw_ref.at[0], left_x_out.ref, parts)
    left_x_out.send()
    rev_ref = rev_late.get()
    turn_rows(lambda col: rev_ref[:, col : col + 256], raw_ref.at[1], left_rev_out.ref, parts)
    left_rev_out.send()


def project(parts, h, g, seg, flag, order, wq, wk, wv, wr, rel, rev, deps):
    length, width = h.shape
    two = 2 * length
    outs = [
        ("v", (two, width), F32), ("v", (length, width), BF), ("v", (length, width), BF), ("v", (two, width), BF),
        ("v", (two, length), F32), ("v", (length, LANES), F32), ("e", (two, width), BF), ("e", (width, two), BF),
        ("e", (width, two), BF),
    ]
    ins = [("l", value) for value in (h, g, wq, wk, wv, rel, wr, rev)] + [("v", value) for value in (seg, flag, order)]
    scratch = [pltpu.VMEM((two, width), BF), pltpu.VMEM((2, width, two), BF)]
    return call(functools.partial(project_kernel, parts), outs, ins, deps, scratch, "project", 5 * 10**9)


def attention_first_kernel(
    q_ref, key_ref, value_ref, relkey_ref, mask_ref, half_ref, bias_ref, seg_ref, att_ref, prob_out
):
    def pair_step(pair, carry):
        attend_pair(
            pair, 0, q_ref, key_ref, value_ref, relkey_ref, mask_ref, half_ref, bias_ref, seg_ref, prob_out.ref, att_ref
        )
        return carry

    for first in range(0, FIRST_PAIRS, 2):
        lax.fori_loop(first, first + 2, pair_step, 0)
        prob_out.send(pl.ds(2 * first, 4))


def attention_first(q, key, value, relkey, mask, half, bias, table, deps):
    two, length = mask.shape
    outs = [("v", (two, FIRST_PAIRS * LANES), BF), ("e", (2 * FIRST_PAIRS, two, length), BF)]
    ins = [("v", x) for x in (q, key, value, relkey, mask, half, bias, table)]
    return call(attention_first_kernel, outs, ins, deps, [], "attention_first", 5 * 10**9)


def attention_second_kernel(
    parts, wo_late, h_late, g_late, q_ref, key_ref, value_ref, relkey_ref, mask_ref, half_ref, att_first_ref,
    bias_ref, seg_ref, gain_ref, shift_ref,
    resid_ref, mid_ref, prob_out, att_out, left_att_out,
    raw_ref,
):
    length, width = key_ref.shape
    att_ref = att_out.ref
    att_ref[:, : FIRST_PAIRS * LANES] = att_first_ref[...]

    def pair_step(pair, carry):
        attend_pair(
            pair, FIRST_PAIRS, q_ref, key_ref, value_ref, relkey_ref, mask_ref, half_ref, bias_ref, seg_ref, prob_out.ref, att_ref
        )
        return carry

    for first in range(FIRST_PAIRS, PAIRS, 2):
        lax.fori_loop(first, first + 2, pair_step, 0)
        prob_out.send(pl.ds(2 * (first - FIRST_PAIRS), 4))
    att_out.send()
    wo_ref, h_ref, g_ref = wo_late.get(), h_late.get(), g_late.get()
    for col in range(0, width, 256):
        cols = slice(col, col + 256)
        total = nn(att_ref[...], wo_ref[:, cols])
        resid_ref[:length, cols] = h_ref[:, cols].astype(F32) + total[:length]
        resid_ref[length:, cols] = g_ref[:, cols].astype(F32) + total[length:]
    turn_rows(lambda col: att_ref[:, col : col + 256], raw_ref, left_att_out.ref, parts)
    left_att_out.send()
    for row in range(0, 2 * length, 64):
        xhat, _ = norm_stats(resid_ref[row : row + 64, :])
        mid_ref[row : row + 64, :] = (xhat * gain_ref[0:1, :width] + shift_ref[0:1, :width]).astype(BF)


def attention_second(parts, wo, h, g, q, key, value, relkey, mask, half, att, bias, table, gain, shift, deps):
    length, width = h.shape
    two = 2 * length
    outs = [
        ("v", (two, width), F32), ("v", (two, width), BF), ("e", (HEADS - 2 * FIRST_PAIRS, two, length), BF),
        ("e", (two, width), BF), ("e", (width, two), BF),
    ]
    ins = [("l", value) for value in (wo, h, g)]
    ins += [("v", value) for value in (q, key, value, relkey, mask, half, att, bias, table, gain, shift)]
    return call(
        functools.partial(attention_second_kernel, parts), outs, ins, deps, [pltpu.VMEM((width, two), BF)],
        "attention_second", 10 * 10**9,
    )


def place_rows(raw_ref, out_ref, parts):
    rows = raw_ref.shape[0] // parts
    me = lax.axis_index("dp") if parts > 1 else 0
    order = [low | (rest << 1) for low in (0, 1) for rest in range(parts // 2)] if parts > 1 else [0]
    for at, block in enumerate(order):
        source = pl.multiple_of((me ^ block) * rows, rows)
        out_ref[at * rows : (at + 1) * rows, :] = raw_ref[pl.ds(source, rows), :]


def turn_rows(source, raw_ref, out_ref, parts):
    for col in range(0, raw_ref.shape[0], 256):
        raw_ref[col : col + 256, :] = source(col).astype(F32).T.astype(BF)
    place_rows(raw_ref, out_ref, parts)


def back_pairs(
    pairs, dproj_ref, wo_ref, q_ref, att_ref, key_ref, value_ref, prob_one, prob_two, relrev_ref, half_ref, bias_ref, seg_ref,
    dq_ref, dkey_ref, dvalue_ref, drel_ref, vec_ref, datt_ref,
):
    length, width = key_ref.shape
    block = length // 2
    for at, pair in enumerate(pairs):
        rows = slice(pair * LANES, (pair + 1) * LANES)
        datt_ref[:, at * LANES : (at + 1) * LANES] = nt(dproj_ref[...], wo_ref[rows, :]).astype(BF)

    def pair_step(at, pair):
        lanes = slice(pair * LANES, (pair + 1) * LANES)
        own = slice(at * LANES, (at + 1) * LANES)
        prob_ref, prob_at = (prob_one, 2 * pair) if pair < FIRST_PAIRS else (prob_two, 2 * (pair - FIRST_PAIRS))
        lane_q = lane_index(2 * length)
        lane_k = lane_index(length)
        low_q = lane_q < HEAD_DIM
        low_k = lane_k < HEAD_DIM
        half_w = half_ref[...]
        flip_row = lax.broadcasted_iota(jnp.int32, (length, length), 0)
        flip_col = lax.broadcasted_iota(jnp.int32, (length, length), 1)
        flip = jnp.where(flip_row + flip_col == length - 1, 1.0, 0.0).astype(BF)
        sel_row = lax.broadcasted_iota(jnp.int32, (2 * LANES, LANES), 0) % LANES
        sel_col = lax.broadcasted_iota(jnp.int32, (2 * LANES, LANES), 1)
        select = jnp.where(
            ((sel_row < HEAD_DIM) & ((sel_col == HEAD_DIM) | (sel_col == HEAD_DIM + 1)))
            | ((sel_row >= HEAD_DIM) & (sel_col < 2)),
            1.0,
            0.0,
        ).astype(BF)
        query = q_ref[:, lanes]
        word = query + bias_ref[0:1, lanes]
        relq = query + bias_ref[0:1, row_lanes(1, pair, width)]
        segq = (query + bias_ref[0:1, row_lanes(2, pair, width)]).astype(BF)
        word_t = word.T.astype(BF)
        relq_t = relq.T.astype(BF)
        datt = datt_ref[:, own]
        datt_wide = datt.astype(F32)
        datt_t = datt_wide.T.astype(BF)
        datt_scaled = datt_wide * (1.0 / math.sqrt(HEAD_DIM))
        product = datt_scaled * att_ref[:, lanes].astype(F32)
        product_high = product.astype(BF)
        product_low = (product - product_high.astype(F32)).astype(BF)
        delta = nn(jnp.concatenate([product_high, product_low], axis=1), select)
        delta_high = delta.astype(BF).astype(F32)
        minus = jnp.where(lane_q % HEAD_DIM == 0, -delta_high, delta_high - delta).astype(BF)
        datt_low = datt_scaled.astype(BF)
        key_extra = seg_keys(half_w, lane_k).astype(BF)
        ones_extra = jnp.where(lane_k % HEAD_DIM < 2, 1.0, 0.0).astype(BF)
        key = key_ref[:, lanes]
        value = value_ref[:, lanes]
        dword, drel = [], []
        for head in (0, 1):
            rows_t = slice(HEAD_DIM * head, HEAD_DIM * head + HEAD_DIM)
            if head == 0:
                datt_one = jnp.where(low_q, datt_low, minus)
                value_one = jnp.where(low_k, value, ones_extra)
                key_one = jnp.where(low_k, key, key_extra)
            else:
                datt_one = jnp.where(low_q, minus, datt_low)
                value_one = jnp.where(low_k, ones_extra, value)
                key_one = jnp.where(low_k, key_extra, key)
            prob = prob_ref[prob_at + head]
            dprob = nt(datt_one, value_one)
            dscore = (prob.astype(F32) * dprob).astype(BF)
            dword.append(nn(dscore, key_one))
            rows_out = slice(at * LANES + HEAD_DIM * head, at * LANES + HEAD_DIM * (head + 1))
            dkey_ref[rows_out, :] = nn(word_t[rows_t], dscore).astype(BF)
            dvalue_ref[rows_out, :] = nn(datt_t[rows_t], prob).astype(BF)
            flipped = nn(dscore, flip).astype(BF)
            pad = jnp.zeros((block, block), BF)
            rel_parts, drel_t = [], []
            for part in (0, 1):
                rows_h = slice(block * part, block * part + block)
                rows_g = slice(length + block * part, length + block * part + block)
                draw = jnp.concatenate(
                    [
                        pltpu.roll(jnp.concatenate([flipped[rows], pad], axis=1), 0, 1, stride=1, stride_axis=0)
                        for rows in (rows_h, rows_g)
                    ],
                    axis=0,
                )
                rel_parts.append(nn(draw, relrev_ref[block * part : block * part + 3 * block, lanes]))
                rel_cols = jnp.concatenate([relq_t[rows_t, rows_h], relq_t[rows_t, rows_g]], axis=1)
                drel_t.append(nn(rel_cols, draw))
            drel.append(
                jnp.concatenate(
                    [rel_parts[0][:block], rel_parts[1][:block], rel_parts[0][block:], rel_parts[1][block:]], axis=0
                )
            )
            drel_ref[rows_out, :] = jnp.concatenate(
                [
                    drel_t[0][:, :block],
                    drel_t[0][:, block:] + drel_t[1][:, : 2 * block],
                    drel_t[1][:, 2 * block :],
                ],
                axis=1,
            ).astype(BF)
        extra = jnp.where(low_q, dword[1], dword[0])
        dword_all = jnp.where(low_q, dword[0], dword[1])
        drel_all = jnp.where(low_q, drel[0], drel[1])
        coef = seg_coefficients(jnp.concatenate([half_w, half_w], axis=0), lane_q)
        dterms = jnp.concatenate([extra, extra * coef], axis=1).astype(BF)
        dsegq = nt(dterms, seg_table(seg_ref, pair, width))
        dtable = tn(dterms, segq)
        dq_ref[:, own] = (dword_all + drel_all + dsegq).astype(BF)
        low_one = lane_index(1) < HEAD_DIM
        first = jnp.where(low_one, dtable[HEAD_DIM : HEAD_DIM + 1], dtable[0:1])
        far = LANES + HEAD_DIM
        second = jnp.where(
            low_one, dtable[far : far + 1] + dtable[far + 1 : far + 2], dtable[LANES : LANES + 1] + dtable[LANES + 1 : LANES + 2]
        )
        vec_ref[0:1, own] = jnp.sum(dword_all, axis=0, keepdims=True)
        vec_ref[1:2, own] = jnp.sum(drel_all, axis=0, keepdims=True)
        vec_ref[2:3, own] = jnp.sum(dsegq, axis=0, keepdims=True)
        vec_ref[3:4, own] = first - second
        vec_ref[4:5, own] = second
    for at, pair in enumerate(pairs):
        pair_step(at, pair)


def attention_back_first_kernel(
    pairs, wo_ref, dproj_ref, q_ref, att_ref, key_ref, value_ref, prob_one, prob_two, relrev_ref, half_ref, bias_ref, seg_ref,
    dq_ref, dkey_ref, dvalue_ref, drel_ref, vec_ref, datt_ref,
):
    vec_ref[...] = jnp.zeros_like(vec_ref)
    back_pairs(
        pairs, dproj_ref, wo_ref, q_ref, att_ref, key_ref, value_ref, prob_one, prob_two, relrev_ref, half_ref, bias_ref,
        seg_ref, dq_ref, dkey_ref, dvalue_ref, drel_ref, vec_ref, datt_ref,
    )


def attention_back_first(pairs, common, bias, table, deps):
    two, width = common[1].shape
    length, size = two // 2, len(pairs) * LANES
    outs = [
        ("v", (two, size), BF), ("v", (size, length), BF), ("v", (size, length), BF), ("v", (size, two), BF), ("v", (8, size), F32),
    ]
    ins = [("v", common[0])] + [("v", x) for x in (*common[1:], bias, table)]
    kernel = functools.partial(attention_back_first_kernel, pairs)
    return call(kernel, outs, ins, deps, [pltpu.VMEM((two, size), BF)], "attention_back_first", 12 * 10**9)


def attention_back_kernel(
    pairs, wo_ref, dproj_ref, q_ref, att_ref, key_ref, value_ref, prob_one, prob_two, relrev_ref, half_ref, bias_ref, seg_ref,
    left_x_ref, left_rev_ref, left_att_ref, dq_one, dkey_one, dvalue_one, drel_one, vec_one, norm_one, norm_two, hidden_ref,
    dq_ref, dkey_ref, dvalue_ref, keep_out, send_out, datt_ref, drel_ref, vec_ref, packed_ref,
):
    length, width = key_ref.shape
    split = width // 2
    size = dq_one.shape[1]
    dq_ref[:, :size], dkey_ref[:size], dvalue_ref[:size], drel_ref[:size] = dq_one[...], dkey_one[...], dvalue_one[...], drel_one[...]
    vec_ref[...] = jnp.zeros_like(vec_ref)
    vec_ref[:, :size] = vec_one[...]
    back_pairs(
        pairs, dproj_ref, wo_ref, q_ref, att_ref, key_ref, value_ref, prob_one, prob_two, relrev_ref, half_ref, bias_ref,
        seg_ref, dq_ref.at[:, size:], dkey_ref.at[size:], dvalue_ref.at[size:], drel_ref.at[size:], vec_ref.at[:, size:], datt_ref,
    )
    shards = hidden_ref.shape[1] // width
    packed_ref[...] = jnp.zeros_like(packed_ref)
    packed_ref[0:5, :] = vec_ref[0:5, :]
    packed_ref[5:6, :] = norm_one[0:1, :]
    packed_ref[6:7, :] = norm_two[0:1, :]
    packed_ref[7:8, :] = norm_one[1:2, :]
    packed_ref[8:10, :] = norm_two[1:3, :]
    for shard in range(shards):
        place = 10 + (lax.axis_index("tensor") ^ shard)
        packed_ref[pl.ds(place, 1), :] = hidden_ref[0:1, shard * width : (shard + 1) * width]
    packed = packed_ref[...].astype(BF)
    for out in (send_out, keep_out):
        out.ref[split:, :width] = packed
        out.ref[split:, width:] = jnp.zeros((16, 4 * width), BF)
        out.send(pl.ds(split, 16))
    todo = [
        (left_x_ref[...], dq_ref, nn), (left_x_ref[:, :length], dkey_ref, nt), (left_x_ref[:, :length], dvalue_ref, nt),
        (left_att_ref[...], dproj_ref, nn), (left_rev_ref[...], drel_ref, nt),
    ]
    at = 0
    for left, right, dot in todo:
        count = right.shape[1] if dot is nn else right.shape[0]
        for col in range(0, count, 256):
            cols = slice(col, col + 256)
            piece = dot(left, right[:, cols] if dot is nn else right[cols, :]).astype(BF)
            keep_out.ref[:split, at + col : at + col + 256] = piece[:split]
            send_out.ref[:split, at + col : at + col + 256] = piece[split:]
        done = pl.ds(at, count)
        send_out.send(pl.ds(0, split), done)
        keep_out.send(pl.ds(0, split), done)
        at += count


def attention_back(pairs, common, lefts, first, vectors, bias, table, deps):
    two, width = common[1].shape
    length, size = two // 2, len(pairs) * LANES
    outs = [
        ("v", (two, width), BF), ("v", (width, length), BF), ("v", (width, length), BF),
        ("e", (width // 2 + 16, 5 * width), BF), ("e", (width // 2 + 16, 5 * width), BF),
    ]
    ins = [("v", common[0])] + [("v", x) for x in (*common[1:], bias, table, *lefts, *first, *vectors)]
    scratch = [
        pltpu.VMEM((two, size), BF), pltpu.VMEM((width, two), BF), pltpu.VMEM((8, width), F32), pltpu.VMEM((16, width), F32),
    ]
    return call(functools.partial(attention_back_kernel, pairs), outs, ins, deps, scratch, "attention_back", 12 * 10**9)


def input_grads_kernel(wq_late, wk_late, wv_late, dq_ref, dkey_ref, dvalue_ref, dresid_ref, grad_h, grad_g, sum_ref):
    length, width = grad_h.ref.shape
    wq_ref = wq_late.get()
    for col in range(0, width, 256):
        cols = slice(col, col + 256)
        low = nt(dq_ref[...], wq_ref[cols, :])
        sum_ref[:, cols] = dresid_ref[:length, cols] + low[:length]
        grad_g.ref[:, cols] = dresid_ref[length:, cols] + low[length:]
    grad_g.send()
    dkey, dvalue = dkey_ref[...].astype(F32).T.astype(BF), dvalue_ref[...].astype(F32).T.astype(BF)
    wk_ref, wv_ref = wk_late.get(), wv_late.get()
    for col in range(0, width, 256):
        cols = slice(col, col + 256)
        grad_h.ref[:, cols] = sum_ref[:, cols] + nt(dkey, wk_ref[cols, :]) + nt(dvalue, wv_ref[cols, :])
    grad_h.send()


def input_grads(wq, wk, wv, dq, dkey, dvalue, dresid, deps):
    two, width = dresid.shape
    outs = [("e", (two // 2, width), F32), ("e", (two // 2, width), F32)]
    ins = [("l", wq), ("l", wk), ("l", wv), ("v", dq), ("v", dkey), ("v", dvalue), ("v", dresid)]
    scratch = [pltpu.VMEM((two // 2, width), F32)]
    return call(input_grads_kernel, outs, ins, deps, scratch, "input_grads", 10**9)


def share_kernel(parts, up_hbm, down_hbm, bias_ref, out_ref, sem):
    rows = up_hbm.shape[0] // parts
    start = pl.multiple_of(lax.axis_index("dp") * rows, rows) if parts > 1 else 0
    one = pltpu.make_async_copy(up_hbm.at[pl.ds(start, rows)], out_ref.at[pl.ds(0, rows)], sem.at[0])
    two = pltpu.make_async_copy(down_hbm.at[pl.ds(start, rows)], out_ref.at[pl.ds(rows, rows)], sem.at[1])
    one.start()
    two.start()
    out_ref[2 * rows :, :] = jnp.broadcast_to(bias_ref[...], (16, bias_ref.shape[1]))
    one.wait()
    two.wait()


def share_slices(parts, up, down, bias):
    rows, width = up.shape[0] // parts, up.shape[1]
    outs = [("v", (2 * rows + 16, width), BF)]
    ins = [("b", up), ("b", down), ("v", bias)]
    return call(functools.partial(share_kernel, parts), outs, ins, (), [pltpu.SemaphoreType.DMA((2,))], "share_slices", 10**7)[0]


def start_pieces(pieces, piece_refs, target_ref, sem):
    copies = []
    for count, ((block, rows), source) in enumerate(zip(pieces, piece_refs, strict=True)):
        where = 0
        if rows < target_ref.shape[1]:
            where = pl.multiple_of((lax.axis_index("dp") ^ block) * rows, rows)
        copies.append(pltpu.make_async_copy(source, target_ref.at[:, pl.ds(where, rows)], sem.at[count]))
        copies[-1].start()
    return copies


def gelu_parts(pre):
    root = math.sqrt(2.0 / math.pi)
    square = pre * pre
    bend = jnp.tanh(root * pre * (1.0 + 0.044715 * square))
    upper = 0.5 + 0.5 * bend
    slope = upper + (0.5 * root) * pre * (1.0 - bend * bend) * (1.0 + (3 * 0.044715) * square)
    return (pre * upper).astype(BF), slope.astype(BF)


def feed_up_own_kernel(mid_ref, up_late, bias_ref, act_ref, slope_ref):
    width = mid_ref.shape[1]
    up_ref = up_late.get()
    for col in range(0, width, 256):
        cols = slice(col, col + 256)
        bias = bias_ref[0:1, cols].astype(F32)
        act_ref[:, cols], slope_ref[:, cols] = gelu_parts(nn(mid_ref[...], up_ref[:, cols]) + bias)


def feed_up_own(mid, up, bias, deps):
    outs = [("v", mid.shape, BF), ("v", mid.shape, BF)]
    return call(feed_up_own_kernel, outs, [("v", mid), ("l", up), ("v", bias)], deps, [], "feed_up_own", 3 * 10**9)


def feed_up_kernel(shards, pieces, rows, mid_ref, *refs):
    bias_refs, piece_refs = refs[: shards - 1], refs[shards - 1 : shards - 1 + len(pieces)]
    act_ref, slope_ref, up_ref, bias_ref, in_sem, bias_sem = refs[shards - 1 + len(pieces) :]
    width = mid_ref.shape[1]
    copies = start_pieces(pieces, piece_refs, up_ref, in_sem)
    biases = [
        pltpu.make_async_copy(ref.at[pl.ds(rows, 16)], bias_ref.at[shard], bias_sem.at[shard])
        for shard, ref in enumerate(bias_refs)
    ]
    for copy in biases:
        copy.start()
    for copy in biases:
        copy.wait()
    for copy in copies:
        copy.wait()
    for shard in range(shards - 1):
        for col in range(0, width, 256):
            cols = slice(shard * width + col, shard * width + col + 256)
            pre = nn(mid_ref[...], up_ref[shard, :, col : col + 256])
            act_ref[:, cols], slope_ref[:, cols] = gelu_parts(
                pre + bias_ref[shard, 0:1, col : col + 256].astype(F32)
            )


def feed_up(shards, mid, rows, biases, pieces, deps):
    rows_all, width = mid.shape
    hidden = (shards - 1) * width
    names = [entry[:-1] for entry in pieces]
    outs = [("v", (rows_all, hidden), BF), ("v", (rows_all, hidden), BF), ("v", (shards - 1, width, width), BF)]
    ins = [("v", mid)] + [("h", value) for value in biases] + [("h", entry[-1]) for entry in pieces]
    scratch = [
        pltpu.VMEM((shards - 1, 16, width), BF), pltpu.SemaphoreType.DMA((len(names),)), pltpu.SemaphoreType.DMA((shards - 1,)),
    ]
    return call(functools.partial(feed_up_kernel, shards, names, rows), outs, ins, deps, scratch, "feed_up", 6 * 10**9)


def feed_down_kernel(parts, shards, pieces, own_down, dh_ref, dg_ref, act_own, resid_ref, act_rest, *refs):
    down_bias, gain_ref, shift_ref = refs[:3]
    piece_refs = refs[3 : 3 + len(pieces)]
    out_h, out_g, dresid_ref, dbranch_ref, keep_out, send_out, vec_ref, down_ref, raw_ref, left_ref, in_sem = refs[3 + len(pieces) :]
    rows_all, width = resid_ref.shape
    length = rows_all // 2
    split = width // 2
    copies = start_pieces(pieces, piece_refs, down_ref, in_sem)
    for col in range(0, width, 256):
        cols = slice(col, col + 256)
        dresid_ref[:, cols] = nn(act_own[...], own_down[:, cols])
    for copy in copies:
        copy.wait()
    down_all = down_ref.reshape((shards - 1) * width, width)
    for col in range(0, width, 256):
        cols = slice(col, col + 256)
        dresid_ref[:, cols] += nn(act_rest[...], down_all[:, cols])
    gain_one, gain_two = gain_ref[0:1, :width], gain_ref[0:1, width:]
    shift_one, shift_two = shift_ref[0:1, :width], shift_ref[0:1, width:]
    step_rows = 32
    sums = [jnp.zeros((step_rows, width), F32)] * 3
    for row in range(0, rows_all, step_rows):
        rows = slice(row, row + step_rows)
        grad_ref = dh_ref if row < length else dg_ref
        near = row % length
        xhat_one, _ = norm_stats(resid_ref[rows, :])
        middle = xhat_one * gain_one + shift_one
        xhat, rstd = norm_stats(middle + dresid_ref[rows, :] + down_bias[...])
        out = out_h if row < length else out_g
        out.ref[near : near + step_rows, :] = (xhat * gain_two + shift_two).astype(BF)
        grad = grad_ref[near : near + step_rows, :].astype(F32)
        dresid = norm_back(grad, xhat, rstd, gain_two)
        dresid_ref[rows, :] = dresid
        dbranch = dresid.astype(BF)
        dbranch_ref[rows, :] = dbranch
        sums = [sums[0] + grad * xhat, sums[1] + grad, sums[2] + dbranch.astype(F32)]
    vec_ref[...] = jnp.zeros_like(vec_ref)
    for at, total in enumerate(sums):
        vec_ref[at : at + 1, :] = jnp.sum(total, axis=0, keepdims=True)
    out_h.send()
    out_g.send()
    turn_rows(lambda col: dbranch_ref[:, col : col + 256], raw_ref, left_ref, parts)
    for source, count, offset in ((act_own, 1, 0), (act_rest, shards - 1, width)):
        for col in range(0, count * width, 256):
            piece = nn(left_ref[...], source[:, col : col + 256]).astype(BF)
            cols = slice(col + offset, col + offset + 256)
            keep_out.ref[:, cols] = piece[:split]
            send_out.ref[:, cols] = piece[split:]
            if (col + 256) % width == 0:
                done = pl.ds(col + offset + 256 - width, width)
                send_out.send(slice(None), done)
                keep_out.send(slice(None), done)


def feed_down(parts, shards, own_down, act_own, act_rest, resid_one, down_bias, gains, shifts, dh, dg, pieces, deps):
    rows_all, width = resid_one.shape
    hidden = shards * width
    names = [entry[:-1] for entry in pieces]
    outs = [
        ("e", dh.shape, BF), ("e", dg.shape, BF), ("v", (rows_all, width), F32), ("v", (rows_all, width), BF),
        ("e", (width // 2, hidden), BF), ("e", (width // 2, hidden), BF), ("v", (8, width), F32), ("v", (shards - 1, width, width), BF),
    ]
    ins = [("v", own_down), ("v", dh), ("v", dg)]
    ins += [("v", value) for value in (act_own, resid_one, act_rest, down_bias, gains, shifts)] + [("h", entry[-1]) for entry in pieces]
    scratch = [pltpu.VMEM((width, rows_all), BF), pltpu.VMEM((width, rows_all), BF), pltpu.SemaphoreType.DMA((len(names),))]
    return call(functools.partial(feed_down_kernel, parts, shards, names), outs, ins, deps, scratch, "feed_down", 8 * 10**9)


def left_columns(width):
    return width // 3


def feed_back_up_kernel(
    parts, shards, own_down, mid_ref, dbranch_ref, down_ref, slope_own, slope_rest,
    dpre_ref, keep_out, send_out, dbias_ref, raw_ref, left_ref,
):
    rows_all, width = mid_ref.shape
    split, side = width // 2, left_columns(width)
    turn_rows(lambda col: mid_ref[:, col : col + 256], raw_ref, left_ref, parts)
    for shard in range(shards):
        for col in range(0, width, 256):
            cols = slice(shard * width + col, shard * width + col + 256)
            if shard:
                near = (shard - 1) * width + col
                weight, slope = down_ref[shard - 1, col : col + 256, :], slope_rest[:, near : near + 256]
            else:
                weight, slope = own_down[col : col + 256, :], slope_own[:, col : col + 256]
            dpre = (nt(dbranch_ref[...], weight) * slope.astype(F32)).astype(BF)
            dpre_ref[:, cols] = dpre
            dbias_ref[:, cols] = jnp.sum(dpre.astype(F32), axis=0, keepdims=True)
            piece = nn(left_ref[...], dpre).astype(BF)
            for at in range(col, col + 256, LANES):
                if at < side:
                    to = shard * side + at
                else:
                    to = shards * side + shard * (width - side) + at - side
                part = slice(at - col, at - col + LANES)
                keep_out.ref[:, to : to + LANES] = piece[:split, part]
                send_out.ref[:, to : to + LANES] = piece[split:, part]
        for start, size in ((shard * side, side), (shards * side + shard * (width - side), width - side)):
            done = pl.ds(start, size)
            send_out.send(slice(None), done)
            keep_out.send(slice(None), done)


def feed_back_up(parts, shards, own_down, down_rest, dbranch, mid, slope_own, slope_rest, deps):
    rows_all, width = mid.shape
    hidden = shards * width
    outs = [("v", (rows_all, hidden), BF), ("e", (width // 2, hidden), BF), ("e", (width // 2, hidden), BF), ("v", (1, hidden), F32)]
    ins = [("v", own_down)] + [("v", value) for value in (mid, dbranch, down_rest, slope_own, slope_rest)]
    scratch = [pltpu.VMEM((width, rows_all), BF), pltpu.VMEM((width, rows_all), BF)]
    return call(functools.partial(feed_back_up_kernel, parts, shards), outs, ins, deps, scratch, "feed_back_up", 8 * 10**9)


def feed_back_mid_kernel(shards, own_late, dpre_ref, up_ref, dresid_ref, resid_ref, gain_ref, dproj_ref, dresid_one_ref, vec_ref):
    rows_all, width = dresid_one_ref.shape
    own_up = own_late.get()
    for col in range(0, width, 256):
        cols = slice(col, col + 256)
        total = nt(dpre_ref[:, :width], own_up[cols, :])
        for shard in range(1, shards):
            total += nt(dpre_ref[:, shard * width : (shard + 1) * width], up_ref[shard - 1, cols, :])
        dresid_one_ref[:, cols] = total
    gain_one = gain_ref[0:1, :width]
    step_rows = 32
    sums = [jnp.zeros((step_rows, width), F32)] * 2
    for row in range(0, rows_all, step_rows):
        rows = slice(row, row + step_rows)
        xhat, rstd = norm_stats(resid_ref[rows, :])
        grad = dresid_ref[rows, :] + dresid_one_ref[rows, :]
        dresid = norm_back(grad, xhat, rstd, gain_one)
        dresid_one_ref[rows, :] = dresid
        dproj_ref[rows, :] = dresid.astype(BF)
        sums = [sums[0] + grad * xhat, sums[1] + grad]
    vec_ref[...] = jnp.zeros_like(vec_ref)
    for at, total in enumerate(sums):
        vec_ref[at : at + 1, :] = jnp.sum(total, axis=0, keepdims=True)


def feed_back_mid(shards, own_up, up_rest, dpre, dresid, resid_one, gains, deps):
    rows_all, width = resid_one.shape
    outs = [("v", (rows_all, width), BF), ("v", (rows_all, width), F32), ("v", (8, width), F32)]
    ins = [("l", own_up)] + [("v", value) for value in (dpre, up_rest, dresid, resid_one, gains)]
    return call(functools.partial(feed_back_mid_kernel, shards), outs, ins, deps, [], "feed_back_mid", 5 * 10**9)


def pack_rows_kernel(count, rows, *refs):
    one_ref, two_ref, sem = refs[count:]
    copies = [
        pltpu.make_async_copy(ref.at[pl.ds(half * rows, rows)], out.at[at], sem.at[half, at])
        for half, out in enumerate((one_ref, two_ref))
        for at, ref in enumerate(refs[:count])
    ]
    for copy in copies:
        copy.start()
    for copy in copies:
        copy.wait()


def pack_rows(arrays, rows, deps):
    outs = [("v", (len(arrays), rows, arrays[0].shape[1]), BF)] * 2
    scratch = [pltpu.SemaphoreType.DMA((2, len(arrays)))]
    kernel = functools.partial(pack_rows_kernel, len(arrays), rows)
    return call(kernel, outs, [("h", value) for value in arrays], deps, scratch, "pack_rows", 10**6)


def combine(arrays, outs, deps=(), name="combine_late"):
    outs = [(rows, cols, [(*part, 0, cols)[:5] for part in parts]) for rows, cols, parts in outs]
    ranges = {}
    for _, _, parts in outs:
        for _, count, sources, _, cols in parts:
            for source, row, col in sources:
                low, high = ranges.get((source, row, count), (col, col + cols))
                ranges[source, row, count] = (min(low, col), max(high, col + cols))
    buffers = [pltpu.VMEM((count, high - low), BF) for (_, _, count), (low, high) in ranges.items()]

    def kernel(*refs):
        out_refs = refs[len(arrays) : len(arrays) + len(outs)]
        *held, sem = refs[len(arrays) + len(outs) :]
        copies = {}
        for at, ((source, row, count), (low, high)) in enumerate(ranges.items()):
            piece = refs[source].at[pl.ds(row, count), pl.ds(low, high - low)]
            copies[source, row, count] = (pltpu.make_async_copy(piece, held[at], sem.at[at]), held[at], low)
            copies[source, row, count][0].start()
        waited = set()
        for (_, _, parts), out_ref in zip(outs, out_refs, strict=True):
            for first, count, sources, to, cols in parts:
                values = []
                for source, row, col in sources:
                    copy, buffer, low = copies[source, row, count]
                    if (source, row, count) not in waited:
                        copy.wait()
                        waited.add((source, row, count))
                    values.append(buffer[:, col - low : col - low + cols])
                out_ref[first : first + count, to : to + cols] = add_all(values).astype(BF)

    shapes = [("v", (rows, cols), BF) for rows, cols, _ in outs]
    scratch = [*buffers, pltpu.SemaphoreType.DMA((len(buffers),))]
    return call(kernel, shapes, [("b", value) for value in arrays], deps, scratch, name, 10**9 if name == "combine_left" else 10**6)


def regroup_kernel(shards, keep_ref, core_ref, first_a, first_b, second_a, second_b, *refs):
    outs, (held_wide, held_a, held_b, group_ref, sem, out_sem) = refs[:shards], refs[shards:]
    rows, total = held_wide.shape[1] - 16, held_wide.shape[2]
    width = total // 5
    part = width // shards
    copies = [
        pltpu.make_async_copy(ref.at[pl.ds(0, rows)], held.at[pl.ds(0, rows)], sem.at[at])
        for at, (ref, held) in enumerate(
            (
                (keep_ref, held_wide.at[0]), (core_ref, held_wide.at[1]), (first_a, held_a.at[0]), (first_b, held_b.at[0]),
                (second_a, held_a.at[1]), (second_b, held_b.at[1]),
            )
        )
    ]
    copies += [
        pltpu.make_async_copy(ref.at[pl.ds(ref.shape[0] - 16, 16)], held.at[pl.ds(rows, 16)], sem.at[6 + at])
        for at, (ref, held) in enumerate(
            ((keep_ref, held_wide.at[0]), (core_ref, held_wide.at[1]), (first_a, held_a.at[0]), (second_a, held_a.at[1]))
        )
    ]
    for copy in copies:
        copy.start()
    for copy in copies:
        copy.wait()
    sums = []
    for half, held in enumerate((held_a, held_b)):
        cols = slice(half * total // 2, (half + 1) * total // 2)
        value = held_wide[0, :rows, cols].astype(F32) + held_wide[1, :rows, cols].astype(F32)
        sums.append(value + held[0, :rows].astype(F32) + held[1, :rows].astype(F32))
    whole = jnp.concatenate(sums, axis=1)
    vectors = [held[at, rows:, :width].astype(F32) for held in (held_wide, held_a) for at in (0, 1)]
    vectors = add_all(vectors).astype(BF)
    for shard in range(shards):
        for slot in range(5):
            at = slot * width + shard * part
            group_ref[shard, :rows, slot * part : (slot + 1) * part] = whole[:, at : at + part].astype(BF)
        group_ref[shard, rows:, :width] = vectors
        group_ref[shard, rows:, width:] = jnp.zeros((16, 5 * part - width), BF)
    me = lax.axis_index("tensor")
    backs = [pltpu.make_async_copy(group_ref.at[me ^ bits], outs[bits], out_sem.at[bits]) for bits in range(shards)]
    for back in backs:
        back.start()
    for back in backs:
        back.wait()


def regroup(shards, keep, core, first, second, deps=()):
    total = keep.shape[1]
    rows = second[0].shape[0]
    shape = (rows, total // shards)
    scratch = [
        pltpu.VMEM((2, rows, total), BF), pltpu.VMEM((2, rows, total // 2), BF), pltpu.VMEM((2, rows, total // 2), BF),
        pltpu.VMEM((shards, *shape), BF), pltpu.SemaphoreType.DMA((10,)), pltpu.SemaphoreType.DMA((shards,)),
    ]
    ins = [("b", value) for value in (keep, core, *first, *second)]
    outs = [("b", shape, BF)] * shards
    return call(functools.partial(regroup_kernel, shards), outs, ins, deps, scratch, "regroup", 10**6)


class Exchange:
    def __init__(self, width):
        self.data = lax.axis_size("dp")
        self.tensor = lax.axis_size("tensor")
        self.by_hand = self.data == 8 and width % (32 * self.data) == 0
        self.blocks = self.data if self.by_hand else 1

    def data_swap(self, value, bit):
        pairs = [(at, at ^ bit) for at in range(self.data)]
        return lax.ppermute(value, "dp", pairs)

    def tensor_swap(self, value, bits):
        pairs = [(at, at ^ bits) for at in range(self.tensor)]
        return lax.ppermute(value, "tensor", pairs)


def add_low(left, right):
    return (left.astype(F32) + right.astype(F32)).astype(BF)


class Share:
    def __init__(self, swap, rows, first):
        self.swap, self.rows, self.first = swap, rows, first
        self.count = swap.tensor - 1

    def spread(self, packed):
        self.found = [(0, packed)]
        if self.swap.blocks > 1:
            bits = [1 << at for at in range(1, self.swap.data.bit_length() - 1)]
            mine = self.found[0][1]
            self.near = [(bit, self.swap.data_swap(mine, bit)) for bit in bits]
            self.found += self.near

    def cross(self):
        if self.swap.data == 8 and self.swap.blocks == 8:
            other = 6 - self.first
            self.found.append((6, self.swap.data_swap(dict(self.near)[self.first], other)))

    def finish(self):
        found = list(self.found)
        if self.swap.blocks > 1:
            found += [(block | 1, self.swap.data_swap(value, 1)) for block, value in self.found]
        return [(block, self.rows, value) for block, value in found]


def add_all(terms):
    total = terms[0].astype(F32)
    for term in terms[1:]:
        total += term.astype(F32)
    return total


def tensor_sum(swap, parts):
    return add_all([parts[0]] + [swap.tensor_swap(parts[bits], bits) for bits in range(1, swap.tensor)])


def per_device(
    h_in, g_in, seg_ids, target_flags, perm_order, w_query, w_key, w_value, w_out, w_rel, attn_bias, seg_embed,
    norm_gain, norm_bias, w_up, b_up, w_down, b_down, d_h_out, d_g_out,
):
    seq_count, length, width = h_in.shape
    assert seq_count == 1
    swap = Exchange(width)
    parts, shards = swap.blocks, swap.tensor
    by_hand = swap.by_hand
    dp_at, tensor_at = lax.axis_index("dp"), lax.axis_index("tensor")
    own_part = width // shards
    rel_host = rel_table(length, width)
    rel, rev = jnp.asarray(rel_host), jnp.asarray(np.ascontiguousarray(rel_host[::-1]))
    h, g = h_in[0], g_in[0]
    up, down = w_up[0], w_down[0]
    bias, table = attn_bias.reshape(1, -1), seg_embed.reshape(1, -1)
    gains, shifts = norm_gain.reshape(1, -1), norm_bias.reshape(1, -1)

    mine = share_slices(parts, up, down, b_up)
    rows = (mine.shape[0] - 16) // 2
    fetched = [swap.tensor_swap(mine, bits) for bits in range(1, shards)]
    share_up, share_down = Share(swap, rows, 2), Share(swap, rows, 4)
    q, key, value, relkey, mask, half, relrev, left_x, left_rev = project(
        parts, h, g, seg_ids, target_flags, perm_order, w_query[0], w_key[0], w_value[0], w_rel[0], rel, rev, ()
    )
    att_one, prob_one = attention_first(q, key, value, relkey, mask, half, bias, table, ())
    packed_up, packed_down = pack_rows(fetched, rows, [att_one])
    share_up.spread(packed_up)
    share_down.spread(packed_down)
    resid_one, mid, prob_two, att, left_att = attention_second(
        parts, w_out[0], h, g, q, key, value, relkey, mask, half, att_one, bias, table, gains, shifts,
        [share_up.found[0][1], share_down.found[0][1]],
    )
    if by_hand:
        share_up.near = [(bit, lax.optimization_barrier((value, mid))[0]) for bit, value in share_up.near]
    share_up.cross()
    act_own, slope_own = feed_up_own(mid, up, b_up, [found for _, found in share_up.found[:3]])
    share_down.cross()
    act_rest, slope_rest, up_rest = feed_up(
        shards, mid, 2 * rows, fetched, share_up.finish(), [found for _, found in share_down.found]
    )
    out_h, out_g, dresid_two, dbranch, keep_down, send_down, vec_two, down_rest = feed_down(
        parts, shards, down, act_own, act_rest, resid_one, b_down, gains, shifts, d_h_out[0], d_g_out[0],
        share_down.finish(), (),
    )

    hidden, wide = shards * width, 5 * width
    block, middle = width // 8, width // 4
    size = (10 + shards) * width

    def first_far(keep, core, deps, name):
        cut = keep.shape[1] // 2
        odd = [(at, block, [(0, block + 2 * at, 0), (1, block + 2 * at, 0)]) for at in (0, block)]
        upper = [(0, middle, [(0, middle, cut), (1, middle, cut)])]
        more = keep.shape[0] - 2 * middle
        if more:
            odd.append((middle, more, [(0, 2 * middle, 0), (1, 2 * middle, 0)]))
        return combine([keep, core], [(middle + more, cut, odd), (middle, cut, upper)], deps, name)

    def first_swap(far):
        return swap.data_swap(far[0], 2), swap.data_swap(far[1], 4)

    def second_far(keep, core, first, deps, name):
        cut = keep.shape[1] // 2
        more = keep.shape[0] - 2 * middle
        upper = [(0, block, [(0, middle, 0), (1, middle, 0), (2, block, 0)])]
        if more:
            upper.append((block, more, [(0, 2 * middle, 0), (1, 2 * middle, 0), (2, middle, 0)]))
        return combine(
            [keep, core, *first],
            [
                (block + more, cut, upper),
                (block, cut, [(0, block, [(0, block, cut), (1, block, cut), (3, block, 0)])]),
            ],
            deps,
            name,
        )

    def second_swap(far):
        return swap.data_swap(far[0], 4), swap.data_swap(far[1], 2)

    if by_hand:
        core_down = swap.data_swap(send_down, 1)
    dpre, keep_up, send_up, dbias_up = feed_back_up(parts, shards, down, down_rest, dbranch, mid, slope_own, slope_rest, ())
    deps = ()
    if by_hand:
        core_up = swap.data_swap(send_up, 1)
        far_down = first_far(keep_down, core_down, (), "combine")
        first_down = first_swap(far_down)
        side = left_columns(width)
        rest = width - side
        cut, quarter = shards * side, shards * rest // 2
        odd = [(at, block, [(0, block + 2 * at, cut), (1, block + 2 * at, cut)]) for at in (0, block)]
        far_up = combine(
            [keep_up, core_up],
            [
                *((2 * middle, side, [(0, 2 * middle, [(0, 0, k * side), (1, 0, k * side)])]) for k in range(1, shards)),
                (middle, quarter, odd),
                (middle, quarter, [(0, middle, [(0, middle, cut + quarter), (1, middle, cut + quarter)])]),
            ],
            far_down,
            "combine",
        )
        came_up = [swap.tensor_swap(far_up[bits - 1], bits) for bits in range(1, shards)]
        first_up = first_swap(far_up[-2:])
        deps = far_up[-1:]
    dproj, dresid_one, vec_one = feed_back_mid(shards, up, up_rest, dpre, dresid_two, resid_one, gains, deps)
    common = (w_out[0], dproj, q, att, key, value, prob_one, prob_two, relrev, half)
    back_first = attention_back_first(tuple(range(PAIRS // 2)), common, bias, table, ())
    deps = ()
    if by_hand:
        far_down = second_far(keep_down, core_down, first_down, back_first[-1:], "combine")
        second_down = second_swap(far_down)
        deps = far_down
    dq, dkey, dvalue, keep_att, send_att = attention_back(
        tuple(range(PAIRS // 2, PAIRS)), common, (left_x, left_rev, left_att), back_first, (vec_one, vec_two, dbias_up),
        bias, table, [*deps, *came_up] if by_hand else deps,
    )
    if by_hand:
        (send_att, keep_att), (first_up, second_down) = lax.optimization_barrier(
            ((send_att, keep_att), (first_up, second_down))
        )
        core_att = swap.data_swap(send_att, 1)
        all_up = [keep_up, core_up, *came_up]
        left = range(len(all_up))
        far_up = combine(
            [*all_up, *first_up],
            [
                (block, quarter, [(0, block, [(0, middle, cut), (1, middle, cut), (shards + 1, block, 0)])]),
                (block, quarter, [(0, block, [(0, block, cut + quarter), (1, block, cut + quarter), (shards + 2, block, 0)])]),
                (middle, side, [(0, middle, [(at, middle, 0) for at in left])]),
            ],
        )
        second_up = second_swap(far_up[:2])
        left_y = swap.data_swap(far_up[2], 4)
        far_att = first_far(keep_att, core_att, second_up, "combine_late")
        first_att = first_swap(far_att)
        arrays = [keep_down, core_down, *first_down, *second_down, *all_up, *first_up, *second_up]
        up_at, per, outs = 6, shards // 2, []
        half_at = up_at + len(all_up)
        for k in range(shards):
            half, near = k // per, k % per
            outs.append(
                (
                    block,
                    width + rest,
                    [
                        (0, block, [(0, 0, k * width), (1, 0, k * width), (2 + half, 0, near * width), (4 + half, 0, near * width)],
                         0, width),
                        (0, block, [(up_at, 0, cut + k * rest), (up_at + 1, 0, cut + k * rest), (half_at + half, 0, near * rest),
                                    (half_at + 2 + half, 0, near * rest)], width, rest),
                    ],
                )
            )
        feed_parts = combine(arrays, outs, far_att)
        came = [swap.tensor_swap(feed_parts[bits], bits) for bits in range(1, shards)]
        grad_h, grad_g = input_grads(w_query[0], w_key[0], w_value[0], dq, dkey, dvalue, dresid_one, feed_parts[:1])
        far_att = second_far(keep_att, core_att, first_att, [*came[:1], grad_h], "combine_att")
        second_att = second_swap(far_att)
        left_own, far_left = combine(
            [*all_up, left_y],
            [(block, side, [(0, block, [(at, row, 0) for at in range(shards + 2)])]) for row in (0, block)],
            [*far_att],
            "combine_left",
        )
        left_x = swap.data_swap(far_left, 2)
        att_parts = regroup(shards, keep_att, core_att, first_att, second_att, came)
    else:
        grad_h, grad_g = input_grads(w_query[0], w_key[0], w_value[0], dq, dkey, dvalue, dresid_one, ())
        vectors = lax.psum(keep_att[width // 2 : width // 2 + 10 + shards, :width].astype(F32), AXES)
        keep_att, send_att = keep_att[: width // 2], send_att[: width // 2]

        def rows_sum(keep, send):
            whole = jnp.concatenate([keep, send], axis=0)
            return lax.psum_scatter(whole, "dp", scatter_dimension=0, tiled=True)

        sum_up, sum_down, sum_att = (
            rows_sum(keep, send) for keep, send in ((keep_up, send_up), (keep_down, send_down), (keep_att, send_att))
        )
        cols = [slice(shard * width, (shard + 1) * width) for shard in range(shards)]
        side = left_columns(width)
        left, right = sum_up[:, : shards * side], sum_up[:, shards * side :]
        rest = width - side
        d_up = [
            jnp.concatenate([left[:, k * side : (k + 1) * side], right[:, k * rest : (k + 1) * rest]], axis=1)
            for k in range(shards)
        ]
        d_up = tensor_sum(swap, d_up)
        d_down = tensor_sum(swap, [sum_down[:, part] for part in cols]).T
        split = sum_att.reshape(-1, 5, shards, own_part).transpose(2, 0, 1, 3).reshape(shards, -1, 5 * own_part)
        att_parts = [lax.dynamic_index_in_dim(split, tensor_at ^ bits, 0, keepdims=False) for bits in range(shards)]
    att_parts = [att_parts[0]] + [swap.tensor_swap(att_parts[bits], bits) for bits in range(1, shards)]
    if by_hand:
        came, _ = lax.optimization_barrier((came, att_parts[1]))
        d_feed = add_all([feed_parts[0], *came])
        d_up = jnp.concatenate([add_all([left_own, left_x]), d_feed[:, width:]], axis=1)
        d_down = d_feed[:, :width].T
        (d_up, d_down), att_parts = lax.optimization_barrier(((d_up, d_down), att_parts))
    d_att = add_all(att_parts)
    if by_hand:
        d_att, vectors = d_att[:block], d_att[block : block + 10 + shards, :width]
    d_att = [d_att[:, slot * own_part : (slot + 1) * own_part] for slot in range(5)]

    own = size // (swap.data * shards)
    d_vectors = lax.dynamic_slice_in_dim(vectors.reshape(-1), (dp_at * shards + tensor_at) * own, own, 0)

    return (
        out_h[None], out_g[None], grad_h[None], grad_g[None],
        d_att[0][None], d_att[1][None], d_att[2][None], d_att[3][None], d_att[4][None],
        d_up[None], d_down[None], d_vectors[None],
    )


def solution(mesh):
    every = P(AXES, None, None)
    rows = P(AXES, None)
    in_specs = (
        every, every, rows, rows, rows, P(), P(), P(), P(), P(), P(), P(), P(), P(),
        P(None, None, "tensor"), P(None, "tensor"), P(None, "tensor", None), P(), every, every,
    )
    grads = P(None, "dp", "tensor")
    out_specs = (
        every, every, every, every, grads, grads, grads, grads, grads, grads,
        P(None, "tensor", "dp"), P(None, AXES),
    )
    return jax.shard_map(per_device, mesh=mesh, in_specs=in_specs, out_specs=out_specs, check_vma=False)
```
